32 devices in a mesh: seq: 16 (over z, y, x), tp: 2 (over core).
Axes of the slice: x: 2, y: 2, z: 4, core: 2. Of those that a mesh axis runs over, the one named last changes fastest.
Arguments:
- activations: float32 [2, 1024, 1024], P(None, 'seq'), may hold values from -6 to 6
- cotangent: float32 [2, 1024, 1024], P(None, 'seq')
- segment_ids: int32 [2, 1024], P(None, 'seq'), may hold values from 0 to 7, as said below
- position_ids: int32 [2, 1024], P(None, 'seq'), may hold values from 0 to 2046, as said below
- qkv_weight: float32 [2, 1024, 3, 1024], P(None, 'seq', None, 'tp')
- out_weight: float32 [2, 1024, 1024], P(None, 'seq', 'tp')
- in_weight: float32 [2, 1024, 4096], P(None, 'seq', 'tp')
- down_weight: float32 [2, 1024, 4096], P(None, 'seq', 'tp')
- norm_params: float32 [2, 3, 1024], P(None, None, 'seq')
- qkv_first: float32 [2, 1024, 3, 1024], P(None, 'seq', None, 'tp'), may hold values from -0.4375 to 0.4375
- out_first: float32 [2, 1024, 1024], P(None, 'seq', 'tp'), may hold values from -0.4375 to 0.4375
- in_first: float32 [2, 1024, 4096], P(None, 'seq', 'tp'), may hold values from -0.4375 to 0.4375
- down_first: float32 [2, 1024, 4096], P(None, 'seq', 'tp'), may hold values from -0.4375 to 0.4375
- norm_first: float32 [2, 3, 1024], P(None, None, 'seq'), may hold values from -1.5 to 1.5
- qkv_second: float32 [2, 1024, 3, 1024], P(None, 'seq', None, 'tp'), may hold values from 6.25e-05 to 0.00025
- out_second: float32 [2, 1024, 1024], P(None, 'seq', 'tp'), may hold values from 6.25e-05 to 0.00025
- in_second: float32 [2, 1024, 4096], P(None, 'seq', 'tp'), may hold values from 2e-05 to 8e-05
- down_second: float32 [2, 1024, 4096], P(None, 'seq', 'tp'), may hold values from 6.25e-05 to 0.00025
- norm_second: float32 [2, 3, 1024], P(None, None, 'seq'), may hold values from 0.0008 to 0.0032
Outputs:
- result: float32 [2, 1024, 1024], P(None, 'seq')
- input_grad: float32 [2, 1024, 1024], P(None, 'seq')
- grad_norm: float32 [], replicated
- qkv_new: float32 [2, 1024, 3, 1024], P(None, 'seq', None, 'tp')
- out_new: float32 [2, 1024, 1024], P(None, 'seq', 'tp')
- in_new: float32 [2, 1024, 4096], P(None, 'seq', 'tp')
- down_new: float32 [2, 1024, 4096], P(None, 'seq', 'tp')
- norm_new: float32 [2, 3, 1024], P(None, None, 'seq')
- qkv_first_new: float32 [2, 1024, 3, 1024], P(None, 'seq', None, 'tp')
- out_first_new: float32 [2, 1024, 1024], P(None, 'seq', 'tp')
- in_first_new: float32 [2, 1024, 4096], P(None, 'seq', 'tp')
- down_first_new: float32 [2, 1024, 4096], P(None, 'seq', 'tp')
- norm_first_new: float32 [2, 3, 1024], P(None, None, 'seq')
- qkv_second_new: float32 [2, 1024, 3, 1024], P(None, 'seq', None, 'tp')
- out_second_new: float32 [2, 1024, 1024], P(None, 'seq', 'tp')
- in_second_new: float32 [2, 1024, 4096], P(None, 'seq', 'tp')
- down_second_new: float32 [2, 1024, 4096], P(None, 'seq', 'tp')
- norm_second_new: float32 [2, 3, 1024], P(None, None, 'seq')
- bias_clipped: float32 [2, 1024], P(None, 'seq')
The draws below stay inside these ranges and needn't reach their ends.
Inputs may be any that keep to these rules, and one draw needn't show every extreme that they name: `segment_ids`: in every row the protein numbers start at 0 and never fall along the row; one of the 2 rows holds a single protein, every other row exactly 8 proteins. `position_ids`: within a protein the positions start at 0 and rise by 1 or 2 from one residue to the next; in the row that holds a single protein they rise by 2.
All inputs are finite; a program needn't handle non-finite values.
Results may differ from the reference program's by a relative error of at most 0.03.
The reference program's roundings to bfloat16 on the way count: a program that leaves them out, or rounds other values in their place, can miss the bound.
Values may be sent and summed in bfloat16 or wider, within the bound.
A program may use at most 192 MiB of HBM per device.

```python
import math
import jax
import jax.numpy as jnp
from jax import lax

D = 1024
FF = 4096
HEAD = 64
ROTARY = 32
LAYERS = 2
ROWS = 2
KEY_BLOCK = 512
STEP = 10
LENGTH = 1024
NPARAM = 25171968


border_count = 7


def shared_segments(key):
    border_key, whole_key = jax.random.split(key)
    row_keys = jax.random.split(border_key, ROWS)

    def pick_borders(row_key):
        return jax.random.permutation(row_key, LENGTH - 1)[:border_count] + 1
    chosen = jax.vmap(pick_borders)(row_keys).astype(jnp.int32)
    boundary = jnp.zeros((ROWS, LENGTH), jnp.int32)
    boundary = boundary.at[jnp.arange(ROWS)[:, None], chosen].set(1)
    whole_row = jax.random.randint(whole_key, (), 0, ROWS)
    is_whole = jnp.arange(ROWS)[:, None] == whole_row
    boundary = jnp.where(is_whole, 0, boundary)
    return (jnp.cumsum(boundary, axis=1).astype(jnp.int32), is_whole)


def draw_segment_ids(key, part):
    segments, is_whole = shared_segments(key)
    return segments


def draw_position_ids(key, part):
    segments, is_whole = shared_segments(key)
    key = jax.random.fold_in(key, 5)
    strides = jax.random.randint(key, (ROWS, LENGTH), 1, 3)
    strides = jnp.where(is_whole, 2, strides)
    climbed = jnp.cumsum(strides, axis=1).astype(jnp.int32)
    columns = jnp.broadcast_to(jnp.arange(LENGTH, dtype=jnp.int32), (ROWS, LENGTH))
    starts = jnp.concatenate([jnp.ones((ROWS, 1), dtype=bool), segments[:, 1:] != segments[:, :-1]], axis=1)
    start_col = lax.cummax(jnp.where(starts, columns, 0), axis=1)
    offsets = jnp.take_along_axis(climbed, start_col, axis=1)
    return (climbed - offsets).astype(jnp.int32)


def rising_normal(key, extent, fan_in, low_end, high_end):
    samples = jax.random.normal(key, extent, jnp.float32)
    growth = low_end + (high_end - low_end) * jnp.arange(extent[-1], dtype=jnp.float32) / (extent[-1] - 1)
    return samples * growth / jnp.sqrt(jnp.float32(fan_in))


def draw_qkv_weight(key, part):
    key = jax.random.fold_in(key, 21)
    return rising_normal(key, (LAYERS, D, 3, D), D, 0.75, 1.3)


def draw_out_weight(key, part):
    key = jax.random.fold_in(key, 22)
    return rising_normal(key, (LAYERS, D, D), D // 16, 0.75, 1.3)


def draw_in_weight(key, part):
    key = jax.random.fold_in(key, 23)
    return rising_normal(key, (LAYERS, D, FF), D, 0.75, 1.3)


def draw_down_weight(key, part):
    key = jax.random.fold_in(key, 24)
    return rising_normal(key, (LAYERS, D, FF), FF, 0.75, 1.3)


def draw_norm_params(key, part):
    key = jax.random.fold_in(key, 25)
    gain_key, bias_key = jax.random.split(key)
    place = jnp.arange(D, dtype=jnp.float32) / (D - 1)
    gains = (0.6 + 1.2 * place) * jax.random.uniform(gain_key, (LAYERS, D), jnp.float32, 0.8, 1.2)
    shifts = 0.3 * jax.random.normal(bias_key, (LAYERS, 2, D), jnp.float32)
    return jnp.concatenate([gains[:, None, :], shifts], axis=1)


def draw_cotangent(key, part):
    key = jax.random.fold_in(key, 26)
    place = jnp.arange(D, dtype=jnp.float32) / (D - 1)
    samples = jax.random.normal(key, (ROWS, LENGTH, D), jnp.float32)
    return samples * (0.6 + 1.2 * place)


def steps_of(key, shape, shards, smallest, largest):
    def one(position, blocks):
        draws = jax.random.uniform(jax.random.fold_in(jax.random.fold_in(key, 6), position), (blocks,), jnp.float32, smallest / len(shards), largest / len(shards))
        return jnp.repeat(jnp.exp(draws), shape[position] // blocks).reshape((-1,) + (1,) * (len(shape) - position - 1))

    factor_of = one(*shards[0])
    for cut in shards[1:]:
        factor_of = factor_of * one(*cut)
    return factor_of


def scatter_about(stream_key, dims, deviation, most, cuts=(), kind=jnp.bfloat16):
    loudness = steps_of(stream_key, dims, cuts, -0.22, 0.18) if cuts else 1.0
    values = jax.random.normal(stream_key, dims, jnp.float32) * deviation * loudness
    return jnp.minimum(jnp.maximum(values, -most), most).astype(kind)


def setup_inputs(seed: int = 0) -> dict:
    key_of = jax.random.split(jax.random.key(seed), 20)
    return {
        "activations": scatter_about(key_of[0], (ROWS, LENGTH, D), 1.0, 6.0, ((1, 16),), jnp.float32),
        "cotangent": draw_cotangent(jax.random.fold_in(key_of[19], 71), 0),
        "segment_ids": draw_segment_ids(jax.random.fold_in(key_of[19], 71), 0),
        "position_ids": draw_position_ids(jax.random.fold_in(key_of[19], 71), 0),
        "qkv_weight": draw_qkv_weight(jax.random.fold_in(key_of[19], 71), 0),
        "out_weight": draw_out_weight(jax.random.fold_in(key_of[19], 71), 0),
        "in_weight": draw_in_weight(jax.random.fold_in(key_of[19], 71), 0),
        "down_weight": draw_down_weight(jax.random.fold_in(key_of[19], 71), 0),
        "norm_params": draw_norm_params(jax.random.fold_in(key_of[19], 71), 0),
        "qkv_first": scatter_about(key_of[9], (LAYERS, D, 3, D), (0.25 / 9), 0.4375, ((1, 16), (3, 2)), jnp.float32),
        "out_first": scatter_about(key_of[10], (LAYERS, D, D), (0.25 / 9), 0.4375, ((1, 16), (2, 2)), jnp.float32),
        "in_first": scatter_about(key_of[11], (LAYERS, D, FF), (0.25 / 9), 0.4375, ((1, 16), (2, 2)), jnp.float32),
        "down_first": scatter_about(key_of[12], (LAYERS, D, FF), (0.25 / 9), 0.4375, ((1, 16), (2, 2)), jnp.float32),
        "norm_first": scatter_about(key_of[13], (LAYERS, 3, D), 0.1, 1.5, ((2, 16),), jnp.float32),
        "qkv_second": jnp.clip(jnp.exp(math.log(0.00025) - 1.3862944 * jax.random.uniform(key_of[14], (LAYERS, D, 3, D), jnp.float32) ** steps_of(key_of[14], (LAYERS, D, 3, D), ((1, 16), (3, 2)), -0.2, 0.2)), 6.25000029685907e-05, 0.00025),
        "out_second": jnp.clip(jnp.exp(math.log(0.00025) - 1.3862944 * jax.random.uniform(key_of[15], (LAYERS, D, D), jnp.float32) ** steps_of(key_of[15], (LAYERS, D, D), ((1, 16), (2, 2)), -0.2, 0.2)), 6.25000029685907e-05, 0.00025),
        "in_second": jnp.clip(jnp.exp(math.log(7.999999797903001e-05) - 1.3862944 * jax.random.uniform(key_of[16], (LAYERS, D, FF), jnp.float32) ** steps_of(key_of[16], (LAYERS, D, FF), ((1, 16), (2, 2)), -0.2, 0.2)), 1.9999999494757503e-05, 7.999999797903001e-05),
        "down_second": jnp.clip(jnp.exp(math.log(0.00025) - 1.3862944 * jax.random.uniform(key_of[17], (LAYERS, D, FF), jnp.float32) ** steps_of(key_of[17], (LAYERS, D, FF), ((1, 16), (2, 2)), -0.2, 0.2)), 6.25000029685907e-05, 0.00025),
        "norm_second": jnp.clip(jnp.exp(math.log(0.0032) - 1.3862944 * jax.random.uniform(key_of[18], (LAYERS, 3, D), jnp.float32) ** steps_of(key_of[18], (LAYERS, 3, D), ((2, 16),), -0.2, 0.2)), 0.0008, 0.0032),
    }


norm_eps = 1e-05
beta_one = 0.9
beta_two = 0.999
adam_eps = 1e-08
rate_matrix = 0.05
rate_output = 0.15
rate_vector = 1.0
decay_matrix = 0.1
clip_share = 0.25
low_score = -1e+30

@jax.custom_vjp
def low(v):
    return lax.optimization_barrier(v.astype(jnp.bfloat16)).astype(jnp.float32)

@jax.custom_vjp
def low_back(v):
    return v

def low_keep(v):
    return (low(v), None)

def low_pass(kept, grad):
    return (grad,)

def back_keep(v):
    return (v, None)

def back_low(kept, grad):
    return (low(grad),)
low.defvjp(low_keep, low_pass)
low_back.defvjp(back_keep, back_low)

def layer_norm(inputs, gain_row, shift_row):
    average = lax.optimization_barrier(jnp.mean(inputs, axis=-1, keepdims=True))
    centred = inputs - average
    spread = lax.optimization_barrier(jnp.mean(centred * centred, axis=-1, keepdims=True))
    return centred * lax.rsqrt(spread + norm_eps) * gain_row + shift_row

def rotary_tables(positions, columns_total):
    column = jnp.arange(columns_total) % HEAD
    inside = column < ROTARY
    pair_index = column % ROTARY // 2
    frequency = jnp.exp(pair_index.astype(jnp.float32) * (-2.0 * math.log(10000.0) / ROTARY))
    angles = positions.astype(jnp.float32)[..., None] * frequency
    cosine = jnp.where(inside, jnp.cos(angles), 1.0)
    signed = jnp.where(column % 2 == 0, -1.0, 1.0)
    sine = jnp.where(inside, signed * jnp.sin(angles), 0.0)
    return (cosine, sine)

def swap_pairs(values):
    extent = values.shape
    paired = values.reshape(extent[:-1] + (extent[-1] // 2, 2))
    return jnp.flip(paired, axis=-1).reshape(extent)

def rotate(values, cosine, sine):
    return values * cosine + swap_pairs(values) * sine

def attend_block(key_rows, value_rows, key_segments, block_queries, block_places, block_segments):
    key_places = jnp.arange(key_rows.shape[0])
    scores = jnp.einsum('qhd,khd->hqk', block_queries, key_rows, precision=lax.Precision.HIGHEST) * HEAD ** (-0.5)
    scores = low_back(scores)
    causal = key_places[None, :] <= block_places[:, None]
    matching = block_segments[:, None] == key_segments[None, :]
    allowed = (causal & matching)[None]
    scores = jnp.where(allowed, scores, low_score)
    peak_score = lax.optimization_barrier(jnp.max(scores, axis=-1, keepdims=True))
    weights = jnp.where(allowed, jnp.exp(scores - peak_score), 0.0)
    shares = weights / lax.optimization_barrier(jnp.sum(weights, axis=-1, keepdims=True))
    return jnp.einsum('hqk,khd->qhd', low(shares), value_rows, precision=lax.Precision.HIGHEST)

def attend_row(row_items):
    queries, key_rows, value_rows, segments = row_items
    length = queries.shape[0]
    blocks = length // KEY_BLOCK
    places = jnp.arange(length)
    checked = jax.checkpoint(attend_block)

    def one_block(block_items):
        block_queries, block_places, block_segments = block_items
        return checked(key_rows, value_rows, segments, block_queries, block_places, block_segments)
    outputs = lax.map(one_block, (queries.reshape((blocks, KEY_BLOCK) + queries.shape[1:]), places.reshape(blocks, KEY_BLOCK), segments.reshape(blocks, KEY_BLOCK)))
    return outputs.reshape(queries.shape)

def one_layer(inputs, qkv_matrix, out_matrix, in_matrix, down_matrix, norm_rows, segments, cosine, sine):
    highest = lax.Precision.HIGHEST
    normed = low(layer_norm(inputs, norm_rows[0], norm_rows[1]))
    mixed = jnp.einsum('rtd,dcn->rtcn', normed, qkv_matrix, precision=highest)
    queries = low(rotate(low_back(mixed[:, :, 0]), cosine, sine))
    key_rows = low(rotate(low_back(mixed[:, :, 1]), cosine, sine))
    value_rows = low(low_back(mixed[:, :, 2]))
    head_count = queries.shape[-1] // HEAD
    extent = queries.shape[:2] + (head_count, HEAD)
    outputs = lax.map(attend_row, (queries.reshape(extent), key_rows.reshape(extent), value_rows.reshape(extent), segments))
    outputs = low(low_back(outputs.reshape(queries.shape)))
    attend_part = jnp.einsum('rtn,dn->rtd', outputs, out_matrix, precision=highest)
    hidden = low_back(jnp.einsum('rtd,df->rtf', normed, in_matrix, precision=highest))
    active = low(jax.nn.gelu(hidden, approximate=True))
    feed_part = jnp.einsum('rtf,df->rtd', active, down_matrix, precision=highest)
    return inputs + low_back(attend_part + feed_part) + norm_rows[2]

def adam_update(weight, first, second, gradient, factor_clip, rate, decay):
    clipped = gradient * factor_clip
    first_new = beta_one * first + (1.0 - beta_one) * clipped
    second_new = beta_two * second + (1.0 - beta_two) * clipped * clipped
    first_hat = first_new / (1.0 - beta_one ** STEP)
    second_hat = second_new / (1.0 - beta_two ** STEP)
    weight_new = weight - rate * (first_hat / (jnp.sqrt(second_hat) + adam_eps) + decay * weight)
    return (weight_new, first_new, second_new)

def reference(activations, cotangent, segment_ids, position_ids, qkv_weight, out_weight, in_weight, down_weight, norm_params, qkv_first, out_first, in_first, down_first, norm_first, qkv_second, out_second, in_second, down_second, norm_second):
    cosine, sine = rotary_tables(position_ids, D)

    def apply_layers(inputs, qkv_matrix, out_matrix, in_matrix, down_matrix, norm_matrix):
        qkv_low = low(qkv_matrix)
        out_low = low(out_matrix)
        in_low = low(in_matrix)
        down_low = low(down_matrix)
        norm_low = low(norm_matrix)
        current = inputs
        for layer_index in range(LAYERS):
            current = one_layer(current, qkv_low[layer_index], out_low[layer_index], in_low[layer_index], down_low[layer_index], norm_low[layer_index], segment_ids, cosine, sine)
        return current
    result, pull_back = jax.vjp(apply_layers, activations, qkv_weight, out_weight, in_weight, down_weight, norm_params)
    gradients = pull_back(cotangent)
    input_grad = gradients[0]
    weight_grads = gradients[1:]
    total_squares = sum((jnp.sum(grad_block * grad_block) for grad_block in weight_grads))
    grad_norm = jnp.sqrt(total_squares)
    factor_clip = jnp.minimum(1.0, clip_share * math.sqrt(NPARAM) / (grad_norm + 1e-06))
    qkv_new, qkv_first_new, qkv_second_new = adam_update(qkv_weight, qkv_first, qkv_second, weight_grads[0], factor_clip, rate_matrix, decay_matrix)
    out_new, out_first_new, out_second_new = adam_update(out_weight, out_first, out_second, weight_grads[1], factor_clip, rate_output, decay_matrix)
    in_new, in_first_new, in_second_new = adam_update(in_weight, in_first, in_second, weight_grads[2], factor_clip, rate_matrix, decay_matrix)
    down_new, down_first_new, down_second_new = adam_update(down_weight, down_first, down_second, weight_grads[3], factor_clip, rate_matrix, decay_matrix)
    norm_new, norm_first_new, norm_second_new = adam_update(norm_params, norm_first, norm_second, weight_grads[4], factor_clip, rate_vector, 0.0)
    bias_clipped = weight_grads[4][:, 2] * factor_clip
    return (result, input_grad, grad_norm, qkv_new, out_new, in_new, down_new, norm_new, qkv_first_new, out_first_new, in_first_new, down_first_new, norm_first_new, qkv_second_new, out_second_new, in_second_new, down_second_new, norm_second_new, bias_clipped)
```

```python
import functools
import math

import jax
import jax.numpy as jnp
from jax import lax
from jax.experimental import pallas as pl
from jax.experimental.pallas import tpu as pltpu
from jax.sharding import PartitionSpec as P

HEAD = 64
ROTARY = 32
LAYERS = 2
STEP = 10
TILE = 256

norm_eps = 1e-05
beta_one = 0.9
beta_two = 0.999
adam_eps = 1e-08
rate_matrix = 0.05
rate_output = 0.15
rate_vector = 1.0
decay_matrix = 0.1
clip_share = 0.25
low_score = -1e30

MESH = pl.DeviceIdType.MESH
VM = pltpu.VMEM
DMA = pltpu.SemaphoreType.DMA
bf16 = jnp.bfloat16
f32 = jnp.float32
megabyte = 1 << 20


def split_sizes(members):
    nb = 1 << ((members.bit_length() - 1) // 2)
    return (members // nb, nb)


class Place:
    def __init__(self, n, rows):
        self.n, self.rows = n, rows
        self.members = n // rows
        self.na, self.nb = split_sizes(self.members)
        self.seq = lax.axis_index("seq")
        self.core = lax.axis_index("tp")
        self.row = lax.rem(self.seq, rows)
        self.member = self.seq // rows
        self.a = self.member // self.nb
        self.b = lax.rem(self.member, self.nb)

    def am(self, step):
        return lax.rem(self.a + step, self.na)

    def bm(self, step):
        return lax.rem(self.b + step, self.nb)

    def device(self, member, row=None, core=None):
        row = self.row if row is None else row
        return {"seq": member * self.rows + row, "tp": self.core if core is None else core}

    def at(self, a, b):
        return self.device(a * self.nb + b)

    def sibling(self):
        return self.device(self.member, core=1 - self.core)

    def partners(self):
        return [self.device(self.member, row=lax.rem(self.row + i, self.rows)) for i in range(1, self.rows)]

    def axis_peers(self):
        peers = [self.at(self.am(i), self.b) for i in range(1, self.na)]
        peers += [self.at(self.a, self.bm(j)) for j in range(1, self.nb)]
        return peers

    def other_members(self):
        return [self.device(lax.rem(self.member + i, self.members)) for i in range(1, self.members)]


def greet(devices):
    barrier = pltpu.get_barrier_semaphore()
    for device in devices:
        pl.semaphore_signal(barrier, inc=1, device_id=device, device_id_type=MESH)
    pl.semaphore_wait(barrier, len(devices))


class Sender:
    def __init__(self, send_sems):
        self.send_sems, self.copies = send_sems, []

    def send(self, src, dst, recv_sem, device):
        copy = pltpu.make_async_remote_copy(
            src_ref=src,
            dst_ref=dst,
            send_sem=self.send_sems.at[len(self.copies)],
            recv_sem=recv_sem,
            device_id=device,
            device_id_type=MESH,
        )
        copy.start()
        self.copies.append(copy)

    def arrived(self, dst, recv_sem, device):
        pltpu.make_async_remote_copy(
            src_ref=dst,
            dst_ref=dst,
            send_sem=self.send_sems.at[0],
            recv_sem=recv_sem,
            device_id=device,
            device_id_type=MESH,
        ).wait_recv()

    def finish(self):
        for copy in self.copies:
            copy.wait_send()


def remote_params(collective_id):
    return pltpu.CompilerParams(
        collective_id=collective_id, has_side_effects=True, vmem_limit_bytes=56 * megabyte
    )


def vmem_specs(count):
    return [pl.BlockSpec(memory_space=VM)] * count


def spread_kernel(n, rows, wide_ref, small_ref, pack_ref, chunk_ref, table_ref, weight_ref, *sems):
    (send_sems, chunk_sems, table_sems, block_sems, cross_sems, local_sems) = sems
    p = Place(n, rows)
    members = p.members
    everybody = [
        {"seq": lax.rem(p.seq + i, n), "tp": p.core} for i in range(1, n)
    ]
    greet(everybody)
    sender = Sender(send_sems)
    partners = [
        (lax.rem(p.row + i, rows), p.device(p.member, row=lax.rem(p.row + i, rows)))
        for i in range(1, rows)
    ]
    for device in everybody:
        sender.send(small_ref, table_ref.at[p.seq], table_sems.at[p.seq], device)
    for row, device in partners:
        sender.send(wide_ref.at[row], chunk_ref.at[p.row], chunk_sems.at[p.row], device)
    for layer in range(LAYERS):
        for i in range(1, members):
            member = lax.rem(p.member + i, members)
            sender.send(
                pack_ref.at[layer, member],
                weight_ref.at[layer, p.seq],
                block_sems.at[layer, p.member],
                p.device(member),
            )
        for row, device in partners:
            sender.send(
                pack_ref.at[layer, p.member],
                weight_ref.at[layer, p.seq],
                cross_sems.at[layer, p.seq],
                device,
            )
    own = [
        pltpu.make_async_copy(small_ref, table_ref.at[p.seq], local_sems.at[0]),
        pltpu.make_async_copy(wide_ref.at[p.row], chunk_ref.at[p.row], local_sems.at[1]),
    ]
    for layer in range(LAYERS):
        own.append(
            pltpu.make_async_copy(
                pack_ref.at[layer, p.member], weight_ref.at[layer, p.seq], local_sems.at[2 + layer]
            )
        )
    for copy in own:
        copy.start()
    for layer in range(LAYERS):
        for i in range(1, members):
            member = lax.rem(p.member + members - i, members)
            block = weight_ref.at[layer, member * rows + p.row]
            sender.arrived(block, block_sems.at[layer, member], p.sibling())
            for row, device in partners:
                sender.send(block, block, cross_sems.at[layer, member * rows + p.row], device)
    for i in range(1, n):
        seq = lax.rem(p.seq + i, n)
        sender.arrived(table_ref.at[seq], table_sems.at[seq], p.sibling())
    for row, device in partners:
        sender.arrived(chunk_ref.at[row], chunk_sems.at[row], p.sibling())
    for layer in range(LAYERS):
        for i in range(members):
            member = lax.rem(p.member + members - i, members)
            for row, device in partners:
                block = weight_ref.at[layer, member * rows + row]
                sender.arrived(block, cross_sems.at[layer, member * rows + row], p.sibling())
    sender.finish()
    for copy in own:
        copy.wait()


def spread(n, rows, wide, small, pack, collective_id):
    layers, members, height, columns = pack.shape
    sends = (n - 1) + (rows - 1) + layers * (members - 1 + members * (rows - 1))
    return pl.pallas_call(
        functools.partial(spread_kernel, n, rows),
        out_shape=(
            jax.ShapeDtypeStruct(wide.shape, wide.dtype),
            jax.ShapeDtypeStruct((n,) + small.shape, small.dtype),
            jax.ShapeDtypeStruct((layers, n, height, columns), pack.dtype),
        ),
        in_specs=vmem_specs(3),
        out_specs=tuple(vmem_specs(3)),
        scratch_shapes=[
            DMA((sends,)),
            DMA((rows,)),
            DMA((n,)),
            DMA((layers, members)),
            DMA((layers, n)),
            DMA((2 + layers,)),
        ],
        compiler_params=remote_params(collective_id),
        name="spread_inputs",
    )(wide, small, pack)


def gather_kernel(n, rows, count, x_ref, out_ref, *sems):
    send_sems, a_sems, b_sems, core_sems, local_sem = sems
    p = Place(n, rows)
    na, nb, core = p.na, p.nb, p.core
    sibling = p.sibling()
    greet(p.axis_peers() + [sibling])
    sender = Sender(send_sems)
    a_steps = [1, na - 1] + list(range(2, na - 1)) if na > 2 else [1]

    def slot(k, a, b):
        return out_ref.at[k, a * nb + b, core]

    for k in range(count):
        mine = x_ref.at[k, core]
        for i in a_steps:
            sender.send(mine, slot(k, p.a, p.b), a_sems.at[k, p.a], p.at(p.am(i), p.b))
        for j in range(1, nb):
            sender.send(mine, slot(k, p.a, p.b), b_sems.at[k, p.member], p.at(p.a, p.bm(j)))
    own = pltpu.make_async_copy(x_ref, out_ref.at[:, p.member], local_sem)
    own.start()
    for k in range(count):
        for i in a_steps:
            a = p.am(i)
            here = slot(k, a, p.b)
            sender.arrived(here, a_sems.at[k, a], sibling)
            for j in range(1, nb):
                sender.send(here, here, b_sems.at[k, a * nb + p.b], p.at(p.a, p.bm(j)))
            sender.send(here, here, core_sems.at[k, a * nb + p.b], sibling)
    for k in range(count):
        for i in [0] + a_steps:
            for j in range(1, nb):
                a, b = p.am(i), p.bm(j)
                here = slot(k, a, b)
                sender.arrived(here, b_sems.at[k, a * nb + b], sibling)
                sender.send(here, here, core_sems.at[k, a * nb + b], sibling)
    for k in range(count):
        for i in range(1, p.members):
            member = lax.rem(p.member + i, p.members)
            sender.arrived(out_ref.at[k, member, 1 - core], core_sems.at[k, member], sibling)
    sender.finish()
    own.wait()


def gather(n, rows, pieces, collective_id):
    stacked = jnp.stack(pieces)
    count, two, height, width = stacked.shape
    members = n // rows
    na, nb = split_sizes(members)
    sends = count * ((na - 1) * (nb + 1) + nb - 1 + na * (nb - 1))
    return pl.pallas_call(
        functools.partial(gather_kernel, n, rows, count),
        out_shape=jax.ShapeDtypeStruct((count, members, two, height, width), stacked.dtype),
        in_specs=vmem_specs(1),
        out_specs=vmem_specs(1)[0],
        scratch_shapes=[
            DMA((sends,)),
            DMA((count, na)),
            DMA((count, members)),
            DMA((count, members)),
            DMA,
        ],
        compiler_params=remote_params(collective_id),
        name="gather_tokens",
    )(stacked)


def reduce_kernel(n, rows, count, *refs):
    x_refs, (out_ref, core_buf, b_buf, a_buf, b_out, a_out) = refs[:count], refs[count : count + 6]
    send_sems, core_sems, b_sems, a_sems, out_sems = refs[count + 6 :]
    p = Place(n, rows)
    na, nb, core = p.na, p.nb, p.core
    sibling = p.sibling()
    greet(p.axis_peers() + [sibling])
    sender = Sender(send_sems)
    a_steps = list(range(2, na - 1)) + [1, na - 1, 0] if na > 2 else [1, 0]
    for k in range(count):
        for i in a_steps:
            for j in list(range(1, nb)) + [0]:
                m = p.am(i) * nb + p.bm(j)
                sender.send(x_refs[k].at[m, 1 - core], core_buf.at[k, m], core_sems.at[k, m], sibling)
    for k in range(count):
        for i in a_steps:
            for j in range(1, nb):
                a, b = p.am(i), p.bm(j)
                m = a * nb + b
                sender.arrived(core_buf.at[k, m], core_sems.at[k, m], sibling)
                b_out[k, m] = (x_refs[k][m, core].astype(f32) + core_buf[k, m].astype(f32)).astype(bf16)
                landing = a * nb + p.b
                sender.send(b_out.at[k, m], b_buf.at[k, landing], b_sems.at[k, landing], p.at(p.a, b))
    for k in range(count):
        for i in a_steps:
            a = p.am(i)
            m = a * nb + p.b
            sender.arrived(core_buf.at[k, m], core_sems.at[k, m], sibling)
            total = x_refs[k][m, core].astype(f32) + core_buf[k, m].astype(f32)
            for j in range(1, nb):
                q = a * nb + p.bm(j)
                sender.arrived(b_buf.at[k, q], b_sems.at[k, q], sibling)
                total = total + b_buf[k, q].astype(f32)
            if i:
                a_out[k, a] = total.astype(bf16)
                sender.send(a_out.at[k, a], a_buf.at[k, p.a], a_sems.at[k, p.a], p.at(a, p.b))
            else:
                out_ref[k, core] = total
    for k in range(count):
        for i in range(1, na):
            a = p.am(i)
            sender.arrived(a_buf.at[k, a], a_sems.at[k, a], sibling)
            out_ref[k, core] += a_buf[k, a].astype(f32)
        sender.send(out_ref.at[k, core], out_ref.at[k, core], out_sems.at[k], sibling)
    for k in range(count):
        sender.arrived(out_ref.at[k, 1 - core], out_sems.at[k], sibling)
    sender.finish()


def reduce(n, rows, pieces, collective_id):
    count = len(pieces)
    members, two, height, width = pieces[0].shape
    na, nb = split_sizes(members)
    sends = count * (members + na * (nb - 1) + na)
    return pl.pallas_call(
        functools.partial(reduce_kernel, n, rows, count),
        out_shape=jax.ShapeDtypeStruct((count, two, height, width), f32),
        in_specs=vmem_specs(count),
        out_specs=vmem_specs(1)[0],
        scratch_shapes=[
            VM((count, members, height, width), bf16),
            VM((count, members, height, width), bf16),
            VM((count, na, height, width), bf16),
            VM((count, members, height, width), bf16),
            VM((count, na, height, width), bf16),
            DMA((sends,)),
            DMA((count, members)),
            DMA((count, members)),
            DMA((count, na)),
            DMA((count,)),
        ],
        compiler_params=remote_params(collective_id),
        name="reduce_tokens",
    )(*pieces)


def collect_kernel(n, rows, *refs):
    (first_ref, second_ref, wide_ref, small_ref, grad_ref, back_ref, table_ref) = refs[:7]
    (cross_buf, block_out, send_sems, cross_sems, block_sems, back_sems, table_sems, local_sems) = refs[7:]
    grads = (first_ref, second_ref)
    p = Place(n, rows)
    members = p.members
    everybody = [{"seq": lax.rem(p.seq + i, n), "tp": p.core} for i in range(1, n)]
    greet(everybody)
    sender = Sender(send_sems)
    partners = [
        (lax.rem(p.row + i, rows), p.device(p.member, row=lax.rem(p.row + i, rows)))
        for i in range(1, rows)
    ]
    order = [lax.rem(p.member + i, members) for i in range(1, members)] + [p.member]
    for i in range(1, n):
        seq = lax.rem(p.seq + i, n)
        sender.send(small_ref.at[seq], table_ref.at[p.seq], table_sems.at[p.seq], {"seq": seq, "tp": p.core})
    for layer in range(LAYERS):
        for member in order:
            for row, device in partners:
                sender.send(
                    grads[layer].at[member * rows + row],
                    cross_buf.at[layer, p.row, member],
                    cross_sems.at[layer, p.row, member],
                    device,
                )
    for row, device in partners:
        sender.send(wide_ref.at[row], back_ref.at[p.row], back_sems.at[p.row], device)
    own = [
        pltpu.make_async_copy(small_ref.at[p.seq], table_ref.at[p.seq], local_sems.at[0]),
        pltpu.make_async_copy(wide_ref.at[p.row], back_ref.at[p.row], local_sems.at[1]),
    ]
    for copy in own:
        copy.start()
    for layer in range(LAYERS):
        for i in list(range(1, members)) + [0]:
            member = lax.rem(p.member + i, members)
            total = grads[layer][member * rows + p.row].astype(f32)
            for row, device in partners:
                buffer = cross_buf.at[layer, row, member]
                sender.arrived(buffer, cross_sems.at[layer, row, member], p.sibling())
                total = total + buffer[...].astype(f32)
            if i:
                block_out[layer, member] = total.astype(bf16)
                sender.send(
                    block_out.at[layer, member],
                    grad_ref.at[layer, p.member],
                    block_sems.at[layer, p.member],
                    p.device(member),
                )
            else:
                grad_ref[layer, member] = total.astype(bf16)
    for i in range(1, n):
        seq = lax.rem(p.seq + i, n)
        sender.arrived(table_ref.at[seq], table_sems.at[seq], p.sibling())
    for row, device in partners:
        sender.arrived(back_ref.at[row], back_sems.at[row], p.sibling())
    for layer in range(LAYERS):
        for i in range(1, members):
            member = lax.rem(p.member + members - i, members)
            sender.arrived(grad_ref.at[layer, member], block_sems.at[layer, member], p.sibling())
    sender.finish()
    for copy in own:
        copy.wait()


def collect(n, rows, first, second, wide, small, collective_id):
    unused, height, columns = first.shape
    members = n // rows
    sends = (n - 1) + (rows - 1) + LAYERS * (members * (rows - 1) + members - 1)
    return pl.pallas_call(
        functools.partial(collect_kernel, n, rows),
        out_shape=(
            jax.ShapeDtypeStruct((LAYERS, members, height, columns), bf16),
            jax.ShapeDtypeStruct(wide.shape, wide.dtype),
            jax.ShapeDtypeStruct(small.shape, small.dtype),
        ),
        in_specs=vmem_specs(4),
        out_specs=tuple(vmem_specs(3)),
        scratch_shapes=[
            VM((LAYERS, rows, members, height, columns), bf16),
            VM((LAYERS, members, height, columns), bf16),
            DMA((sends,)),
            DMA((LAYERS, rows, members)),
            DMA((LAYERS, members)),
            DMA((rows,)),
            DMA((n,)),
            DMA((2,)),
        ],
        compiler_params=remote_params(collective_id),
        name="collect_gradients",
    )(first, second, wide, small)


def share_kernel(n, x_ref, out_ref, send_sems, recv_sems, local_sem):
    seq, core = lax.axis_index("seq"), lax.axis_index("tp")
    others = []
    for i in range(n):
        for j in range(2):
            if i or j:
                others.append((lax.rem(seq + i, n), lax.rem(core + j, 2)))
    greet([{"seq": s, "tp": c} for s, c in others])
    sender = Sender(send_sems)
    here = seq * 2 + core
    for s, c in others:
        sender.send(x_ref, out_ref.at[here], recv_sems.at[here], {"seq": s, "tp": c})
    own = pltpu.make_async_copy(x_ref, out_ref.at[here], local_sem)
    own.start()
    for s, c in others:
        sender.arrived(out_ref.at[s * 2 + c], recv_sems.at[s * 2 + c], {"seq": s, "tp": c})
    sender.finish()
    own.wait()


def share(n, x, collective_id):
    return pl.pallas_call(
        functools.partial(share_kernel, n),
        out_shape=jax.ShapeDtypeStruct((2 * n,) + x.shape, x.dtype),
        in_specs=vmem_specs(1),
        out_specs=vmem_specs(1)[0],
        scratch_shapes=[DMA((2 * n,)), DMA((2 * n,)), DMA],
        compiler_params=remote_params(collective_id),
        name="share_squares",
    )(x)


def dot(left, right):
    return jnp.dot(left, right, preferred_element_type=f32)


def dot_nt(left, right):
    return lax.dot_general(left, right, (((1,), (1,)), ((), ())), preferred_element_type=f32)


def dot_tn(left, right):
    return lax.dot_general(left, right, (((0,), (0,)), ((), ())), preferred_element_type=f32)


def swap_lanes(values):
    width = values.shape[-1]
    lane = lax.broadcasted_iota(jnp.int32, values.shape, 1)
    after = pltpu.roll(values, width - 1, 1)
    before = pltpu.roll(values, 1, 1)
    return jnp.where(lane % 2 == 0, after, before)


gelu_scale = 0.7978845608
gelu_cubic = 0.044715


def gelu(z):
    return 0.5 * z * (1.0 + jnp.tanh(gelu_scale * (z + gelu_cubic * z * z * z)))


def gelu_slope(z):
    inner = jnp.tanh(gelu_scale * (z + gelu_cubic * z * z * z))
    slope = gelu_scale * (1.0 + 3.0 * gelu_cubic * z * z)
    return 0.5 * (1.0 + inner) + 0.5 * z * (1.0 - inner * inner) * slope


def query_tiles(length, share, rows):
    tile = max(64, min(TILE, TILE * 1024 // length))
    first = 0
    if share > 1:
        first = lax.rem(lax.axis_index("seq") // rows, share) * (length // share)
    for i in range(length // share // tile):
        start = pl.multiple_of(first + i * tile, tile) if share > 1 else i * tile
        yield pl.ds(start, tile), start, ((i + 1) * tile if share == 1 else length)


def visible(start, keys, seg_col, seg_row):
    tile = seg_col.shape[0]
    place = start + lax.broadcasted_iota(jnp.int32, (tile, keys), 0)
    other = lax.broadcasted_iota(jnp.int32, (tile, keys), 1)
    return (other <= place) & (seg_col == seg_row)


def forward_kernel(batch, share, ff, h_ref, w_ref, cos_ref, sin_ref, segc_ref, segr_ref, *outs):
    part_ref, q_ref, k_ref, v_ref, o_ref, lse_ref, a_ref, z_ref = outs
    length = h_ref.shape[0]
    f = 4 * HEAD

    @pl.loop(0, length // TILE)
    def project(t):
        rows = pl.ds(t * TILE, TILE)
        h = h_ref[rows, :]
        mixed = dot(h, w_ref[:, :f])
        qk = mixed[:, : 2 * HEAD]
        qk = qk * cos_ref[rows, :] + swap_lanes(qk) * sin_ref[rows, :]
        q_ref[rows, :] = (qk[:, :HEAD].astype(bf16).astype(f32) * HEAD**-0.5).astype(bf16)
        k_ref[rows, :] = qk[:, HEAD:].astype(bf16)
        v_ref[rows, :] = mixed[:, 2 * HEAD : 3 * HEAD].astype(bf16)
        z = dot(h, w_ref[:, f : f + ff])
        z_ref[rows, :] = z
        a_ref[rows, :] = gelu(z).astype(bf16)

    if share > 1:
        o_ref[...] = jnp.zeros_like(o_ref)
        lse_ref[...] = jnp.zeros_like(lse_ref)
    for rows, start, keys in query_tiles(length, share, batch):
        scores = dot_nt(q_ref[rows, :], k_ref[:keys, :])
        seen = visible(start, keys, segc_ref[rows, :], segr_ref[:, :keys])
        scores = jnp.where(seen, scores, low_score)
        peak = jnp.max(scores, axis=1, keepdims=True)
        weights = jnp.exp(scores - peak)
        total = jnp.sum(weights, axis=1, keepdims=True)
        lse_ref[rows, :] = peak + jnp.log(total)
        shares = (weights * (1.0 / total)).astype(bf16)
        o_ref[rows, :] = dot(shares, v_ref[:keys, :]).astype(bf16)

    @pl.loop(0, length // TILE)
    def branch(t):
        rows = pl.ds(t * TILE, TILE)
        out = dot_nt(o_ref[rows, :], w_ref[:, 3 * HEAD : f])
        out = out + dot_nt(a_ref[rows, :], w_ref[:, f + ff : f + 2 * ff])
        part_ref[rows, :] = out.astype(bf16)


def forward(batch, share, ff, h, w, cosine, sine, seg_col, seg_row):
    length, width = h.shape
    column = jax.ShapeDtypeStruct((length, HEAD), bf16)
    return pl.pallas_call(
        functools.partial(forward_kernel, batch, share, ff),
        out_shape=(
            jax.ShapeDtypeStruct((length, width), bf16),
            column,
            column,
            column,
            column,
            jax.ShapeDtypeStruct((length, 1), f32),
            jax.ShapeDtypeStruct((length, ff), bf16),
            jax.ShapeDtypeStruct((length, ff), f32),
        ),
        in_specs=vmem_specs(6),
        out_specs=tuple(vmem_specs(8)),
        compiler_params=pltpu.CompilerParams(vmem_limit_bytes=56 * megabyte),
        name="layer_forward",
    )(h, w, cosine, sine, seg_col, seg_row)


def backward_kernel(batch, share, ff, g_ref, h_ref, w_ref, cos_ref, sin_ref, segc_ref, segr_ref, *refs):
    q_ref, k_ref, v_ref, o_ref, lse_ref, a_ref, z_ref, part_ref, dw_ref = refs[:9]
    dz_ref, do_ref, dq_ref, dk_ref, dv_ref, mix_ref = refs[9:]
    length, width = h_ref.shape
    f = 4 * HEAD

    @pl.loop(0, length // TILE)
    def feed(t):
        rows = pl.ds(t * TILE, TILE)
        g = g_ref[rows, :]
        da = dot(g, w_ref[:, f + ff : f + 2 * ff])
        dz_ref[rows, :] = (da * gelu_slope(z_ref[rows, :])).astype(bf16)
        do_ref[rows, :] = dot(g, w_ref[:, :f])[:, 3 * HEAD :].astype(bf16)

    dk_ref[...] = jnp.zeros_like(dk_ref)
    dv_ref[...] = jnp.zeros_like(dv_ref)
    if share > 1:
        dq_ref[...] = jnp.zeros_like(dq_ref)
    for rows, start, keys in query_tiles(length, share, batch):
        q, head_grad = q_ref[rows, :], do_ref[rows, :]
        scores = dot_nt(q, k_ref[:keys, :])
        seen = visible(start, keys, segc_ref[rows, :], segr_ref[:, :keys])
        shares = jnp.where(seen, jnp.exp(scores - lse_ref[rows, :]), 0.0)
        share_grads = dot_nt(head_grad, v_ref[:keys, :])
        delta = jnp.sum(shares * share_grads, axis=1, keepdims=True)
        score_grads = (shares * (share_grads - delta)).astype(bf16)
        dq_ref[rows, :] = dot(score_grads, k_ref[:keys, :]) * HEAD**-0.5
        dk_ref[:keys, :] += dot_tn(score_grads, q)
        dv_ref[:keys, :] += dot_tn(shares.astype(bf16), head_grad)

    @pl.loop(0, length // TILE)
    def inward(t):
        rows = pl.ds(t * TILE, TILE)
        qk = jnp.concatenate([dq_ref[rows, :], dk_ref[rows, :]], axis=1)
        qk = qk * cos_ref[rows, :] + swap_lanes(qk * sin_ref[rows, :])
        rest = jnp.concatenate([dv_ref[rows, :], jnp.zeros((TILE, HEAD), f32)], axis=1)
        mix = jnp.concatenate([qk, rest], axis=1).astype(bf16)
        mix_ref[rows, :] = mix
        out = dot_nt(mix, w_ref[:, :f]) + dot_nt(dz_ref[rows, :], w_ref[:, f : f + ff])
        part_ref[rows, :] = out.astype(bf16)

    @pl.loop(0, width // TILE)
    def weights(t):
        rows = pl.ds(t * TILE, TILE)
        h, g = h_ref[:, rows], g_ref[:, rows]
        mixed = dot_tn(h, mix_ref[...])
        out = dot_tn(g, o_ref[...])
        dw_ref[rows, :f] = jnp.concatenate([mixed[:, : 3 * HEAD], out], axis=1).astype(bf16)
        dw_ref[rows, f : f + ff] = dot_tn(h, dz_ref[...]).astype(bf16)
        dw_ref[rows, f + ff : f + 2 * ff] = dot_tn(g, a_ref[...]).astype(bf16)


def backward(batch, share, ff, g, h, w, cosine, sine, seg_col, seg_row, kept):
    length, width = h.shape
    return pl.pallas_call(
        functools.partial(backward_kernel, batch, share, ff),
        out_shape=(
            jax.ShapeDtypeStruct((length, width), bf16),
            jax.ShapeDtypeStruct(w.shape, bf16),
        ),
        in_specs=vmem_specs(14),
        out_specs=tuple(vmem_specs(2)),
        scratch_shapes=[
            VM((length, ff), bf16),
            VM((length, HEAD), bf16),
            VM((length, HEAD), f32),
            VM((length, HEAD), f32),
            VM((length, HEAD), f32),
            VM((length, 4 * HEAD), bf16),
        ],
        compiler_params=pltpu.CompilerParams(vmem_limit_bytes=60 * megabyte),
        name="layer_backward",
    )(g, h, w, cosine, sine, seg_col, seg_row, *kept)


def layer_norm(inputs):
    average = jnp.mean(inputs, axis=-1, keepdims=True)
    centred = inputs - average
    spread_here = jnp.mean(centred * centred, axis=-1, keepdims=True)
    inverse = lax.rsqrt(spread_here + norm_eps)
    return (centred * inverse, inverse)


def norm_back(grads, normed_grads, xhat, inverse, gain):
    scaled = normed_grads * gain
    average = jnp.mean(scaled, axis=-1, keepdims=True)
    along = jnp.mean(scaled * xhat, axis=-1, keepdims=True)
    return grads + (scaled - average - xhat * along) * inverse


def rotary_tables(positions):
    column = jnp.arange(HEAD)
    inside = column < ROTARY
    pair_index = column % ROTARY // 2
    frequency = jnp.exp(pair_index.astype(f32) * (-2.0 * math.log(10000.0) / ROTARY))
    angles = positions[:, None] * frequency
    cosine = jnp.where(inside, jnp.cos(angles), 1.0)
    signed = jnp.where(column % 2 == 0, -1.0, 1.0)
    sine = jnp.where(inside, signed * jnp.sin(angles), 0.0)
    return (jnp.tile(cosine, (1, 2)), jnp.tile(sine, (1, 2)))


def pad_lanes(values, width=128):
    return jnp.pad(values, [(0, 0)] * (values.ndim - 1) + [(0, width - values.shape[-1])])


def adam_update(weight, first, second, gradient, factor_clip, rate, decay):
    clipped = gradient * factor_clip
    first_new = beta_one * first + (1.0 - beta_one) * clipped
    second_new = beta_two * second + (1.0 - beta_two) * clipped * clipped
    first_hat = first_new / (1.0 - beta_one**STEP)
    second_hat = second_new / (1.0 - beta_two**STEP)
    weight_new = weight - rate * (first_hat / (jnp.sqrt(second_hat) + adam_eps) + decay * weight)
    return (weight_new, first_new, second_new)


def pack_weights(n, rows, qkv_weight, out_weight, in_weight, down_weight):
    layers, height = qkv_weight.shape[:2]
    members = n // rows
    heads = qkv_weight.shape[3] // HEAD
    share = members // heads
    ff = in_weight.shape[2] // members
    mixed = jnp.concatenate([qkv_weight, out_weight[:, :, None, :]], axis=2).astype(bf16)
    mixed = mixed.reshape(layers, height, 4, heads, HEAD).transpose(0, 3, 1, 2, 4)
    mixed = mixed.reshape(layers, heads, height, 4 * HEAD)
    if share > 1:
        mixed = jnp.repeat(mixed, share, axis=1)
    feeds = [
        weight.astype(bf16).reshape(layers, height, members, ff).transpose(0, 2, 1, 3)
        for weight in (in_weight, down_weight)
    ]
    return jnp.concatenate([mixed] + feeds, axis=3)


def unpack_gradients(grads, heads, ff):
    layers, members, height, unused = grads.shape
    grads = grads.astype(f32)
    share = members // heads
    mixed = grads[..., : 4 * HEAD]
    if share > 1:
        mixed = mixed.reshape(layers, heads, share, height, 4 * HEAD).sum(2)
    mixed = mixed.reshape(layers, heads, height, 4, HEAD).transpose(0, 2, 3, 1, 4)
    mixed = mixed.reshape(layers, height, 4, heads * HEAD)
    feeds = [
        grads[..., 4 * HEAD + k * ff : 4 * HEAD + (k + 1) * ff]
        .transpose(0, 2, 1, 3)
        .reshape(layers, height, members * ff)
        for k in range(2)
    ]
    return (mixed[:, :, :3], mixed[:, :, 3], feeds[0], feeds[1])


def shards(
    n,
    activations,
    cotangent,
    segment_ids,
    position_ids,
    qkv_weight,
    out_weight,
    in_weight,
    down_weight,
    norm_params,
    qkv_first,
    out_first,
    in_first,
    down_first,
    norm_first,
    qkv_second,
    out_second,
    in_second,
    down_second,
    norm_second,
):
    rows, span, width = activations.shape
    members = n // rows
    length = n * span
    half = rows * span // 2
    heads = qkv_weight.shape[3] // HEAD
    share_queries = members // heads
    ff = in_weight.shape[2] // members
    row = lax.axis_index("seq") % rows

    pack = pack_weights(n, rows, qkv_weight, out_weight, in_weight, down_weight)
    norm_low = norm_params.astype(bf16).astype(f32).reshape(LAYERS * 3, -1)
    small = jnp.concatenate(
        [
            pad_lanes(norm_low),
            pad_lanes(position_ids.astype(f32)),
            pad_lanes(segment_ids.astype(f32)),
        ]
    )
    small = jnp.pad(small, ((0, -small.shape[0] % 8), (0, 0)))
    wide = jnp.stack([activations, cotangent], axis=1)
    chunk, table, weights = spread(n, rows, wide, small, pack, 0)
    weights = weights.reshape(LAYERS, width, -1)
    inputs = chunk[:, 0].reshape(rows * span, width)
    out_grads = chunk[:, 1].reshape(rows * span, width)
    own_columns = norm_params.shape[-1]
    norms = table[:, : LAYERS * 3, :own_columns].transpose(1, 0, 2).reshape(LAYERS, 3, width)
    positions = lax.dynamic_index_in_dim(table, LAYERS * 3 + row, 1, False)[:, :span].reshape(length)
    segments = lax.dynamic_index_in_dim(table, LAYERS * 3 + rows + row, 1, False)[:, :span].reshape(length)
    cosine, sine = rotary_tables(positions)
    places = (cosine, sine, segments[:, None], segments[None, :])

    def halves(values):
        return values.astype(bf16).reshape(2, half, width)

    def whole(values):
        return values.reshape(length, width)

    def parts(values):
        return values.reshape(members, 2, half, width)

    xhat_0, inverse_0 = layer_norm(inputs)
    normed = xhat_0 * norms[0, 0] + norms[0, 1]
    got = gather(n, rows, [halves(normed), halves(out_grads)], 1)
    normed_0, grads_1 = whole(got[0]), whole(got[1])
    part, *kept_0 = forward(rows, share_queries, ff, normed_0, weights[0], *places)
    branch = reduce(n, rows, [parts(part)], 2)[0].reshape(inputs.shape)
    middle = inputs + branch + norms[0, 2]
    xhat_1, inverse_1 = layer_norm(middle)
    normed = xhat_1 * norms[1, 0] + norms[1, 1]
    normed_1 = whole(gather(n, rows, [halves(normed)], 3)[0])
    part, *kept_1 = forward(rows, share_queries, ff, normed_1, weights[1], *places)
    back_part, weight_grads_1 = backward(rows, share_queries, ff, grads_1, normed_1, weights[1], *places, kept_1)
    sums = reduce(n, rows, [parts(part), parts(back_part)], 4).reshape((2,) + inputs.shape)
    result = middle + sums[0] + norms[1, 2]
    normed_grads_1 = sums[1]
    grads_mid = norm_back(out_grads, normed_grads_1, xhat_1, inverse_1, norms[1, 0])
    grads_0 = whole(gather(n, rows, [halves(grads_mid)], 5)[0])
    back_part, weight_grads_0 = backward(rows, share_queries, ff, grads_0, normed_0, weights[0], *places, kept_0)
    normed_grads_0 = reduce(n, rows, [parts(back_part)], 6)[0].reshape(inputs.shape)
    input_grad = norm_back(grads_mid, normed_grads_0, xhat_0, inverse_0, norms[0, 0])

    small_grads = jnp.stack(
        [
            jnp.sum(normed_grads_0 * xhat_0, axis=0),
            jnp.sum(normed_grads_0, axis=0),
            jnp.sum(grads_mid, axis=0),
            jnp.sum(normed_grads_1 * xhat_1, axis=0),
            jnp.sum(normed_grads_1, axis=0),
            jnp.sum(out_grads, axis=0),
        ]
    )
    small_grads = pad_lanes(small_grads.reshape(LAYERS * 3, n, own_columns).transpose(1, 0, 2))
    small_grads = jnp.pad(small_grads, ((0, 0), (0, 8 - LAYERS * 3), (0, 0)))
    wide_out = jnp.stack([result.reshape(rows, span, width), input_grad.reshape(rows, span, width)], axis=1)
    height = width // n
    grads, wide_back, table_back = collect(
        n,
        rows,
        weight_grads_0.reshape(n, height, -1),
        weight_grads_1.reshape(n, height, -1),
        wide_out,
        small_grads,
        7,
    )
    norm_grads = jnp.sum(table_back, axis=0)[: LAYERS * 3, :own_columns].reshape(norm_params.shape)
    qkv_grads, out_weight_grads, in_grads, down_grads = unpack_gradients(grads, heads, ff)
    matrix_squares = sum(
        (jnp.sum(block * block) for block in (qkv_grads, out_weight_grads, in_grads, down_grads))
    )
    squares = matrix_squares + jnp.sum(norm_grads * norm_grads) / 2
    everyone = share(n, jnp.full((8, 128), squares, f32), 8)
    grad_norm = jnp.sqrt(jnp.sum(everyone[:, 0, 0]))
    total_parameters = LAYERS * width * (4 * 2 * heads * HEAD + 2 * 2 * members * ff + 3)
    factor_clip = jnp.minimum(1.0, clip_share * math.sqrt(total_parameters) / (grad_norm + 1e-06))
    qkv_new, qkv_first_new, qkv_second_new = adam_update(
        qkv_weight, qkv_first, qkv_second, qkv_grads, factor_clip, rate_matrix, decay_matrix
    )
    out_new, out_first_new, out_second_new = adam_update(
        out_weight, out_first, out_second, out_weight_grads, factor_clip, rate_output, decay_matrix
    )
    in_new, in_first_new, in_second_new = adam_update(
        in_weight, in_first, in_second, in_grads, factor_clip, rate_matrix, decay_matrix
    )
    down_new, down_first_new, down_second_new = adam_update(
        down_weight, down_first, down_second, down_grads, factor_clip, rate_matrix, decay_matrix
    )
    norm_new, norm_first_new, norm_second_new = adam_update(
        norm_params, norm_first, norm_second, norm_grads, factor_clip, rate_vector, 0.0
    )
    bias_clipped = norm_grads[:, 2] * factor_clip
    return (
        wide_back[:, 0],
        wide_back[:, 1],
        grad_norm,
        qkv_new,
        out_new,
        in_new,
        down_new,
        norm_new,
        qkv_first_new,
        out_first_new,
        in_first_new,
        down_first_new,
        norm_first_new,
        qkv_second_new,
        out_second_new,
        in_second_new,
        down_second_new,
        norm_second_new,
        bias_clipped,
    )


def solution(mesh):
    tokens = P(None, "seq", None)
    qkv = P(None, "seq", None, "tp")
    matrix = P(None, "seq", "tp")
    norm = P(None, None, "seq")
    kinds = (qkv, matrix, matrix, matrix, norm)
    return jax.shard_map(
        functools.partial(shards, mesh.shape["seq"]),
        mesh=mesh,
        in_specs=(tokens, tokens, P(None, "seq"), P(None, "seq")) + kinds * 3,
        out_specs=(tokens, tokens, P()) + kinds * 3 + (P(None, "seq"),),
        check_vma=False,
    )
```

```python
import functools
import math
import types

import jax
import jax.numpy as jnp
from jax import lax
from jax.experimental import pallas as pl
from jax.experimental.pallas import tpu as pltpu
from jax.sharding import PartitionSpec as P

HEAD = 64
ROTARY = 32
LAYERS = 2
STEP = 10
TILE = 256

norm_eps = 1e-05
beta_one = 0.9
beta_two = 0.999
adam_eps = 1e-08
rate_matrix = 0.05
rate_output = 0.15
rate_vector = 1.0
decay_matrix = 0.1
clip_share = 0.25
low_score = -1e30

MESH = pl.DeviceIdType.MESH
VM = pltpu.VMEM
DMA = pltpu.SemaphoreType.DMA
bf16 = jnp.bfloat16
f32 = jnp.float32
megabyte = 1 << 20


def split_sizes(members):
    nb = 1 << ((members.bit_length() - 1) // 2)
    return (members // nb, nb)


class Place:
    def __init__(self, n, rows):
        self.n, self.rows = n, rows
        self.members = n // rows
        self.na, self.nb = split_sizes(self.members)
        self.seq = lax.axis_index("seq")
        self.core = lax.axis_index("tp")
        self.row = lax.rem(self.seq, rows)
        self.member = self.seq // rows
        self.a = self.member // self.nb
        self.b = lax.rem(self.member, self.nb)

    def am(self, step):
        return lax.rem(self.a + step, self.na)

    def bm(self, step):
        return lax.rem(self.b + step, self.nb)

    def device(self, member, row=None, core=None):
        row = self.row if row is None else row
        return {"seq": member * self.rows + row, "tp": self.core if core is None else core}

    def at(self, a, b):
        return self.device(a * self.nb + b)

    def sibling(self):
        return self.device(self.member, core=1 - self.core)

    def partners(self):
        return [self.device(self.member, row=lax.rem(self.row + i, self.rows)) for i in range(1, self.rows)]

    def axis_peers(self):
        peers = [self.at(self.am(i), self.b) for i in range(1, self.na)]
        peers += [self.at(self.a, self.bm(j)) for j in range(1, self.nb)]
        return peers

    def other_members(self):
        return [self.device(lax.rem(self.member + i, self.members)) for i in range(1, self.members)]


def greet(devices):
    barrier = pltpu.get_barrier_semaphore()
    for device in devices:
        pl.semaphore_signal(barrier, inc=1, device_id=device, device_id_type=MESH)
    pl.semaphore_wait(barrier, len(devices))


class Sender:
    def __init__(self, send_sems):
        self.send_sems, self.copies = send_sems, []

    def send(self, src, dst, recv_sem, device):
        copy = pltpu.make_async_remote_copy(
            src_ref=src,
            dst_ref=dst,
            send_sem=self.send_sems.at[len(self.copies)],
            recv_sem=recv_sem,
            device_id=device,
            device_id_type=MESH,
        )
        copy.start()
        self.copies.append(copy)

    def arrived(self, dst, recv_sem, device):
        pltpu.make_async_remote_copy(
            src_ref=dst,
            dst_ref=dst,
            send_sem=self.send_sems.at[0],
            recv_sem=recv_sem,
            device_id=device,
            device_id_type=MESH,
        ).wait_recv()

    def finish(self):
        for copy in self.copies:
            copy.wait_send()


def remote_params(collective_id):
    return pltpu.CompilerParams(
        collective_id=collective_id, has_side_effects=True, vmem_limit_bytes=56 * megabyte
    )


def vmem_specs(count):
    return [pl.BlockSpec(memory_space=VM)] * count


def spread_kernel(n, rows, wide_ref, small_ref, pack_ref, chunk_ref, table_ref, weight_ref, *sems):
    (send_sems, chunk_sems, table_sems, block_sems, cross_sems, local_sems) = sems
    p = Place(n, rows)
    members = p.members
    everybody = [
        {"seq": lax.rem(p.seq + i, n), "tp": p.core} for i in range(1, n)
    ]
    greet(everybody)
    sender = Sender(send_sems)
    partners = [
        (lax.rem(p.row + i, rows), p.device(p.member, row=lax.rem(p.row + i, rows)))
        for i in range(1, rows)
    ]
    for device in everybody:
        sender.send(small_ref, table_ref.at[p.seq], table_sems.at[p.seq], device)
    for row, device in partners:
        sender.send(wide_ref.at[row], chunk_ref.at[p.row], chunk_sems.at[p.row], device)
    for layer in range(LAYERS):
        for i in range(1, members):
            member = lax.rem(p.member + i, members)
            sender.send(
                pack_ref.at[layer, member],
                weight_ref.at[layer, p.seq],
                block_sems.at[layer, p.member],
                p.device(member),
            )
        for row, device in partners:
            sender.send(
                pack_ref.at[layer, p.member],
                weight_ref.at[layer, p.seq],
                cross_sems.at[layer, p.seq],
                device,
            )
    own = [
        pltpu.make_async_copy(small_ref, table_ref.at[p.seq], local_sems.at[0]),
        pltpu.make_async_copy(wide_ref.at[p.row], chunk_ref.at[p.row], local_sems.at[1]),
    ]
    for layer in range(LAYERS):
        own.append(
            pltpu.make_async_copy(
                pack_ref.at[layer, p.member], weight_ref.at[layer, p.seq], local_sems.at[2 + layer]
            )
        )
    for copy in own:
        copy.start()
    for layer in range(LAYERS):
        for i in range(1, members):
            member = lax.rem(p.member + members - i, members)
            block = weight_ref.at[layer, member * rows + p.row]
            sender.arrived(block, block_sems.at[layer, member], p.sibling())
            for row, device in partners:
                sender.send(block, block, cross_sems.at[layer, member * rows + p.row], device)
    for i in range(1, n):
        seq = lax.rem(p.seq + i, n)
        sender.arrived(table_ref.at[seq], table_sems.at[seq], p.sibling())
    for row, device in partners:
        sender.arrived(chunk_ref.at[row], chunk_sems.at[row], p.sibling())
    for layer in range(LAYERS):
        for i in range(members):
            member = lax.rem(p.member + members - i, members)
            for row, device in partners:
                block = weight_ref.at[layer, member * rows + row]
                sender.arrived(block, cross_sems.at[layer, member * rows + row], p.sibling())
    sender.finish()
    for copy in own:
        copy.wait()


def spread(n, rows, wide, small, pack, collective_id):
    layers, members, height, columns = pack.shape
    sends = (n - 1) + (rows - 1) + layers * (members - 1 + members * (rows - 1))
    return pl.pallas_call(
        functools.partial(spread_kernel, n, rows),
        out_shape=(
            jax.ShapeDtypeStruct(wide.shape, wide.dtype),
            jax.ShapeDtypeStruct((n,) + small.shape, small.dtype),
            jax.ShapeDtypeStruct((layers, n, height, columns), pack.dtype),
        ),
        in_specs=vmem_specs(3),
        out_specs=tuple(vmem_specs(3)),
        scratch_shapes=[
            DMA((sends,)),
            DMA((rows,)),
            DMA((n,)),
            DMA((layers, members)),
            DMA((layers, n)),
            DMA((2 + layers,)),
        ],
        compiler_params=remote_params(collective_id),
        name="spread_inputs",
    )(wide, small, pack)


def gather_kernel(n, rows, count, x_ref, out_ref, *sems):
    send_sems, a_sems, b_sems, core_sems, local_sem = sems
    p = Place(n, rows)
    na, nb, core = p.na, p.nb, p.core
    sibling = p.sibling()
    greet(p.axis_peers() + [sibling])
    sender = Sender(send_sems)
    a_steps = [1, na - 1] + list(range(2, na - 1)) if na > 2 else [1]

    def slot(k, a, b):
        return out_ref.at[k, a * nb + b, core]

    for k in range(count):
        mine = x_ref.at[k, core]
        for i in a_steps:
            sender.send(mine, slot(k, p.a, p.b), a_sems.at[k, p.a], p.at(p.am(i), p.b))
        for j in range(1, nb):
            sender.send(mine, slot(k, p.a, p.b), b_sems.at[k, p.member], p.at(p.a, p.bm(j)))
    own = pltpu.make_async_copy(x_ref, out_ref.at[:, p.member], local_sem)
    own.start()
    for k in range(count):
        for i in a_steps:
            a = p.am(i)
            here = slot(k, a, p.b)
            sender.arrived(here, a_sems.at[k, a], sibling)
            for j in range(1, nb):
                sender.send(here, here, b_sems.at[k, a * nb + p.b], p.at(p.a, p.bm(j)))
            sender.send(here, here, core_sems.at[k, a * nb + p.b], sibling)
    for k in range(count):
        for i in [0] + a_steps:
            for j in range(1, nb):
                a, b = p.am(i), p.bm(j)
                here = slot(k, a, b)
                sender.arrived(here, b_sems.at[k, a * nb + b], sibling)
                sender.send(here, here, core_sems.at[k, a * nb + b], sibling)
    for k in range(count):
        for i in range(1, p.members):
            member = lax.rem(p.member + i, p.members)
            sender.arrived(out_ref.at[k, member, 1 - core], core_sems.at[k, member], sibling)
    sender.finish()
    own.wait()


def gather(n, rows, pieces, collective_id):
    stacked = jnp.stack(pieces)
    count, two, height, width = stacked.shape
    members = n // rows
    na, nb = split_sizes(members)
    sends = count * ((na - 1) * (nb + 1) + nb - 1 + na * (nb - 1))
    return pl.pallas_call(
        functools.partial(gather_kernel, n, rows, count),
        out_shape=jax.ShapeDtypeStruct((count, members, two, height, width), stacked.dtype),
        in_specs=vmem_specs(1),
        out_specs=vmem_specs(1)[0],
        scratch_shapes=[
            DMA((sends,)),
            DMA((count, na)),
            DMA((count, members)),
            DMA((count, members)),
            DMA,
        ],
        compiler_params=remote_params(collective_id),
        name="gather_tokens",
    )(stacked)


def reduce_kernel(n, rows, count, *refs):
    x_refs, (out_ref, core_buf, b_buf, a_buf, b_out, a_out) = refs[:count], refs[count : count + 6]
    send_sems, core_sems, b_sems, a_sems, out_sems = refs[count + 6 :]
    p = Place(n, rows)
    na, nb, core = p.na, p.nb, p.core
    sibling = p.sibling()
    greet(p.axis_peers() + [sibling])
    sender = Sender(send_sems)
    a_steps = list(range(2, na - 1)) + [1, na - 1, 0] if na > 2 else [1, 0]
    for k in range(count):
        for i in a_steps:
            for j in list(range(1, nb)) + [0]:
                m = p.am(i) * nb + p.bm(j)
                sender.send(x_refs[k].at[m, 1 - core], core_buf.at[k, m], core_sems.at[k, m], sibling)
    for k in range(count):
        for i in a_steps:
            for j in range(1, nb):
                a, b = p.am(i), p.bm(j)
                m = a * nb + b
                sender.arrived(core_buf.at[k, m], core_sems.at[k, m], sibling)
                b_out[k, m] = (x_refs[k][m, core].astype(f32) + core_buf[k, m].astype(f32)).astype(bf16)
                landing = a * nb + p.b
                sender.send(b_out.at[k, m], b_buf.at[k, landing], b_sems.at[k, landing], p.at(p.a, b))
    for k in range(count):
        for i in a_steps:
            a = p.am(i)
            m = a * nb + p.b
            sender.arrived(core_buf.at[k, m], core_sems.at[k, m], sibling)
            total = x_refs[k][m, core].astype(f32) + core_buf[k, m].astype(f32)
            for j in range(1, nb):
                q = a * nb + p.bm(j)
                sender.arrived(b_buf.at[k, q], b_sems.at[k, q], sibling)
                total = total + b_buf[k, q].astype(f32)
            if i:
                a_out[k, a] = total.astype(bf16)
                sender.send(a_out.at[k, a], a_buf.at[k, p.a], a_sems.at[k, p.a], p.at(a, p.b))
            else:
                out_ref[k, core] = total
    for k in range(count):
        for i in range(1, na):
            a = p.am(i)
            sender.arrived(a_buf.at[k, a], a_sems.at[k, a], sibling)
            out_ref[k, core] += a_buf[k, a].astype(f32)
        sender.send(out_ref.at[k, core], out_ref.at[k, core], out_sems.at[k], sibling)
    for k in range(count):
        sender.arrived(out_ref.at[k, 1 - core], out_sems.at[k], sibling)
    sender.finish()


def reduce(n, rows, pieces, collective_id):
    count = len(pieces)
    members, two, height, width = pieces[0].shape
    na, nb = split_sizes(members)
    sends = count * (members + na * (nb - 1) + na)
    return pl.pallas_call(
        functools.partial(reduce_kernel, n, rows, count),
        out_shape=jax.ShapeDtypeStruct((count, two, height, width), f32),
        in_specs=vmem_specs(count),
        out_specs=vmem_specs(1)[0],
        scratch_shapes=[
            VM((count, members, height, width), bf16),
            VM((count, members, height, width), bf16),
            VM((count, na, height, width), bf16),
            VM((count, members, height, width), bf16),
            VM((count, na, height, width), bf16),
            DMA((sends,)),
            DMA((count, members)),
            DMA((count, members)),
            DMA((count, na)),
            DMA((count,)),
        ],
        compiler_params=remote_params(collective_id),
        name="reduce_tokens",
    )(*pieces)


def collect_kernel(n, rows, *refs):
    (first_ref, second_ref, wide_ref, small_ref, grad_ref, back_ref, table_ref) = refs[:7]
    (cross_buf, block_out, send_sems, cross_sems, block_sems, back_sems, table_sems, local_sems) = refs[7:]
    grads = (first_ref, second_ref)
    p = Place(n, rows)
    members = p.members
    everybody = [{"seq": lax.rem(p.seq + i, n), "tp": p.core} for i in range(1, n)]
    greet(everybody)
    sender = Sender(send_sems)
    partners = [
        (lax.rem(p.row + i, rows), p.device(p.member, row=lax.rem(p.row + i, rows)))
        for i in range(1, rows)
    ]
    order = [lax.rem(p.member + i, members) for i in range(1, members)] + [p.member]
    for i in range(1, n):
        seq = lax.rem(p.seq + i, n)
        sender.send(small_ref.at[seq], table_ref.at[p.seq], table_sems.at[p.seq], {"seq": seq, "tp": p.core})
    for layer in range(LAYERS):
        for member in order:
            for row, device in partners:
                sender.send(
                    grads[layer].at[member * rows + row],
                    cross_buf.at[layer, p.row, member],
                    cross_sems.at[layer, p.row, member],
                    device,
                )
    for row, device in partners:
        sender.send(wide_ref.at[row], back_ref.at[p.row], back_sems.at[p.row], device)
    own = [
        pltpu.make_async_copy(small_ref.at[p.seq], table_ref.at[p.seq], local_sems.at[0]),
        pltpu.make_async_copy(wide_ref.at[p.row], back_ref.at[p.row], local_sems.at[1]),
    ]
    for copy in own:
        copy.start()
    for layer in range(LAYERS):
        for i in list(range(1, members)) + [0]:
            member = lax.rem(p.member + i, members)
            total = grads[layer][member * rows + p.row].astype(f32)
            for row, device in partners:
                buffer = cross_buf.at[layer, row, member]
                sender.arrived(buffer, cross_sems.at[layer, row, member], p.sibling())
                total = total + buffer[...].astype(f32)
            if i:
                block_out[layer, member] = total.astype(bf16)
                sender.send(
                    block_out.at[layer, member],
                    grad_ref.at[layer, p.member],
                    block_sems.at[layer, p.member],
                    p.device(member),
                )
            else:
                grad_ref[layer, member] = total.astype(bf16)
    for i in range(1, n):
        seq = lax.rem(p.seq + i, n)
        sender.arrived(table_ref.at[seq], table_sems.at[seq], p.sibling())
    for row, device in partners:
        sender.arrived(back_ref.at[row], back_sems.at[row], p.sibling())
    for layer in range(LAYERS):
        for i in range(1, members):
            member = lax.rem(p.member + members - i, members)
            sender.arrived(grad_ref.at[layer, member], block_sems.at[layer, member], p.sibling())
    sender.finish()
    for copy in own:
        copy.wait()


def collect(n, rows, first, second, wide, small, collective_id):
    unused, height, columns = first.shape
    members = n // rows
    sends = (n - 1) + (rows - 1) + LAYERS * (members * (rows - 1) + members - 1)
    return pl.pallas_call(
        functools.partial(collect_kernel, n, rows),
        out_shape=(
            jax.ShapeDtypeStruct((LAYERS, members, height, columns), bf16),
            jax.ShapeDtypeStruct(wide.shape, wide.dtype),
            jax.ShapeDtypeStruct(small.shape, small.dtype),
        ),
        in_specs=vmem_specs(4),
        out_specs=tuple(vmem_specs(3)),
        scratch_shapes=[
            VM((LAYERS, rows, members, height, columns), bf16),
            VM((LAYERS, members, height, columns), bf16),
            DMA((sends,)),
            DMA((LAYERS, rows, members)),
            DMA((LAYERS, members)),
            DMA((rows,)),
            DMA((n,)),
            DMA((2,)),
        ],
        compiler_params=remote_params(collective_id),
        name="collect_gradients",
    )(first, second, wide, small)


def share_kernel(n, x_ref, out_ref, send_sems, recv_sems, local_sem):
    seq, core = lax.axis_index("seq"), lax.axis_index("tp")
    others = []
    for i in range(n):
        for j in range(2):
            if i or j:
                others.append((lax.rem(seq + i, n), lax.rem(core + j, 2)))
    greet([{"seq": s, "tp": c} for s, c in others])
    sender = Sender(send_sems)
    here = seq * 2 + core
    for s, c in others:
        sender.send(x_ref, out_ref.at[here], recv_sems.at[here], {"seq": s, "tp": c})
    own = pltpu.make_async_copy(x_ref, out_ref.at[here], local_sem)
    own.start()
    for s, c in others:
        sender.arrived(out_ref.at[s * 2 + c], recv_sems.at[s * 2 + c], {"seq": s, "tp": c})
    sender.finish()
    own.wait()


def share(n, x, collective_id):
    return pl.pallas_call(
        functools.partial(share_kernel, n),
        out_shape=jax.ShapeDtypeStruct((2 * n,) + x.shape, x.dtype),
        in_specs=vmem_specs(1),
        out_specs=vmem_specs(1)[0],
        scratch_shapes=[DMA((2 * n,)), DMA((2 * n,)), DMA],
        compiler_params=remote_params(collective_id),
        name="share_squares",
    )(x)


def dot(left, right):
    return jnp.dot(left, right, preferred_element_type=f32)


def dot_nt(left, right):
    return lax.dot_general(left, right, (((1,), (1,)), ((), ())), preferred_element_type=f32)


def dot_tn(left, right):
    return lax.dot_general(left, right, (((0,), (0,)), ((), ())), preferred_element_type=f32)


def swap_lanes(values):
    width = values.shape[-1]
    lane = lax.broadcasted_iota(jnp.int32, values.shape, 1)
    after = pltpu.roll(values, width - 1, 1)
    before = pltpu.roll(values, 1, 1)
    return jnp.where(lane % 2 == 0, after, before)


gelu_scale = 0.7978845608
gelu_cubic = 0.044715


def gelu(z):
    return 0.5 * z * (1.0 + jnp.tanh(gelu_scale * (z + gelu_cubic * z * z * z)))


def gelu_slope(z):
    inner = jnp.tanh(gelu_scale * (z + gelu_cubic * z * z * z))
    slope = gelu_scale * (1.0 + 3.0 * gelu_cubic * z * z)
    return 0.5 * (1.0 + inner) + 0.5 * z * (1.0 - inner * inner) * slope


def query_tiles(length, share, rows):
    tile = max(64, min(TILE, TILE * 1024 // length))
    first = 0
    if share > 1:
        first = lax.rem(lax.axis_index("seq") // rows, share) * (length // share)
    for i in range(length // share // tile):
        start = pl.multiple_of(first + i * tile, tile) if share > 1 else i * tile
        yield pl.ds(start, tile), start, ((i + 1) * tile if share == 1 else length)


def visible(start, keys, seg_col, seg_row):
    tile = seg_col.shape[0]
    place = start + lax.broadcasted_iota(jnp.int32, (tile, keys), 0)
    other = lax.broadcasted_iota(jnp.int32, (tile, keys), 1)
    return (other <= place) & (seg_col == seg_row)


def forward_kernel(batch, share, ff, h_ref, w_ref, cos_ref, sin_ref, segc_ref, segr_ref, *outs):
    part_ref, q_ref, k_ref, v_ref, o_ref, lse_ref, a_ref, z_ref = outs
    length = h_ref.shape[0]
    f = 4 * HEAD

    @pl.loop(0, length // TILE)
    def project(t):
        rows = pl.ds(t * TILE, TILE)
        h = h_ref[rows, :]
        mixed = dot(h, w_ref[:, :f])
        qk = mixed[:, : 2 * HEAD]
        qk = qk * cos_ref[rows, :] + swap_lanes(qk) * sin_ref[rows, :]
        q_ref[rows, :] = (qk[:, :HEAD].astype(bf16).astype(f32) * HEAD**-0.5).astype(bf16)
        k_ref[rows, :] = qk[:, HEAD:].astype(bf16)
        v_ref[rows, :] = mixed[:, 2 * HEAD : 3 * HEAD].astype(bf16)
        z = dot(h, w_ref[:, f : f + ff])
        z_ref[rows, :] = z
        a_ref[rows, :] = gelu(z).astype(bf16)

    if share > 1:
        o_ref[...] = jnp.zeros_like(o_ref)
        lse_ref[...] = jnp.zeros_like(lse_ref)
    for rows, start, keys in query_tiles(length, share, batch):
        scores = dot_nt(q_ref[rows, :], k_ref[:keys, :])
        seen = visible(start, keys, segc_ref[rows, :], segr_ref[:, :keys])
        scores = jnp.where(seen, scores, low_score)
        peak = jnp.max(scores, axis=1, keepdims=True)
        weights = jnp.exp(scores - peak)
        total = jnp.sum(weights, axis=1, keepdims=True)
        lse_ref[rows, :] = peak + jnp.log(total)
        shares = (weights * (1.0 / total)).astype(bf16)
        o_ref[rows, :] = dot(shares, v_ref[:keys, :]).astype(bf16)

    @pl.loop(0, length // TILE)
    def branch(t):
        rows = pl.ds(t * TILE, TILE)
        out = dot_nt(o_ref[rows, :], w_ref[:, 3 * HEAD : f])
        out = out + dot_nt(a_ref[rows, :], w_ref[:, f + ff : f + 2 * ff])
        part_ref[rows, :] = out.astype(bf16)


def forward(batch, share, ff, h, w, cosine, sine, seg_col, seg_row):
    length, width = h.shape
    column = jax.ShapeDtypeStruct((length, HEAD), bf16)
    return pl.pallas_call(
        functools.partial(forward_kernel, batch, share, ff),
        out_shape=(
            jax.ShapeDtypeStruct((length, width), bf16),
            column,
            column,
            column,
            column,
            jax.ShapeDtypeStruct((length, 1), f32),
            jax.ShapeDtypeStruct((length, ff), bf16),
            jax.ShapeDtypeStruct((length, ff), f32),
        ),
        in_specs=vmem_specs(6),
        out_specs=tuple(vmem_specs(8)),
        compiler_params=pltpu.CompilerParams(vmem_limit_bytes=56 * megabyte),
        name="layer_forward",
    )(h, w, cosine, sine, seg_col, seg_row)


def backward_kernel(batch, share, ff, g_ref, h_ref, w_ref, cos_ref, sin_ref, segc_ref, segr_ref, *refs):
    q_ref, k_ref, v_ref, o_ref, lse_ref, a_ref, z_ref, part_ref, dw_ref = refs[:9]
    dz_ref, do_ref, dq_ref, dk_ref, dv_ref, mix_ref = refs[9:]
    length, width = h_ref.shape
    f = 4 * HEAD

    @pl.loop(0, length // TILE)
    def feed(t):
        rows = pl.ds(t * TILE, TILE)
        g = g_ref[rows, :]
        da = dot(g, w_ref[:, f + ff : f + 2 * ff])
        dz_ref[rows, :] = (da * gelu_slope(z_ref[rows, :])).astype(bf16)
        do_ref[rows, :] = dot(g, w_ref[:, :f])[:, 3 * HEAD :].astype(bf16)

    dk_ref[...] = jnp.zeros_like(dk_ref)
    dv_ref[...] = jnp.zeros_like(dv_ref)
    if share > 1:
        dq_ref[...] = jnp.zeros_like(dq_ref)
    for rows, start, keys in query_tiles(length, share, batch):
        q, head_grad = q_ref[rows, :], do_ref[rows, :]
        scores = dot_nt(q, k_ref[:keys, :])
        seen = visible(start, keys, segc_ref[rows, :], segr_ref[:, :keys])
        shares = jnp.where(seen, jnp.exp(scores - lse_ref[rows, :]), 0.0)
        share_grads = dot_nt(head_grad, v_ref[:keys, :])
        delta = jnp.sum(shares * share_grads, axis=1, keepdims=True)
        score_grads = (shares * (share_grads - delta)).astype(bf16)
        dq_ref[rows, :] = dot(score_grads, k_ref[:keys, :]) * HEAD**-0.5
        dk_ref[:keys, :] += dot_tn(score_grads, q)
        dv_ref[:keys, :] += dot_tn(shares.astype(bf16), head_grad)

    @pl.loop(0, length // TILE)
    def inward(t):
        rows = pl.ds(t * TILE, TILE)
        qk = jnp.concatenate([dq_ref[rows, :], dk_ref[rows, :]], axis=1)
        qk = qk * cos_ref[rows, :] + swap_lanes(qk * sin_ref[rows, :])
        rest = jnp.concatenate([dv_ref[rows, :], jnp.zeros((TILE, HEAD), f32)], axis=1)
        mix = jnp.concatenate([qk, rest], axis=1).astype(bf16)
        mix_ref[rows, :] = mix
        out = dot_nt(mix, w_ref[:, :f]) + dot_nt(dz_ref[rows, :], w_ref[:, f : f + ff])
        part_ref[rows, :] = out.astype(bf16)

    @pl.loop(0, width // TILE)
    def weights(t):
        rows = pl.ds(t * TILE, TILE)
        h, g = h_ref[:, rows], g_ref[:, rows]
        mixed = dot_tn(h, mix_ref[...])
        out = dot_tn(g, o_ref[...])
        dw_ref[rows, :f] = jnp.concatenate([mixed[:, : 3 * HEAD], out], axis=1).astype(bf16)
        dw_ref[rows, f : f + ff] = dot_tn(h, dz_ref[...]).astype(bf16)
        dw_ref[rows, f + ff : f + 2 * ff] = dot_tn(g, a_ref[...]).astype(bf16)


def backward(batch, share, ff, g, h, w, cosine, sine, seg_col, seg_row, kept):
    length, width = h.shape
    return pl.pallas_call(
        functools.partial(backward_kernel, batch, share, ff),
        out_shape=(
            jax.ShapeDtypeStruct((length, width), bf16),
            jax.ShapeDtypeStruct(w.shape, bf16),
        ),
        in_specs=vmem_specs(14),
        out_specs=tuple(vmem_specs(2)),
        scratch_shapes=[
            VM((length, ff), bf16),
            VM((length, HEAD), bf16),
            VM((length, HEAD), f32),
            VM((length, HEAD), f32),
            VM((length, HEAD), f32),
            VM((length, 4 * HEAD), bf16),
        ],
        compiler_params=pltpu.CompilerParams(vmem_limit_bytes=60 * megabyte),
        name="layer_backward",
    )(g, h, w, cosine, sine, seg_col, seg_row, *kept)


def layer_norm(inputs):
    average = jnp.mean(inputs, axis=-1, keepdims=True)
    centred = inputs - average
    spread_here = jnp.mean(centred * centred, axis=-1, keepdims=True)
    inverse = lax.rsqrt(spread_here + norm_eps)
    return (centred * inverse, inverse)


def norm_back(grads, normed_grads, xhat, inverse, gain):
    scaled = normed_grads * gain
    average = jnp.mean(scaled, axis=-1, keepdims=True)
    along = jnp.mean(scaled * xhat, axis=-1, keepdims=True)
    return grads + (scaled - average - xhat * along) * inverse


def rotary_tables(positions):
    column = jnp.arange(HEAD)
    inside = column < ROTARY
    pair_index = column % ROTARY // 2
    frequency = jnp.exp(pair_index.astype(f32) * (-2.0 * math.log(10000.0) / ROTARY))
    angles = positions[:, None] * frequency
    cosine = jnp.where(inside, jnp.cos(angles), 1.0)
    signed = jnp.where(column % 2 == 0, -1.0, 1.0)
    sine = jnp.where(inside, signed * jnp.sin(angles), 0.0)
    return (jnp.tile(cosine, (1, 2)), jnp.tile(sine, (1, 2)))


def pad_lanes(values, width=128):
    return jnp.pad(values, [(0, 0)] * (values.ndim - 1) + [(0, width - values.shape[-1])])


def adam_update(weight, first, second, gradient, factor_clip, rate, decay):
    clipped = gradient * factor_clip
    first_new = beta_one * first + (1.0 - beta_one) * clipped
    second_new = beta_two * second + (1.0 - beta_two) * clipped * clipped
    first_hat = first_new / (1.0 - beta_one**STEP)
    second_hat = second_new / (1.0 - beta_two**STEP)
    weight_new = weight - rate * (first_hat / (jnp.sqrt(second_hat) + adam_eps) + decay * weight)
    return (weight_new, first_new, second_new)


def pack_weights(n, rows, qkv_weight, out_weight, in_weight, down_weight):
    layers, height = qkv_weight.shape[:2]
    members = n // rows
    heads = qkv_weight.shape[3] // HEAD
    share = members // heads
    ff = in_weight.shape[2] // members
    mixed = jnp.concatenate([qkv_weight, out_weight[:, :, None, :]], axis=2).astype(bf16)
    mixed = mixed.reshape(layers, height, 4, heads, HEAD).transpose(0, 3, 1, 2, 4)
    mixed = mixed.reshape(layers, heads, height, 4 * HEAD)
    if share > 1:
        mixed = jnp.repeat(mixed, share, axis=1)
    feeds = [
        weight.astype(bf16).reshape(layers, height, members, ff).transpose(0, 2, 1, 3)
        for weight in (in_weight, down_weight)
    ]
    return jnp.concatenate([mixed] + feeds, axis=3)


def unpack_gradients(grads, heads, ff):
    layers, members, height, unused = grads.shape
    grads = grads.astype(f32)
    share = members // heads
    mixed = grads[..., : 4 * HEAD]
    if share > 1:
        mixed = mixed.reshape(layers, heads, share, height, 4 * HEAD).sum(2)
    mixed = mixed.reshape(layers, heads, height, 4, HEAD).transpose(0, 2, 3, 1, 4)
    mixed = mixed.reshape(layers, height, 4, heads * HEAD)
    feeds = [
        grads[..., 4 * HEAD + k * ff : 4 * HEAD + (k + 1) * ff]
        .transpose(0, 2, 1, 3)
        .reshape(layers, height, members * ff)
        for k in range(2)
    ]
    return (mixed[:, :, :3], mixed[:, :, 3], feeds[0], feeds[1])


def shards_apart(
    n,
    activations,
    cotangent,
    segment_ids,
    position_ids,
    qkv_weight,
    out_weight,
    in_weight,
    down_weight,
    norm_params,
    qkv_first,
    out_first,
    in_first,
    down_first,
    norm_first,
    qkv_second,
    out_second,
    in_second,
    down_second,
    norm_second,
):
    rows, span, width = activations.shape
    members = n // rows
    length = n * span
    half = rows * span // 2
    heads = qkv_weight.shape[3] // HEAD
    share_queries = members // heads
    ff = in_weight.shape[2] // members
    row = lax.axis_index("seq") % rows

    pack = pack_weights(n, rows, qkv_weight, out_weight, in_weight, down_weight)
    norm_low = norm_params.astype(bf16).astype(f32).reshape(LAYERS * 3, -1)
    small = jnp.concatenate(
        [
            pad_lanes(norm_low),
            pad_lanes(position_ids.astype(f32)),
            pad_lanes(segment_ids.astype(f32)),
        ]
    )
    small = jnp.pad(small, ((0, -small.shape[0] % 8), (0, 0)))
    wide = jnp.stack([activations, cotangent], axis=1)
    chunk, table, weights = spread(n, rows, wide, small, pack, 0)
    weights = weights.reshape(LAYERS, width, -1)
    inputs = chunk[:, 0].reshape(rows * span, width)
    out_grads = chunk[:, 1].reshape(rows * span, width)
    own_columns = norm_params.shape[-1]
    norms = table[:, : LAYERS * 3, :own_columns].transpose(1, 0, 2).reshape(LAYERS, 3, width)
    positions = lax.dynamic_index_in_dim(table, LAYERS * 3 + row, 1, False)[:, :span].reshape(length)
    segments = lax.dynamic_index_in_dim(table, LAYERS * 3 + rows + row, 1, False)[:, :span].reshape(length)
    cosine, sine = rotary_tables(positions)
    places = (cosine, sine, segments[:, None], segments[None, :])

    def halves(values):
        return values.astype(bf16).reshape(2, half, width)

    def whole(values):
        return values.reshape(length, width)

    def parts(values):
        return values.reshape(members, 2, half, width)

    xhat_0, inverse_0 = layer_norm(inputs)
    normed = xhat_0 * norms[0, 0] + norms[0, 1]
    got = gather(n, rows, [halves(normed), halves(out_grads)], 1)
    normed_0, grads_1 = whole(got[0]), whole(got[1])
    part, *kept_0 = forward(rows, share_queries, ff, normed_0, weights[0], *places)
    branch = reduce(n, rows, [parts(part)], 2)[0].reshape(inputs.shape)
    middle = inputs + branch + norms[0, 2]
    xhat_1, inverse_1 = layer_norm(middle)
    normed = xhat_1 * norms[1, 0] + norms[1, 1]
    normed_1 = whole(gather(n, rows, [halves(normed)], 3)[0])
    part, *kept_1 = forward(rows, share_queries, ff, normed_1, weights[1], *places)
    back_part, weight_grads_1 = backward(rows, share_queries, ff, grads_1, normed_1, weights[1], *places, kept_1)
    sums = reduce(n, rows, [parts(part), parts(back_part)], 4).reshape((2,) + inputs.shape)
    result = middle + sums[0] + norms[1, 2]
    normed_grads_1 = sums[1]
    grads_mid = norm_back(out_grads, normed_grads_1, xhat_1, inverse_1, norms[1, 0])
    grads_0 = whole(gather(n, rows, [halves(grads_mid)], 5)[0])
    back_part, weight_grads_0 = backward(rows, share_queries, ff, grads_0, normed_0, weights[0], *places, kept_0)
    normed_grads_0 = reduce(n, rows, [parts(back_part)], 6)[0].reshape(inputs.shape)
    input_grad = norm_back(grads_mid, normed_grads_0, xhat_0, inverse_0, norms[0, 0])

    small_grads = jnp.stack(
        [
            jnp.sum(normed_grads_0 * xhat_0, axis=0),
            jnp.sum(normed_grads_0, axis=0),
            jnp.sum(grads_mid, axis=0),
            jnp.sum(normed_grads_1 * xhat_1, axis=0),
            jnp.sum(normed_grads_1, axis=0),
            jnp.sum(out_grads, axis=0),
        ]
    )
    small_grads = pad_lanes(small_grads.reshape(LAYERS * 3, n, own_columns).transpose(1, 0, 2))
    small_grads = jnp.pad(small_grads, ((0, 0), (0, 8 - LAYERS * 3), (0, 0)))
    wide_out = jnp.stack([result.reshape(rows, span, width), input_grad.reshape(rows, span, width)], axis=1)
    height = width // n
    grads, wide_back, table_back = collect(
        n,
        rows,
        weight_grads_0.reshape(n, height, -1),
        weight_grads_1.reshape(n, height, -1),
        wide_out,
        small_grads,
        7,
    )
    norm_grads = jnp.sum(table_back, axis=0)[: LAYERS * 3, :own_columns].reshape(norm_params.shape)
    qkv_grads, out_weight_grads, in_grads, down_grads = unpack_gradients(grads, heads, ff)
    matrix_squares = sum(
        (jnp.sum(block * block) for block in (qkv_grads, out_weight_grads, in_grads, down_grads))
    )
    squares = matrix_squares + jnp.sum(norm_grads * norm_grads) / 2
    everyone = share(n, jnp.full((8, 128), squares, f32), 8)
    grad_norm = jnp.sqrt(jnp.sum(everyone[:, 0, 0]))
    total_parameters = LAYERS * width * (4 * 2 * heads * HEAD + 2 * 2 * members * ff + 3)
    factor_clip = jnp.minimum(1.0, clip_share * math.sqrt(total_parameters) / (grad_norm + 1e-06))
    qkv_new, qkv_first_new, qkv_second_new = adam_update(
        qkv_weight, qkv_first, qkv_second, qkv_grads, factor_clip, rate_matrix, decay_matrix
    )
    out_new, out_first_new, out_second_new = adam_update(
        out_weight, out_first, out_second, out_weight_grads, factor_clip, rate_output, decay_matrix
    )
    in_new, in_first_new, in_second_new = adam_update(
        in_weight, in_first, in_second, in_grads, factor_clip, rate_matrix, decay_matrix
    )
    down_new, down_first_new, down_second_new = adam_update(
        down_weight, down_first, down_second, down_grads, factor_clip, rate_matrix, decay_matrix
    )
    norm_new, norm_first_new, norm_second_new = adam_update(
        norm_params, norm_first, norm_second, norm_grads, factor_clip, rate_vector, 0.0
    )
    bias_clipped = norm_grads[:, 2] * factor_clip
    return (
        wide_back[:, 0],
        wide_back[:, 1],
        grad_norm,
        qkv_new,
        out_new,
        in_new,
        down_new,
        norm_new,
        qkv_first_new,
        out_first_new,
        in_first_new,
        down_first_new,
        norm_first_new,
        qkv_second_new,
        out_second_new,
        in_second_new,
        down_second_new,
        norm_second_new,
        bias_clipped,
    )


def flip(index, bits):
    bit = 1
    while bit <= bits:
        if bits & bit:
            index = index + bit * (1 - 2 * lax.rem(index // bit, 2))
        bit *= 2
    return index


class Net:
    def __init__(self, n, rows, half, pieces, send_sems):
        self.p = Place(n, rows)
        self.half, self.pieces = half, pieces
        self.send_sems, self.used = send_sems, 0
        self.sibling = self.p.sibling()

    def send_sem(self):
        self.used += 1
        return self.send_sems.at[self.used - 1]

    def everybody(self):
        p = self.p
        return [{"seq": lax.rem(p.seq + i, p.n), "tp": p.core} for i in range(1, p.n)]

    def everyone(self):
        p = self.p
        return self.everybody() + [
            {"seq": lax.rem(p.seq + i, p.n), "tp": 1 - p.core} for i in range(p.n)
        ]

    def partner(self):
        return self.p.device(self.p.member, row=1 - self.p.row)

    def a_of(self, k):
        return flip(self.p.a, k)

    def b_of(self, j):
        return flip(self.p.b, j)

    def tokens(self, member, core, piece):
        size = self.half // self.pieces
        start = (member * 2 + core) * self.half + piece * size
        return pl.ds(pl.multiple_of(start, size), size)

    def lines(self, slot, piece):
        size = self.half // self.pieces
        return pl.ds(pl.multiple_of(slot * self.half + piece * size, size), size)

    def own(self):
        start = (self.p.member * 2 + self.p.core) * self.half
        return pl.ds(pl.multiple_of(start, self.half), self.half)

    def tile_rows(self, a):
        size = self.p.nb * 2 * self.half
        return pl.ds(pl.multiple_of(a * size, size), size)

    def tile(self, k):
        return self.tile_rows(self.a_of(k))

    def far_first(self):
        a, na = self.p.a, self.p.na
        if na != 4:
            return [self.a_of(k) for k in range(na - 1, -1, -1)]
        upper = a // 2
        low = a + upper * (3 - 2 * a)
        order = [3, 2, 1 - low, low]
        return [v + upper * (3 - 2 * v) for v in order]

    def sides(self, distance):
        a, na = self.p.a, self.p.na
        return [
            (a >= distance, a - distance, a < na - 1, a + 1),
            (a + distance < na, a + distance, a > 0, a - 1),
        ]


class Sends:
    def __init__(self, net, lone=0):
        self.sibling = net.sibling
        self.shared = net.send_sem()
        self.lone = [net.send_sem() for _ in range(lone)]
        self.made, self.conditional = 0, []

    def copy(self, src, dst, sem, device, send_sem):
        return pltpu.make_async_remote_copy(
            src_ref=src, dst_ref=dst, send_sem=send_sem, recv_sem=sem, device_id=device, device_id_type=MESH
        )

    def send(self, src, dst, sem, device):
        self.copy(src, dst, sem, device, self.shared).start()
        self.made += 1

    def send_if(self, when, src, dst, sem, device):
        number = len(self.conditional)
        self.conditional.append((when, src, dst, sem, device))
        pl.when(when)(lambda: self.copy(src, dst, sem, device, self.lone[number]).start())

    def finish(self, whole):
        self.copy(whole, whole, self.shared, self.sibling, self.shared).wait_send()
        for number, (when, *copy) in enumerate(self.conditional):
            pl.when(when)(lambda number=number, copy=copy: self.copy(*copy, self.lone[number]).wait_send())
        self.made, self.conditional = 0, []


def wait_for(net, dst, sem):
    pltpu.make_async_remote_copy(
        src_ref=dst,
        dst_ref=dst,
        send_sem=net.send_sems.at[0],
        recv_sem=sem,
        device_id=net.sibling,
        device_id_type=MESH,
    ).wait_recv()


class Gather:
    def __init__(self, net, sems):
        self.net = net
        self.a_sems, self.b_sems, self.core_sems = sems
        self.sends = Sends(net, lone=2 * net.pieces * net.p.na)

    def slot(self, a, b, core, q):
        return self.out.at[self.net.tokens(a * self.net.p.nb + b, core, q), :]

    def to_line(self, a, q, to, when):
        p = self.net.p
        here = self.slot(a, p.b, p.core, q)
        self.sends.send_if(when, here, here, self.a_sems.at[a, q], p.at(to, p.b))

    def to_rest(self, a, q):
        net, p = self.net, self.net.p
        here = self.slot(a, p.b, p.core, q)
        for j in range(1, p.nb):
            self.sends.send(here, here, self.b_sems.at[a * p.nb + p.b, q], p.at(p.a, net.b_of(j)))
        self.sends.send(here, here, self.core_sems.at[a, q], net.sibling)

    def start(self, out):
        p = self.net.p
        self.out = out
        for q in range(self.net.pieces):
            self.to_line(p.a, q, p.a + 1, p.a < p.na - 1)
            self.to_line(p.a, q, p.a - 1, p.a > 0)
            self.to_rest(p.a, q)

    def hop(self, distance):
        net, p = self.net, self.net.p
        for q in range(net.pieces):
            for there, a, more, beyond in net.sides(distance):

                @pl.when(there)
                def _():
                    wait_for(net, self.slot(a, p.b, p.core, q), self.a_sems.at[a, q])

                self.to_line(a, q, beyond, jnp.logical_and(there, more))
                pl.when(there)(lambda: self.to_rest(a, q))

    def side(self, distance):
        net, p = self.net, self.net.p
        for j in range(1, p.nb):
            b = net.b_of(j)
            for q in range(net.pieces):
                for there, a, more, beyond in net.sides(distance)[: 2 if distance else 1]:

                    @pl.when(there)
                    def _():
                        here = self.slot(a, b, p.core, q)
                        wait_for(net, here, self.b_sems.at[a * p.nb + b, q])
                        self.sends.send(here, here, self.core_sems.at[a, q], net.sibling)

    def settle(self, distance):
        net, p = self.net, self.net.p
        size = p.nb * net.half // net.pieces
        for q in range(net.pieces):
            for there, a, more, beyond in net.sides(distance)[: 2 if distance else 1]:

                @pl.when(there)
                def _():
                    wait_for(net, self.out.at[pl.ds(0, size), :], self.core_sems.at[a, q])

    def steps(self):
        na = self.net.p.na
        if na > 1:
            self.hop(1)
        self.side(0)
        yield None
        for k in range(na):
            if k + 2 < na:
                self.hop(k + 2)
            if k + 1 < na:
                self.side(k + 1)
            self.settle(k)
            yield k

    def finish(self):
        p = self.net.p
        self.sends.finish(self.out.at[pl.ds(0, (p.na * (p.nb - 1) + p.members) * self.net.half), :])


class Reduce:
    def __init__(self, net, x, total, bufs, sems):
        self.net, self.x, self.total = net, x, total
        self.core_buf, self.b_out, self.b_buf, self.a_out, self.a_buf, self.sum_buf = bufs
        self.core_sems, self.b_sems, self.a_sems = sems
        self.sends = Sends(net, lone=2 * net.pieces * (net.p.na - 1))

    def offer(self, a):
        net, p = self.net, self.net.p
        for j in list(range(1, p.nb)) + [0]:
            m = a * p.nb + net.b_of(j)
            for q in range(net.pieces):
                self.sends.send(
                    self.x.at[net.tokens(m, 1 - p.core, q), :],
                    self.core_buf.at[net.lines(m, q), :],
                    self.core_sems.at[m, q],
                    net.sibling,
                )

    def pair_sum(self, m, q):
        net = self.net
        lines = net.lines(m, q)
        wait_for(net, self.core_buf.at[lines, :], self.core_sems.at[m, q])
        return self.x[net.tokens(m, net.p.core, q), :].astype(f32) + self.core_buf[lines, :].astype(f32)

    def targets(self, distance):
        return self.net.sides(distance)[: 2 if distance else 1]

    def relay(self, distance):
        net, p = self.net, self.net.p
        for there, a, unused_more, unused_beyond in self.targets(distance):
            for j in range(1, p.nb):
                b = net.b_of(j)
                for q in range(net.pieces):

                    @pl.when(there)
                    def _():
                        m, landing = a * p.nb + b, a * p.nb + p.b
                        self.b_out[net.lines(m, q), :] = self.pair_sum(m, q).astype(bf16)
                        self.sends.send(
                            self.b_out.at[net.lines(m, q), :],
                            self.b_buf.at[net.lines(landing, q), :],
                            self.b_sems.at[landing, q],
                            p.at(p.a, b),
                        )

    def row_sum(self, a, q):
        net, p = self.net, self.net.p
        total = self.pair_sum(a * p.nb + p.b, q)
        for j in range(1, p.nb):
            m = a * p.nb + net.b_of(j)
            wait_for(net, self.b_buf.at[net.lines(m, q), :], self.b_sems.at[m, q])
            total = total + self.b_buf[net.lines(m, q), :].astype(f32)
        return total

    def passing(self, up, a, q):
        net, p = self.net, self.net.p
        slot = a if up else p.na + a
        wait_for(net, self.a_buf.at[net.lines(slot, q), :], self.a_sems.at[slot, q])
        return self.a_buf[net.lines(slot, q), :].astype(f32)

    def pass_on(self, distance):
        net, p = self.net, self.net.p
        size = net.half // net.pieces
        for side, (there, a, unused_more, unused_beyond) in enumerate(net.sides(distance)):
            up = side == 1
            behind = p.a > 0 if up else p.a < p.na - 1
            slot = a if up else p.na + a
            for q in range(net.pieces):
                part = slice(q * size, (q + 1) * size)

                @pl.when(there)
                def _():
                    self.sum_buf[part, :] = self.row_sum(a, q)

                @pl.when(jnp.logical_and(there, behind))
                def _():
                    self.sum_buf[part, :] += self.passing(up, a, q)

                @pl.when(there)
                def _():
                    self.a_out[net.lines(slot, q), :] = self.sum_buf[part, :].astype(bf16)

                self.sends.send_if(
                    there,
                    self.a_out.at[net.lines(slot, q), :],
                    self.a_buf.at[net.lines(slot, q), :],
                    self.a_sems.at[slot, q],
                    p.at(p.a + 1 if up else p.a - 1, p.b),
                )

    def arrive(self):
        net, p = self.net, self.net.p
        size = net.half // net.pieces
        for q in range(net.pieces):
            part = slice(q * size, (q + 1) * size)
            self.total[part, :] = self.row_sum(p.a, q)
        for q in range(net.pieces):
            part = slice(q * size, (q + 1) * size)

            @pl.when(p.a > 0)
            def _():
                self.total[part, :] += self.passing(True, p.a, q)

            @pl.when(p.a < p.na - 1)
            def _():
                self.total[part, :] += self.passing(False, p.a, q)

    def steps(self):
        na = self.net.p.na
        for distance in range(na - 1, -1, -1):
            self.relay(distance)
            yield
        for distance in range(na - 1, 0, -1):
            self.pass_on(distance)
            yield
        self.arrive()
        yield

    def finish(self):
        p = self.net.p
        self.sends.finish(self.x.at[pl.ds(0, (p.members + p.na * (p.nb - 1)) * self.net.half), :])


class Spread:
    def __init__(self, net, pack, w, block_sems, cross_sems):
        self.net, self.pack, self.w = net, pack, w
        self.block_sems, self.cross_sems = block_sems, cross_sems
        self.height = pack.shape[1]
        self.sends = Sends(net)

    def rows(self, seq):
        return pl.ds(pl.multiple_of(seq * self.height, self.height), self.height)

    def start(self):
        net, p = self.net, self.net.p
        here = self.w.at[self.rows(p.seq), :]
        for k in range(1, p.members):
            member = flip(p.member, k)
            self.sends.send(
                self.pack.at[member], here, self.block_sems.at[p.member], p.device(member)
            )
        self.sends.send(
            self.pack.at[p.member], here, self.cross_sems.at[p.member], net.partner()
        )
        self.w[self.rows(p.seq), :] = self.pack[p.member]

    def steps(self):
        net, p = self.net, self.net.p
        for k in range(1, p.members):
            member = flip(p.member, k)
            seq = member * p.rows + p.row
            here = self.w.at[self.rows(seq), :]
            wait_for(net, here, self.block_sems.at[member])
            self.sends.send(here, here, self.cross_sems.at[member], net.partner())
            yield
        for k in range(p.members):
            member = flip(p.member, k)
            seq = member * p.rows + 1 - p.row
            wait_for(net, self.w.at[self.rows(seq), :], self.cross_sems.at[member])
        yield

    def finish(self):
        self.sends.finish(self.w.at[pl.ds(0, (2 * self.net.p.members - 1) * self.height), :])


class Collect:
    def __init__(self, net, dw, grad, cross_buf, block_out, cross_sems, block_sems):
        self.net, self.dw, self.grad = net, dw, grad
        self.cross_buf, self.block_out = cross_buf, block_out
        self.cross_sems, self.block_sems = cross_sems, block_sems
        self.height = grad.shape[1]
        self.sends = Sends(net)

    def rows(self, seq):
        return pl.ds(pl.multiple_of(seq * self.height, self.height), self.height)

    def order(self):
        return list(range(self.net.p.members - 1, -1, -1))

    def offer(self, start, end):
        net, p = self.net, self.net.p
        step = self.height * p.rows
        for member in range(start // step, end // step):
            self.sends.send(
                self.dw.at[self.rows(member * p.rows + 1 - p.row), :],
                self.cross_buf.at[member],
                self.cross_sems.at[member],
                net.partner(),
            )

    def relay(self, k):
        net, p = self.net, self.net.p
        member = flip(p.member, k)
        wait_for(net, self.cross_buf.at[member], self.cross_sems.at[member])
        mine = self.dw[self.rows(member * p.rows + p.row), :]
        total = (mine.astype(f32) + self.cross_buf[member].astype(f32)).astype(bf16)
        if k:
            self.block_out[member] = total
            self.sends.send(
                self.block_out.at[member],
                self.grad.at[p.member],
                self.block_sems.at[p.member],
                p.device(member),
            )
        else:
            self.grad[member] = total

    def settle(self, k):
        member = flip(self.net.p.member, k)
        wait_for(self.net, self.grad.at[member], self.block_sems.at[member])

    def steps(self):
        for k in self.order():
            self.relay(k)
            yield
        for k in range(1, self.net.p.members):
            self.settle(k)
            yield

    def finish(self):
        self.sends.finish(self.dw.at[pl.ds(0, (2 * self.net.p.members - 1) * self.height), :])


def advance(steps, count=1):
    for _ in range(count):
        next(steps, None)


def drain(steps):
    for _ in steps:
        pass


class Layer:
    def __init__(self, r, layer):
        self.r, self.layer = r, layer
        self.length, self.width = getattr(r, "h%d" % layer).shape
        self.f = 4 * HEAD
        self.ff = (getattr(r, "w%d" % layer).shape[1] - self.f) // 2

    def __getattr__(self, name):
        return getattr(self.r, name + str(self.layer))

    def project(self, rows):
        r, f = self.r, self.f
        h = self.h[rows, :]
        mixed = dot(h, self.w[:, :f])
        qk = mixed[:, : 2 * HEAD]
        qk = qk * r.cos[rows, :] + swap_lanes(qk) * r.sin[rows, :]
        self.q[rows, :] = (qk[:, :HEAD].astype(bf16).astype(f32) * HEAD**-0.5).astype(bf16)
        self.k[rows, :] = qk[:, HEAD:].astype(bf16)
        self.v[rows, :] = mixed[:, 2 * HEAD : 3 * HEAD].astype(bf16)

    def feed(self, rows):
        z = dot(self.h[rows, :], self.w[:, self.f : self.f + self.ff])
        self.z[rows, :] = z
        self.a[rows, :] = gelu(z).astype(bf16)

    def attend(self, i):
        r = self.r
        start, keys = i * TILE, (i + 1) * TILE
        rows = pl.ds(start, TILE)
        scores = dot_nt(self.q[rows, :], self.k[:keys, :])
        seen = visible(start, keys, r.segc[rows, :], r.segr[:, :keys])
        scores = jnp.where(seen, scores, low_score)
        peak = jnp.max(scores, axis=1, keepdims=True)
        weights = jnp.exp(scores - peak)
        total = jnp.sum(weights, axis=1, keepdims=True)
        self.lse[rows, :] = peak + jnp.log(total)
        shares = (weights * (1.0 / total)).astype(bf16)
        self.o[rows, :] = dot(shares, self.v[:keys, :]).astype(bf16)

    def branch(self, rows, part):
        f, ff = self.f, self.ff
        out = dot_nt(self.o[rows, :], self.w[:, 3 * HEAD : f])
        out = out + dot_nt(self.a[rows, :], self.w[:, f + ff : f + 2 * ff])
        part[rows, :] = out.astype(bf16)

    def feed_back(self, rows):
        r, f, ff = self.r, self.f, self.ff
        g = self.g[rows, :]
        da = dot(g, self.w[:, f + ff : f + 2 * ff])
        r.dz[rows, :] = (da * gelu_slope(self.z[rows, :])).astype(bf16)
        r.do[rows, :] = dot(g, self.w[:, :f])[:, 3 * HEAD :].astype(bf16)

    def attend_back(self, i):
        r = self.r
        start, keys = i * TILE, (i + 1) * TILE
        rows = pl.ds(start, TILE)
        q, head_grad = self.q[rows, :], r.do[rows, :]
        scores = dot_nt(q, self.k[:keys, :])
        seen = visible(start, keys, r.segc[rows, :], r.segr[:, :keys])
        shares = jnp.where(seen, jnp.exp(scores - self.lse[rows, :]), 0.0)
        share_grads = dot_nt(head_grad, self.v[:keys, :])
        delta = jnp.sum(shares * share_grads, axis=1, keepdims=True)
        score_grads = (shares * (share_grads - delta)).astype(bf16)
        r.dq[rows, :] = dot(score_grads, self.k[:keys, :]) * HEAD**-0.5
        dk = dot_tn(score_grads, q)
        dv = dot_tn(shares.astype(bf16), head_grad)
        if i + 1 == self.length // TILE:
            r.dk[:keys, :] = dk
            r.dv[:keys, :] = dv
        else:
            r.dk[:keys, :] += dk
            r.dv[:keys, :] += dv

    def inward(self, rows, part):
        r, f, ff = self.r, self.f, self.ff
        qk = jnp.concatenate([r.dq[rows, :], r.dk[rows, :]], axis=1)
        qk = qk * r.cos[rows, :] + swap_lanes(qk * r.sin[rows, :])
        rest = jnp.concatenate([r.dv[rows, :], jnp.zeros((TILE, HEAD), f32)], axis=1)
        mix = jnp.concatenate([qk, rest], axis=1).astype(bf16)
        r.mix[rows, :] = mix
        out = dot_nt(mix, self.w[:, :f]) + dot_nt(r.dz[rows, :], self.w[:, f : f + ff])
        part[rows, :] = out.astype(bf16)

    def weight_grads(self, t):
        r, f, ff = self.r, self.f, self.ff
        rows = pl.ds(t * TILE, TILE)
        h, g = self.h[:, rows], self.g[:, rows]
        mixed = dot_tn(h, r.mix[...])
        out = dot_tn(g, self.o[...])
        self.dw[rows, :f] = jnp.concatenate([mixed[:, : 3 * HEAD], out], axis=1).astype(bf16)
        self.dw[rows, f : f + ff] = dot_tn(h, r.dz[...]).astype(bf16)
        self.dw[rows, f + ff : f + 2 * ff] = dot_tn(g, self.a[...]).astype(bf16)


def norm_row(r, layer, kind):
    return r.norms[layer * 3 + kind : layer * 3 + kind + 1, :]


def column_sums(values):
    return jnp.sum(values, axis=0, keepdims=True)


def cross_rows(net, r):
    p = net.p
    same = p.core == p.row

    def crossing(i):
        source, landing = ((r.act, r.x0), (r.cot, r.gr1))[i]
        return pltpu.make_async_remote_copy(
            src_ref=source.at[1 - p.row],
            dst_ref=landing,
            send_sem=r.x_sems.at[i],
            recv_sem=r.x_sems.at[2 + i],
            device_id=net.partner(),
            device_id_type=MESH,
        )

    @pl.when(same)
    def _():
        crossing(0).start()
        crossing(1).start()
        r.x0[...] = r.act[p.row]
        r.gr1[...] = r.cot[p.row]

    def arrive():
        @pl.when(jnp.logical_not(same))
        def _():
            crossing(0).wait_recv()
            crossing(1).wait_recv()

    def finish():
        @pl.when(same)
        def _():
            crossing(0).wait_send()
            crossing(1).wait_send()

    return (arrive, finish)


def give_back(net, r, i, source, target):
    p = net.p
    same = p.core == p.row

    def copy(j, device, row):
        return pltpu.make_async_remote_copy(
            src_ref=source,
            dst_ref=target.at[row],
            send_sem=r.back_sems.at[i, j],
            recv_sem=r.back_sems.at[i, 2 + row],
            device_id=device,
            device_id_type=MESH,
        )

    def far(j):
        return copy(j, p.device(p.member, row=1 - p.row, core=lax.rem(p.core + j, 2)), p.row)

    @pl.when(same)
    def _():
        copy(0, net.sibling, p.row).start()
        target[p.row] = source[...]

    @pl.when(jnp.logical_not(same))
    def _():
        far(0).start()
        far(1).start()

    def finish():
        @pl.when(same)
        def _():
            copy(0, net.sibling, p.row).wait_send()

        @pl.when(jnp.logical_not(same))
        def _():
            far(0).wait_send()
            far(1).wait_send()
            copy(0, net.sibling, p.row).wait_recv()

        copy(0, net.sibling, 1 - p.row).wait_recv()

    return finish


def share_all(net, sem, out, source):
    p = net.p
    here = p.seq * 2 + p.core
    others = [
        (lax.rem(p.seq + i, p.n), lax.rem(p.core + j, 2)) for i in range(p.n) for j in range(2) if i or j
    ]
    sends = Sends(net)
    for seq, core in others:
        sends.send(source(seq), out.at[here], sem, {"seq": seq, "tp": core})
    whole = out.at[pl.ds(0, len(others))]
    return (lambda: wait_for(net, whole, sem), lambda: sends.finish(whole))


def position_tables(net, r):
    p = net.p
    span = r.act.shape[1]
    lines = []
    for kind in range(2):
        row = LAYERS * 3 + kind * p.rows + p.row
        pieces = [r.table[s, pl.ds(row, 1), :span] for s in range(p.n)]
        lines.append(jnp.concatenate(pieces, axis=1))
    positions, segments = lines
    r.segr[...] = segments
    angles = r.freq[:, :1] * positions
    sign = jnp.where(lax.broadcasted_iota(jnp.int32, angles.shape, 0) % 2 == 0, -1.0, 1.0)
    ones = jnp.ones((HEAD - ROTARY, angles.shape[1]), f32)
    cosine, sine = jnp.cos(angles), jnp.sin(angles) * sign
    cosine = jnp.concatenate([cosine, ones, cosine, ones], axis=0)
    sine = jnp.concatenate([sine, ones * 0.0, sine, ones * 0.0], axis=0)
    segments = jnp.broadcast_to(segments, (128, segments.shape[1]))
    for t in range(angles.shape[1] // 128):
        block = slice(t * 128, (t + 1) * 128)
        r.cos[block, :] = cosine[:, block].T
        r.sin[block, :] = sine[:, block].T
        r.segc[block, :] = segments[:, block].T[:, :1]


def whole_part(net, r):
    p = net.p
    n, width = p.n, r.act.shape[2]
    finishes = []

    greet(net.everyone())
    gathers = [Gather(net, r.gather_a), Gather(net, r.gather_b)]
    reduces = [
        Reduce(net, r.part_a, r.total_a, r.bufs_a, r.reduce_a),
        Reduce(net, r.part_b, r.total_b, r.bufs_b, r.reduce_b),
    ]
    table_sends = Sends(net)
    finishes.append(lambda: table_sends.finish(r.table.at[pl.ds(0, n - 1)]))
    for i in range(1, n):
        device = {"seq": lax.rem(p.seq + i, n), "tp": p.core}
        table_sends.send(r.small, r.table.at[p.seq], r.table_sem, device)
    r.table[p.seq] = r.small[...]
    cross_arrive, cross_finish = cross_rows(net, r)
    finishes.append(cross_finish)
    spreads = [
        Spread(net, r.pack.at[k], (r.w0, r.w1)[k], r.block_sems.at[k], r.cross_sems.at[k]) for k in range(LAYERS)
    ]
    collects = [
        Collect(
            net,
            (r.dw0, r.dw1)[k],
            r.grads.at[k],
            r.cross_buf.at[k],
            r.block_out.at[k],
            r.collect_sems.at[k],
            r.block_sems.at[k],
        )
        for k in range(LAYERS)
    ]
    finishes.extend(collect.finish for collect in collects)
    spreads[0].start()
    wait_for(net, r.table.at[pl.ds(0, n - 1)], r.table_sem)
    own_columns = width // n
    many = 128 // own_columns
    for s in range(0, n, many):
        r.norms[:, s * own_columns : (s + many) * own_columns] = jnp.concatenate(
            [r.table[s + i, 0:8, :own_columns] for i in range(many)], axis=1
        )
    cross_arrive()
    xhat, inverse = layer_norm(r.x0[...])
    normed = xhat * norm_row(r, 0, 0) + norm_row(r, 0, 1)
    r.h0[net.own(), :] = normed.astype(bf16)
    gather = gathers[0]
    gather.start(r.h0)
    r.g1[net.own(), :] = r.gr1[...].astype(bf16)
    position_tables(net, r)

    layer = Layer(r, 0)
    tiles = range(layer.length // TILE)
    weight_steps = spreads[0].steps()
    gather_steps = gather.steps()
    advance(gather_steps)
    advance(weight_steps, p.members - 1)
    advance(gather_steps, 4)
    drain(weight_steps)
    spreads[1].start()
    weight_steps = spreads[1].steps()
    for k in tiles:
        layer.project(net.tile(k))
        layer.feed(net.tile(k))
    drain(gather_steps)
    for i in tiles:
        layer.attend(i)
        advance(weight_steps)
    reduce = reduces[0]
    for a in net.far_first():
        layer.branch(net.tile_rows(a), r.part_a)
        reduce.offer(a)
    drain(reduce.steps())
    middle = r.x0[...] + (r.total_a[...] + norm_row(r, 0, 2))
    r.x1[...] = middle
    xhat, inverse = layer_norm(middle)
    normed = xhat * norm_row(r, 1, 0) + norm_row(r, 1, 1)
    r.h1[net.own(), :] = normed.astype(bf16)
    gathers[0].finish()
    gather = gathers[1]
    gather.start(r.h1)

    layer = Layer(r, 1)
    drain(weight_steps)
    gather_steps = gather.steps()
    grad_gather = gathers[0]
    for k in tiles:
        if k == 0:
            advance(gather_steps, 2)
        else:
            advance(gather_steps)
        if k == len(tiles) - 2:
            grad_gather.start(r.g1)
        layer.project(net.tile(k))
        layer.feed(net.tile(k))
    drain(gather_steps)
    grad_steps = grad_gather.steps()
    for i in tiles:
        layer.attend(i)
        advance(grad_steps)
    drain(grad_steps)
    forward_reduce = reduces[1]
    forward_steps = forward_reduce.steps()
    for a in net.far_first():
        layer.branch(net.tile_rows(a), r.part_b)
        forward_reduce.offer(a)

    for k in tiles:
        layer.feed_back(net.tile(k))
        advance(forward_steps)
    for i in reversed(tiles):
        layer.attend_back(i)
        advance(forward_steps)
    reduce = reduces[0]
    reduce.finish()
    for spread in spreads:
        spread.finish()
    steps = reduce.steps()
    for a in net.far_first():
        layer.inward(net.tile_rows(a), r.part_a)
        reduce.offer(a)
    drain(forward_steps)
    for t in range(layer.width // TILE):
        layer.weight_grads(t)
        collects[1].offer(t * TILE, (t + 1) * TILE)
        advance(steps, 2)
    drain(steps)
    xhat, inverse = layer_norm(r.x1[...])
    normed_grads = r.total_a[...]
    r.sums1[...] = jnp.concatenate(
        [
            column_sums(normed_grads * xhat),
            column_sums(normed_grads),
            column_sums(r.gr1[...]),
            jnp.zeros((5, layer.width), f32),
        ]
    )
    below = norm_back(r.gr1[...], normed_grads, xhat, inverse, norm_row(r, 1, 0))
    r.gr0[...] = below
    r.g0[net.own(), :] = below.astype(bf16)
    gather = gathers[1]
    gather.finish()
    gather.start(r.g0)
    r.result[...] = r.x1[...] + (r.total_b[...] + norm_row(r, 1, 2))
    finishes.append(give_back(net, r, 0, r.result, r.results))

    layer = Layer(r, 0)
    gather_steps = gather.steps()
    collect_steps = collects[1].steps()
    for k in tiles:
        if k == 0:
            advance(gather_steps, 2)
        else:
            advance(gather_steps)
        layer.feed_back(net.tile(k))
    drain(gather_steps)
    for i in reversed(tiles):
        layer.attend_back(i)
        advance(collect_steps, 2)
    reduce = forward_reduce
    reduce.finish()
    steps = reduce.steps()
    for a in net.far_first():
        layer.inward(net.tile_rows(a), r.part_b)
        reduce.offer(a)
    for t in range(layer.width // TILE):
        layer.weight_grads(t)
        collects[0].offer(t * TILE, (t + 1) * TILE)
        advance(steps, 2)
    drain(steps)
    normed_grads = r.total_b[...]
    xhat, inverse = layer_norm(r.x0[...])
    r.in_grad[...] = norm_back(r.gr0[...], normed_grads, xhat, inverse, norm_row(r, 0, 0))
    finishes.append(give_back(net, r, 1, r.in_grad, r.in_grads))
    rows = [
        column_sums(normed_grads * xhat),
        column_sums(normed_grads),
        column_sums(r.gr0[...]),
        r.sums1[0:3, :],
        jnp.zeros((2, width), f32),
    ]
    rows = jnp.concatenate(rows)
    for s in range(n):
        r.small_out[s] = pad_lanes(rows[:, s * own_columns : (s + 1) * own_columns])
    here = p.seq * 2 + p.core
    small_arrive, small_finish = share_all(net, r.small_sem, r.small_in, lambda seq: r.small_out.at[seq])
    finishes.append(small_finish)
    r.small_in[here] = r.small_out[p.seq]
    drain(collect_steps)
    drain(collects[0].steps())
    small_arrive()
    norm_grads = jnp.sum(r.small_in[...], axis=0)
    r.norm_grads[...] = norm_grads
    squares = 0.5 * jnp.sum(norm_grads * norm_grads, axis=(0, 1), keepdims=True)
    for layer_index in range(LAYERS):
        for member in range(p.members):
            block = r.grads[layer_index, member].astype(f32)
            squares = squares + jnp.sum(block * block, axis=(0, 1), keepdims=True)
    r.squares[here] = jnp.broadcast_to(squares, (8, 128))
    square_arrive, square_finish = share_all(net, r.square_sem, r.squares, lambda seq: r.squares.at[here])
    finishes.append(square_finish)
    square_arrive()
    r.norm_out[...] = jnp.sqrt(jnp.sum(r.squares[...], axis=0))
    for part in gathers + reduces:
        part.finish()
    for finish in finishes:
        finish()


def fused_call(name, part, geometry, ins, outs, scratch, collective_id):
    flat, places = [], []
    for key, spec in scratch.items():
        group = spec if isinstance(spec, tuple) else (spec,)
        places.append((key, len(flat), len(group), isinstance(spec, tuple)))
        flat.extend(group)

    def kernel(*refs):
        r = types.SimpleNamespace(**dict(zip([*ins, *outs], refs)))
        rest = refs[len(ins) + len(outs) :]
        for key, start, count, grouped in places:
            setattr(r, key, rest[start : start + count] if grouped else rest[start])
        part(Net(*geometry, r.send_sems), r)

    results = pl.pallas_call(
        kernel,
        out_shape=tuple(outs.values()),
        in_specs=vmem_specs(len(ins)),
        out_specs=tuple(vmem_specs(len(outs))),
        scratch_shapes=flat,
        compiler_params=remote_params(collective_id),
        name=name,
    )(*ins.values())
    return types.SimpleNamespace(**dict(zip(outs, results)))


def shards_together(
    n,
    activations,
    cotangent,
    segment_ids,
    position_ids,
    qkv_weight,
    out_weight,
    in_weight,
    down_weight,
    norm_params,
    qkv_first,
    out_first,
    in_first,
    down_first,
    norm_first,
    qkv_second,
    out_second,
    in_second,
    down_second,
    norm_second,
):
    rows, span, width = activations.shape
    members = n // rows
    na, nb = split_sizes(members)
    length = n * span
    half = rows * span // 2
    pieces = 2
    heads = qkv_weight.shape[3] // HEAD
    ff = in_weight.shape[2] // members
    height = width // n
    columns = 4 * HEAD + 2 * ff
    geometry = (n, rows, half, pieces)

    def shape(*extent, kind=f32):
        return jax.ShapeDtypeStruct(extent, kind)

    def scratch_like(shapes, suffix):
        return {key + suffix: VM(value.shape, value.dtype) for key, value in shapes.items()}

    gather_sems = (DMA((na, pieces)), DMA((members, pieces)), DMA((na, pieces)))
    reduce_sems = (DMA((members, pieces)), DMA((members, pieces)), DMA((2 * na, pieces)))
    reduce_bufs = tuple(
        VM((count * half, width), bf16) for count in (members, members, members, 2 * na, 2 * na)
    ) + (VM((half, width), f32),)
    kept = dict(
        q=shape(length, HEAD, kind=bf16),
        k=shape(length, HEAD, kind=bf16),
        v=shape(length, HEAD, kind=bf16),
        o=shape(length, HEAD, kind=bf16),
        lse=shape(length, 1),
        a=shape(length, ff, kind=bf16),
        z=shape(length, ff),
        w=shape(width, columns, kind=bf16),
        dw=shape(width, columns, kind=bf16),
        h=shape(length, width, kind=bf16),
        g=shape(length, width, kind=bf16),
        x=shape(half, width),
        gr=shape(half, width),
    )
    pack = pack_weights(n, rows, qkv_weight, out_weight, in_weight, down_weight)
    norm_low = norm_params.astype(bf16).astype(f32).reshape(LAYERS * 3, -1)
    small = jnp.concatenate(
        [
            pad_lanes(norm_low),
            pad_lanes(position_ids.astype(f32)),
            pad_lanes(segment_ids.astype(f32)),
        ]
    )
    small = jnp.pad(small, ((0, -small.shape[0] % 8), (0, 0)))
    pair = jnp.arange(ROTARY) // 2
    frequency = jnp.exp(pair.astype(f32) * (-2.0 * math.log(10000.0) / ROTARY))
    frequency = jnp.broadcast_to(frequency[:, None], (ROTARY, 128))
    three = fused_call(
        "whole_part",
        whole_part,
        geometry,
        dict(act=activations, cot=cotangent, small=small, freq=frequency, pack=pack),
        dict(
            results=shape(rows, span, width),
            in_grads=shape(rows, span, width),
            grads=shape(LAYERS, members, height, columns, kind=bf16),
            norm_grads=shape(8, 128),
            norm_out=shape(8, 128),
        ),
        dict(
            table=VM((n,) + small.shape, f32),
            norms=VM((8, width), f32),
            cos=VM((length, 128), f32),
            sin=VM((length, 128), f32),
            segc=VM((length, 1), f32),
            segr=VM((1, length), f32),
            **scratch_like(kept, "0"),
            **scratch_like(kept, "1"),
            dz=VM((length, ff), bf16),
            do=VM((length, HEAD), bf16),
            dq=VM((length, HEAD), f32),
            dk=VM((length, HEAD), f32),
            dv=VM((length, HEAD), f32),
            mix=VM((length, 4 * HEAD), bf16),
            part_a=VM((length, width), bf16),
            part_b=VM((length, width), bf16),
            total_a=VM((half, width), f32),
            total_b=VM((half, width), f32),
            bufs_a=reduce_bufs,
            bufs_b=reduce_bufs,
            result=VM((half, width), f32),
            in_grad=VM((half, width), f32),
            sums1=VM((8, width), f32),
            cross_buf=VM((LAYERS, members, height, columns), bf16),
            block_out=VM((LAYERS, members, height, columns), bf16),
            small_out=VM((n, 8, 128), f32),
            small_in=VM((2 * n, 8, 128), f32),
            squares=VM((2 * n, 8, 128), f32),
            reduce_a=reduce_sems,
            reduce_b=reduce_sems,
            gather_a=gather_sems,
            gather_b=gather_sems,
            x_sems=DMA((4,)),
            back_sems=DMA((2, 4)),
            table_sem=DMA,
            small_sem=DMA,
            square_sem=DMA,
            block_sems=DMA((LAYERS, members)),
            cross_sems=DMA((LAYERS, members)),
            collect_sems=DMA((LAYERS, members)),
            send_sems=DMA((2 * (1 + 2 * pieces * na) + 2 * (1 + 2 * pieces * (na - 1)) + 7,)),
        ),
        0,
    )
    own_columns = norm_params.shape[-1]
    norm_grads = three.norm_grads[: LAYERS * 3, :own_columns].reshape(norm_params.shape)
    qkv_grads, out_weight_grads, in_grads, down_grads = unpack_gradients(three.grads, heads, ff)
    grad_norm = three.norm_out[0, 0]
    total_parameters = LAYERS * width * (4 * 2 * heads * HEAD + 2 * 2 * members * ff + 3)
    factor_clip = jnp.minimum(1.0, clip_share * math.sqrt(total_parameters) / (grad_norm + 1e-06))
    qkv_new, qkv_first_new, qkv_second_new = adam_update(
        qkv_weight, qkv_first, qkv_second, qkv_grads, factor_clip, rate_matrix, decay_matrix
    )
    out_new, out_first_new, out_second_new = adam_update(
        out_weight, out_first, out_second, out_weight_grads, factor_clip, rate_output, decay_matrix
    )
    in_new, in_first_new, in_second_new = adam_update(
        in_weight, in_first, in_second, in_grads, factor_clip, rate_matrix, decay_matrix
    )
    down_new, down_first_new, down_second_new = adam_update(
        down_weight, down_first, down_second, down_grads, factor_clip, rate_matrix, decay_matrix
    )
    norm_new, norm_first_new, norm_second_new = adam_update(
        norm_params, norm_first, norm_second, norm_grads, factor_clip, rate_vector, 0.0
    )
    bias_clipped = norm_grads[:, 2] * factor_clip
    return (
        three.results,
        three.in_grads,
        grad_norm,
        qkv_new,
        out_new,
        in_new,
        down_new,
        norm_new,
        qkv_first_new,
        out_first_new,
        in_first_new,
        down_first_new,
        norm_first_new,
        qkv_second_new,
        out_second_new,
        in_second_new,
        down_second_new,
        norm_second_new,
        bias_clipped,
    )


def shards(n, activations, *others):
    rows, span, width = activations.shape
    together = 12 * n * span * width * 2 <= 40 * megabyte and rows == 2 and n * span % TILE == 0
    return (shards_together if together else shards_apart)(n, activations, *others)


def solution(mesh):
    tokens = P(None, "seq", None)
    qkv = P(None, "seq", None, "tp")
    matrix = P(None, "seq", "tp")
    norm = P(None, None, "seq")
    kinds = (qkv, matrix, matrix, matrix, norm)
    return jax.shard_map(
        functools.partial(shards, mesh.shape["seq"]),
        mesh=mesh,
        in_specs=(tokens, tokens, P(None, "seq"), P(None, "seq")) + kinds * 3,
        out_specs=(tokens, tokens, P()) + kinds * 3 + (P(None, "seq"),),
        check_vma=False,
    )
```

```python
import functools
import math
import types

import jax
import jax.numpy as jnp
from jax import lax
from jax.experimental import pallas as pl
from jax.experimental.pallas import tpu as pltpu
from jax.sharding import PartitionSpec as P

HEAD = 64
ROTARY = 32
LAYERS = 2
STEP = 10
TILE = 256

norm_eps = 1e-05
beta_one = 0.9
beta_two = 0.999
adam_eps = 1e-08
rate_matrix = 0.05
rate_output = 0.15
rate_vector = 1.0
decay_matrix = 0.1
clip_share = 0.25
low_score = -1e30

MESH = pl.DeviceIdType.MESH
VM = pltpu.VMEM
DMA = pltpu.SemaphoreType.DMA
bf16 = jnp.bfloat16
f32 = jnp.float32
megabyte = 1 << 20


def split_sizes(members):
    nb = 1 << ((members.bit_length() - 1) // 2)
    return (members // nb, nb)


class Place:
    def __init__(self, n, rows):
        self.n, self.rows = n, rows
        self.members = n // rows
        self.na, self.nb = split_sizes(self.members)
        self.seq = lax.axis_index("seq")
        self.core = lax.axis_index("tp")
        self.row = lax.rem(self.seq, rows)
        self.member = self.seq // rows
        self.a = self.member // self.nb
        self.b = lax.rem(self.member, self.nb)

    def am(self, step):
        return lax.rem(self.a + step, self.na)

    def bm(self, step):
        return lax.rem(self.b + step, self.nb)

    def device(self, member, row=None, core=None):
        row = self.row if row is None else row
        return {"seq": member * self.rows + row, "tp": self.core if core is None else core}

    def at(self, a, b):
        return self.device(a * self.nb + b)

    def sibling(self):
        return self.device(self.member, core=1 - self.core)

    def partners(self):
        return [self.device(self.member, row=lax.rem(self.row + i, self.rows)) for i in range(1, self.rows)]

    def axis_peers(self):
        peers = [self.at(self.am(i), self.b) for i in range(1, self.na)]
        peers += [self.at(self.a, self.bm(j)) for j in range(1, self.nb)]
        return peers

    def other_members(self):
        return [self.device(lax.rem(self.member + i, self.members)) for i in range(1, self.members)]


def greet(devices):
    barrier = pltpu.get_barrier_semaphore()
    for device in devices:
        pl.semaphore_signal(barrier, inc=1, device_id=device, device_id_type=MESH)
    pl.semaphore_wait(barrier, len(devices))


class Sender:
    def __init__(self, send_sems):
        self.send_sems, self.copies = send_sems, []

    def send(self, src, dst, recv_sem, device):
        copy = pltpu.make_async_remote_copy(
            src_ref=src,
            dst_ref=dst,
            send_sem=self.send_sems.at[len(self.copies)],
            recv_sem=recv_sem,
            device_id=device,
            device_id_type=MESH,
        )
        copy.start()
        self.copies.append(copy)

    def arrived(self, dst, recv_sem, device):
        pltpu.make_async_remote_copy(
            src_ref=dst,
            dst_ref=dst,
            send_sem=self.send_sems.at[0],
            recv_sem=recv_sem,
            device_id=device,
            device_id_type=MESH,
        ).wait_recv()

    def finish(self):
        for copy in self.copies:
            copy.wait_send()


def remote_params(collective_id):
    return pltpu.CompilerParams(
        collective_id=collective_id, has_side_effects=True, vmem_limit_bytes=56 * megabyte
    )


def vmem_specs(count):
    return [pl.BlockSpec(memory_space=VM)] * count


def spread_kernel(n, rows, wide_ref, small_ref, pack_ref, chunk_ref, table_ref, weight_ref, *sems):
    (send_sems, chunk_sems, table_sems, block_sems, cross_sems, local_sems) = sems
    p = Place(n, rows)
    members = p.members
    everybody = [
        {"seq": lax.rem(p.seq + i, n), "tp": p.core} for i in range(1, n)
    ]
    greet(everybody)
    sender = Sender(send_sems)
    partners = [
        (lax.rem(p.row + i, rows), p.device(p.member, row=lax.rem(p.row + i, rows)))
        for i in range(1, rows)
    ]
    for device in everybody:
        sender.send(small_ref, table_ref.at[p.seq], table_sems.at[p.seq], device)
    for row, device in partners:
        sender.send(wide_ref.at[row], chunk_ref.at[p.row], chunk_sems.at[p.row], device)
    for layer in range(LAYERS):
        for i in range(1, members):
            member = lax.rem(p.member + i, members)
            sender.send(
                pack_ref.at[layer, member],
                weight_ref.at[layer, p.seq],
                block_sems.at[layer, p.member],
                p.device(member),
            )
        for row, device in partners:
            sender.send(
                pack_ref.at[layer, p.member],
                weight_ref.at[layer, p.seq],
                cross_sems.at[layer, p.seq],
                device,
            )
    own = [
        pltpu.make_async_copy(small_ref, table_ref.at[p.seq], local_sems.at[0]),
        pltpu.make_async_copy(wide_ref.at[p.row], chunk_ref.at[p.row], local_sems.at[1]),
    ]
    for layer in range(LAYERS):
        own.append(
            pltpu.make_async_copy(
                pack_ref.at[layer, p.member], weight_ref.at[layer, p.seq], local_sems.at[2 + layer]
            )
        )
    for copy in own:
        copy.start()
    for layer in range(LAYERS):
        for i in range(1, members):
            member = lax.rem(p.member + members - i, members)
            block = weight_ref.at[layer, member * rows + p.row]
            sender.arrived(block, block_sems.at[layer, member], p.sibling())
            for row, device in partners:
                sender.send(block, block, cross_sems.at[layer, member * rows + p.row], device)
    for i in range(1, n):
        seq = lax.rem(p.seq + i, n)
        sender.arrived(table_ref.at[seq], table_sems.at[seq], p.sibling())
    for row, device in partners:
        sender.arrived(chunk_ref.at[row], chunk_sems.at[row], p.sibling())
    for layer in range(LAYERS):
        for i in range(members):
            member = lax.rem(p.member + members - i, members)
            for row, device in partners:
                block = weight_ref.at[layer, member * rows + row]
                sender.arrived(block, cross_sems.at[layer, member * rows + row], p.sibling())
    sender.finish()
    for copy in own:
        copy.wait()


def spread(n, rows, wide, small, pack, collective_id):
    layers, members, height, columns = pack.shape
    sends = (n - 1) + (rows - 1) + layers * (members - 1 + members * (rows - 1))
    return pl.pallas_call(
        functools.partial(spread_kernel, n, rows),
        out_shape=(
            jax.ShapeDtypeStruct(wide.shape, wide.dtype),
            jax.ShapeDtypeStruct((n,) + small.shape, small.dtype),
            jax.ShapeDtypeStruct((layers, n, height, columns), pack.dtype),
        ),
        in_specs=vmem_specs(3),
        out_specs=tuple(vmem_specs(3)),
        scratch_shapes=[
            DMA((sends,)),
            DMA((rows,)),
            DMA((n,)),
            DMA((layers, members)),
            DMA((layers, n)),
            DMA((2 + layers,)),
        ],
        compiler_params=remote_params(collective_id),
        name="spread_inputs",
    )(wide, small, pack)


def gather_kernel(n, rows, count, x_ref, out_ref, *sems):
    send_sems, a_sems, b_sems, core_sems, local_sem = sems
    p = Place(n, rows)
    na, nb, core = p.na, p.nb, p.core
    sibling = p.sibling()
    greet(p.axis_peers() + [sibling])
    sender = Sender(send_sems)
    a_steps = [1, na - 1] + list(range(2, na - 1)) if na > 2 else [1]

    def slot(k, a, b):
        return out_ref.at[k, a * nb + b, core]

    for k in range(count):
        mine = x_ref.at[k, core]
        for i in a_steps:
            sender.send(mine, slot(k, p.a, p.b), a_sems.at[k, p.a], p.at(p.am(i), p.b))
        for j in range(1, nb):
            sender.send(mine, slot(k, p.a, p.b), b_sems.at[k, p.member], p.at(p.a, p.bm(j)))
    own = pltpu.make_async_copy(x_ref, out_ref.at[:, p.member], local_sem)
    own.start()
    for k in range(count):
        for i in a_steps:
            a = p.am(i)
            here = slot(k, a, p.b)
            sender.arrived(here, a_sems.at[k, a], sibling)
            for j in range(1, nb):
                sender.send(here, here, b_sems.at[k, a * nb + p.b], p.at(p.a, p.bm(j)))
            sender.send(here, here, core_sems.at[k, a * nb + p.b], sibling)
    for k in range(count):
        for i in [0] + a_steps:
            for j in range(1, nb):
                a, b = p.am(i), p.bm(j)
                here = slot(k, a, b)
                sender.arrived(here, b_sems.at[k, a * nb + b], sibling)
                sender.send(here, here, core_sems.at[k, a * nb + b], sibling)
    for k in range(count):
        for i in range(1, p.members):
            member = lax.rem(p.member + i, p.members)
            sender.arrived(out_ref.at[k, member, 1 - core], core_sems.at[k, member], sibling)
    sender.finish()
    own.wait()


def gather(n, rows, pieces, collective_id):
    stacked = jnp.stack(pieces)
    count, two, height, width = stacked.shape
    members = n // rows
    na, nb = split_sizes(members)
    sends = count * ((na - 1) * (nb + 1) + nb - 1 + na * (nb - 1))
    return pl.pallas_call(
        functools.partial(gather_kernel, n, rows, count),
        out_shape=jax.ShapeDtypeStruct((count, members, two, height, width), stacked.dtype),
        in_specs=vmem_specs(1),
        out_specs=vmem_specs(1)[0],
        scratch_shapes=[
            DMA((sends,)),
            DMA((count, na)),
            DMA((count, members)),
            DMA((count, members)),
            DMA,
        ],
        compiler_params=remote_params(collective_id),
        name="gather_tokens",
    )(stacked)


def reduce_kernel(n, rows, count, *refs):
    x_refs, (out_ref, core_buf, b_buf, a_buf, b_out, a_out) = refs[:count], refs[count : count + 6]
    send_sems, core_sems, b_sems, a_sems, out_sems = refs[count + 6 :]
    p = Place(n, rows)
    na, nb, core = p.na, p.nb, p.core
    sibling = p.sibling()
    greet(p.axis_peers() + [sibling])
    sender = Sender(send_sems)
    a_steps = list(range(2, na - 1)) + [1, na - 1, 0] if na > 2 else [1, 0]
    for k in range(count):
        for i in a_steps:
            for j in list(range(1, nb)) + [0]:
                m = p.am(i) * nb + p.bm(j)
                sender.send(x_refs[k].at[m, 1 - core], core_buf.at[k, m], core_sems.at[k, m], sibling)
    for k in range(count):
        for i in a_steps:
            for j in range(1, nb):
                a, b = p.am(i), p.bm(j)
                m = a * nb + b
                sender.arrived(core_buf.at[k, m], core_sems.at[k, m], sibling)
                b_out[k, m] = (x_refs[k][m, core].astype(f32) + core_buf[k, m].astype(f32)).astype(bf16)
                landing = a * nb + p.b
                sender.send(b_out.at[k, m], b_buf.at[k, landing], b_sems.at[k, landing], p.at(p.a, b))
    for k in range(count):
        for i in a_steps:
            a = p.am(i)
            m = a * nb + p.b
            sender.arrived(core_buf.at[k, m], core_sems.at[k, m], sibling)
            total = x_refs[k][m, core].astype(f32) + core_buf[k, m].astype(f32)
            for j in range(1, nb):
                q = a * nb + p.bm(j)
                sender.arrived(b_buf.at[k, q], b_sems.at[k, q], sibling)
                total = total + b_buf[k, q].astype(f32)
            if i:
                a_out[k, a] = total.astype(bf16)
                sender.send(a_out.at[k, a], a_buf.at[k, p.a], a_sems.at[k, p.a], p.at(a, p.b))
            else:
                out_ref[k, core] = total
    for k in range(count):
        for i in range(1, na):
            a = p.am(i)
            sender.arrived(a_buf.at[k, a], a_sems.at[k, a], sibling)
            out_ref[k, core] += a_buf[k, a].astype(f32)
        sender.send(out_ref.at[k, core], out_ref.at[k, core], out_sems.at[k], sibling)
    for k in range(count):
        sender.arrived(out_ref.at[k, 1 - core], out_sems.at[k], sibling)
    sender.finish()


def reduce(n, rows, pieces, collective_id):
    count = len(pieces)
    members, two, height, width = pieces[0].shape
    na, nb = split_sizes(members)
    sends = count * (members + na * (nb - 1) + na)
    return pl.pallas_call(
        functools.partial(reduce_kernel, n, rows, count),
        out_shape=jax.ShapeDtypeStruct((count, two, height, width), f32),
        in_specs=vmem_specs(count),
        out_specs=vmem_specs(1)[0],
        scratch_shapes=[
            VM((count, members, height, width), bf16),
            VM((count, members, height, width), bf16),
            VM((count, na, height, width), bf16),
            VM((count, members, height, width), bf16),
            VM((count, na, height, width), bf16),
            DMA((sends,)),
            DMA((count, members)),
            DMA((count, members)),
            DMA((count, na)),
            DMA((count,)),
        ],
        compiler_params=remote_params(collective_id),
        name="reduce_tokens",
    )(*pieces)


def collect_kernel(n, rows, *refs):
    (first_ref, second_ref, wide_ref, small_ref, grad_ref, back_ref, table_ref) = refs[:7]
    (cross_buf, block_out, send_sems, cross_sems, block_sems, back_sems, table_sems, local_sems) = refs[7:]
    grads = (first_ref, second_ref)
    p = Place(n, rows)
    members = p.members
    everybody = [{"seq": lax.rem(p.seq + i, n), "tp": p.core} for i in range(1, n)]
    greet(everybody)
    sender = Sender(send_sems)
    partners = [
        (lax.rem(p.row + i, rows), p.device(p.member, row=lax.rem(p.row + i, rows)))
        for i in range(1, rows)
    ]
    order = [lax.rem(p.member + i, members) for i in range(1, members)] + [p.member]
    for i in range(1, n):
        seq = lax.rem(p.seq + i, n)
        sender.send(small_ref.at[seq], table_ref.at[p.seq], table_sems.at[p.seq], {"seq": seq, "tp": p.core})
    for layer in range(LAYERS):
        for member in order:
            for row, device in partners:
                sender.send(
                    grads[layer].at[member * rows + row],
                    cross_buf.at[layer, p.row, member],
                    cross_sems.at[layer, p.row, member],
                    device,
                )
    for row, device in partners:
        sender.send(wide_ref.at[row], back_ref.at[p.row], back_sems.at[p.row], device)
    own = [
        pltpu.make_async_copy(small_ref.at[p.seq], table_ref.at[p.seq], local_sems.at[0]),
        pltpu.make_async_copy(wide_ref.at[p.row], back_ref.at[p.row], local_sems.at[1]),
    ]
    for copy in own:
        copy.start()
    for layer in range(LAYERS):
        for i in list(range(1, members)) + [0]:
            member = lax.rem(p.member + i, members)
            total = grads[layer][member * rows + p.row].astype(f32)
            for row, device in partners:
                buffer = cross_buf.at[layer, row, member]
                sender.arrived(buffer, cross_sems.at[layer, row, member], p.sibling())
                total = total + buffer[...].astype(f32)
            if i:
                block_out[layer, member] = total.astype(bf16)
                sender.send(
                    block_out.at[layer, member],
                    grad_ref.at[layer, p.member],
                    block_sems.at[layer, p.member],
                    p.device(member),
                )
            else:
                grad_ref[layer, member] = total.astype(bf16)
    for i in range(1, n):
        seq = lax.rem(p.seq + i, n)
        sender.arrived(table_ref.at[seq], table_sems.at[seq], p.sibling())
    for row, device in partners:
        sender.arrived(back_ref.at[row], back_sems.at[row], p.sibling())
    for layer in range(LAYERS):
        for i in range(1, members):
            member = lax.rem(p.member + members - i, members)
            sender.arrived(grad_ref.at[layer, member], block_sems.at[layer, member], p.sibling())
    sender.finish()
    for copy in own:
        copy.wait()


def collect(n, rows, first, second, wide, small, collective_id):
    unused, height, columns = first.shape
    members = n // rows
    sends = (n - 1) + (rows - 1) + LAYERS * (members * (rows - 1) + members - 1)
    return pl.pallas_call(
        functools.partial(collect_kernel, n, rows),
        out_shape=(
            jax.ShapeDtypeStruct((LAYERS, members, height, columns), bf16),
            jax.ShapeDtypeStruct(wide.shape, wide.dtype),
            jax.ShapeDtypeStruct(small.shape, small.dtype),
        ),
        in_specs=vmem_specs(4),
        out_specs=tuple(vmem_specs(3)),
        scratch_shapes=[
            VM((LAYERS, rows, members, height, columns), bf16),
            VM((LAYERS, members, height, columns), bf16),
            DMA((sends,)),
            DMA((LAYERS, rows, members)),
            DMA((LAYERS, members)),
            DMA((rows,)),
            DMA((n,)),
            DMA((2,)),
        ],
        compiler_params=remote_params(collective_id),
        name="collect_gradients",
    )(first, second, wide, small)


def share_kernel(n, x_ref, out_ref, send_sems, recv_sems, local_sem):
    seq, core = lax.axis_index("seq"), lax.axis_index("tp")
    others = []
    for i in range(n):
        for j in range(2):
            if i or j:
                others.append((lax.rem(seq + i, n), lax.rem(core + j, 2)))
    greet([{"seq": s, "tp": c} for s, c in others])
    sender = Sender(send_sems)
    here = seq * 2 + core
    for s, c in others:
        sender.send(x_ref, out_ref.at[here], recv_sems.at[here], {"seq": s, "tp": c})
    own = pltpu.make_async_copy(x_ref, out_ref.at[here], local_sem)
    own.start()
    for s, c in others:
        sender.arrived(out_ref.at[s * 2 + c], recv_sems.at[s * 2 + c], {"seq": s, "tp": c})
    sender.finish()
    own.wait()


def share(n, x, collective_id):
    return pl.pallas_call(
        functools.partial(share_kernel, n),
        out_shape=jax.ShapeDtypeStruct((2 * n,) + x.shape, x.dtype),
        in_specs=vmem_specs(1),
        out_specs=vmem_specs(1)[0],
        scratch_shapes=[DMA((2 * n,)), DMA((2 * n,)), DMA],
        compiler_params=remote_params(collective_id),
        name="share_squares",
    )(x)


def dot(left, right):
    return jnp.dot(left, right, preferred_element_type=f32)


def dot_nt(left, right):
    return lax.dot_general(left, right, (((1,), (1,)), ((), ())), preferred_element_type=f32)


def dot_tn(left, right):
    return lax.dot_general(left, right, (((0,), (0,)), ((), ())), preferred_element_type=f32)


def swap_lanes(values):
    width = values.shape[-1]
    lane = lax.broadcasted_iota(jnp.int32, values.shape, 1)
    after = pltpu.roll(values, width - 1, 1)
    before = pltpu.roll(values, 1, 1)
    return jnp.where(lane % 2 == 0, after, before)


gelu_scale = 0.7978845608
gelu_cubic = 0.044715


def gelu(z):
    return 0.5 * z * (1.0 + jnp.tanh(gelu_scale * (z + gelu_cubic * z * z * z)))


def gelu_slope(z):
    inner = jnp.tanh(gelu_scale * (z + gelu_cubic * z * z * z))
    slope = gelu_scale * (1.0 + 3.0 * gelu_cubic * z * z)
    return 0.5 * (1.0 + inner) + 0.5 * z * (1.0 - inner * inner) * slope


def query_tiles(length, share, rows):
    tile = max(64, min(TILE, TILE * 1024 // length))
    first = 0
    if share > 1:
        first = lax.rem(lax.axis_index("seq") // rows, share) * (length // share)
    for i in range(length // share // tile):
        start = pl.multiple_of(first + i * tile, tile) if share > 1 else i * tile
        yield pl.ds(start, tile), start, ((i + 1) * tile if share == 1 else length)


def visible(start, keys, seg_col, seg_row):
    tile = seg_col.shape[0]
    place = start + lax.broadcasted_iota(jnp.int32, (tile, keys), 0)
    other = lax.broadcasted_iota(jnp.int32, (tile, keys), 1)
    return (other <= place) & (seg_col == seg_row)


def forward_kernel(batch, share, ff, h_ref, w_ref, cos_ref, sin_ref, segc_ref, segr_ref, *outs):
    part_ref, q_ref, k_ref, v_ref, o_ref, lse_ref, a_ref, z_ref = outs
    length = h_ref.shape[0]
    f = 4 * HEAD

    @pl.loop(0, length // TILE)
    def project(t):
        rows = pl.ds(t * TILE, TILE)
        h = h_ref[rows, :]
        mixed = dot(h, w_ref[:, :f])
        qk = mixed[:, : 2 * HEAD]
        qk = qk * cos_ref[rows, :] + swap_lanes(qk) * sin_ref[rows, :]
        q_ref[rows, :] = (qk[:, :HEAD].astype(bf16).astype(f32) * HEAD**-0.5).astype(bf16)
        k_ref[rows, :] = qk[:, HEAD:].astype(bf16)
        v_ref[rows, :] = mixed[:, 2 * HEAD : 3 * HEAD].astype(bf16)
        z = dot(h, w_ref[:, f : f + ff])
        z_ref[rows, :] = z
        a_ref[rows, :] = gelu(z).astype(bf16)

    if share > 1:
        o_ref[...] = jnp.zeros_like(o_ref)
        lse_ref[...] = jnp.zeros_like(lse_ref)
    for rows, start, keys in query_tiles(length, share, batch):
        scores = dot_nt(q_ref[rows, :], k_ref[:keys, :])
        seen = visible(start, keys, segc_ref[rows, :], segr_ref[:, :keys])
        scores = jnp.where(seen, scores, low_score)
        peak = jnp.max(scores, axis=1, keepdims=True)
        weights = jnp.exp(scores - peak)
        total = jnp.sum(weights, axis=1, keepdims=True)
        lse_ref[rows, :] = peak + jnp.log(total)
        shares = (weights * (1.0 / total)).astype(bf16)
        o_ref[rows, :] = dot(shares, v_ref[:keys, :]).astype(bf16)

    @pl.loop(0, length // TILE)
    def branch(t):
        rows = pl.ds(t * TILE, TILE)
        out = dot_nt(o_ref[rows, :], w_ref[:, 3 * HEAD : f])
        out = out + dot_nt(a_ref[rows, :], w_ref[:, f + ff : f + 2 * ff])
        part_ref[rows, :] = out.astype(bf16)


def forward(batch, share, ff, h, w, cosine, sine, seg_col, seg_row):
    length, width = h.shape
    column = jax.ShapeDtypeStruct((length, HEAD), bf16)
    return pl.pallas_call(
        functools.partial(forward_kernel, batch, share, ff),
        out_shape=(
            jax.ShapeDtypeStruct((length, width), bf16),
            column,
            column,
            column,
            column,
            jax.ShapeDtypeStruct((length, 1), f32),
            jax.ShapeDtypeStruct((length, ff), bf16),
            jax.ShapeDtypeStruct((length, ff), f32),
        ),
        in_specs=vmem_specs(6),
        out_specs=tuple(vmem_specs(8)),
        compiler_params=pltpu.CompilerParams(vmem_limit_bytes=56 * megabyte),
        name="layer_forward",
    )(h, w, cosine, sine, seg_col, seg_row)


def backward_kernel(batch, share, ff, g_ref, h_ref, w_ref, cos_ref, sin_ref, segc_ref, segr_ref, *refs):
    q_ref, k_ref, v_ref, o_ref, lse_ref, a_ref, z_ref, part_ref, dw_ref = refs[:9]
    dz_ref, do_ref, dq_ref, dk_ref, dv_ref, mix_ref = refs[9:]
    length, width = h_ref.shape
    f = 4 * HEAD

    @pl.loop(0, length // TILE)
    def feed(t):
        rows = pl.ds(t * TILE, TILE)
        g = g_ref[rows, :]
        da = dot(g, w_ref[:, f + ff : f + 2 * ff])
        dz_ref[rows, :] = (da * gelu_slope(z_ref[rows, :])).astype(bf16)
        do_ref[rows, :] = dot(g, w_ref[:, :f])[:, 3 * HEAD :].astype(bf16)

    dk_ref[...] = jnp.zeros_like(dk_ref)
    dv_ref[...] = jnp.zeros_like(dv_ref)
    if share > 1:
        dq_ref[...] = jnp.zeros_like(dq_ref)
    for rows, start, keys in query_tiles(length, share, batch):
        q, head_grad = q_ref[rows, :], do_ref[rows, :]
        scores = dot_nt(q, k_ref[:keys, :])
        seen = visible(start, keys, segc_ref[rows, :], segr_ref[:, :keys])
        shares = jnp.where(seen, jnp.exp(scores - lse_ref[rows, :]), 0.0)
        share_grads = dot_nt(head_grad, v_ref[:keys, :])
        delta = jnp.sum(shares * share_grads, axis=1, keepdims=True)
        score_grads = (shares * (share_grads - delta)).astype(bf16)
        dq_ref[rows, :] = dot(score_grads, k_ref[:keys, :]) * HEAD**-0.5
        dk_ref[:keys, :] += dot_tn(score_grads, q)
        dv_ref[:keys, :] += dot_tn(shares.astype(bf16), head_grad)

    @pl.loop(0, length // TILE)
    def inward(t):
        rows = pl.ds(t * TILE, TILE)
        qk = jnp.concatenate([dq_ref[rows, :], dk_ref[rows, :]], axis=1)
        qk = qk * cos_ref[rows, :] + swap_lanes(qk * sin_ref[rows, :])
        rest = jnp.concatenate([dv_ref[rows, :], jnp.zeros((TILE, HEAD), f32)], axis=1)
        mix = jnp.concatenate([qk, rest], axis=1).astype(bf16)
        mix_ref[rows, :] = mix
        out = dot_nt(mix, w_ref[:, :f]) + dot_nt(dz_ref[rows, :], w_ref[:, f : f + ff])
        part_ref[rows, :] = out.astype(bf16)

    @pl.loop(0, width // TILE)
    def weights(t):
        rows = pl.ds(t * TILE, TILE)
        h, g = h_ref[:, rows], g_ref[:, rows]
        mixed = dot_tn(h, mix_ref[...])
        out = dot_tn(g, o_ref[...])
        dw_ref[rows, :f] = jnp.concatenate([mixed[:, : 3 * HEAD], out], axis=1).astype(bf16)
        dw_ref[rows, f : f + ff] = dot_tn(h, dz_ref[...]).astype(bf16)
        dw_ref[rows, f + ff : f + 2 * ff] = dot_tn(g, a_ref[...]).astype(bf16)


def backward(batch, share, ff, g, h, w, cosine, sine, seg_col, seg_row, kept):
    length, width = h.shape
    return pl.pallas_call(
        functools.partial(backward_kernel, batch, share, ff),
        out_shape=(
            jax.ShapeDtypeStruct((length, width), bf16),
            jax.ShapeDtypeStruct(w.shape, bf16),
        ),
        in_specs=vmem_specs(14),
        out_specs=tuple(vmem_specs(2)),
        scratch_shapes=[
            VM((length, ff), bf16),
            VM((length, HEAD), bf16),
            VM((length, HEAD), f32),
            VM((length, HEAD), f32),
            VM((length, HEAD), f32),
            VM((length, 4 * HEAD), bf16),
        ],
        compiler_params=pltpu.CompilerParams(vmem_limit_bytes=60 * megabyte),
        name="layer_backward",
    )(g, h, w, cosine, sine, seg_col, seg_row, *kept)


def layer_norm(inputs):
    average = jnp.mean(inputs, axis=-1, keepdims=True)
    centred = inputs - average
    spread_here = jnp.mean(centred * centred, axis=-1, keepdims=True)
    inverse = lax.rsqrt(spread_here + norm_eps)
    return (centred * inverse, inverse)


def norm_back(grads, normed_grads, xhat, inverse, gain):
    scaled = normed_grads * gain
    average = jnp.mean(scaled, axis=-1, keepdims=True)
    along = jnp.mean(scaled * xhat, axis=-1, keepdims=True)
    return grads + (scaled - average - xhat * along) * inverse


def rotary_tables(positions):
    column = jnp.arange(HEAD)
    inside = column < ROTARY
    pair_index = column % ROTARY // 2
    frequency = jnp.exp(pair_index.astype(f32) * (-2.0 * math.log(10000.0) / ROTARY))
    angles = positions[:, None] * frequency
    cosine = jnp.where(inside, jnp.cos(angles), 1.0)
    signed = jnp.where(column % 2 == 0, -1.0, 1.0)
    sine = jnp.where(inside, signed * jnp.sin(angles), 0.0)
    return (jnp.tile(cosine, (1, 2)), jnp.tile(sine, (1, 2)))


def pad_lanes(values, width=128):
    return jnp.pad(values, [(0, 0)] * (values.ndim - 1) + [(0, width - values.shape[-1])])


def adam_update(weight, first, second, gradient, factor_clip, rate, decay):
    clipped = gradient * factor_clip
    first_new = beta_one * first + (1.0 - beta_one) * clipped
    second_new = beta_two * second + (1.0 - beta_two) * clipped * clipped
    first_hat = first_new / (1.0 - beta_one**STEP)
    second_hat = second_new / (1.0 - beta_two**STEP)
    weight_new = weight - rate * (first_hat / (jnp.sqrt(second_hat) + adam_eps) + decay * weight)
    return (weight_new, first_new, second_new)


def pack_weights(n, rows, qkv_weight, out_weight, in_weight, down_weight):
    layers, height = qkv_weight.shape[:2]
    members = n // rows
    heads = qkv_weight.shape[3] // HEAD
    share = members // heads
    ff = in_weight.shape[2] // members
    mixed = jnp.concatenate([qkv_weight, out_weight[:, :, None, :]], axis=2).astype(bf16)
    mixed = mixed.reshape(layers, height, 4, heads, HEAD).transpose(0, 3, 1, 2, 4)
    mixed = mixed.reshape(layers, heads, height, 4 * HEAD)
    if share > 1:
        mixed = jnp.repeat(mixed, share, axis=1)
    feeds = [
        weight.astype(bf16).reshape(layers, height, members, ff).transpose(0, 2, 1, 3)
        for weight in (in_weight, down_weight)
    ]
    return jnp.concatenate([mixed] + feeds, axis=3)


def unpack_gradients(grads, heads, ff):
    layers, members, height, unused = grads.shape
    grads = grads.astype(f32)
    share = members // heads
    mixed = grads[..., : 4 * HEAD]
    if share > 1:
        mixed = mixed.reshape(layers, heads, share, height, 4 * HEAD).sum(2)
    mixed = mixed.reshape(layers, heads, height, 4, HEAD).transpose(0, 2, 3, 1, 4)
    mixed = mixed.reshape(layers, height, 4, heads * HEAD)
    feeds = [
        grads[..., 4 * HEAD + k * ff : 4 * HEAD + (k + 1) * ff]
        .transpose(0, 2, 1, 3)
        .reshape(layers, height, members * ff)
        for k in range(2)
    ]
    return (mixed[:, :, :3], mixed[:, :, 3], feeds[0], feeds[1])


def shards_apart(
    n,
    activations,
    cotangent,
    segment_ids,
    position_ids,
    qkv_weight,
    out_weight,
    in_weight,
    down_weight,
    norm_params,
    qkv_first,
    out_first,
    in_first,
    down_first,
    norm_first,
    qkv_second,
    out_second,
    in_second,
    down_second,
    norm_second,
):
    rows, span, width = activations.shape
    members = n // rows
    length = n * span
    half = rows * span // 2
    heads = qkv_weight.shape[3] // HEAD
    share_queries = members // heads
    ff = in_weight.shape[2] // members
    row = lax.axis_index("seq") % rows

    pack = pack_weights(n, rows, qkv_weight, out_weight, in_weight, down_weight)
    norm_low = norm_params.astype(bf16).astype(f32).reshape(LAYERS * 3, -1)
    small = jnp.concatenate(
        [
            pad_lanes(norm_low),
            pad_lanes(position_ids.astype(f32)),
            pad_lanes(segment_ids.astype(f32)),
        ]
    )
    small = jnp.pad(small, ((0, -small.shape[0] % 8), (0, 0)))
    wide = jnp.stack([activations, cotangent], axis=1)
    chunk, table, weights = spread(n, rows, wide, small, pack, 0)
    weights = weights.reshape(LAYERS, width, -1)
    inputs = chunk[:, 0].reshape(rows * span, width)
    out_grads = chunk[:, 1].reshape(rows * span, width)
    own_columns = norm_params.shape[-1]
    norms = table[:, : LAYERS * 3, :own_columns].transpose(1, 0, 2).reshape(LAYERS, 3, width)
    positions = lax.dynamic_index_in_dim(table, LAYERS * 3 + row, 1, False)[:, :span].reshape(length)
    segments = lax.dynamic_index_in_dim(table, LAYERS * 3 + rows + row, 1, False)[:, :span].reshape(length)
    cosine, sine = rotary_tables(positions)
    places = (cosine, sine, segments[:, None], segments[None, :])

    def halves(values):
        return values.astype(bf16).reshape(2, half, width)

    def whole(values):
        return values.reshape(length, width)

    def parts(values):
        return values.reshape(members, 2, half, width)

    xhat_0, inverse_0 = layer_norm(inputs)
    normed = xhat_0 * norms[0, 0] + norms[0, 1]
    got = gather(n, rows, [halves(normed), halves(out_grads)], 1)
    normed_0, grads_1 = whole(got[0]), whole(got[1])
    part, *kept_0 = forward(rows, share_queries, ff, normed_0, weights[0], *places)
    branch = reduce(n, rows, [parts(part)], 2)[0].reshape(inputs.shape)
    middle = inputs + branch + norms[0, 2]
    xhat_1, inverse_1 = layer_norm(middle)
    normed = xhat_1 * norms[1, 0] + norms[1, 1]
    normed_1 = whole(gather(n, rows, [halves(normed)], 3)[0])
    part, *kept_1 = forward(rows, share_queries, ff, normed_1, weights[1], *places)
    back_part, weight_grads_1 = backward(rows, share_queries, ff, grads_1, normed_1, weights[1], *places, kept_1)
    sums = reduce(n, rows, [parts(part), parts(back_part)], 4).reshape((2,) + inputs.shape)
    result = middle + sums[0] + norms[1, 2]
    normed_grads_1 = sums[1]
    grads_mid = norm_back(out_grads, normed_grads_1, xhat_1, inverse_1, norms[1, 0])
    grads_0 = whole(gather(n, rows, [halves(grads_mid)], 5)[0])
    back_part, weight_grads_0 = backward(rows, share_queries, ff, grads_0, normed_0, weights[0], *places, kept_0)
    normed_grads_0 = reduce(n, rows, [parts(back_part)], 6)[0].reshape(inputs.shape)
    input_grad = norm_back(grads_mid, normed_grads_0, xhat_0, inverse_0, norms[0, 0])

    small_grads = jnp.stack(
        [
            jnp.sum(normed_grads_0 * xhat_0, axis=0),
            jnp.sum(normed_grads_0, axis=0),
            jnp.sum(grads_mid, axis=0),
            jnp.sum(normed_grads_1 * xhat_1, axis=0),
            jnp.sum(normed_grads_1, axis=0),
            jnp.sum(out_grads, axis=0),
        ]
    )
    small_grads = pad_lanes(small_grads.reshape(LAYERS * 3, n, own_columns).transpose(1, 0, 2))
    small_grads = jnp.pad(small_grads, ((0, 0), (0, 8 - LAYERS * 3), (0, 0)))
    wide_out = jnp.stack([result.reshape(rows, span, width), input_grad.reshape(rows, span, width)], axis=1)
    height = width // n
    grads, wide_back, table_back = collect(
        n,
        rows,
        weight_grads_0.reshape(n, height, -1),
        weight_grads_1.reshape(n, height, -1),
        wide_out,
        small_grads,
        7,
    )
    norm_grads = jnp.sum(table_back, axis=0)[: LAYERS * 3, :own_columns].reshape(norm_params.shape)
    qkv_grads, out_weight_grads, in_grads, down_grads = unpack_gradients(grads, heads, ff)
    matrix_squares = sum(
        (jnp.sum(block * block) for block in (qkv_grads, out_weight_grads, in_grads, down_grads))
    )
    squares = matrix_squares + jnp.sum(norm_grads * norm_grads) / 2
    everyone = share(n, jnp.full((8, 128), squares, f32), 8)
    grad_norm = jnp.sqrt(jnp.sum(everyone[:, 0, 0]))
    total_parameters = LAYERS * width * (4 * 2 * heads * HEAD + 2 * 2 * members * ff + 3)
    factor_clip = jnp.minimum(1.0, clip_share * math.sqrt(total_parameters) / (grad_norm + 1e-06))
    qkv_new, qkv_first_new, qkv_second_new = adam_update(
        qkv_weight, qkv_first, qkv_second, qkv_grads, factor_clip, rate_matrix, decay_matrix
    )
    out_new, out_first_new, out_second_new = adam_update(
        out_weight, out_first, out_second, out_weight_grads, factor_clip, rate_output, decay_matrix
    )
    in_new, in_first_new, in_second_new = adam_update(
        in_weight, in_first, in_second, in_grads, factor_clip, rate_matrix, decay_matrix
    )
    down_new, down_first_new, down_second_new = adam_update(
        down_weight, down_first, down_second, down_grads, factor_clip, rate_matrix, decay_matrix
    )
    norm_new, norm_first_new, norm_second_new = adam_update(
        norm_params, norm_first, norm_second, norm_grads, factor_clip, rate_vector, 0.0
    )
    bias_clipped = norm_grads[:, 2] * factor_clip
    return (
        wide_back[:, 0],
        wide_back[:, 1],
        grad_norm,
        qkv_new,
        out_new,
        in_new,
        down_new,
        norm_new,
        qkv_first_new,
        out_first_new,
        in_first_new,
        down_first_new,
        norm_first_new,
        qkv_second_new,
        out_second_new,
        in_second_new,
        down_second_new,
        norm_second_new,
        bias_clipped,
    )


def flip(index, bits):
    bit = 1
    while bit <= bits:
        if bits & bit:
            index = index + bit * (1 - 2 * lax.rem(index // bit, 2))
        bit *= 2
    return index


class Net:
    def __init__(self, n, rows, half, pieces, send_sems):
        self.p = Place(n, rows)
        self.half, self.pieces = half, pieces
        self.send_sems, self.used = send_sems, 0
        self.sibling = self.p.sibling()

    def send_sem(self):
        self.used += 1
        return self.send_sems.at[self.used - 1]

    def everybody(self):
        p = self.p
        return [{"seq": lax.rem(p.seq + i, p.n), "tp": p.core} for i in range(1, p.n)]

    def everyone(self):
        p = self.p
        return self.everybody() + [
            {"seq": lax.rem(p.seq + i, p.n), "tp": 1 - p.core} for i in range(p.n)
        ]

    def partner(self):
        return self.p.device(self.p.member, row=1 - self.p.row)

    def a_of(self, k):
        return flip(self.p.a, k)

    def b_of(self, j):
        return flip(self.p.b, j)

    def tokens(self, member, core, piece):
        size = self.half // self.pieces
        start = (member * 2 + core) * self.half + piece * size
        return pl.ds(pl.multiple_of(start, size), size)

    def lines(self, slot, piece):
        size = self.half // self.pieces
        return pl.ds(pl.multiple_of(slot * self.half + piece * size, size), size)

    def own(self):
        start = (self.p.member * 2 + self.p.core) * self.half
        return pl.ds(pl.multiple_of(start, self.half), self.half)

    def tile_rows(self, a):
        size = self.p.nb * 2 * self.half
        return pl.ds(pl.multiple_of(a * size, size), size)

    def tile(self, k):
        return self.tile_rows(self.a_of(k))

    def far_first(self):
        a, na = self.p.a, self.p.na
        if na != 4:
            return [self.a_of(k) for k in range(na - 1, -1, -1)]
        upper = a // 2
        low = a + upper * (3 - 2 * a)
        order = [3, 2, 1 - low, low]
        return [v + upper * (3 - 2 * v) for v in order]

    def sides(self, distance):
        a, na = self.p.a, self.p.na
        return [
            (a >= distance, a - distance, a < na - 1, a + 1),
            (a + distance < na, a + distance, a > 0, a - 1),
        ]


class Sends:
    def __init__(self, net, lone=0):
        self.sibling = net.sibling
        self.shared = net.send_sem()
        self.lone = [net.send_sem() for _ in range(lone)]
        self.made, self.conditional = 0, []

    def copy(self, src, dst, sem, device, send_sem):
        return pltpu.make_async_remote_copy(
            src_ref=src, dst_ref=dst, send_sem=send_sem, recv_sem=sem, device_id=device, device_id_type=MESH
        )

    def send(self, src, dst, sem, device):
        self.copy(src, dst, sem, device, self.shared).start()
        self.made += 1

    def send_if(self, when, src, dst, sem, device):
        number = len(self.conditional)
        self.conditional.append((when, src, dst, sem, device))
        pl.when(when)(lambda: self.copy(src, dst, sem, device, self.lone[number]).start())

    def finish(self, whole):
        self.copy(whole, whole, self.shared, self.sibling, self.shared).wait_send()
        for number, (when, *copy) in enumerate(self.conditional):
            pl.when(when)(lambda number=number, copy=copy: self.copy(*copy, self.lone[number]).wait_send())
        self.made, self.conditional = 0, []


def wait_for(net, dst, sem):
    pltpu.make_async_remote_copy(
        src_ref=dst,
        dst_ref=dst,
        send_sem=net.send_sems.at[0],
        recv_sem=sem,
        device_id=net.sibling,
        device_id_type=MESH,
    ).wait_recv()


class Gather:
    def __init__(self, net, sems):
        self.net = net
        self.a_sems, self.b_sems, self.core_sems = sems
        self.sends = Sends(net, lone=2 * net.pieces * net.p.na)

    def slot(self, a, b, core, q):
        return self.out.at[self.net.tokens(a * self.net.p.nb + b, core, q), :]

    def to_line(self, a, q, to, when):
        p = self.net.p
        here = self.slot(a, p.b, p.core, q)
        self.sends.send_if(when, here, here, self.a_sems.at[a, q], p.at(to, p.b))

    def to_rest(self, a, q):
        net, p = self.net, self.net.p
        here = self.slot(a, p.b, p.core, q)
        for j in range(1, p.nb):
            self.sends.send(here, here, self.b_sems.at[a * p.nb + p.b, q], p.at(p.a, net.b_of(j)))
        self.sends.send(here, here, self.core_sems.at[a, q], net.sibling)

    def start(self, out):
        p = self.net.p
        self.out = out
        for q in range(self.net.pieces):
            self.to_line(p.a, q, p.a + 1, p.a < p.na - 1)
            self.to_line(p.a, q, p.a - 1, p.a > 0)
            self.to_rest(p.a, q)

    def hop(self, distance):
        net, p = self.net, self.net.p
        for q in range(net.pieces):
            for there, a, more, beyond in net.sides(distance):

                @pl.when(there)
                def _():
                    wait_for(net, self.slot(a, p.b, p.core, q), self.a_sems.at[a, q])

                self.to_line(a, q, beyond, jnp.logical_and(there, more))
                pl.when(there)(lambda: self.to_rest(a, q))

    def side(self, distance):
        net, p = self.net, self.net.p
        for j in range(1, p.nb):
            b = net.b_of(j)
            for q in range(net.pieces):
                for there, a, more, beyond in net.sides(distance)[: 2 if distance else 1]:

                    @pl.when(there)
                    def _():
                        here = self.slot(a, b, p.core, q)
                        wait_for(net, here, self.b_sems.at[a * p.nb + b, q])
                        self.sends.send(here, here, self.core_sems.at[a, q], net.sibling)

    def settle(self, distance):
        net, p = self.net, self.net.p
        size = p.nb * net.half // net.pieces
        for q in range(net.pieces):
            for there, a, more, beyond in net.sides(distance)[: 2 if distance else 1]:

                @pl.when(there)
                def _():
                    wait_for(net, self.out.at[pl.ds(0, size), :], self.core_sems.at[a, q])

    def steps(self):
        na = self.net.p.na
        if na > 1:
            self.hop(1)
        self.side(0)
        yield None
        for k in range(na):
            if k + 2 < na:
                self.hop(k + 2)
            if k + 1 < na:
                self.side(k + 1)
            self.settle(k)
            yield k

    def finish(self):
        p = self.net.p
        self.sends.finish(self.out.at[pl.ds(0, (p.na * (p.nb - 1) + p.members) * self.net.half), :])


class Reduce:
    def __init__(self, net, x, total, bufs, sems):
        self.net, self.x, self.total = net, x, total
        self.core_buf, self.b_out, self.b_buf, self.a_out, self.a_buf, self.sum_buf = bufs
        self.core_sems, self.b_sems, self.a_sems = sems
        self.sends = Sends(net, lone=2 * net.pieces * (net.p.na - 1))

    def offer(self, a):
        net, p = self.net, self.net.p
        for j in list(range(1, p.nb)) + [0]:
            m = a * p.nb + net.b_of(j)
            for q in range(net.pieces):
                self.sends.send(
                    self.x.at[net.tokens(m, 1 - p.core, q), :],
                    self.core_buf.at[net.lines(m, q), :],
                    self.core_sems.at[m, q],
                    net.sibling,
                )

    def pair_sum(self, m, q):
        net = self.net
        lines = net.lines(m, q)
        wait_for(net, self.core_buf.at[lines, :], self.core_sems.at[m, q])
        return self.x[net.tokens(m, net.p.core, q), :].astype(f32) + self.core_buf[lines, :].astype(f32)

    def targets(self, distance):
        return self.net.sides(distance)[: 2 if distance else 1]

    def relay(self, distance):
        net, p = self.net, self.net.p
        for there, a, unused_more, unused_beyond in self.targets(distance):
            for j in range(1, p.nb):
                b = net.b_of(j)
                for q in range(net.pieces):

                    @pl.when(there)
                    def _():
                        m, landing = a * p.nb + b, a * p.nb + p.b
                        self.b_out[net.lines(m, q), :] = self.pair_sum(m, q).astype(bf16)
                        self.sends.send(
                            self.b_out.at[net.lines(m, q), :],
                            self.b_buf.at[net.lines(landing, q), :],
                            self.b_sems.at[landing, q],
                            p.at(p.a, b),
                        )

    def row_sum(self, a, q):
        net, p = self.net, self.net.p
        total = self.pair_sum(a * p.nb + p.b, q)
        for j in range(1, p.nb):
            m = a * p.nb + net.b_of(j)
            wait_for(net, self.b_buf.at[net.lines(m, q), :], self.b_sems.at[m, q])
            total = total + self.b_buf[net.lines(m, q), :].astype(f32)
        return total

    def passing(self, up, a, q):
        net, p = self.net, self.net.p
        slot = a if up else p.na + a
        wait_for(net, self.a_buf.at[net.lines(slot, q), :], self.a_sems.at[slot, q])
        return self.a_buf[net.lines(slot, q), :].astype(f32)

    def pass_on(self, distance):
        net, p = self.net, self.net.p
        size = net.half // net.pieces
        for side, (there, a, unused_more, unused_beyond) in enumerate(net.sides(distance)):
            up = side == 1
            behind = p.a > 0 if up else p.a < p.na - 1
            slot = a if up else p.na + a
            for q in range(net.pieces):
                part = slice(q * size, (q + 1) * size)

                @pl.when(there)
                def _():
                    self.sum_buf[part, :] = self.row_sum(a, q)

                @pl.when(jnp.logical_and(there, behind))
                def _():
                    self.sum_buf[part, :] += self.passing(up, a, q)

                @pl.when(there)
                def _():
                    self.a_out[net.lines(slot, q), :] = self.sum_buf[part, :].astype(bf16)

                self.sends.send_if(
                    there,
                    self.a_out.at[net.lines(slot, q), :],
                    self.a_buf.at[net.lines(slot, q), :],
                    self.a_sems.at[slot, q],
                    p.at(p.a + 1 if up else p.a - 1, p.b),
                )

    def arrive(self):
        net, p = self.net, self.net.p
        size = net.half // net.pieces
        for q in range(net.pieces):
            part = slice(q * size, (q + 1) * size)
            self.total[part, :] = self.row_sum(p.a, q)
        for q in range(net.pieces):
            part = slice(q * size, (q + 1) * size)

            @pl.when(p.a > 0)
            def _():
                self.total[part, :] += self.passing(True, p.a, q)

            @pl.when(p.a < p.na - 1)
            def _():
                self.total[part, :] += self.passing(False, p.a, q)

    def steps(self):
        na = self.net.p.na
        for distance in range(na - 1, -1, -1):
            self.relay(distance)
            yield
        for distance in range(na - 1, 0, -1):
            self.pass_on(distance)
            yield
        self.arrive()
        yield

    def finish(self):
        p = self.net.p
        self.sends.finish(self.x.at[pl.ds(0, (p.members + p.na * (p.nb - 1)) * self.net.half), :])


class Spread:
    def __init__(self, net, pack, w, block_sems, cross_sems):
        self.net, self.pack, self.w = net, pack, w
        self.block_sems, self.cross_sems = block_sems, cross_sems
        self.height = pack.shape[1]
        self.sends = Sends(net)

    def rows(self, seq):
        return pl.ds(pl.multiple_of(seq * self.height, self.height), self.height)

    def start(self):
        net, p = self.net, self.net.p
        here = self.w.at[self.rows(p.seq), :]
        for k in range(1, p.members):
            member = flip(p.member, k)
            self.sends.send(
                self.pack.at[member], here, self.block_sems.at[p.member], p.device(member)
            )
        self.sends.send(
            self.pack.at[p.member], here, self.cross_sems.at[p.member], net.partner()
        )
        self.w[self.rows(p.seq), :] = self.pack[p.member]

    def steps(self):
        net, p = self.net, self.net.p
        for k in range(1, p.members):
            member = flip(p.member, k)
            seq = member * p.rows + p.row
            here = self.w.at[self.rows(seq), :]
            wait_for(net, here, self.block_sems.at[member])
            self.sends.send(here, here, self.cross_sems.at[member], net.partner())
            yield
        for k in range(p.members):
            member = flip(p.member, k)
            seq = member * p.rows + 1 - p.row
            wait_for(net, self.w.at[self.rows(seq), :], self.cross_sems.at[member])
        yield

    def finish(self):
        self.sends.finish(self.w.at[pl.ds(0, (2 * self.net.p.members - 1) * self.height), :])


class Collect:
    def __init__(self, net, dw, grad, cross_buf, block_out, cross_sems, block_sems):
        self.net, self.dw, self.grad = net, dw, grad
        self.cross_buf, self.block_out = cross_buf, block_out
        self.cross_sems, self.block_sems = cross_sems, block_sems
        self.height = grad.shape[1]
        self.sends = Sends(net)

    def rows(self, seq):
        return pl.ds(pl.multiple_of(seq * self.height, self.height), self.height)

    def order(self):
        return list(range(self.net.p.members - 1, -1, -1))

    def offer(self, start, end):
        net, p = self.net, self.net.p
        step = self.height * p.rows
        for member in range(start // step, end // step):
            self.sends.send(
                self.dw.at[self.rows(member * p.rows + 1 - p.row), :],
                self.cross_buf.at[member],
                self.cross_sems.at[member],
                net.partner(),
            )

    def relay(self, k):
        net, p = self.net, self.net.p
        member = flip(p.member, k)
        wait_for(net, self.cross_buf.at[member], self.cross_sems.at[member])
        mine = self.dw[self.rows(member * p.rows + p.row), :]
        total = (mine.astype(f32) + self.cross_buf[member].astype(f32)).astype(bf16)
        if k:
            self.block_out[member] = total
            self.sends.send(
                self.block_out.at[member],
                self.grad.at[p.member],
                self.block_sems.at[p.member],
                p.device(member),
            )
        else:
            self.grad[member] = total

    def settle(self, k):
        member = flip(self.net.p.member, k)
        wait_for(self.net, self.grad.at[member], self.block_sems.at[member])

    def steps(self):
        for k in self.order():
            self.relay(k)
            yield
        for k in range(1, self.net.p.members):
            self.settle(k)
            yield

    def finish(self):
        self.sends.finish(self.dw.at[pl.ds(0, (2 * self.net.p.members - 1) * self.height), :])


def advance(steps, count=1):
    for _ in range(count):
        next(steps, None)


def drain(steps):
    for _ in steps:
        pass


class Layer:
    def __init__(self, r, layer):
        self.r, self.layer = r, layer
        self.length, self.width = getattr(r, "h%d" % layer).shape
        self.f = 4 * HEAD
        self.ff = (getattr(r, "w%d" % layer).shape[1] - self.f) // 2

    def __getattr__(self, name):
        return getattr(self.r, name + str(self.layer))

    def project(self, rows):
        r, f = self.r, self.f
        h = self.h[rows, :]
        mixed = dot(h, self.w[:, :f])
        qk = mixed[:, : 2 * HEAD]
        qk = qk * r.cos[rows, :] + swap_lanes(qk) * r.sin[rows, :]
        self.q[rows, :] = (qk[:, :HEAD].astype(bf16).astype(f32) * HEAD**-0.5).astype(bf16)
        self.k[rows, :] = qk[:, HEAD:].astype(bf16)
        self.v[rows, :] = mixed[:, 2 * HEAD : 3 * HEAD].astype(bf16)

    def feed(self, rows):
        z = dot(self.h[rows, :], self.w[:, self.f : self.f + self.ff])
        self.z[rows, :] = z
        self.a[rows, :] = gelu(z).astype(bf16)

    def attend(self, i):
        r = self.r
        start, keys = i * TILE, (i + 1) * TILE
        rows = pl.ds(start, TILE)
        scores = dot_nt(self.q[rows, :], self.k[:keys, :])
        seen = visible(start, keys, r.segc[rows, :], r.segr[:, :keys])
        scores = jnp.where(seen, scores, low_score)
        peak = jnp.max(scores, axis=1, keepdims=True)
        weights = jnp.exp(scores - peak)
        total = jnp.sum(weights, axis=1, keepdims=True)
        self.lse[rows, :] = peak + jnp.log(total)
        shares = (weights * (1.0 / total)).astype(bf16)
        self.o[rows, :] = dot(shares, self.v[:keys, :]).astype(bf16)

    def branch(self, rows, part):
        f, ff = self.f, self.ff
        out = dot_nt(self.o[rows, :], self.w[:, 3 * HEAD : f])
        out = out + dot_nt(self.a[rows, :], self.w[:, f + ff : f + 2 * ff])
        part[rows, :] = out.astype(bf16)

    def feed_back(self, rows):
        r, f, ff = self.r, self.f, self.ff
        g = self.g[rows, :]
        da = dot(g, self.w[:, f + ff : f + 2 * ff])
        r.dz[rows, :] = (da * gelu_slope(self.z[rows, :])).astype(bf16)
        r.do[rows, :] = dot(g, self.w[:, :f])[:, 3 * HEAD :].astype(bf16)

    def attend_back(self, i):
        r = self.r
        start, keys = i * TILE, (i + 1) * TILE
        rows = pl.ds(start, TILE)
        q, head_grad = self.q[rows, :], r.do[rows, :]
        scores = dot_nt(q, self.k[:keys, :])
        seen = visible(start, keys, r.segc[rows, :], r.segr[:, :keys])
        shares = jnp.where(seen, jnp.exp(scores - self.lse[rows, :]), 0.0)
        share_grads = dot_nt(head_grad, self.v[:keys, :])
        delta = jnp.sum(shares * share_grads, axis=1, keepdims=True)
        score_grads = (shares * (share_grads - delta)).astype(bf16)
        r.dq[rows, :] = dot(score_grads, self.k[:keys, :]) * HEAD**-0.5
        dk = dot_tn(score_grads, q)
        dv = dot_tn(shares.astype(bf16), head_grad)
        if i + 1 == self.length // TILE:
            r.dk[:keys, :] = dk
            r.dv[:keys, :] = dv
        else:
            r.dk[:keys, :] += dk
            r.dv[:keys, :] += dv

    def inward(self, rows, part):
        r, f, ff = self.r, self.f, self.ff
        qk = jnp.concatenate([r.dq[rows, :], r.dk[rows, :]], axis=1)
        qk = qk * r.cos[rows, :] + swap_lanes(qk * r.sin[rows, :])
        rest = jnp.concatenate([r.dv[rows, :], jnp.zeros((TILE, HEAD), f32)], axis=1)
        mix = jnp.concatenate([qk, rest], axis=1).astype(bf16)
        r.mix[rows, :] = mix
        out = dot_nt(mix, self.w[:, :f]) + dot_nt(r.dz[rows, :], self.w[:, f : f + ff])
        part[rows, :] = out.astype(bf16)

    def weight_grads(self, t):
        r, f, ff = self.r, self.f, self.ff
        rows = pl.ds(t * TILE, TILE)
        h, g = self.h[:, rows], self.g[:, rows]
        mixed = dot_tn(h, r.mix[...])
        out = dot_tn(g, self.o[...])
        self.dw[rows, :f] = jnp.concatenate([mixed[:, : 3 * HEAD], out], axis=1).astype(bf16)
        self.dw[rows, f : f + ff] = dot_tn(h, r.dz[...]).astype(bf16)
        self.dw[rows, f + ff : f + 2 * ff] = dot_tn(g, self.a[...]).astype(bf16)


def norm_row(r, layer, kind):
    return r.norms[layer * 3 + kind : layer * 3 + kind + 1, :]


def column_sums(values):
    return jnp.sum(values, axis=0, keepdims=True)


def cross_rows(net, r):
    p = net.p
    same = p.core == p.row

    def crossing(i):
        source, landing = ((r.act, r.x0), (r.cot, r.gr1))[i]
        return pltpu.make_async_remote_copy(
            src_ref=source.at[1 - p.row],
            dst_ref=landing,
            send_sem=r.x_sems.at[i],
            recv_sem=r.x_sems.at[2 + i],
            device_id=net.partner(),
            device_id_type=MESH,
        )

    @pl.when(same)
    def _():
        crossing(0).start()
        crossing(1).start()
        r.x0[...] = r.act[p.row]
        r.gr1[...] = r.cot[p.row]

    def arrive():
        @pl.when(jnp.logical_not(same))
        def _():
            crossing(0).wait_recv()
            crossing(1).wait_recv()

    def finish():
        @pl.when(same)
        def _():
            crossing(0).wait_send()
            crossing(1).wait_send()

    return (arrive, finish)


def give_back(net, r, i, source, target):
    p = net.p
    same = p.core == p.row

    def copy(j, device, row):
        return pltpu.make_async_remote_copy(
            src_ref=source,
            dst_ref=target.at[row],
            send_sem=r.back_sems.at[i, j],
            recv_sem=r.back_sems.at[i, 2 + row],
            device_id=device,
            device_id_type=MESH,
        )

    def far(j):
        return copy(j, p.device(p.member, row=1 - p.row, core=lax.rem(p.core + j, 2)), p.row)

    @pl.when(same)
    def _():
        copy(0, net.sibling, p.row).start()
        target[p.row] = source[...]

    @pl.when(jnp.logical_not(same))
    def _():
        far(0).start()
        far(1).start()

    def finish():
        @pl.when(same)
        def _():
            copy(0, net.sibling, p.row).wait_send()

        @pl.when(jnp.logical_not(same))
        def _():
            far(0).wait_send()
            far(1).wait_send()
            copy(0, net.sibling, p.row).wait_recv()

        copy(0, net.sibling, 1 - p.row).wait_recv()

    return finish


def share_all(net, sem, out, source):
    p = net.p
    here = p.seq * 2 + p.core
    others = [
        (lax.rem(p.seq + i, p.n), lax.rem(p.core + j, 2)) for i in range(p.n) for j in range(2) if i or j
    ]
    sends = Sends(net)
    for seq, core in others:
        sends.send(source(seq), out.at[here], sem, {"seq": seq, "tp": core})
    whole = out.at[pl.ds(0, len(others))]
    return (lambda: wait_for(net, whole, sem), lambda: sends.finish(whole))


def position_tables(net, r):
    p = net.p
    span = r.act.shape[1]
    lines = []
    for kind in range(2):
        row = LAYERS * 3 + kind * p.rows + p.row
        pieces = [r.table[s, pl.ds(row, 1), :span] for s in range(p.n)]
        lines.append(jnp.concatenate(pieces, axis=1))
    positions, segments = lines
    r.segr[...] = segments
    pair = lax.broadcasted_iota(jnp.int32, (ROTARY, positions.shape[1]), 0) // 2
    angles = jnp.exp(pair.astype(f32) * (-2.0 * math.log(10000.0) / ROTARY)) * positions
    sign = jnp.where(lax.broadcasted_iota(jnp.int32, angles.shape, 0) % 2 == 0, -1.0, 1.0)
    ones = jnp.ones((HEAD - ROTARY, angles.shape[1]), f32)
    cosine, sine = jnp.cos(angles), jnp.sin(angles) * sign
    cosine = jnp.concatenate([cosine, ones, cosine, ones], axis=0)
    sine = jnp.concatenate([sine, ones * 0.0, sine, ones * 0.0], axis=0)
    segments = jnp.broadcast_to(segments, (128, segments.shape[1]))
    for t in range(angles.shape[1] // 128):
        block = slice(t * 128, (t + 1) * 128)
        r.cos[block, :] = cosine[:, block].T
        r.sin[block, :] = sine[:, block].T
        r.segc[block, :] = segments[:, block].T[:, :1]


def pack_layer(r, layer):
    members, ff = r.pack.shape[1], (r.pack.shape[3] - 4 * HEAD) // 2
    f = 4 * HEAD
    for pair in range(members // 2):
        lanes = slice(pair * 2 * HEAD, (pair + 1) * 2 * HEAD)
        kinds = [r.qkv[layer, kind, :, lanes].astype(bf16) for kind in range(3)]
        kinds.append(r.out[layer, :, lanes].astype(bf16))
        for i in range(2):
            own = slice(i * HEAD, (i + 1) * HEAD)
            r.pack[layer, 2 * pair + i, :, :f] = jnp.concatenate([kind[:, own] for kind in kinds], axis=1)
    for member in range(members):
        lanes = slice(member * ff, (member + 1) * ff)
        r.pack[layer, member, :, f : f + ff] = getattr(r, "in")[layer, :, lanes].astype(bf16)
        r.pack[layer, member, :, f + ff :] = r.down[layer, :, lanes].astype(bf16)


def pack_small(r):
    rows, span = r.pos.shape
    r.small[...] = jnp.zeros_like(r.small)
    columns = r.norm.shape[2]
    for layer in range(LAYERS):
        r.small[layer * 3 : layer * 3 + 3, :columns] = r.norm[:, layer, :].astype(bf16).astype(f32)
    r.small[LAYERS * 3 : LAYERS * 3 + rows, :span] = r.pos[...].astype(f32)
    r.small[LAYERS * 3 + rows : LAYERS * 3 + 2 * rows, :span] = r.seg[...].astype(f32)


def whole_part(net, r):
    p = net.p
    n, width = p.n, r.act.shape[2]
    finishes = []

    pack_small(r)
    greet(net.everyone())
    gathers = [Gather(net, r.gather_a), Gather(net, r.gather_b)]
    reduces = [
        Reduce(net, r.part_a, r.total_a, r.bufs_a, r.reduce_a),
        Reduce(net, r.part_b, r.total_b, r.bufs_b, r.reduce_b),
    ]
    table_sends = Sends(net)
    finishes.append(lambda: table_sends.finish(r.table.at[pl.ds(0, n - 1)]))
    for i in range(1, n):
        device = {"seq": lax.rem(p.seq + i, n), "tp": p.core}
        table_sends.send(r.small, r.table.at[p.seq], r.table_sem, device)
    r.table[p.seq] = r.small[...]
    cross_arrive, cross_finish = cross_rows(net, r)
    finishes.append(cross_finish)
    spreads = [
        Spread(net, r.pack.at[k], (r.w0, r.w1)[k], r.block_sems.at[k], r.cross_sems.at[k]) for k in range(LAYERS)
    ]
    collects = [
        Collect(
            net,
            (r.dw0, r.dw1)[k],
            r.grads.at[k],
            r.cross_buf.at[k],
            r.block_out.at[k],
            r.collect_sems.at[k],
            r.block_sems.at[k],
        )
        for k in range(LAYERS)
    ]
    finishes.extend(collect.finish for collect in collects)
    pack_layer(r, 0)
    spreads[0].start()
    wait_for(net, r.table.at[pl.ds(0, n - 1)], r.table_sem)
    own_columns = width // n
    many = 128 // own_columns
    for s in range(0, n, many):
        r.norms[:, s * own_columns : (s + many) * own_columns] = jnp.concatenate(
            [r.table[s + i, 0:8, :own_columns] for i in range(many)], axis=1
        )
    cross_arrive()
    xhat, inverse = layer_norm(r.x0[...])
    normed = xhat * norm_row(r, 0, 0) + norm_row(r, 0, 1)
    r.h0[net.own(), :] = normed.astype(bf16)
    gather = gathers[0]
    gather.start(r.h0)
    r.g1[net.own(), :] = r.gr1[...].astype(bf16)
    position_tables(net, r)
    pack_layer(r, 1)

    layer = Layer(r, 0)
    tiles = range(layer.length // TILE)
    weight_steps = spreads[0].steps()
    gather_steps = gather.steps()
    advance(gather_steps)
    advance(weight_steps, p.members - 1)
    advance(gather_steps, 4)
    drain(weight_steps)
    spreads[1].start()
    weight_steps = spreads[1].steps()
    for k in tiles:
        layer.project(net.tile(k))
        layer.feed(net.tile(k))
    drain(gather_steps)
    for i in tiles:
        layer.attend(i)
        advance(weight_steps)
    reduce = reduces[0]
    for a in net.far_first():
        layer.branch(net.tile_rows(a), r.part_a)
        reduce.offer(a)
    drain(reduce.steps())
    middle = r.x0[...] + (r.total_a[...] + norm_row(r, 0, 2))
    r.x1[...] = middle
    xhat, inverse = layer_norm(middle)
    normed = xhat * norm_row(r, 1, 0) + norm_row(r, 1, 1)
    r.h1[net.own(), :] = normed.astype(bf16)
    gathers[0].finish()
    gather = gathers[1]
    gather.start(r.h1)

    layer = Layer(r, 1)
    drain(weight_steps)
    gather_steps = gather.steps()
    grad_gather = gathers[0]
    for k in tiles:
        if k == 0:
            advance(gather_steps, 2)
        else:
            advance(gather_steps)
        if k == len(tiles) - 2:
            grad_gather.start(r.g1)
        layer.project(net.tile(k))
        layer.feed(net.tile(k))
    drain(gather_steps)
    grad_steps = grad_gather.steps()
    for i in tiles:
        layer.attend(i)
        advance(grad_steps)
    drain(grad_steps)
    forward_reduce = reduces[1]
    forward_steps = forward_reduce.steps()
    for a in net.far_first():
        layer.branch(net.tile_rows(a), r.part_b)
        forward_reduce.offer(a)

    for k in tiles:
        layer.feed_back(net.tile(k))
        advance(forward_steps)
    for i in reversed(tiles):
        layer.attend_back(i)
        advance(forward_steps)
    reduce = reduces[0]
    reduce.finish()
    for spread in spreads:
        spread.finish()
    steps = reduce.steps()
    for a in net.far_first():
        layer.inward(net.tile_rows(a), r.part_a)
        reduce.offer(a)
    drain(forward_steps)
    for t in range(layer.width // TILE):
        layer.weight_grads(t)
        collects[1].offer(t * TILE, (t + 1) * TILE)
        advance(steps, 2)
    drain(steps)
    xhat, inverse = layer_norm(r.x1[...])
    normed_grads = r.total_a[...]
    r.sums1[...] = jnp.concatenate(
        [
            column_sums(normed_grads * xhat),
            column_sums(normed_grads),
            column_sums(r.gr1[...]),
            jnp.zeros((5, layer.width), f32),
        ]
    )
    below = norm_back(r.gr1[...], normed_grads, xhat, inverse, norm_row(r, 1, 0))
    r.gr0[...] = below
    r.g0[net.own(), :] = below.astype(bf16)
    gather = gathers[1]
    gather.finish()
    gather.start(r.g0)
    r.result[...] = r.x1[...] + (r.total_b[...] + norm_row(r, 1, 2))
    finishes.append(give_back(net, r, 0, r.result, r.results))

    layer = Layer(r, 0)
    gather_steps = gather.steps()
    collect_steps = collects[1].steps()
    for k in tiles:
        if k == 0:
            advance(gather_steps, 2)
        else:
            advance(gather_steps)
        layer.feed_back(net.tile(k))
    drain(gather_steps)
    for i in reversed(tiles):
        layer.attend_back(i)
        advance(collect_steps, 2)
    reduce = forward_reduce
    reduce.finish()
    steps = reduce.steps()
    for a in net.far_first():
        layer.inward(net.tile_rows(a), r.part_b)
        reduce.offer(a)
    for t in range(layer.width // TILE):
        layer.weight_grads(t)
        collects[0].offer(t * TILE, (t + 1) * TILE)
        advance(steps, 2)
    drain(steps)
    normed_grads = r.total_b[...]
    xhat, inverse = layer_norm(r.x0[...])
    r.in_grad[...] = norm_back(r.gr0[...], normed_grads, xhat, inverse, norm_row(r, 0, 0))
    finishes.append(give_back(net, r, 1, r.in_grad, r.in_grads))
    rows = [
        column_sums(normed_grads * xhat),
        column_sums(normed_grads),
        column_sums(r.gr0[...]),
        r.sums1[0:3, :],
        jnp.zeros((2, width), f32),
    ]
    rows = jnp.concatenate(rows)
    for s in range(n):
        r.small_out[s] = pad_lanes(rows[:, s * own_columns : (s + 1) * own_columns])
    here = p.seq * 2 + p.core
    small_arrive, small_finish = share_all(net, r.small_sem, r.small_in, lambda seq: r.small_out.at[seq])
    finishes.append(small_finish)
    r.small_in[here] = r.small_out[p.seq]
    drain(collect_steps)
    drain(collects[0].steps())
    small_arrive()
    norm_grads = jnp.sum(r.small_in[...], axis=0)
    r.norm_grads[...] = norm_grads
    squares = 0.5 * jnp.sum(norm_grads * norm_grads, axis=(0, 1), keepdims=True)
    for layer_index in range(LAYERS):
        for member in range(p.members):
            block = r.grads[layer_index, member].astype(f32)
            squares = squares + jnp.sum(block * block, axis=(0, 1), keepdims=True)
    r.squares[here] = jnp.broadcast_to(squares, (8, 128))
    square_arrive, square_finish = share_all(net, r.square_sem, r.squares, lambda seq: r.squares.at[here])
    finishes.append(square_finish)
    square_arrive()
    r.norm_out[...] = jnp.sqrt(jnp.sum(r.squares[...], axis=0))
    for part in gathers + reduces:
        part.finish()
    for finish in finishes:
        finish()


def fused_call(name, part, geometry, ins, outs, scratch, collective_id):
    flat, places = [], []
    for key, spec in scratch.items():
        group = spec if isinstance(spec, tuple) else (spec,)
        places.append((key, len(flat), len(group), isinstance(spec, tuple)))
        flat.extend(group)

    def kernel(*refs):
        r = types.SimpleNamespace(**dict(zip([*ins, *outs], refs)))
        rest = refs[len(ins) + len(outs) :]
        for key, start, count, grouped in places:
            setattr(r, key, rest[start : start + count] if grouped else rest[start])
        part(Net(*geometry, r.send_sems), r)

    results = pl.pallas_call(
        kernel,
        out_shape=tuple(outs.values()),
        in_specs=vmem_specs(len(ins)),
        out_specs=tuple(vmem_specs(len(outs))),
        scratch_shapes=flat,
        compiler_params=remote_params(collective_id),
        name=name,
    )(*ins.values())
    return types.SimpleNamespace(**dict(zip(outs, results)))


def by_kind(array):
    return jnp.swapaxes(array, array.ndim - 3, array.ndim - 2)


def optimizer_kernel(limit, grads_ref, norm_grads_ref, norm_ref, result_ref, in_grad_ref, *refs):
    weights, firsts, seconds = refs[:5], refs[5:10], refs[10:15]
    new_weights, new_firsts, new_seconds = refs[15:20], refs[20:25], refs[25:30]
    bias_ref, total_ref, result_out_ref, in_grad_out_ref = refs[30:]
    result_out_ref[...] = result_ref[...]
    in_grad_out_ref[...] = in_grad_ref[...]
    norm = norm_ref[0:1, 0:1]
    factor = jnp.minimum(1.0, limit / (norm + 1e-06))
    members, ff = grads_ref.shape[1], (grads_ref.shape[3] - 4 * HEAD) // 2
    f = 4 * HEAD

    def update(kind, where, gradient, rate, decay):
        found = adam_update(
            weights[kind][where], firsts[kind][where], seconds[kind][where], gradient, factor, rate, decay
        )
        for ref, value in zip((new_weights[kind], new_firsts[kind], new_seconds[kind]), found):
            ref[where] = value

    blocks = [grads_ref[0, member].astype(f32) for member in range(members)]
    for part in range(4):
        lanes = slice(part * HEAD, (part + 1) * HEAD)
        gradient = jnp.concatenate([block[:, lanes] for block in blocks], axis=1)
        if part < 3:
            update(0, (0, part), gradient, rate_matrix, decay_matrix)
        else:
            update(1, (0,), gradient, rate_output, decay_matrix)
    for member in range(members):
        lanes = slice(member * ff, (member + 1) * ff)
        update(2, (0, slice(None), lanes), blocks[member][:, f : f + ff], rate_matrix, decay_matrix)
        update(3, (0, slice(None), lanes), blocks[member][:, f + ff :], rate_matrix, decay_matrix)

    @pl.when((pl.program_id(0) == 0) & (pl.program_id(1) == 0))
    def _():
        columns = weights[4].shape[2]
        for layer in range(LAYERS):
            gradient = norm_grads_ref[layer * 3 : layer * 3 + 3, :columns]
            update(4, (slice(None), layer), gradient, rate_vector, 0.0)
            bias_ref[layer : layer + 1, :] = gradient[2:3, :] * factor
        total_ref[...] = norm


def optimizer(found, weights, firsts, seconds, parameters):
    layers, height = weights[1].shape[:2]
    rows = height // 2
    grads = found.grads

    def spec(array):
        extent = array.shape
        if extent[0] == 3:
            return pl.BlockSpec(extent, lambda i, j: (0, 0, 0))
        if array.ndim == 4:
            return pl.BlockSpec((1, 3, rows, extent[3]), lambda i, j: (i, 0, j, 0))
        return pl.BlockSpec((1, rows * extent[1] // height, extent[2]), lambda i, j: (i, j, 0))

    def fixed(*extent):
        return pl.BlockSpec(extent, lambda i, j: (0,) * len(extent))

    arrays = [by_kind(array) if i % 5 in (0, 4) else array for i, array in enumerate(weights + firsts + seconds)]
    tokens = [found.results, found.in_grads]
    bias_shape = (layers, weights[4].shape[2])
    made = pl.pallas_call(
        functools.partial(optimizer_kernel, clip_share * math.sqrt(parameters)),
        grid=(layers, height // rows),
        in_specs=[
            pl.BlockSpec((1, grads.shape[1], rows, grads.shape[3]), lambda i, j: (i, 0, j, 0)),
            fixed(8, 128),
            fixed(8, 128),
        ]
        + [spec(array) for array in tokens + arrays],
        out_specs=tuple(
            [spec(array) for array in arrays]
            + [fixed(*bias_shape), fixed(1, 1)]
            + [spec(array) for array in tokens]
        ),
        out_shape=tuple(
            [jax.ShapeDtypeStruct(array.shape, array.dtype) for array in arrays]
            + [jax.ShapeDtypeStruct(bias_shape, f32), jax.ShapeDtypeStruct((1, 1), f32)]
            + [jax.ShapeDtypeStruct(array.shape, array.dtype) for array in tokens]
        ),
        compiler_params=pltpu.CompilerParams(vmem_limit_bytes=56 * megabyte),
        name="optimizer",
    )(grads, found.norm_grads, found.norm_out, *tokens, *arrays)
    count = len(arrays)
    updated = [by_kind(array) if i % 5 in (0, 4) else array for i, array in enumerate(made[:count])]
    bias, norm, result, in_grad = made[count:]
    return (result, in_grad, norm.reshape(()), *updated, bias)


def shards_together(
    n,
    activations,
    cotangent,
    segment_ids,
    position_ids,
    qkv_weight,
    out_weight,
    in_weight,
    down_weight,
    norm_params,
    qkv_first,
    out_first,
    in_first,
    down_first,
    norm_first,
    qkv_second,
    out_second,
    in_second,
    down_second,
    norm_second,
):
    rows, span, width = activations.shape
    members = n // rows
    na, nb = split_sizes(members)
    length = n * span
    half = rows * span // 2
    pieces = 2
    heads = qkv_weight.shape[3] // HEAD
    ff = in_weight.shape[2] // members
    height = width // n
    columns = 4 * HEAD + 2 * ff
    geometry = (n, rows, half, pieces)

    def shape(*extent, kind=f32):
        return jax.ShapeDtypeStruct(extent, kind)

    def scratch_like(shapes, suffix):
        return {key + suffix: VM(value.shape, value.dtype) for key, value in shapes.items()}

    gather_sems = (DMA((na, pieces)), DMA((members, pieces)), DMA((na, pieces)))
    reduce_sems = (DMA((members, pieces)), DMA((members, pieces)), DMA((2 * na, pieces)))
    reduce_bufs = tuple(
        VM((count * half, width), bf16) for count in (members, members, members, 2 * na, 2 * na)
    ) + (VM((half, width), f32),)
    kept = dict(
        q=shape(length, HEAD, kind=bf16),
        k=shape(length, HEAD, kind=bf16),
        v=shape(length, HEAD, kind=bf16),
        o=shape(length, HEAD, kind=bf16),
        lse=shape(length, 1),
        a=shape(length, ff, kind=bf16),
        z=shape(length, ff),
        w=shape(width, columns, kind=bf16),
        dw=shape(width, columns, kind=bf16),
        h=shape(length, width, kind=bf16),
        g=shape(length, width, kind=bf16),
        x=shape(half, width),
        gr=shape(half, width),
    )
    lines = LAYERS * 3 + 2 * rows
    three = fused_call(
        "whole_part",
        whole_part,
        geometry,
        {
            "act": activations,
            "cot": cotangent,
            "seg": segment_ids,
            "pos": position_ids,
            "qkv": by_kind(qkv_weight),
            "out": out_weight,
            "in": in_weight,
            "down": down_weight,
            "norm": by_kind(norm_params),
        },
        dict(
            results=shape(rows, span, width),
            in_grads=shape(rows, span, width),
            grads=shape(LAYERS, members, height, columns, kind=bf16),
            norm_grads=shape(8, 128),
            norm_out=shape(8, 128),
        ),
        dict(
            small=VM((-(-lines // 8) * 8, 128), f32),
            table=VM((n, -(-lines // 8) * 8, 128), f32),
            pack=VM((LAYERS, members, height, columns), bf16),
            norms=VM((8, width), f32),
            cos=VM((length, 128), f32),
            sin=VM((length, 128), f32),
            segc=VM((length, 1), f32),
            segr=VM((1, length), f32),
            **scratch_like(kept, "0"),
            **scratch_like(kept, "1"),
            dz=VM((length, ff), bf16),
            do=VM((length, HEAD), bf16),
            dq=VM((length, HEAD), f32),
            dk=VM((length, HEAD), f32),
            dv=VM((length, HEAD), f32),
            mix=VM((length, 4 * HEAD), bf16),
            part_a=VM((length, width), bf16),
            part_b=VM((length, width), bf16),
            total_a=VM((half, width), f32),
            total_b=VM((half, width), f32),
            bufs_a=reduce_bufs,
            bufs_b=reduce_bufs,
            result=VM((half, width), f32),
            in_grad=VM((half, width), f32),
            sums1=VM((8, width), f32),
            cross_buf=VM((LAYERS, members, height, columns), bf16),
            block_out=VM((LAYERS, members, height, columns), bf16),
            small_out=VM((n, 8, 128), f32),
            small_in=VM((2 * n, 8, 128), f32),
            squares=VM((2 * n, 8, 128), f32),
            reduce_a=reduce_sems,
            reduce_b=reduce_sems,
            gather_a=gather_sems,
            gather_b=gather_sems,
            x_sems=DMA((4,)),
            back_sems=DMA((2, 4)),
            table_sem=DMA,
            small_sem=DMA,
            square_sem=DMA,
            block_sems=DMA((LAYERS, members)),
            cross_sems=DMA((LAYERS, members)),
            collect_sems=DMA((LAYERS, members)),
            send_sems=DMA((2 * (1 + 2 * pieces * na) + 2 * (1 + 2 * pieces * (na - 1)) + 7,)),
        ),
        0,
    )
    return optimizer(
        three,
        (qkv_weight, out_weight, in_weight, down_weight, norm_params),
        (qkv_first, out_first, in_first, down_first, norm_first),
        (qkv_second, out_second, in_second, down_second, norm_second),
        LAYERS * width * (4 * 2 * heads * HEAD + 2 * 2 * members * ff + 3),
    )


def shards(n, activations, *others):
    rows, span, width = activations.shape
    together = 12 * n * span * width * 2 <= 40 * megabyte and rows == 2 and n * span % TILE == 0
    return (shards_together if together else shards_apart)(n, activations, *others)


def solution(mesh):
    tokens = P(None, "seq", None)
    qkv = P(None, "seq", None, "tp")
    matrix = P(None, "seq", "tp")
    norm = P(None, None, "seq")
    kinds = (qkv, matrix, matrix, matrix, norm)
    return jax.shard_map(
        functools.partial(shards, mesh.shape["seq"]),
        mesh=mesh,
        in_specs=(tokens, tokens, P(None, "seq"), P(None, "seq")) + kinds * 3,
        out_specs=(tokens, tokens, P()) + kinds * 3 + (P(None, "seq"),),
        check_vma=False,
    )
```

```python
import functools
import math
import types

import jax
import jax.numpy as jnp
from jax import lax
from jax.experimental import pallas as pl
from jax.experimental.pallas import tpu as pltpu
from jax.sharding import PartitionSpec as P

HEAD = 64
ROTARY = 32
LAYERS = 2
STEP = 10
TILE = 256

norm_eps = 1e-05
beta_one = 0.9
beta_two = 0.999
adam_eps = 1e-08
rate_matrix = 0.05
rate_output = 0.15
rate_vector = 1.0
decay_matrix = 0.1
clip_share = 0.25
low_score = -1e30

MESH = pl.DeviceIdType.MESH
VM = pltpu.VMEM
DMA = pltpu.SemaphoreType.DMA
bf16 = jnp.bfloat16
f32 = jnp.float32
megabyte = 1 << 20


def split_sizes(members):
    nb = 1 << ((members.bit_length() - 1) // 2)
    return (members // nb, nb)


class Place:
    def __init__(self, n, rows):
        self.n, self.rows = n, rows
        self.members = n // rows
        self.na, self.nb = split_sizes(self.members)
        self.seq = lax.axis_index("seq")
        self.core = lax.axis_index("tp")
        self.row = lax.rem(self.seq, rows)
        self.member = self.seq // rows
        self.a = self.member // self.nb
        self.b = lax.rem(self.member, self.nb)

    def am(self, step):
        return lax.rem(self.a + step, self.na)

    def bm(self, step):
        return lax.rem(self.b + step, self.nb)

    def device(self, member, row=None, core=None):
        row = self.row if row is None else row
        return {"seq": member * self.rows + row, "tp": self.core if core is None else core}

    def at(self, a, b):
        return self.device(a * self.nb + b)

    def sibling(self):
        return self.device(self.member, core=1 - self.core)

    def partners(self):
        return [self.device(self.member, row=lax.rem(self.row + i, self.rows)) for i in range(1, self.rows)]

    def axis_peers(self):
        peers = [self.at(self.am(i), self.b) for i in range(1, self.na)]
        peers += [self.at(self.a, self.bm(j)) for j in range(1, self.nb)]
        return peers

    def other_members(self):
        return [self.device(lax.rem(self.member + i, self.members)) for i in range(1, self.members)]


def greet(devices):
    barrier = pltpu.get_barrier_semaphore()
    for device in devices:
        pl.semaphore_signal(barrier, inc=1, device_id=device, device_id_type=MESH)
    pl.semaphore_wait(barrier, len(devices))


class Sender:
    def __init__(self, send_sems):
        self.send_sems, self.copies = send_sems, []

    def send(self, src, dst, recv_sem, device):
        copy = pltpu.make_async_remote_copy(
            src_ref=src,
            dst_ref=dst,
            send_sem=self.send_sems.at[len(self.copies)],
            recv_sem=recv_sem,
            device_id=device,
            device_id_type=MESH,
        )
        copy.start()
        self.copies.append(copy)

    def arrived(self, dst, recv_sem, device):
        pltpu.make_async_remote_copy(
            src_ref=dst,
            dst_ref=dst,
            send_sem=self.send_sems.at[0],
            recv_sem=recv_sem,
            device_id=device,
            device_id_type=MESH,
        ).wait_recv()

    def finish(self):
        for copy in self.copies:
            copy.wait_send()


def remote_params(collective_id):
    return pltpu.CompilerParams(
        collective_id=collective_id, has_side_effects=True, vmem_limit_bytes=56 * megabyte
    )


def vmem_specs(count):
    return [pl.BlockSpec(memory_space=VM)] * count


def spread_kernel(n, rows, wide_ref, small_ref, pack_ref, chunk_ref, table_ref, weight_ref, *sems):
    (send_sems, chunk_sems, table_sems, block_sems, cross_sems, local_sems) = sems
    p = Place(n, rows)
    members = p.members
    everybody = [
        {"seq": lax.rem(p.seq + i, n), "tp": p.core} for i in range(1, n)
    ]
    greet(everybody)
    sender = Sender(send_sems)
    partners = [
        (lax.rem(p.row + i, rows), p.device(p.member, row=lax.rem(p.row + i, rows)))
        for i in range(1, rows)
    ]
    for device in everybody:
        sender.send(small_ref, table_ref.at[p.seq], table_sems.at[p.seq], device)
    for row, device in partners:
        sender.send(wide_ref.at[row], chunk_ref.at[p.row], chunk_sems.at[p.row], device)
    for layer in range(LAYERS):
        for i in range(1, members):
            member = lax.rem(p.member + i, members)
            sender.send(
                pack_ref.at[layer, member],
                weight_ref.at[layer, p.seq],
                block_sems.at[layer, p.member],
                p.device(member),
            )
        for row, device in partners:
            sender.send(
                pack_ref.at[layer, p.member],
                weight_ref.at[layer, p.seq],
                cross_sems.at[layer, p.seq],
                device,
            )
    own = [
        pltpu.make_async_copy(small_ref, table_ref.at[p.seq], local_sems.at[0]),
        pltpu.make_async_copy(wide_ref.at[p.row], chunk_ref.at[p.row], local_sems.at[1]),
    ]
    for layer in range(LAYERS):
        own.append(
            pltpu.make_async_copy(
                pack_ref.at[layer, p.member], weight_ref.at[layer, p.seq], local_sems.at[2 + layer]
            )
        )
    for copy in own:
        copy.start()
    for layer in range(LAYERS):
        for i in range(1, members):
            member = lax.rem(p.member + members - i, members)
            block = weight_ref.at[layer, member * rows + p.row]
            sender.arrived(block, block_sems.at[layer, member], p.sibling())
            for row, device in partners:
                sender.send(block, block, cross_sems.at[layer, member * rows + p.row], device)
    for i in range(1, n):
        seq = lax.rem(p.seq + i, n)
        sender.arrived(table_ref.at[seq], table_sems.at[seq], p.sibling())
    for row, device in partners:
        sender.arrived(chunk_ref.at[row], chunk_sems.at[row], p.sibling())
    for layer in range(LAYERS):
        for i in range(members):
            member = lax.rem(p.member + members - i, members)
            for row, device in partners:
                block = weight_ref.at[layer, member * rows + row]
                sender.arrived(block, cross_sems.at[layer, member * rows + row], p.sibling())
    sender.finish()
    for copy in own:
        copy.wait()


def spread(n, rows, wide, small, pack, collective_id):
    layers, members, height, columns = pack.shape
    sends = (n - 1) + (rows - 1) + layers * (members - 1 + members * (rows - 1))
    return pl.pallas_call(
        functools.partial(spread_kernel, n, rows),
        out_shape=(
            jax.ShapeDtypeStruct(wide.shape, wide.dtype),
            jax.ShapeDtypeStruct((n,) + small.shape, small.dtype),
            jax.ShapeDtypeStruct((layers, n, height, columns), pack.dtype),
        ),
        in_specs=vmem_specs(3),
        out_specs=tuple(vmem_specs(3)),
        scratch_shapes=[
            DMA((sends,)),
            DMA((rows,)),
            DMA((n,)),
            DMA((layers, members)),
            DMA((layers, n)),
            DMA((2 + layers,)),
        ],
        compiler_params=remote_params(collective_id),
        name="spread_inputs",
    )(wide, small, pack)


def gather_kernel(n, rows, count, x_ref, out_ref, *sems):
    send_sems, a_sems, b_sems, core_sems, local_sem = sems
    p = Place(n, rows)
    na, nb, core = p.na, p.nb, p.core
    sibling = p.sibling()
    greet(p.axis_peers() + [sibling])
    sender = Sender(send_sems)
    a_steps = [1, na - 1] + list(range(2, na - 1)) if na > 2 else [1]

    def slot(k, a, b):
        return out_ref.at[k, a * nb + b, core]

    for k in range(count):
        mine = x_ref.at[k, core]
        for i in a_steps:
            sender.send(mine, slot(k, p.a, p.b), a_sems.at[k, p.a], p.at(p.am(i), p.b))
        for j in range(1, nb):
            sender.send(mine, slot(k, p.a, p.b), b_sems.at[k, p.member], p.at(p.a, p.bm(j)))
    own = pltpu.make_async_copy(x_ref, out_ref.at[:, p.member], local_sem)
    own.start()
    for k in range(count):
        for i in a_steps:
            a = p.am(i)
            here = slot(k, a, p.b)
            sender.arrived(here, a_sems.at[k, a], sibling)
            for j in range(1, nb):
                sender.send(here, here, b_sems.at[k, a * nb + p.b], p.at(p.a, p.bm(j)))
            sender.send(here, here, core_sems.at[k, a * nb + p.b], sibling)
    for k in range(count):
        for i in [0] + a_steps:
            for j in range(1, nb):
                a, b = p.am(i), p.bm(j)
                here = slot(k, a, b)
                sender.arrived(here, b_sems.at[k, a * nb + b], sibling)
                sender.send(here, here, core_sems.at[k, a * nb + b], sibling)
    for k in range(count):
        for i in range(1, p.members):
            member = lax.rem(p.member + i, p.members)
            sender.arrived(out_ref.at[k, member, 1 - core], core_sems.at[k, member], sibling)
    sender.finish()
    own.wait()


def gather(n, rows, pieces, collective_id):
    stacked = jnp.stack(pieces)
    count, two, height, width = stacked.shape
    members = n // rows
    na, nb = split_sizes(members)
    sends = count * ((na - 1) * (nb + 1) + nb - 1 + na * (nb - 1))
    return pl.pallas_call(
        functools.partial(gather_kernel, n, rows, count),
        out_shape=jax.ShapeDtypeStruct((count, members, two, height, width), stacked.dtype),
        in_specs=vmem_specs(1),
        out_specs=vmem_specs(1)[0],
        scratch_shapes=[
            DMA((sends,)),
            DMA((count, na)),
            DMA((count, members)),
            DMA((count, members)),
            DMA,
        ],
        compiler_params=remote_params(collective_id),
        name="gather_tokens",
    )(stacked)


def reduce_kernel(n, rows, count, *refs):
    x_refs, (out_ref, core_buf, b_buf, a_buf, b_out, a_out) = refs[:count], refs[count : count + 6]
    send_sems, core_sems, b_sems, a_sems, out_sems = refs[count + 6 :]
    p = Place(n, rows)
    na, nb, core = p.na, p.nb, p.core
    sibling = p.sibling()
    greet(p.axis_peers() + [sibling])
    sender = Sender(send_sems)
    a_steps = list(range(2, na - 1)) + [1, na - 1, 0] if na > 2 else [1, 0]
    for k in range(count):
        for i in a_steps:
            for j in list(range(1, nb)) + [0]:
                m = p.am(i) * nb + p.bm(j)
                sender.send(x_refs[k].at[m, 1 - core], core_buf.at[k, m], core_sems.at[k, m], sibling)
    for k in range(count):
        for i in a_steps:
            for j in range(1, nb):
                a, b = p.am(i), p.bm(j)
                m = a * nb + b
                sender.arrived(core_buf.at[k, m], core_sems.at[k, m], sibling)
                b_out[k, m] = (x_refs[k][m, core].astype(f32) + core_buf[k, m].astype(f32)).astype(bf16)
                landing = a * nb + p.b
                sender.send(b_out.at[k, m], b_buf.at[k, landing], b_sems.at[k, landing], p.at(p.a, b))
    for k in range(count):
        for i in a_steps:
            a = p.am(i)
            m = a * nb + p.b
            sender.arrived(core_buf.at[k, m], core_sems.at[k, m], sibling)
            total = x_refs[k][m, core].astype(f32) + core_buf[k, m].astype(f32)
            for j in range(1, nb):
                q = a * nb + p.bm(j)
                sender.arrived(b_buf.at[k, q], b_sems.at[k, q], sibling)
                total = total + b_buf[k, q].astype(f32)
            if i:
                a_out[k, a] = total.astype(bf16)
                sender.send(a_out.at[k, a], a_buf.at[k, p.a], a_sems.at[k, p.a], p.at(a, p.b))
            else:
                out_ref[k, core] = total
    for k in range(count):
        for i in range(1, na):
            a = p.am(i)
            sender.arrived(a_buf.at[k, a], a_sems.at[k, a], sibling)
            out_ref[k, core] += a_buf[k, a].astype(f32)
        sender.send(out_ref.at[k, core], out_ref.at[k, core], out_sems.at[k], sibling)
    for k in range(count):
        sender.arrived(out_ref.at[k, 1 - core], out_sems.at[k], sibling)
    sender.finish()


def reduce(n, rows, pieces, collective_id):
    count = len(pieces)
    members, two, height, width = pieces[0].shape
    na, nb = split_sizes(members)
    sends = count * (members + na * (nb - 1) + na)
    return pl.pallas_call(
        functools.partial(reduce_kernel, n, rows, count),
        out_shape=jax.ShapeDtypeStruct((count, two, height, width), f32),
        in_specs=vmem_specs(count),
        out_specs=vmem_specs(1)[0],
        scratch_shapes=[
            VM((count, members, height, width), bf16),
            VM((count, members, height, width), bf16),
            VM((count, na, height, width), bf16),
            VM((count, members, height, width), bf16),
            VM((count, na, height, width), bf16),
            DMA((sends,)),
            DMA((count, members)),
            DMA((count, members)),
            DMA((count, na)),
            DMA((count,)),
        ],
        compiler_params=remote_params(collective_id),
        name="reduce_tokens",
    )(*pieces)


def collect_kernel(n, rows, *refs):
    (first_ref, second_ref, wide_ref, small_ref, grad_ref, back_ref, table_ref) = refs[:7]
    (cross_buf, block_out, send_sems, cross_sems, block_sems, back_sems, table_sems, local_sems) = refs[7:]
    grads = (first_ref, second_ref)
    p = Place(n, rows)
    members = p.members
    everybody = [{"seq": lax.rem(p.seq + i, n), "tp": p.core} for i in range(1, n)]
    greet(everybody)
    sender = Sender(send_sems)
    partners = [
        (lax.rem(p.row + i, rows), p.device(p.member, row=lax.rem(p.row + i, rows)))
        for i in range(1, rows)
    ]
    order = [lax.rem(p.member + i, members) for i in range(1, members)] + [p.member]
    for i in range(1, n):
        seq = lax.rem(p.seq + i, n)
        sender.send(small_ref.at[seq], table_ref.at[p.seq], table_sems.at[p.seq], {"seq": seq, "tp": p.core})
    for layer in range(LAYERS):
        for member in order:
            for row, device in partners:
                sender.send(
                    grads[layer].at[member * rows + row],
                    cross_buf.at[layer, p.row, member],
                    cross_sems.at[layer, p.row, member],
                    device,
                )
    for row, device in partners:
        sender.send(wide_ref.at[row], back_ref.at[p.row], back_sems.at[p.row], device)
    own = [
        pltpu.make_async_copy(small_ref.at[p.seq], table_ref.at[p.seq], local_sems.at[0]),
        pltpu.make_async_copy(wide_ref.at[p.row], back_ref.at[p.row], local_sems.at[1]),
    ]
    for copy in own:
        copy.start()
    for layer in range(LAYERS):
        for i in list(range(1, members)) + [0]:
            member = lax.rem(p.member + i, members)
            total = grads[layer][member * rows + p.row].astype(f32)
            for row, device in partners:
                buffer = cross_buf.at[layer, row, member]
                sender.arrived(buffer, cross_sems.at[layer, row, member], p.sibling())
                total = total + buffer[...].astype(f32)
            if i:
                block_out[layer, member] = total.astype(bf16)
                sender.send(
                    block_out.at[layer, member],
                    grad_ref.at[layer, p.member],
                    block_sems.at[layer, p.member],
                    p.device(member),
                )
            else:
                grad_ref[layer, member] = total.astype(bf16)
    for i in range(1, n):
        seq = lax.rem(p.seq + i, n)
        sender.arrived(table_ref.at[seq], table_sems.at[seq], p.sibling())
    for row, device in partners:
        sender.arrived(back_ref.at[row], back_sems.at[row], p.sibling())
    for layer in range(LAYERS):
        for i in range(1, members):
            member = lax.rem(p.member + members - i, members)
            sender.arrived(grad_ref.at[layer, member], block_sems.at[layer, member], p.sibling())
    sender.finish()
    for copy in own:
        copy.wait()


def collect(n, rows, first, second, wide, small, collective_id):
    unused, height, columns = first.shape
    members = n // rows
    sends = (n - 1) + (rows - 1) + LAYERS * (members * (rows - 1) + members - 1)
    return pl.pallas_call(
        functools.partial(collect_kernel, n, rows),
        out_shape=(
            jax.ShapeDtypeStruct((LAYERS, members, height, columns), bf16),
            jax.ShapeDtypeStruct(wide.shape, wide.dtype),
            jax.ShapeDtypeStruct(small.shape, small.dtype),
        ),
        in_specs=vmem_specs(4),
        out_specs=tuple(vmem_specs(3)),
        scratch_shapes=[
            VM((LAYERS, rows, members, height, columns), bf16),
            VM((LAYERS, members, height, columns), bf16),
            DMA((sends,)),
            DMA((LAYERS, rows, members)),
            DMA((LAYERS, members)),
            DMA((rows,)),
            DMA((n,)),
            DMA((2,)),
        ],
        compiler_params=remote_params(collective_id),
        name="collect_gradients",
    )(first, second, wide, small)


def share_kernel(n, x_ref, out_ref, send_sems, recv_sems, local_sem):
    seq, core = lax.axis_index("seq"), lax.axis_index("tp")
    others = []
    for i in range(n):
        for j in range(2):
            if i or j:
                others.append((lax.rem(seq + i, n), lax.rem(core + j, 2)))
    greet([{"seq": s, "tp": c} for s, c in others])
    sender = Sender(send_sems)
    here = seq * 2 + core
    for s, c in others:
        sender.send(x_ref, out_ref.at[here], recv_sems.at[here], {"seq": s, "tp": c})
    own = pltpu.make_async_copy(x_ref, out_ref.at[here], local_sem)
    own.start()
    for s, c in others:
        sender.arrived(out_ref.at[s * 2 + c], recv_sems.at[s * 2 + c], {"seq": s, "tp": c})
    sender.finish()
    own.wait()


def share(n, x, collective_id):
    return pl.pallas_call(
        functools.partial(share_kernel, n),
        out_shape=jax.ShapeDtypeStruct((2 * n,) + x.shape, x.dtype),
        in_specs=vmem_specs(1),
        out_specs=vmem_specs(1)[0],
        scratch_shapes=[DMA((2 * n,)), DMA((2 * n,)), DMA],
        compiler_params=remote_params(collective_id),
        name="share_squares",
    )(x)


def dot(left, right):
    return jnp.dot(left, right, preferred_element_type=f32)


def dot_nt(left, right):
    return lax.dot_general(left, right, (((1,), (1,)), ((), ())), preferred_element_type=f32)


def dot_tn(left, right):
    return lax.dot_general(left, right, (((0,), (0,)), ((), ())), preferred_element_type=f32)


def swap_lanes(values):
    width = values.shape[-1]
    lane = lax.broadcasted_iota(jnp.int32, values.shape, 1)
    after = pltpu.roll(values, width - 1, 1)
    before = pltpu.roll(values, 1, 1)
    return jnp.where(lane % 2 == 0, after, before)


gelu_scale = 0.7978845608
gelu_cubic = 0.044715


def gelu(z):
    return 0.5 * z * (1.0 + jnp.tanh(gelu_scale * (z + gelu_cubic * z * z * z)))


def gelu_slope(z):
    inner = jnp.tanh(gelu_scale * (z + gelu_cubic * z * z * z))
    slope = gelu_scale * (1.0 + 3.0 * gelu_cubic * z * z)
    return 0.5 * (1.0 + inner) + 0.5 * z * (1.0 - inner * inner) * slope


def query_tiles(length, share, rows):
    tile = max(64, min(TILE, TILE * 1024 // length))
    first = 0
    if share > 1:
        first = lax.rem(lax.axis_index("seq") // rows, share) * (length // share)
    for i in range(length // share // tile):
        start = pl.multiple_of(first + i * tile, tile) if share > 1 else i * tile
        yield pl.ds(start, tile), start, ((i + 1) * tile if share == 1 else length)


def visible(start, keys, seg_col, seg_row):
    tile = seg_col.shape[0]
    place = start + lax.broadcasted_iota(jnp.int32, (tile, keys), 0)
    other = lax.broadcasted_iota(jnp.int32, (tile, keys), 1)
    return (other <= place) & (seg_col == seg_row)


def forward_kernel(batch, share, ff, h_ref, w_ref, cos_ref, sin_ref, segc_ref, segr_ref, *outs):
    part_ref, q_ref, k_ref, v_ref, o_ref, lse_ref, a_ref, z_ref = outs
    length = h_ref.shape[0]
    f = 4 * HEAD

    @pl.loop(0, length // TILE)
    def project(t):
        rows = pl.ds(t * TILE, TILE)
        h = h_ref[rows, :]
        mixed = dot(h, w_ref[:, :f])
        qk = mixed[:, : 2 * HEAD]
        qk = qk * cos_ref[rows, :] + swap_lanes(qk) * sin_ref[rows, :]
        q_ref[rows, :] = (qk[:, :HEAD].astype(bf16).astype(f32) * HEAD**-0.5).astype(bf16)
        k_ref[rows, :] = qk[:, HEAD:].astype(bf16)
        v_ref[rows, :] = mixed[:, 2 * HEAD : 3 * HEAD].astype(bf16)
        z = dot(h, w_ref[:, f : f + ff])
        z_ref[rows, :] = z
        a_ref[rows, :] = gelu(z).astype(bf16)

    if share > 1:
        o_ref[...] = jnp.zeros_like(o_ref)
        lse_ref[...] = jnp.zeros_like(lse_ref)
    for rows, start, keys in query_tiles(length, share, batch):
        scores = dot_nt(q_ref[rows, :], k_ref[:keys, :])
        seen = visible(start, keys, segc_ref[rows, :], segr_ref[:, :keys])
        scores = jnp.where(seen, scores, low_score)
        peak = jnp.max(scores, axis=1, keepdims=True)
        weights = jnp.exp(scores - peak)
        total = jnp.sum(weights, axis=1, keepdims=True)
        lse_ref[rows, :] = peak + jnp.log(total)
        shares = (weights * (1.0 / total)).astype(bf16)
        o_ref[rows, :] = dot(shares, v_ref[:keys, :]).astype(bf16)

    @pl.loop(0, length // TILE)
    def branch(t):
        rows = pl.ds(t * TILE, TILE)
        out = dot_nt(o_ref[rows, :], w_ref[:, 3 * HEAD : f])
        out = out + dot_nt(a_ref[rows, :], w_ref[:, f + ff : f + 2 * ff])
        part_ref[rows, :] = out.astype(bf16)


def forward(batch, share, ff, h, w, cosine, sine, seg_col, seg_row):
    length, width = h.shape
    column = jax.ShapeDtypeStruct((length, HEAD), bf16)
    return pl.pallas_call(
        functools.partial(forward_kernel, batch, share, ff),
        out_shape=(
            jax.ShapeDtypeStruct((length, width), bf16),
            column,
            column,
            column,
            column,
            jax.ShapeDtypeStruct((length, 1), f32),
            jax.ShapeDtypeStruct((length, ff), bf16),
            jax.ShapeDtypeStruct((length, ff), f32),
        ),
        in_specs=vmem_specs(6),
        out_specs=tuple(vmem_specs(8)),
        compiler_params=pltpu.CompilerParams(vmem_limit_bytes=56 * megabyte),
        name="layer_forward",
    )(h, w, cosine, sine, seg_col, seg_row)


def backward_kernel(batch, share, ff, g_ref, h_ref, w_ref, cos_ref, sin_ref, segc_ref, segr_ref, *refs):
    q_ref, k_ref, v_ref, o_ref, lse_ref, a_ref, z_ref, part_ref, dw_ref = refs[:9]
    dz_ref, do_ref, dq_ref, dk_ref, dv_ref, mix_ref = refs[9:]
    length, width = h_ref.shape
    f = 4 * HEAD

    @pl.loop(0, length // TILE)
    def feed(t):
        rows = pl.ds(t * TILE, TILE)
        g = g_ref[rows, :]
        da = dot(g, w_ref[:, f + ff : f + 2 * ff])
        dz_ref[rows, :] = (da * gelu_slope(z_ref[rows, :])).astype(bf16)
        do_ref[rows, :] = dot(g, w_ref[:, :f])[:, 3 * HEAD :].astype(bf16)

    dk_ref[...] = jnp.zeros_like(dk_ref)
    dv_ref[...] = jnp.zeros_like(dv_ref)
    if share > 1:
        dq_ref[...] = jnp.zeros_like(dq_ref)
    for rows, start, keys in query_tiles(length, share, batch):
        q, head_grad = q_ref[rows, :], do_ref[rows, :]
        scores = dot_nt(q, k_ref[:keys, :])
        seen = visible(start, keys, segc_ref[rows, :], segr_ref[:, :keys])
        shares = jnp.where(seen, jnp.exp(scores - lse_ref[rows, :]), 0.0)
        share_grads = dot_nt(head_grad, v_ref[:keys, :])
        delta = jnp.sum(shares * share_grads, axis=1, keepdims=True)
        score_grads = (shares * (share_grads - delta)).astype(bf16)
        dq_ref[rows, :] = dot(score_grads, k_ref[:keys, :]) * HEAD**-0.5
        dk_ref[:keys, :] += dot_tn(score_grads, q)
        dv_ref[:keys, :] += dot_tn(shares.astype(bf16), head_grad)

    @pl.loop(0, length // TILE)
    def inward(t):
        rows = pl.ds(t * TILE, TILE)
        qk = jnp.concatenate([dq_ref[rows, :], dk_ref[rows, :]], axis=1)
        qk = qk * cos_ref[rows, :] + swap_lanes(qk * sin_ref[rows, :])
        rest = jnp.concatenate([dv_ref[rows, :], jnp.zeros((TILE, HEAD), f32)], axis=1)
        mix = jnp.concatenate([qk, rest], axis=1).astype(bf16)
        mix_ref[rows, :] = mix
        out = dot_nt(mix, w_ref[:, :f]) + dot_nt(dz_ref[rows, :], w_ref[:, f : f + ff])
        part_ref[rows, :] = out.astype(bf16)

    @pl.loop(0, width // TILE)
    def weights(t):
        rows = pl.ds(t * TILE, TILE)
        h, g = h_ref[:, rows], g_ref[:, rows]
        mixed = dot_tn(h, mix_ref[...])
        out = dot_tn(g, o_ref[...])
        dw_ref[rows, :f] = jnp.concatenate([mixed[:, : 3 * HEAD], out], axis=1).astype(bf16)
        dw_ref[rows, f : f + ff] = dot_tn(h, dz_ref[...]).astype(bf16)
        dw_ref[rows, f + ff : f + 2 * ff] = dot_tn(g, a_ref[...]).astype(bf16)


def backward(batch, share, ff, g, h, w, cosine, sine, seg_col, seg_row, kept):
    length, width = h.shape
    return pl.pallas_call(
        functools.partial(backward_kernel, batch, share, ff),
        out_shape=(
            jax.ShapeDtypeStruct((length, width), bf16),
            jax.ShapeDtypeStruct(w.shape, bf16),
        ),
        in_specs=vmem_specs(14),
        out_specs=tuple(vmem_specs(2)),
        scratch_shapes=[
            VM((length, ff), bf16),
            VM((length, HEAD), bf16),
            VM((length, HEAD), f32),
            VM((length, HEAD), f32),
            VM((length, HEAD), f32),
            VM((length, 4 * HEAD), bf16),
        ],
        compiler_params=pltpu.CompilerParams(vmem_limit_bytes=60 * megabyte),
        name="layer_backward",
    )(g, h, w, cosine, sine, seg_col, seg_row, *kept)


def layer_norm(inputs):
    average = jnp.mean(inputs, axis=-1, keepdims=True)
    centred = inputs - average
    spread_here = jnp.mean(centred * centred, axis=-1, keepdims=True)
    inverse = lax.rsqrt(spread_here + norm_eps)
    return (centred * inverse, inverse)


def norm_back(grads, normed_grads, xhat, inverse, gain):
    scaled = normed_grads * gain
    average = jnp.mean(scaled, axis=-1, keepdims=True)
    along = jnp.mean(scaled * xhat, axis=-1, keepdims=True)
    return grads + (scaled - average - xhat * along) * inverse


def rotary_tables(positions):
    column = jnp.arange(HEAD)
    inside = column < ROTARY
    pair_index = column % ROTARY // 2
    frequency = jnp.exp(pair_index.astype(f32) * (-2.0 * math.log(10000.0) / ROTARY))
    angles = positions[:, None] * frequency
    cosine = jnp.where(inside, jnp.cos(angles), 1.0)
    signed = jnp.where(column % 2 == 0, -1.0, 1.0)
    sine = jnp.where(inside, signed * jnp.sin(angles), 0.0)
    return (jnp.tile(cosine, (1, 2)), jnp.tile(sine, (1, 2)))


def pad_lanes(values, width=128):
    return jnp.pad(values, [(0, 0)] * (values.ndim - 1) + [(0, width - values.shape[-1])])


def adam_update(weight, first, second, gradient, factor_clip, rate, decay):
    clipped = gradient * factor_clip
    first_new = beta_one * first + (1.0 - beta_one) * clipped
    second_new = beta_two * second + (1.0 - beta_two) * clipped * clipped
    first_hat = first_new / (1.0 - beta_one**STEP)
    second_hat = second_new / (1.0 - beta_two**STEP)
    weight_new = weight - rate * (first_hat / (jnp.sqrt(second_hat) + adam_eps) + decay * weight)
    return (weight_new, first_new, second_new)


def pack_weights(n, rows, qkv_weight, out_weight, in_weight, down_weight):
    layers, height = qkv_weight.shape[:2]
    members = n // rows
    heads = qkv_weight.shape[3] // HEAD
    share = members // heads
    ff = in_weight.shape[2] // members
    mixed = jnp.concatenate([qkv_weight, out_weight[:, :, None, :]], axis=2).astype(bf16)
    mixed = mixed.reshape(layers, height, 4, heads, HEAD).transpose(0, 3, 1, 2, 4)
    mixed = mixed.reshape(layers, heads, height, 4 * HEAD)
    if share > 1:
        mixed = jnp.repeat(mixed, share, axis=1)
    feeds = [
        weight.astype(bf16).reshape(layers, height, members, ff).transpose(0, 2, 1, 3)
        for weight in (in_weight, down_weight)
    ]
    return jnp.concatenate([mixed] + feeds, axis=3)


def unpack_gradients(grads, heads, ff):
    layers, members, height, unused = grads.shape
    grads = grads.astype(f32)
    share = members // heads
    mixed = grads[..., : 4 * HEAD]
    if share > 1:
        mixed = mixed.reshape(layers, heads, share, height, 4 * HEAD).sum(2)
    mixed = mixed.reshape(layers, heads, height, 4, HEAD).transpose(0, 2, 3, 1, 4)
    mixed = mixed.reshape(layers, height, 4, heads * HEAD)
    feeds = [
        grads[..., 4 * HEAD + k * ff : 4 * HEAD + (k + 1) * ff]
        .transpose(0, 2, 1, 3)
        .reshape(layers, height, members * ff)
        for k in range(2)
    ]
    return (mixed[:, :, :3], mixed[:, :, 3], feeds[0], feeds[1])


def shards_apart(
    n,
    activations,
    cotangent,
    segment_ids,
    position_ids,
    qkv_weight,
    out_weight,
    in_weight,
    down_weight,
    norm_params,
    qkv_first,
    out_first,
    in_first,
    down_first,
    norm_first,
    qkv_second,
    out_second,
    in_second,
    down_second,
    norm_second,
):
    rows, span, width = activations.shape
    members = n // rows
    length = n * span
    half = rows * span // 2
    heads = qkv_weight.shape[3] // HEAD
    share_queries = members // heads
    ff = in_weight.shape[2] // members
    row = lax.axis_index("seq") % rows

    pack = pack_weights(n, rows, qkv_weight, out_weight, in_weight, down_weight)
    norm_low = norm_params.astype(bf16).astype(f32).reshape(LAYERS * 3, -1)
    small = jnp.concatenate(
        [
            pad_lanes(norm_low),
            pad_lanes(position_ids.astype(f32)),
            pad_lanes(segment_ids.astype(f32)),
        ]
    )
    small = jnp.pad(small, ((0, -small.shape[0] % 8), (0, 0)))
    wide = jnp.stack([activations, cotangent], axis=1)
    chunk, table, weights = spread(n, rows, wide, small, pack, 0)
    weights = weights.reshape(LAYERS, width, -1)
    inputs = chunk[:, 0].reshape(rows * span, width)
    out_grads = chunk[:, 1].reshape(rows * span, width)
    own_columns = norm_params.shape[-1]
    norms = table[:, : LAYERS * 3, :own_columns].transpose(1, 0, 2).reshape(LAYERS, 3, width)
    positions = lax.dynamic_index_in_dim(table, LAYERS * 3 + row, 1, False)[:, :span].reshape(length)
    segments = lax.dynamic_index_in_dim(table, LAYERS * 3 + rows + row, 1, False)[:, :span].reshape(length)
    cosine, sine = rotary_tables(positions)
    places = (cosine, sine, segments[:, None], segments[None, :])

    def halves(values):
        return values.astype(bf16).reshape(2, half, width)

    def whole(values):
        return values.reshape(length, width)

    def parts(values):
        return values.reshape(members, 2, half, width)

    xhat_0, inverse_0 = layer_norm(inputs)
    normed = xhat_0 * norms[0, 0] + norms[0, 1]
    got = gather(n, rows, [halves(normed), halves(out_grads)], 1)
    normed_0, grads_1 = whole(got[0]), whole(got[1])
    part, *kept_0 = forward(rows, share_queries, ff, normed_0, weights[0], *places)
    branch = reduce(n, rows, [parts(part)], 2)[0].reshape(inputs.shape)
    middle = inputs + branch + norms[0, 2]
    xhat_1, inverse_1 = layer_norm(middle)
    normed = xhat_1 * norms[1, 0] + norms[1, 1]
    normed_1 = whole(gather(n, rows, [halves(normed)], 3)[0])
    part, *kept_1 = forward(rows, share_queries, ff, normed_1, weights[1], *places)
    back_part, weight_grads_1 = backward(rows, share_queries, ff, grads_1, normed_1, weights[1], *places, kept_1)
    sums = reduce(n, rows, [parts(part), parts(back_part)], 4).reshape((2,) + inputs.shape)
    result = middle + sums[0] + norms[1, 2]
    normed_grads_1 = sums[1]
    grads_mid = norm_back(out_grads, normed_grads_1, xhat_1, inverse_1, norms[1, 0])
    grads_0 = whole(gather(n, rows, [halves(grads_mid)], 5)[0])
    back_part, weight_grads_0 = backward(rows, share_queries, ff, grads_0, normed_0, weights[0], *places, kept_0)
    normed_grads_0 = reduce(n, rows, [parts(back_part)], 6)[0].reshape(inputs.shape)
    input_grad = norm_back(grads_mid, normed_grads_0, xhat_0, inverse_0, norms[0, 0])

    small_grads = jnp.stack(
        [
            jnp.sum(normed_grads_0 * xhat_0, axis=0),
            jnp.sum(normed_grads_0, axis=0),
            jnp.sum(grads_mid, axis=0),
            jnp.sum(normed_grads_1 * xhat_1, axis=0),
            jnp.sum(normed_grads_1, axis=0),
            jnp.sum(out_grads, axis=0),
        ]
    )
    small_grads = pad_lanes(small_grads.reshape(LAYERS * 3, n, own_columns).transpose(1, 0, 2))
    small_grads = jnp.pad(small_grads, ((0, 0), (0, 8 - LAYERS * 3), (0, 0)))
    wide_out = jnp.stack([result.reshape(rows, span, width), input_grad.reshape(rows, span, width)], axis=1)
    height = width // n
    grads, wide_back, table_back = collect(
        n,
        rows,
        weight_grads_0.reshape(n, height, -1),
        weight_grads_1.reshape(n, height, -1),
        wide_out,
        small_grads,
        7,
    )
    norm_grads = jnp.sum(table_back, axis=0)[: LAYERS * 3, :own_columns].reshape(norm_params.shape)
    qkv_grads, out_weight_grads, in_grads, down_grads = unpack_gradients(grads, heads, ff)
    matrix_squares = sum(
        (jnp.sum(block * block) for block in (qkv_grads, out_weight_grads, in_grads, down_grads))
    )
    squares = matrix_squares + jnp.sum(norm_grads * norm_grads) / 2
    everyone = share(n, jnp.full((8, 128), squares, f32), 8)
    grad_norm = jnp.sqrt(jnp.sum(everyone[:, 0, 0]))
    total_parameters = LAYERS * width * (4 * 2 * heads * HEAD + 2 * 2 * members * ff + 3)
    factor_clip = jnp.minimum(1.0, clip_share * math.sqrt(total_parameters) / (grad_norm + 1e-06))
    qkv_new, qkv_first_new, qkv_second_new = adam_update(
        qkv_weight, qkv_first, qkv_second, qkv_grads, factor_clip, rate_matrix, decay_matrix
    )
    out_new, out_first_new, out_second_new = adam_update(
        out_weight, out_first, out_second, out_weight_grads, factor_clip, rate_output, decay_matrix
    )
    in_new, in_first_new, in_second_new = adam_update(
        in_weight, in_first, in_second, in_grads, factor_clip, rate_matrix, decay_matrix
    )
    down_new, down_first_new, down_second_new = adam_update(
        down_weight, down_first, down_second, down_grads, factor_clip, rate_matrix, decay_matrix
    )
    norm_new, norm_first_new, norm_second_new = adam_update(
        norm_params, norm_first, norm_second, norm_grads, factor_clip, rate_vector, 0.0
    )
    bias_clipped = norm_grads[:, 2] * factor_clip
    return (
        wide_back[:, 0],
        wide_back[:, 1],
        grad_norm,
        qkv_new,
        out_new,
        in_new,
        down_new,
        norm_new,
        qkv_first_new,
        out_first_new,
        in_first_new,
        down_first_new,
        norm_first_new,
        qkv_second_new,
        out_second_new,
        in_second_new,
        down_second_new,
        norm_second_new,
        bias_clipped,
    )


def flip(index, bits):
    bit = 1
    while bit <= bits:
        if bits & bit:
            index = index + bit * (1 - 2 * lax.rem(index // bit, 2))
        bit *= 2
    return index


class Net:
    def __init__(self, n, rows, half, pieces, send_sems):
        self.p = Place(n, rows)
        self.half, self.pieces = half, pieces
        self.send_sems, self.used = send_sems, 0
        self.sibling = self.p.sibling()

    def send_sem(self):
        self.used += 1
        return self.send_sems.at[self.used - 1]

    def everybody(self):
        p = self.p
        return [{"seq": lax.rem(p.seq + i, p.n), "tp": p.core} for i in range(1, p.n)]

    def everyone(self):
        p = self.p
        return self.everybody() + [
            {"seq": lax.rem(p.seq + i, p.n), "tp": 1 - p.core} for i in range(p.n)
        ]

    def partner(self):
        return self.p.device(self.p.member, row=1 - self.p.row)

    def a_of(self, k):
        return flip(self.p.a, k)

    def b_of(self, j):
        return flip(self.p.b, j)

    def tokens(self, member, core, piece):
        size = self.half // self.pieces
        start = (member * 2 + core) * self.half + piece * size
        return pl.ds(pl.multiple_of(start, size), size)

    def lines(self, slot, piece):
        size = self.half // self.pieces
        return pl.ds(pl.multiple_of(slot * self.half + piece * size, size), size)

    def own(self):
        start = (self.p.member * 2 + self.p.core) * self.half
        return pl.ds(pl.multiple_of(start, self.half), self.half)

    def tile_rows(self, a):
        size = self.p.nb * 2 * self.half
        return pl.ds(pl.multiple_of(a * size, size), size)

    def width_rows(self, k, width):
        size = width // self.p.na
        return pl.ds(pl.multiple_of(self.a_of(k) * size, size), size)

    def tile(self, k):
        return self.tile_rows(self.a_of(k))

    def far_first(self):
        a, na = self.p.a, self.p.na
        if na != 4:
            return [self.a_of(k) for k in range(na - 1, -1, -1)]
        upper = a // 2
        low = a + upper * (3 - 2 * a)
        order = [3, 2, 1 - low, low]
        return [v + upper * (3 - 2 * v) for v in order]

    def sides(self, distance):
        a, na = self.p.a, self.p.na
        return [
            (a >= distance, a - distance, a < na - 1, a + 1),
            (a + distance < na, a + distance, a > 0, a - 1),
        ]


class Sends:
    def __init__(self, net, lone=0):
        self.sibling = net.sibling
        self.shared = net.send_sem()
        self.lone = [net.send_sem() for _ in range(lone)]
        self.made, self.conditional = 0, []

    def copy(self, src, dst, sem, device, send_sem):
        return pltpu.make_async_remote_copy(
            src_ref=src, dst_ref=dst, send_sem=send_sem, recv_sem=sem, device_id=device, device_id_type=MESH
        )

    def send(self, src, dst, sem, device):
        self.copy(src, dst, sem, device, self.shared).start()
        self.made += 1

    def send_if(self, when, src, dst, sem, device):
        number = len(self.conditional)
        self.conditional.append((when, src, dst, sem, device))
        pl.when(when)(lambda: self.copy(src, dst, sem, device, self.lone[number]).start())

    def finish(self, whole):
        self.copy(whole, whole, self.shared, self.sibling, self.shared).wait_send()
        for number, (when, *copy) in enumerate(self.conditional):
            pl.when(when)(lambda number=number, copy=copy: self.copy(*copy, self.lone[number]).wait_send())
        self.made, self.conditional = 0, []


def wait_for(net, dst, sem):
    pltpu.make_async_remote_copy(
        src_ref=dst,
        dst_ref=dst,
        send_sem=net.send_sems.at[0],
        recv_sem=sem,
        device_id=net.sibling,
        device_id_type=MESH,
    ).wait_recv()


class Gather:
    def __init__(self, net, sems):
        self.net = net
        self.a_sems, self.b_sems, self.core_sems = sems
        self.sends = Sends(net, lone=2 * net.pieces * net.p.na)

    def slot(self, a, b, core, q):
        return self.out.at[self.net.tokens(a * self.net.p.nb + b, core, q), :]

    def to_line(self, a, q, to, when):
        p = self.net.p
        here = self.slot(a, p.b, p.core, q)
        self.sends.send_if(when, here, here, self.a_sems.at[a, q], p.at(to, p.b))

    def to_rest(self, a, q):
        net, p = self.net, self.net.p
        here = self.slot(a, p.b, p.core, q)
        for j in range(1, p.nb):
            self.sends.send(here, here, self.b_sems.at[a * p.nb + p.b, q], p.at(p.a, net.b_of(j)))
        self.sends.send(here, here, self.core_sems.at[a, q], net.sibling)

    def start(self, out):
        p = self.net.p
        self.out = out
        for q in range(self.net.pieces):
            self.to_line(p.a, q, p.a + 1, p.a < p.na - 1)
            self.to_line(p.a, q, p.a - 1, p.a > 0)
            self.to_rest(p.a, q)

    def hop(self, distance):
        net, p = self.net, self.net.p
        for q in range(net.pieces):
            for there, a, more, beyond in net.sides(distance):

                @pl.when(there)
                def _():
                    wait_for(net, self.slot(a, p.b, p.core, q), self.a_sems.at[a, q])

                self.to_line(a, q, beyond, jnp.logical_and(there, more))
                pl.when(there)(lambda: self.to_rest(a, q))

    def side(self, distance):
        net, p = self.net, self.net.p
        for j in range(1, p.nb):
            b = net.b_of(j)
            for q in range(net.pieces):
                for there, a, more, beyond in net.sides(distance)[: 2 if distance else 1]:

                    @pl.when(there)
                    def _():
                        here = self.slot(a, b, p.core, q)
                        wait_for(net, here, self.b_sems.at[a * p.nb + b, q])
                        self.sends.send(here, here, self.core_sems.at[a, q], net.sibling)

    def settle(self, distance):
        net, p = self.net, self.net.p
        size = p.nb * net.half // net.pieces
        for q in range(net.pieces):
            for there, a, more, beyond in net.sides(distance)[: 2 if distance else 1]:

                @pl.when(there)
                def _():
                    wait_for(net, self.out.at[pl.ds(0, size), :], self.core_sems.at[a, q])

    def steps(self):
        na = self.net.p.na
        if na > 1:
            self.hop(1)
        yield None
        self.side(0)
        yield None
        for k in range(na):
            if k + 2 < na:
                self.hop(k + 2)
            if k + 1 < na:
                self.side(k + 1)
            self.settle(k)
            yield k

    def finish(self):
        p = self.net.p
        self.sends.finish(self.out.at[pl.ds(0, (p.na * (p.nb - 1) + p.members) * self.net.half), :])


class Reduce:
    def __init__(self, net, x, total, bufs, sems):
        self.net, self.x, self.total = net, x, total
        self.core_buf, self.b_out, self.b_buf, self.a_out, self.a_buf, self.sum_buf = bufs
        self.core_sems, self.b_sems, self.a_sems = sems
        self.sends = Sends(net, lone=2 * net.pieces * (net.p.na - 1))

    def offer(self, a):
        net, p = self.net, self.net.p
        for j in list(range(1, p.nb)) + [0]:
            m = a * p.nb + net.b_of(j)
            for q in range(net.pieces):
                self.sends.send(
                    self.x.at[net.tokens(m, 1 - p.core, q), :],
                    self.core_buf.at[net.lines(m, q), :],
                    self.core_sems.at[m, q],
                    net.sibling,
                )

    def pair_sum(self, m, q):
        net = self.net
        lines = net.lines(m, q)
        wait_for(net, self.core_buf.at[lines, :], self.core_sems.at[m, q])
        return self.x[net.tokens(m, net.p.core, q), :].astype(f32) + self.core_buf[lines, :].astype(f32)

    def targets(self, distance):
        return self.net.sides(distance)[: 2 if distance else 1]

    def relay(self, distance):
        net, p = self.net, self.net.p
        for there, a, unused_more, unused_beyond in self.targets(distance):
            for j in range(1, p.nb):
                b = net.b_of(j)
                for q in range(net.pieces):

                    @pl.when(there)
                    def _():
                        m, landing = a * p.nb + b, a * p.nb + p.b
                        self.b_out[net.lines(m, q), :] = self.pair_sum(m, q).astype(bf16)
                        self.sends.send(
                            self.b_out.at[net.lines(m, q), :],
                            self.b_buf.at[net.lines(landing, q), :],
                            self.b_sems.at[landing, q],
                            p.at(p.a, b),
                        )

    def row_sum(self, a, q):
        net, p = self.net, self.net.p
        total = self.pair_sum(a * p.nb + p.b, q)
        for j in range(1, p.nb):
            m = a * p.nb + net.b_of(j)
            wait_for(net, self.b_buf.at[net.lines(m, q), :], self.b_sems.at[m, q])
            total = total + self.b_buf[net.lines(m, q), :].astype(f32)
        return total

    def passing(self, up, a, q):
        net, p = self.net, self.net.p
        slot = a if up else p.na + a
        wait_for(net, self.a_buf.at[net.lines(slot, q), :], self.a_sems.at[slot, q])
        return self.a_buf[net.lines(slot, q), :].astype(f32)

    def pass_on(self, distance):
        net, p = self.net, self.net.p
        size = net.half // net.pieces
        for side, (there, a, unused_more, unused_beyond) in enumerate(net.sides(distance)):
            up = side == 1
            behind = p.a > 0 if up else p.a < p.na - 1
            slot = a if up else p.na + a
            for q in range(net.pieces):
                part = slice(q * size, (q + 1) * size)

                @pl.when(there)
                def _():
                    self.sum_buf[part, :] = self.row_sum(a, q)

                @pl.when(jnp.logical_and(there, behind))
                def _():
                    self.sum_buf[part, :] += self.passing(up, a, q)

                @pl.when(there)
                def _():
                    self.a_out[net.lines(slot, q), :] = self.sum_buf[part, :].astype(bf16)

                self.sends.send_if(
                    there,
                    self.a_out.at[net.lines(slot, q), :],
                    self.a_buf.at[net.lines(slot, q), :],
                    self.a_sems.at[slot, q],
                    p.at(p.a + 1 if up else p.a - 1, p.b),
                )

    def arrive(self):
        net, p = self.net, self.net.p
        size = net.half // net.pieces
        for q in range(net.pieces):
            part = slice(q * size, (q + 1) * size)
            self.total[part, :] = self.row_sum(p.a, q)
        for q in range(net.pieces):
            part = slice(q * size, (q + 1) * size)

            @pl.when(p.a > 0)
            def _():
                self.total[part, :] += self.passing(True, p.a, q)

            @pl.when(p.a < p.na - 1)
            def _():
                self.total[part, :] += self.passing(False, p.a, q)

    def steps(self):
        na = self.net.p.na
        for distance in range(na - 1, -1, -1):
            self.relay(distance)
            yield
        for distance in range(na - 1, 0, -1):
            self.pass_on(distance)
            yield
        self.arrive()
        yield

    def finish(self):
        p = self.net.p
        self.sends.finish(self.x.at[pl.ds(0, (p.members + p.na * (p.nb - 1)) * self.net.half), :])


class Spread:
    def __init__(self, net, pack, w, columns, block_sems, cross_sems):
        self.net, self.pack, self.w, self.columns = net, pack, w, columns
        self.block_sems, self.cross_sems = block_sems, cross_sems
        self.height = pack.shape[1]
        self.sends = Sends(net)
        self.sent, self.received = 1, 1

    def here(self, seq):
        return self.w.at[pl.ds(pl.multiple_of(seq * self.height, self.height), self.height), self.columns]

    def start(self):
        net, p = self.net, self.net.p
        block = self.pack.at[p.member, :, self.columns]
        self.sends.send(block, self.here(p.seq), self.cross_sems.at[p.member], net.partner())
        self.here(p.seq)[...] = block[...]

    def send(self, count=None):
        p = self.net.p
        last = p.members if count is None else min(p.members, self.sent + count)
        for k in range(self.sent, last):
            member = flip(p.member, k)
            block = self.pack.at[member, :, self.columns]
            self.sends.send(block, self.here(p.seq), self.block_sems.at[p.member], p.device(member))
        self.sent = last

    def receive(self, count=None):
        net, p = self.net, self.net.p
        last = p.members if count is None else min(p.members, self.received + count)
        for k in range(self.received, last):
            member = flip(p.member, k)
            here = self.here(member * p.rows + p.row)
            wait_for(net, here, self.block_sems.at[member])
            self.sends.send(here, here, self.cross_sems.at[member], net.partner())
        self.received = last

    def settle(self):
        net, p = self.net, self.net.p
        for k in range(p.members):
            member = flip(p.member, k)
            wait_for(net, self.here(member * p.rows + 1 - p.row), self.cross_sems.at[member])

    def finish(self):
        size = (2 * self.net.p.members - 1) * self.height
        self.sends.finish(self.w.at[pl.ds(0, size), self.columns])


class Collect:
    def __init__(self, net, dw, grad, columns, cross_buf, block_out, cross_sems, block_sems):
        self.net, self.dw, self.grad, self.columns = net, dw, grad, columns
        self.cross_buf, self.block_out = cross_buf, block_out
        self.cross_sems, self.block_sems = cross_sems, block_sems
        self.height = grad.shape[1]
        self.sends = Sends(net)
        self.pending = self.order()

    def at(self, seq):
        return self.dw.at[pl.ds(pl.multiple_of(seq * self.height, self.height), self.height), self.columns]

    def order(self):
        return list(range(self.net.p.members - 1, -1, -1))

    def offer(self, k):
        net, p = self.net, self.net.p
        for j in range(p.nb - 1, -1, -1):
            member = net.a_of(k) * p.nb + net.b_of(j)
            self.sends.send(
                self.at(member * p.rows + 1 - p.row),
                self.cross_buf.at[member, :, self.columns],
                self.cross_sems.at[member],
                net.partner(),
            )

    def relay(self, count=None):
        net, p = self.net, self.net.p
        for k in self.pending[:count]:
            member = flip(p.member, k)
            landed = self.cross_buf.at[member, :, self.columns]
            wait_for(net, landed, self.cross_sems.at[member])
            mine = self.at(member * p.rows + p.row)[...]
            total = (mine.astype(f32) + landed[...].astype(f32)).astype(bf16)
            if k:
                block = self.block_out.at[member, :, self.columns]
                block[...] = total
                target = self.grad.at[p.member, :, self.columns]
                self.sends.send(block, target, self.block_sems.at[p.member], p.device(member))
            else:
                self.grad[member, :, self.columns] = total
        self.pending = self.pending[count:] if count is not None else []

    def settle(self):
        squares = jnp.zeros((1, 1), f32)
        for k in [0] + self.order()[:-1]:
            member = flip(self.net.p.member, k)
            if k:
                wait_for(self.net, self.grad.at[member, :, self.columns], self.block_sems.at[member])
            block = self.grad[member, :, self.columns].astype(f32)
            squares = squares + jnp.sum(block * block, axis=(0, 1), keepdims=True)
        return squares

    def finish(self):
        size = (2 * self.net.p.members - 1) * self.height
        self.sends.finish(self.dw.at[pl.ds(0, size), self.columns])


def advance(steps, count=1):
    for _ in range(count):
        next(steps, None)


def drain(steps):
    for _ in steps:
        pass


class Layer:
    def __init__(self, r, layer):
        self.r, self.layer = r, layer
        self.length, self.width = getattr(r, "h%d" % layer).shape
        self.f = 4 * HEAD
        self.ff = (getattr(r, "w%d" % layer).shape[1] - self.f) // 2

    def __getattr__(self, name):
        return getattr(self.r, name + str(self.layer))

    def project(self, rows):
        r, f = self.r, self.f
        h = self.h[rows, :]
        mixed = dot(h, self.w[:, :f])
        qk = mixed[:, : 2 * HEAD]
        qk = qk * r.cos[rows, :] + swap_lanes(qk) * r.sin[rows, :]
        self.q[rows, :] = (qk[:, :HEAD].astype(bf16).astype(f32) * HEAD**-0.5).astype(bf16)
        self.k[rows, :] = qk[:, HEAD:].astype(bf16)
        self.v[rows, :] = mixed[:, 2 * HEAD : 3 * HEAD].astype(bf16)

    def feed(self, rows):
        z = dot(self.h[rows, :], self.w[:, self.f : self.f + self.ff])
        self.z[rows, :] = z
        self.a[rows, :] = gelu(z).astype(bf16)

    def attend(self, i):
        r = self.r
        start, keys = i * TILE, (i + 1) * TILE
        rows = pl.ds(start, TILE)
        scores = dot_nt(self.q[rows, :], self.k[:keys, :])
        seen = visible(start, keys, r.segc[rows, :], r.segr[:, :keys])
        scores = jnp.where(seen, scores, low_score)
        peak = jnp.max(scores, axis=1, keepdims=True)
        weights = jnp.exp(scores - peak)
        total = jnp.sum(weights, axis=1, keepdims=True)
        self.lse[rows, :] = peak + jnp.log(total)
        shares = (weights * (1.0 / total)).astype(bf16)
        self.o[rows, :] = dot(shares, self.v[:keys, :]).astype(bf16)

    def branch(self, rows, part):
        f, ff = self.f, self.ff
        out = dot_nt(self.o[rows, :], self.w[:, 3 * HEAD : f])
        out = out + dot_nt(self.a[rows, :], self.w[:, f + ff : f + 2 * ff])
        part[rows, :] = out.astype(bf16)

    def feed_back(self, rows):
        r, f, ff = self.r, self.f, self.ff
        g = self.g[rows, :]
        da = dot(g, self.w[:, f + ff : f + 2 * ff])
        r.dz[rows, :] = (da * gelu_slope(self.z[rows, :])).astype(bf16)
        r.do[rows, :] = dot(g, self.w[:, :f])[:, 3 * HEAD :].astype(bf16)

    def attend_back(self, i):
        r = self.r
        start, keys = i * TILE, (i + 1) * TILE
        rows = pl.ds(start, TILE)
        q, head_grad = self.q[rows, :], r.do[rows, :]
        scores = dot_nt(q, self.k[:keys, :])
        seen = visible(start, keys, r.segc[rows, :], r.segr[:, :keys])
        shares = jnp.where(seen, jnp.exp(scores - self.lse[rows, :]), 0.0)
        share_grads = dot_nt(head_grad, self.v[:keys, :])
        delta = jnp.sum(shares * share_grads, axis=1, keepdims=True)
        score_grads = (shares * (share_grads - delta)).astype(bf16)
        r.dq[rows, :] = dot(score_grads, self.k[:keys, :]) * HEAD**-0.5
        dk = dot_tn(score_grads, q)
        dv = dot_tn(shares.astype(bf16), head_grad)
        if i + 1 == self.length // TILE:
            r.dk[:keys, :] = dk
            r.dv[:keys, :] = dv
        else:
            r.dk[:keys, :] += dk
            r.dv[:keys, :] += dv

    def inward(self, rows, part):
        r, f, ff = self.r, self.f, self.ff
        qk = jnp.concatenate([r.dq[rows, :], r.dk[rows, :]], axis=1)
        qk = qk * r.cos[rows, :] + swap_lanes(qk * r.sin[rows, :])
        rest = jnp.concatenate([r.dv[rows, :], jnp.zeros((TILE, HEAD), f32)], axis=1)
        mix = jnp.concatenate([qk, rest], axis=1).astype(bf16)
        r.mix[rows, :] = mix
        out = dot_nt(mix, self.w[:, :f]) + dot_nt(r.dz[rows, :], self.w[:, f : f + ff])
        part[rows, :] = out.astype(bf16)

    def head_grads(self, rows):
        r, f = self.r, self.f
        mixed = dot_tn(self.h[:, rows], r.mix[...])
        out = dot_tn(self.g[:, rows], self.o[...])
        self.dw[rows, :f] = jnp.concatenate([mixed[:, : 3 * HEAD], out], axis=1).astype(bf16)

    def feed_grads(self, rows):
        r, f, ff = self.r, self.f, self.ff
        self.dw[rows, f : f + ff] = dot_tn(self.h[:, rows], r.dz[...]).astype(bf16)
        self.dw[rows, f + ff : f + 2 * ff] = dot_tn(self.g[:, rows], self.a[...]).astype(bf16)


def norm_row(r, layer, kind):
    return r.norms[layer * 3 + kind : layer * 3 + kind + 1, :]


def column_sums(values):
    return jnp.sum(values, axis=0, keepdims=True)


def cross_rows(net, r):
    p = net.p
    same = p.core == p.row

    def crossing(i):
        source, landing = ((r.act, r.x0), (r.cot, r.gr1))[i]
        return pltpu.make_async_remote_copy(
            src_ref=source.at[1 - p.row],
            dst_ref=landing,
            send_sem=r.x_sems.at[i],
            recv_sem=r.x_sems.at[2 + i],
            device_id=net.partner(),
            device_id_type=MESH,
        )

    def start(i):
        @pl.when(same)
        def _():
            crossing(i).start()
            if i:
                r.gr1[...] = r.cot[p.row]
            else:
                r.x0[...] = r.act[p.row]

    def arrive(i):
        @pl.when(jnp.logical_not(same))
        def _():
            crossing(i).wait_recv()

    def finish():
        @pl.when(same)
        def _():
            crossing(0).wait_send()
            crossing(1).wait_send()

    return (start, arrive, finish)


def give_back(net, r, i, source, target):
    p = net.p
    same = p.core == p.row

    def copy(j, device, row):
        return pltpu.make_async_remote_copy(
            src_ref=source,
            dst_ref=target.at[row],
            send_sem=r.back_sems.at[i, j],
            recv_sem=r.back_sems.at[i, 2 + row],
            device_id=device,
            device_id_type=MESH,
        )

    def far(j):
        return copy(j, p.device(p.member, row=1 - p.row, core=lax.rem(p.core + j, 2)), p.row)

    @pl.when(same)
    def _():
        copy(0, net.sibling, p.row).start()
        target[p.row] = source[...]

    @pl.when(jnp.logical_not(same))
    def _():
        far(0).start()
        far(1).start()

    def finish():
        @pl.when(same)
        def _():
            copy(0, net.sibling, p.row).wait_send()

        @pl.when(jnp.logical_not(same))
        def _():
            far(0).wait_send()
            far(1).wait_send()
            copy(0, net.sibling, p.row).wait_recv()

        copy(0, net.sibling, 1 - p.row).wait_recv()

    return finish


def share_all(net, sem, out, source):
    p = net.p
    here = p.seq * 2 + p.core
    others = [
        (lax.rem(p.seq + i, p.n), lax.rem(p.core + j, 2)) for i in range(p.n) for j in range(2) if i or j
    ]
    sends = Sends(net)
    for seq, core in others:
        sends.send(source(seq), out.at[here], sem, {"seq": seq, "tp": core})
    whole = out.at[pl.ds(0, len(others))]
    return (lambda: wait_for(net, whole, sem), lambda: sends.finish(whole))


def position_tables(net, r):
    p = net.p
    span = r.act.shape[1]
    lines = []
    for kind in range(2):
        row = LAYERS * 3 + kind * p.rows + p.row
        pieces = [r.table[s, pl.ds(row, 1), :span] for s in range(p.n)]
        lines.append(jnp.concatenate(pieces, axis=1))
    positions, segments = lines
    r.segr[...] = segments
    pair = lax.broadcasted_iota(jnp.int32, (ROTARY, positions.shape[1]), 0) // 2
    angles = jnp.exp(pair.astype(f32) * (-2.0 * math.log(10000.0) / ROTARY)) * positions
    sign = jnp.where(lax.broadcasted_iota(jnp.int32, angles.shape, 0) % 2 == 0, -1.0, 1.0)
    ones = jnp.ones((HEAD - ROTARY, angles.shape[1]), f32)
    cosine, sine = jnp.cos(angles), jnp.sin(angles) * sign
    cosine = jnp.concatenate([cosine, ones, cosine, ones], axis=0)
    sine = jnp.concatenate([sine, ones * 0.0, sine, ones * 0.0], axis=0)
    segments = jnp.broadcast_to(segments, (128, segments.shape[1]))
    for t in range(angles.shape[1] // 128):
        block = slice(t * 128, (t + 1) * 128)
        r.cos[block, :] = cosine[:, block].T
        r.sin[block, :] = sine[:, block].T
        r.segc[block, :] = segments[:, block].T[:, :1]


def pack_layer(r, layer):
    members, ff = r.pack.shape[1], (r.pack.shape[3] - 4 * HEAD) // 2
    f = 4 * HEAD
    for pair in range(members // 2):
        lanes = slice(pair * 2 * HEAD, (pair + 1) * 2 * HEAD)
        kinds = [r.qkv[layer, kind, :, lanes].astype(bf16) for kind in range(3)]
        kinds.append(r.out[layer, :, lanes].astype(bf16))
        for i in range(2):
            own = slice(i * HEAD, (i + 1) * HEAD)
            r.pack[layer, 2 * pair + i, :, :f] = jnp.concatenate([kind[:, own] for kind in kinds], axis=1)
    for member in range(members):
        lanes = slice(member * ff, (member + 1) * ff)
        r.pack[layer, member, :, f : f + ff] = getattr(r, "in")[layer, :, lanes].astype(bf16)
        r.pack[layer, member, :, f + ff :] = r.down[layer, :, lanes].astype(bf16)


def pack_small(r):
    rows, span = r.pos.shape
    r.small[...] = jnp.zeros_like(r.small)
    columns = r.norm.shape[2]
    for layer in range(LAYERS):
        r.small[layer * 3 : layer * 3 + 3, :columns] = r.norm[:, layer, :].astype(bf16).astype(f32)
    r.small[LAYERS * 3 : LAYERS * 3 + rows, :span] = r.pos[...].astype(f32)
    r.small[LAYERS * 3 + rows : LAYERS * 3 + 2 * rows, :span] = r.seg[...].astype(f32)


def whole_part(net, r):
    p = net.p
    n, width = p.n, r.act.shape[2]
    finishes = []

    pack_small(r)
    greet(net.everyone())
    gathers = [Gather(net, r.gather_a), Gather(net, r.gather_b)]
    reduces = [
        Reduce(net, r.part_a, r.total_a, r.bufs_a, r.reduce_a),
        Reduce(net, r.part_b, r.total_b, r.bufs_b, r.reduce_b),
    ]
    table_sends = Sends(net)
    finishes.append(lambda: table_sends.finish(r.table.at[pl.ds(0, n - 1)]))
    for i in range(1, n):
        device = {"seq": lax.rem(p.seq + i, n), "tp": p.core}
        table_sends.send(r.small, r.table.at[p.seq], r.table_sem, device)
    r.table[p.seq] = r.small[...]
    cross_start, cross_arrive, cross_finish = cross_rows(net, r)
    finishes.append(cross_finish)
    cross_start(0)
    f = 4 * HEAD
    ff = (r.w0.shape[1] - f) // 2
    early, late = slice(0, f + ff), slice(f + ff, f + 2 * ff)
    heads, feeds = slice(0, f), slice(f, f + 2 * ff)
    spreads = [
        [
            Spread(net, r.pack.at[k], (r.w0, r.w1)[k], columns, r.block_sems.at[k, i], r.cross_sems.at[k, i])
            for i, columns in enumerate((early, late))
        ]
        for k in range(LAYERS)
    ]
    collects = [
        [
            Collect(
                net,
                (r.dw0, r.dw1)[k],
                r.grads.at[k],
                columns,
                r.cross_buf.at[k],
                r.block_out.at[k],
                r.collect_sems.at[k, i],
                r.block_sems.at[k, i],
            )
            for i, columns in enumerate((feeds, heads))
        ]
        for k in range(LAYERS)
    ]
    finishes.extend(collect.finish for pair in collects for collect in pair)
    pack_layer(r, 0)
    first, second = spreads[0]
    first.start()
    first.send(3)
    wait_for(net, r.table.at[pl.ds(0, n - 1)], r.table_sem)
    own_columns = width // n
    many = 128 // own_columns
    for s in range(0, n, many):
        r.norms[:, s * own_columns : (s + many) * own_columns] = jnp.concatenate(
            [r.table[s + i, 0:8, :own_columns] for i in range(many)], axis=1
        )
    cross_arrive(0)
    xhat, inverse = layer_norm(r.x0[...])
    normed = xhat * norm_row(r, 0, 0) + norm_row(r, 0, 1)
    r.h0[net.own(), :] = normed.astype(bf16)
    gather = gathers[0]
    gather.start(r.h0)
    position_tables(net, r)

    layer = Layer(r, 0)
    tiles = range(layer.length // TILE)
    gather_steps = gather.steps()
    advance(gather_steps)
    first.send()
    first.receive(3)
    advance(gather_steps)
    pack_layer(r, 1)
    advance(gather_steps)
    first.receive(2)
    advance(gather_steps)
    first.receive()
    drain(gather_steps)
    second.start()
    second.send()
    cross_start(1)
    first.settle()
    for k in tiles:
        layer.project(net.tile(k))
        layer.feed(net.tile(k))
    second.receive()
    first, third = spreads[1]
    first.start()
    first.send()
    for i in tiles:
        layer.attend(i)
    second.settle()
    reduce = reduces[0]
    for a in net.far_first():
        layer.branch(net.tile_rows(a), r.part_a)
        reduce.offer(a)
    steps = reduce.steps()
    advance(steps, p.na + 1)
    first.receive(3)
    drain(steps)
    middle = r.x0[...] + (r.total_a[...] + norm_row(r, 0, 2))
    r.x1[...] = middle
    xhat, inverse = layer_norm(middle)
    normed = xhat * norm_row(r, 1, 0) + norm_row(r, 1, 1)
    r.h1[net.own(), :] = normed.astype(bf16)
    gathers[0].finish()
    gather = gathers[1]
    gather.start(r.h1)
    third.start()
    third.send()

    layer = Layer(r, 1)
    gather_steps = gather.steps()
    advance(gather_steps)
    first.receive()
    advance(gather_steps, 2)
    cross_arrive(1)
    r.g1[net.own(), :] = r.gr1[...].astype(bf16)
    advance(gather_steps)
    third.receive()
    grad_gather = gathers[0]
    grad_gather.start(r.g1)
    first.settle()
    for k in tiles:
        layer.project(net.tile(k))
        layer.feed(net.tile(k))
        advance(gather_steps)
    drain(gather_steps)
    grad_steps = grad_gather.steps()
    advance(grad_steps)
    for i in tiles:
        layer.attend(i)
        advance(grad_steps)
    third.settle()
    forward_reduce = reduces[1]
    forward_steps = forward_reduce.steps()
    for a in net.far_first():
        layer.branch(net.tile_rows(a), r.part_b)
        forward_reduce.offer(a)
    drain(grad_steps)
    advance(forward_steps, p.na)

    fed, headed = collects[1]
    for k in tiles:
        layer.feed_back(net.tile(k))
    for i in reversed(tiles):
        layer.attend_back(i)
    reduce = reduces[0]
    reduce.finish()
    for spread in spreads[0] + spreads[1]:
        spread.finish()
    steps = reduce.steps()
    for a in net.far_first():
        layer.inward(net.tile_rows(a), r.part_a)
        reduce.offer(a)
    advance(steps, p.na)
    for k in range(p.na - 1, -1, -1):
        layer.feed_grads(net.width_rows(k, layer.width))
        fed.offer(k)
    advance(forward_steps, p.na - 1)
    for k in range(p.na - 1, -1, -1):
        layer.head_grads(net.width_rows(k, layer.width))
        headed.offer(k)
        if k:
            advance(steps)
    drain(steps)
    xhat, inverse = layer_norm(r.x1[...])
    normed_grads = r.total_a[...]
    below = norm_back(r.gr1[...], normed_grads, xhat, inverse, norm_row(r, 1, 0))
    r.gr0[...] = below
    r.g0[net.own(), :] = below.astype(bf16)
    gather = gathers[1]
    gather.finish()
    gather.start(r.g0)
    r.sums1[...] = jnp.concatenate(
        [
            column_sums(normed_grads * xhat),
            column_sums(normed_grads),
            column_sums(r.gr1[...]),
            jnp.zeros((5, layer.width), f32),
        ]
    )
    drain(forward_steps)
    r.result[...] = r.x1[...] + (r.total_b[...] + norm_row(r, 1, 2))

    layer = Layer(r, 0)
    gather_steps = gather.steps()
    advance(gather_steps, 2)
    for k in tiles:
        advance(gather_steps)
        layer.feed_back(net.tile(k))
    drain(gather_steps)
    fed.relay()
    finishes.append(give_back(net, r, 0, r.result, r.results))
    fed_0, headed_0 = collects[0]
    for k in range(p.na - 1, -1, -1):
        layer.feed_grads(net.width_rows(k, layer.width))
        fed_0.offer(k)
    headed.relay(4)
    for i in reversed(tiles):
        layer.attend_back(i)
    headed.relay()
    reduce = forward_reduce
    reduce.finish()
    steps = reduce.steps()
    for a in net.far_first():
        layer.inward(net.tile_rows(a), r.part_b)
        reduce.offer(a)
    advance(steps, p.na)
    for k in range(p.na - 1, -1, -1):
        layer.head_grads(net.width_rows(k, layer.width))
        headed_0.offer(k)
        if k:
            advance(steps)
            fed_0.relay(2)
    drain(steps)
    fed_0.relay()
    normed_grads = r.total_b[...]
    xhat, inverse = layer_norm(r.x0[...])
    rows = [
        column_sums(normed_grads * xhat),
        column_sums(normed_grads),
        column_sums(r.gr0[...]),
        r.sums1[0:3, :],
        jnp.zeros((2, width), f32),
    ]
    rows = jnp.concatenate(rows)
    for s in range(n):
        r.small_out[s] = pad_lanes(rows[:, s * own_columns : (s + 1) * own_columns])
    here = p.seq * 2 + p.core
    small_arrive, small_finish = share_all(net, r.small_sem, r.small_in, lambda seq: r.small_out.at[seq])
    finishes.append(small_finish)
    r.small_in[here] = r.small_out[p.seq]
    headed_0.relay()
    r.in_grad[...] = norm_back(r.gr0[...], normed_grads, xhat, inverse, norm_row(r, 0, 0))
    finishes.append(give_back(net, r, 1, r.in_grad, r.in_grads))
    squares = fed.settle() + headed.settle()
    small_arrive()
    norm_grads = jnp.sum(r.small_in[...], axis=0)
    r.norm_grads[...] = norm_grads
    squares = squares + 0.5 * jnp.sum(norm_grads * norm_grads, axis=(0, 1), keepdims=True)
    squares = squares + (fed_0.settle() + headed_0.settle())
    r.squares[here] = jnp.broadcast_to(squares, (8, 128))
    square_arrive, square_finish = share_all(net, r.square_sem, r.squares, lambda seq: r.squares.at[here])
    finishes.append(square_finish)
    square_arrive()
    r.norm_out[...] = jnp.sqrt(jnp.sum(r.squares[...], axis=0))
    for part in gathers + reduces:
        part.finish()
    for finish in finishes:
        finish()


def fused_call(name, part, geometry, ins, outs, scratch, collective_id):
    flat, places = [], []
    for key, spec in scratch.items():
        group = spec if isinstance(spec, tuple) else (spec,)
        places.append((key, len(flat), len(group), isinstance(spec, tuple)))
        flat.extend(group)

    def kernel(*refs):
        r = types.SimpleNamespace(**dict(zip([*ins, *outs], refs)))
        rest = refs[len(ins) + len(outs) :]
        for key, start, count, grouped in places:
            setattr(r, key, rest[start : start + count] if grouped else rest[start])
        part(Net(*geometry, r.send_sems), r)

    results = pl.pallas_call(
        kernel,
        out_shape=tuple(outs.values()),
        in_specs=vmem_specs(len(ins)),
        out_specs=tuple(vmem_specs(len(outs))),
        scratch_shapes=flat,
        compiler_params=remote_params(collective_id),
        name=name,
    )(*ins.values())
    return types.SimpleNamespace(**dict(zip(outs, results)))


def by_kind(array):
    return jnp.swapaxes(array, array.ndim - 3, array.ndim - 2)


def optimizer_kernel(limit, grads_ref, norm_grads_ref, norm_ref, result_ref, in_grad_ref, *refs):
    weights, firsts, seconds = refs[:5], refs[5:10], refs[10:15]
    new_weights, new_firsts, new_seconds = refs[15:20], refs[20:25], refs[25:30]
    bias_ref, total_ref, result_out_ref, in_grad_out_ref = refs[30:]
    result_out_ref[...] = result_ref[...]
    in_grad_out_ref[...] = in_grad_ref[...]
    norm = norm_ref[0:1, 0:1]
    factor = jnp.minimum(1.0, limit / (norm + 1e-06))
    members, ff = grads_ref.shape[1], (grads_ref.shape[3] - 4 * HEAD) // 2
    f = 4 * HEAD

    def update(kind, where, gradient, rate, decay):
        found = adam_update(
            weights[kind][where], firsts[kind][where], seconds[kind][where], gradient, factor, rate, decay
        )
        for ref, value in zip((new_weights[kind], new_firsts[kind], new_seconds[kind]), found):
            ref[where] = value

    blocks = [grads_ref[0, member].astype(f32) for member in range(members)]
    for part in range(4):
        lanes = slice(part * HEAD, (part + 1) * HEAD)
        gradient = jnp.concatenate([block[:, lanes] for block in blocks], axis=1)
        if part < 3:
            update(0, (0, part), gradient, rate_matrix, decay_matrix)
        else:
            update(1, (0,), gradient, rate_output, decay_matrix)
    for member in range(members):
        lanes = slice(member * ff, (member + 1) * ff)
        update(2, (0, slice(None), lanes), blocks[member][:, f : f + ff], rate_matrix, decay_matrix)
        update(3, (0, slice(None), lanes), blocks[member][:, f + ff :], rate_matrix, decay_matrix)

    @pl.when((pl.program_id(0) == 0) & (pl.program_id(1) == 0))
    def _():
        columns = weights[4].shape[2]
        for layer in range(LAYERS):
            gradient = norm_grads_ref[layer * 3 : layer * 3 + 3, :columns]
            update(4, (slice(None), layer), gradient, rate_vector, 0.0)
            bias_ref[layer : layer + 1, :] = gradient[2:3, :] * factor
        total_ref[...] = norm


def optimizer(found, weights, firsts, seconds, parameters):
    layers, height = weights[1].shape[:2]
    rows = height // 2
    grads = found.grads

    def spec(array):
        extent = array.shape
        if extent[0] == 3:
            return pl.BlockSpec(extent, lambda i, j: (0, 0, 0))
        if array.ndim == 4:
            return pl.BlockSpec((1, 3, rows, extent[3]), lambda i, j: (i, 0, j, 0))
        return pl.BlockSpec((1, rows * extent[1] // height, extent[2]), lambda i, j: (i, j, 0))

    def fixed(*extent):
        return pl.BlockSpec(extent, lambda i, j: (0,) * len(extent))

    arrays = [by_kind(array) if i % 5 in (0, 4) else array for i, array in enumerate(weights + firsts + seconds)]
    tokens = [found.results, found.in_grads]
    bias_shape = (layers, weights[4].shape[2])
    made = pl.pallas_call(
        functools.partial(optimizer_kernel, clip_share * math.sqrt(parameters)),
        grid=(layers, height // rows),
        in_specs=[
            pl.BlockSpec((1, grads.shape[1], rows, grads.shape[3]), lambda i, j: (i, 0, j, 0)),
            fixed(8, 128),
            fixed(8, 128),
        ]
        + [spec(array) for array in tokens + arrays],
        out_specs=tuple(
            [spec(array) for array in arrays]
            + [fixed(*bias_shape), fixed(1, 1)]
            + [spec(array) for array in tokens]
        ),
        out_shape=tuple(
            [jax.ShapeDtypeStruct(array.shape, array.dtype) for array in arrays]
            + [jax.ShapeDtypeStruct(bias_shape, f32), jax.ShapeDtypeStruct((1, 1), f32)]
            + [jax.ShapeDtypeStruct(array.shape, array.dtype) for array in tokens]
        ),
        compiler_params=pltpu.CompilerParams(vmem_limit_bytes=56 * megabyte),
        name="optimizer",
    )(grads, found.norm_grads, found.norm_out, *tokens, *arrays)
    count = len(arrays)
    updated = [by_kind(array) if i % 5 in (0, 4) else array for i, array in enumerate(made[:count])]
    bias, norm, result, in_grad = made[count:]
    return (result, in_grad, norm.reshape(()), *updated, bias)


def shards_together(
    n,
    activations,
    cotangent,
    segment_ids,
    position_ids,
    qkv_weight,
    out_weight,
    in_weight,
    down_weight,
    norm_params,
    qkv_first,
    out_first,
    in_first,
    down_first,
    norm_first,
    qkv_second,
    out_second,
    in_second,
    down_second,
    norm_second,
):
    rows, span, width = activations.shape
    members = n // rows
    na, nb = split_sizes(members)
    length = n * span
    half = rows * span // 2
    pieces = 2
    heads = qkv_weight.shape[3] // HEAD
    ff = in_weight.shape[2] // members
    height = width // n
    columns = 4 * HEAD + 2 * ff
    geometry = (n, rows, half, pieces)

    def shape(*extent, kind=f32):
        return jax.ShapeDtypeStruct(extent, kind)

    def scratch_like(shapes, suffix):
        return {key + suffix: VM(value.shape, value.dtype) for key, value in shapes.items()}

    gather_sems = (DMA((na, pieces)), DMA((members, pieces)), DMA((na, pieces)))
    reduce_sems = (DMA((members, pieces)), DMA((members, pieces)), DMA((2 * na, pieces)))
    reduce_bufs = tuple(
        VM((count * half, width), bf16) for count in (members, members, members, 2 * na, 2 * na)
    ) + (VM((half, width), f32),)
    kept = dict(
        q=shape(length, HEAD, kind=bf16),
        k=shape(length, HEAD, kind=bf16),
        v=shape(length, HEAD, kind=bf16),
        o=shape(length, HEAD, kind=bf16),
        lse=shape(length, 1),
        a=shape(length, ff, kind=bf16),
        z=shape(length, ff),
        w=shape(width, columns, kind=bf16),
        dw=shape(width, columns, kind=bf16),
        h=shape(length, width, kind=bf16),
        g=shape(length, width, kind=bf16),
        x=shape(half, width),
        gr=shape(half, width),
    )
    lines = LAYERS * 3 + 2 * rows
    three = fused_call(
        "whole_part",
        whole_part,
        geometry,
        {
            "act": activations,
            "cot": cotangent,
            "seg": segment_ids,
            "pos": position_ids,
            "qkv": by_kind(qkv_weight),
            "out": out_weight,
            "in": in_weight,
            "down": down_weight,
            "norm": by_kind(norm_params),
        },
        dict(
            results=shape(rows, span, width),
            in_grads=shape(rows, span, width),
            grads=shape(LAYERS, members, height, columns, kind=bf16),
            norm_grads=shape(8, 128),
            norm_out=shape(8, 128),
        ),
        dict(
            small=VM((-(-lines // 8) * 8, 128), f32),
            table=VM((n, -(-lines // 8) * 8, 128), f32),
            pack=VM((LAYERS, members, height, columns), bf16),
            norms=VM((8, width), f32),
            cos=VM((length, 128), f32),
            sin=VM((length, 128), f32),
            segc=VM((length, 1), f32),
            segr=VM((1, length), f32),
            **scratch_like(kept, "0"),
            **scratch_like(kept, "1"),
            dz=VM((length, ff), bf16),
            do=VM((length, HEAD), bf16),
            dq=VM((length, HEAD), f32),
            dk=VM((length, HEAD), f32),
            dv=VM((length, HEAD), f32),
            mix=VM((length, 4 * HEAD), bf16),
            part_a=VM((length, width), bf16),
            part_b=VM((length, width), bf16),
            total_a=VM((half, width), f32),
            total_b=VM((half, width), f32),
            bufs_a=reduce_bufs,
            bufs_b=reduce_bufs,
            result=VM((half, width), f32),
            in_grad=VM((half, width), f32),
            sums1=VM((8, width), f32),
            cross_buf=VM((LAYERS, members, height, columns), bf16),
            block_out=VM((LAYERS, members, height, columns), bf16),
            small_out=VM((n, 8, 128), f32),
            small_in=VM((2 * n, 8, 128), f32),
            squares=VM((2 * n, 8, 128), f32),
            reduce_a=reduce_sems,
            reduce_b=reduce_sems,
            gather_a=gather_sems,
            gather_b=gather_sems,
            x_sems=DMA((4,)),
            back_sems=DMA((2, 4)),
            table_sem=DMA,
            small_sem=DMA,
            square_sem=DMA,
            block_sems=DMA((LAYERS, 2, members)),
            cross_sems=DMA((LAYERS, 2, members)),
            collect_sems=DMA((LAYERS, 2, members)),
            send_sems=DMA((2 * (1 + 2 * pieces * na) + 2 * (1 + 2 * pieces * (na - 1)) + 11,)),
        ),
        0,
    )
    return optimizer(
        three,
        (qkv_weight, out_weight, in_weight, down_weight, norm_params),
        (qkv_first, out_first, in_first, down_first, norm_first),
        (qkv_second, out_second, in_second, down_second, norm_second),
        LAYERS * width * (4 * 2 * heads * HEAD + 2 * 2 * members * ff + 3),
    )


def shards(n, activations, *others):
    rows, span, width = activations.shape
    together = 12 * n * span * width * 2 <= 40 * megabyte and rows == 2 and n * span % TILE == 0
    return (shards_together if together else shards_apart)(n, activations, *others)


def solution(mesh):
    tokens = P(None, "seq", None)
    qkv = P(None, "seq", None, "tp")
    matrix = P(None, "seq", "tp")
    norm = P(None, None, "seq")
    kinds = (qkv, matrix, matrix, matrix, norm)
    return jax.shard_map(
        functools.partial(shards, mesh.shape["seq"]),
        mesh=mesh,
        in_specs=(tokens, tokens, P(None, "seq"), P(None, "seq")) + kinds * 3,
        out_specs=(tokens, tokens, P()) + kinds * 3 + (P(None, "seq"),),
        check_vma=False,
    )
```

```python
import functools
import math
import types

import jax
import jax.numpy as jnp
from jax import lax
from jax.experimental import pallas as pl
from jax.experimental.pallas import tpu as pltpu
from jax.sharding import PartitionSpec as P

HEAD = 64
ROTARY = 32
LAYERS = 2
STEP = 10
TILE = 256

norm_eps = 1e-05
beta_one = 0.9
beta_two = 0.999
adam_eps = 1e-08
rate_matrix = 0.05
rate_output = 0.15
rate_vector = 1.0
decay_matrix = 0.1
clip_share = 0.25
low_score = -1e30

MESH = pl.DeviceIdType.MESH
VM = pltpu.VMEM
DMA = pltpu.SemaphoreType.DMA
bf16 = jnp.bfloat16
f32 = jnp.float32
megabyte = 1 << 20


def split_sizes(members):
    nb = 1 << ((members.bit_length() - 1) // 2)
    return (members // nb, nb)


class Place:
    def __init__(self, n, rows):
        self.n, self.rows = n, rows
        self.members = n // rows
        self.na, self.nb = split_sizes(self.members)
        self.seq = lax.axis_index("seq")
        self.core = lax.axis_index("tp")
        self.row = lax.rem(self.seq, rows)
        self.member = self.seq // rows
        self.a = self.member // self.nb
        self.b = lax.rem(self.member, self.nb)

    def am(self, step):
        return lax.rem(self.a + step, self.na)

    def bm(self, step):
        return lax.rem(self.b + step, self.nb)

    def device(self, member, row=None, core=None):
        row = self.row if row is None else row
        return {"seq": member * self.rows + row, "tp": self.core if core is None else core}

    def at(self, a, b):
        return self.device(a * self.nb + b)

    def sibling(self):
        return self.device(self.member, core=1 - self.core)

    def partners(self):
        return [self.device(self.member, row=lax.rem(self.row + i, self.rows)) for i in range(1, self.rows)]

    def axis_peers(self):
        peers = [self.at(self.am(i), self.b) for i in range(1, self.na)]
        peers += [self.at(self.a, self.bm(j)) for j in range(1, self.nb)]
        return peers

    def other_members(self):
        return [self.device(lax.rem(self.member + i, self.members)) for i in range(1, self.members)]


def greet(devices):
    barrier = pltpu.get_barrier_semaphore()
    for device in devices:
        pl.semaphore_signal(barrier, inc=1, device_id=device, device_id_type=MESH)
    pl.semaphore_wait(barrier, len(devices))


class Sender:
    def __init__(self, send_sems):
        self.send_sems, self.copies = send_sems, []

    def send(self, src, dst, recv_sem, device):
        copy = pltpu.make_async_remote_copy(
            src_ref=src,
            dst_ref=dst,
            send_sem=self.send_sems.at[len(self.copies)],
            recv_sem=recv_sem,
            device_id=device,
            device_id_type=MESH,
        )
        copy.start()
        self.copies.append(copy)

    def arrived(self, dst, recv_sem, device):
        pltpu.make_async_remote_copy(
            src_ref=dst,
            dst_ref=dst,
            send_sem=self.send_sems.at[0],
            recv_sem=recv_sem,
            device_id=device,
            device_id_type=MESH,
        ).wait_recv()

    def finish(self):
        for copy in self.copies:
            copy.wait_send()


def remote_params(collective_id):
    return pltpu.CompilerParams(
        collective_id=collective_id, has_side_effects=True, vmem_limit_bytes=56 * megabyte
    )


def vmem_specs(count):
    return [pl.BlockSpec(memory_space=VM)] * count


def spread_kernel(n, rows, wide_ref, small_ref, pack_ref, chunk_ref, table_ref, weight_ref, *sems):
    (send_sems, chunk_sems, table_sems, block_sems, cross_sems, local_sems) = sems
    p = Place(n, rows)
    members = p.members
    everybody = [
        {"seq": lax.rem(p.seq + i, n), "tp": p.core} for i in range(1, n)
    ]
    greet(everybody)
    sender = Sender(send_sems)
    partners = [
        (lax.rem(p.row + i, rows), p.device(p.member, row=lax.rem(p.row + i, rows)))
        for i in range(1, rows)
    ]
    for device in everybody:
        sender.send(small_ref, table_ref.at[p.seq], table_sems.at[p.seq], device)
    for row, device in partners:
        sender.send(wide_ref.at[row], chunk_ref.at[p.row], chunk_sems.at[p.row], device)
    for layer in range(LAYERS):
        for i in range(1, members):
            member = lax.rem(p.member + i, members)
            sender.send(
                pack_ref.at[layer, member],
                weight_ref.at[layer, p.seq],
                block_sems.at[layer, p.member],
                p.device(member),
            )
        for row, device in partners:
            sender.send(
                pack_ref.at[layer, p.member],
                weight_ref.at[layer, p.seq],
                cross_sems.at[layer, p.seq],
                device,
            )
    own = [
        pltpu.make_async_copy(small_ref, table_ref.at[p.seq], local_sems.at[0]),
        pltpu.make_async_copy(wide_ref.at[p.row], chunk_ref.at[p.row], local_sems.at[1]),
    ]
    for layer in range(LAYERS):
        own.append(
            pltpu.make_async_copy(
                pack_ref.at[layer, p.member], weight_ref.at[layer, p.seq], local_sems.at[2 + layer]
            )
        )
    for copy in own:
        copy.start()
    for layer in range(LAYERS):
        for i in range(1, members):
            member = lax.rem(p.member + members - i, members)
            block = weight_ref.at[layer, member * rows + p.row]
            sender.arrived(block, block_sems.at[layer, member], p.sibling())
            for row, device in partners:
                sender.send(block, block, cross_sems.at[layer, member * rows + p.row], device)
    for i in range(1, n):
        seq = lax.rem(p.seq + i, n)
        sender.arrived(table_ref.at[seq], table_sems.at[seq], p.sibling())
    for row, device in partners:
        sender.arrived(chunk_ref.at[row], chunk_sems.at[row], p.sibling())
    for layer in range(LAYERS):
        for i in range(members):
            member = lax.rem(p.member + members - i, members)
            for row, device in partners:
                block = weight_ref.at[layer, member * rows + row]
                sender.arrived(block, cross_sems.at[layer, member * rows + row], p.sibling())
    sender.finish()
    for copy in own:
        copy.wait()


def spread(n, rows, wide, small, pack, collective_id):
    layers, members, height, columns = pack.shape
    sends = (n - 1) + (rows - 1) + layers * (members - 1 + members * (rows - 1))
    return pl.pallas_call(
        functools.partial(spread_kernel, n, rows),
        out_shape=(
            jax.ShapeDtypeStruct(wide.shape, wide.dtype),
            jax.ShapeDtypeStruct((n,) + small.shape, small.dtype),
            jax.ShapeDtypeStruct((layers, n, height, columns), pack.dtype),
        ),
        in_specs=vmem_specs(3),
        out_specs=tuple(vmem_specs(3)),
        scratch_shapes=[
            DMA((sends,)),
            DMA((rows,)),
            DMA((n,)),
            DMA((layers, members)),
            DMA((layers, n)),
            DMA((2 + layers,)),
        ],
        compiler_params=remote_params(collective_id),
        name="spread_inputs",
    )(wide, small, pack)


def gather_kernel(n, rows, count, x_ref, out_ref, *sems):
    send_sems, a_sems, b_sems, core_sems, local_sem = sems
    p = Place(n, rows)
    na, nb, core = p.na, p.nb, p.core
    sibling = p.sibling()
    greet(p.axis_peers() + [sibling])
    sender = Sender(send_sems)
    a_steps = [1, na - 1] + list(range(2, na - 1)) if na > 2 else [1]

    def slot(k, a, b):
        return out_ref.at[k, a * nb + b, core]

    for k in range(count):
        mine = x_ref.at[k, core]
        for i in a_steps:
            sender.send(mine, slot(k, p.a, p.b), a_sems.at[k, p.a], p.at(p.am(i), p.b))
        for j in range(1, nb):
            sender.send(mine, slot(k, p.a, p.b), b_sems.at[k, p.member], p.at(p.a, p.bm(j)))
    own = pltpu.make_async_copy(x_ref, out_ref.at[:, p.member], local_sem)
    own.start()
    for k in range(count):
        for i in a_steps:
            a = p.am(i)
            here = slot(k, a, p.b)
            sender.arrived(here, a_sems.at[k, a], sibling)
            for j in range(1, nb):
                sender.send(here, here, b_sems.at[k, a * nb + p.b], p.at(p.a, p.bm(j)))
            sender.send(here, here, core_sems.at[k, a * nb + p.b], sibling)
    for k in range(count):
        for i in [0] + a_steps:
            for j in range(1, nb):
                a, b = p.am(i), p.bm(j)
                here = slot(k, a, b)
                sender.arrived(here, b_sems.at[k, a * nb + b], sibling)
                sender.send(here, here, core_sems.at[k, a * nb + b], sibling)
    for k in range(count):
        for i in range(1, p.members):
            member = lax.rem(p.member + i, p.members)
            sender.arrived(out_ref.at[k, member, 1 - core], core_sems.at[k, member], sibling)
    sender.finish()
    own.wait()


def gather(n, rows, pieces, collective_id):
    stacked = jnp.stack(pieces)
    count, two, height, width = stacked.shape
    members = n // rows
    na, nb = split_sizes(members)
    sends = count * ((na - 1) * (nb + 1) + nb - 1 + na * (nb - 1))
    return pl.pallas_call(
        functools.partial(gather_kernel, n, rows, count),
        out_shape=jax.ShapeDtypeStruct((count, members, two, height, width), stacked.dtype),
        in_specs=vmem_specs(1),
        out_specs=vmem_specs(1)[0],
        scratch_shapes=[
            DMA((sends,)),
            DMA((count, na)),
            DMA((count, members)),
            DMA((count, members)),
            DMA,
        ],
        compiler_params=remote_params(collective_id),
        name="gather_tokens",
    )(stacked)


def reduce_kernel(n, rows, count, *refs):
    x_refs, (out_ref, core_buf, b_buf, a_buf, b_out, a_out) = refs[:count], refs[count : count + 6]
    send_sems, core_sems, b_sems, a_sems, out_sems = refs[count + 6 :]
    p = Place(n, rows)
    na, nb, core = p.na, p.nb, p.core
    sibling = p.sibling()
    greet(p.axis_peers() + [sibling])
    sender = Sender(send_sems)
    a_steps = list(range(2, na - 1)) + [1, na - 1, 0] if na > 2 else [1, 0]
    for k in range(count):
        for i in a_steps:
            for j in list(range(1, nb)) + [0]:
                m = p.am(i) * nb + p.bm(j)
                sender.send(x_refs[k].at[m, 1 - core], core_buf.at[k, m], core_sems.at[k, m], sibling)
    for k in range(count):
        for i in a_steps:
            for j in range(1, nb):
                a, b = p.am(i), p.bm(j)
                m = a * nb + b
                sender.arrived(core_buf.at[k, m], core_sems.at[k, m], sibling)
                b_out[k, m] = (x_refs[k][m, core].astype(f32) + core_buf[k, m].astype(f32)).astype(bf16)
                landing = a * nb + p.b
                sender.send(b_out.at[k, m], b_buf.at[k, landing], b_sems.at[k, landing], p.at(p.a, b))
    for k in range(count):
        for i in a_steps:
            a = p.am(i)
            m = a * nb + p.b
            sender.arrived(core_buf.at[k, m], core_sems.at[k, m], sibling)
            total = x_refs[k][m, core].astype(f32) + core_buf[k, m].astype(f32)
            for j in range(1, nb):
                q = a * nb + p.bm(j)
                sender.arrived(b_buf.at[k, q], b_sems.at[k, q], sibling)
                total = total + b_buf[k, q].astype(f32)
            if i:
                a_out[k, a] = total.astype(bf16)
                sender.send(a_out.at[k, a], a_buf.at[k, p.a], a_sems.at[k, p.a], p.at(a, p.b))
            else:
                out_ref[k, core] = total
    for k in range(count):
        for i in range(1, na):
            a = p.am(i)
            sender.arrived(a_buf.at[k, a], a_sems.at[k, a], sibling)
            out_ref[k, core] += a_buf[k, a].astype(f32)
        sender.send(out_ref.at[k, core], out_ref.at[k, core], out_sems.at[k], sibling)
    for k in range(count):
        sender.arrived(out_ref.at[k, 1 - core], out_sems.at[k], sibling)
    sender.finish()


def reduce(n, rows, pieces, collective_id):
    count = len(pieces)
    members, two, height, width = pieces[0].shape
    na, nb = split_sizes(members)
    sends = count * (members + na * (nb - 1) + na)
    return pl.pallas_call(
        functools.partial(reduce_kernel, n, rows, count),
        out_shape=jax.ShapeDtypeStruct((count, two, height, width), f32),
        in_specs=vmem_specs(count),
        out_specs=vmem_specs(1)[0],
        scratch_shapes=[
            VM((count, members, height, width), bf16),
            VM((count, members, height, width), bf16),
            VM((count, na, height, width), bf16),
            VM((count, members, height, width), bf16),
            VM((count, na, height, width), bf16),
            DMA((sends,)),
            DMA((count, members)),
            DMA((count, members)),
            DMA((count, na)),
            DMA((count,)),
        ],
        compiler_params=remote_params(collective_id),
        name="reduce_tokens",
    )(*pieces)


def collect_kernel(n, rows, *refs):
    (first_ref, second_ref, wide_ref, small_ref, grad_ref, back_ref, table_ref) = refs[:7]
    (cross_buf, block_out, send_sems, cross_sems, block_sems, back_sems, table_sems, local_sems) = refs[7:]
    grads = (first_ref, second_ref)
    p = Place(n, rows)
    members = p.members
    everybody = [{"seq": lax.rem(p.seq + i, n), "tp": p.core} for i in range(1, n)]
    greet(everybody)
    sender = Sender(send_sems)
    partners = [
        (lax.rem(p.row + i, rows), p.device(p.member, row=lax.rem(p.row + i, rows)))
        for i in range(1, rows)
    ]
    order = [lax.rem(p.member + i, members) for i in range(1, members)] + [p.member]
    for i in range(1, n):
        seq = lax.rem(p.seq + i, n)
        sender.send(small_ref.at[seq], table_ref.at[p.seq], table_sems.at[p.seq], {"seq": seq, "tp": p.core})
    for layer in range(LAYERS):
        for member in order:
            for row, device in partners:
                sender.send(
                    grads[layer].at[member * rows + row],
                    cross_buf.at[layer, p.row, member],
                    cross_sems.at[layer, p.row, member],
                    device,
                )
    for row, device in partners:
        sender.send(wide_ref.at[row], back_ref.at[p.row], back_sems.at[p.row], device)
    own = [
        pltpu.make_async_copy(small_ref.at[p.seq], table_ref.at[p.seq], local_sems.at[0]),
        pltpu.make_async_copy(wide_ref.at[p.row], back_ref.at[p.row], local_sems.at[1]),
    ]
    for copy in own:
        copy.start()
    for layer in range(LAYERS):
        for i in list(range(1, members)) + [0]:
            member = lax.rem(p.member + i, members)
            total = grads[layer][member * rows + p.row].astype(f32)
            for row, device in partners:
                buffer = cross_buf.at[layer, row, member]
                sender.arrived(buffer, cross_sems.at[layer, row, member], p.sibling())
                total = total + buffer[...].astype(f32)
            if i:
                block_out[layer, member] = total.astype(bf16)
                sender.send(
                    block_out.at[layer, member],
                    grad_ref.at[layer, p.member],
                    block_sems.at[layer, p.member],
                    p.device(member),
                )
            else:
                grad_ref[layer, member] = total.astype(bf16)
    for i in range(1, n):
        seq = lax.rem(p.seq + i, n)
        sender.arrived(table_ref.at[seq], table_sems.at[seq], p.sibling())
    for row, device in partners:
        sender.arrived(back_ref.at[row], back_sems.at[row], p.sibling())
    for layer in range(LAYERS):
        for i in range(1, members):
            member = lax.rem(p.member + members - i, members)
            sender.arrived(grad_ref.at[layer, member], block_sems.at[layer, member], p.sibling())
    sender.finish()
    for copy in own:
        copy.wait()


def collect(n, rows, first, second, wide, small, collective_id):
    unused, height, columns = first.shape
    members = n // rows
    sends = (n - 1) + (rows - 1) + LAYERS * (members * (rows - 1) + members - 1)
    return pl.pallas_call(
        functools.partial(collect_kernel, n, rows),
        out_shape=(
            jax.ShapeDtypeStruct((LAYERS, members, height, columns), bf16),
            jax.ShapeDtypeStruct(wide.shape, wide.dtype),
            jax.ShapeDtypeStruct(small.shape, small.dtype),
        ),
        in_specs=vmem_specs(4),
        out_specs=tuple(vmem_specs(3)),
        scratch_shapes=[
            VM((LAYERS, rows, members, height, columns), bf16),
            VM((LAYERS, members, height, columns), bf16),
            DMA((sends,)),
            DMA((LAYERS, rows, members)),
            DMA((LAYERS, members)),
            DMA((rows,)),
            DMA((n,)),
            DMA((2,)),
        ],
        compiler_params=remote_params(collective_id),
        name="collect_gradients",
    )(first, second, wide, small)


def share_kernel(n, x_ref, out_ref, send_sems, recv_sems, local_sem):
    seq, core = lax.axis_index("seq"), lax.axis_index("tp")
    others = []
    for i in range(n):
        for j in range(2):
            if i or j:
                others.append((lax.rem(seq + i, n), lax.rem(core + j, 2)))
    greet([{"seq": s, "tp": c} for s, c in others])
    sender = Sender(send_sems)
    here = seq * 2 + core
    for s, c in others:
        sender.send(x_ref, out_ref.at[here], recv_sems.at[here], {"seq": s, "tp": c})
    own = pltpu.make_async_copy(x_ref, out_ref.at[here], local_sem)
    own.start()
    for s, c in others:
        sender.arrived(out_ref.at[s * 2 + c], recv_sems.at[s * 2 + c], {"seq": s, "tp": c})
    sender.finish()
    own.wait()


def share(n, x, collective_id):
    return pl.pallas_call(
        functools.partial(share_kernel, n),
        out_shape=jax.ShapeDtypeStruct((2 * n,) + x.shape, x.dtype),
        in_specs=vmem_specs(1),
        out_specs=vmem_specs(1)[0],
        scratch_shapes=[DMA((2 * n,)), DMA((2 * n,)), DMA],
        compiler_params=remote_params(collective_id),
        name="share_squares",
    )(x)


def dot(left, right):
    return jnp.dot(left, right, preferred_element_type=f32)


def dot_nt(left, right):
    return lax.dot_general(left, right, (((1,), (1,)), ((), ())), preferred_element_type=f32)


def dot_tn(left, right):
    return lax.dot_general(left, right, (((0,), (0,)), ((), ())), preferred_element_type=f32)


def swap_lanes(values):
    width = values.shape[-1]
    lane = lax.broadcasted_iota(jnp.int32, values.shape, 1)
    after = pltpu.roll(values, width - 1, 1)
    before = pltpu.roll(values, 1, 1)
    return jnp.where(lane % 2 == 0, after, before)


gelu_scale = 0.7978845608
gelu_cubic = 0.044715


def gelu(z):
    return 0.5 * z * (1.0 + jnp.tanh(gelu_scale * (z + gelu_cubic * z * z * z)))


def gelu_slope(z):
    inner = jnp.tanh(gelu_scale * (z + gelu_cubic * z * z * z))
    slope = gelu_scale * (1.0 + 3.0 * gelu_cubic * z * z)
    return 0.5 * (1.0 + inner) + 0.5 * z * (1.0 - inner * inner) * slope


def query_tiles(length, share, rows):
    tile = max(64, min(TILE, TILE * 1024 // length))
    first = 0
    if share > 1:
        first = lax.rem(lax.axis_index("seq") // rows, share) * (length // share)
    for i in range(length // share // tile):
        start = pl.multiple_of(first + i * tile, tile) if share > 1 else i * tile
        yield pl.ds(start, tile), start, ((i + 1) * tile if share == 1 else length)


def visible(start, keys, seg_col, seg_row):
    tile = seg_col.shape[0]
    place = start + lax.broadcasted_iota(jnp.int32, (tile, keys), 0)
    other = lax.broadcasted_iota(jnp.int32, (tile, keys), 1)
    return (other <= place) & (seg_col == seg_row)


def forward_kernel(batch, share, ff, h_ref, w_ref, cos_ref, sin_ref, segc_ref, segr_ref, *outs):
    part_ref, q_ref, k_ref, v_ref, o_ref, lse_ref, a_ref, z_ref = outs
    length = h_ref.shape[0]
    f = 4 * HEAD

    @pl.loop(0, length // TILE)
    def project(t):
        rows = pl.ds(t * TILE, TILE)
        h = h_ref[rows, :]
        mixed = dot(h, w_ref[:, :f])
        qk = mixed[:, : 2 * HEAD]
        qk = qk * cos_ref[rows, :] + swap_lanes(qk) * sin_ref[rows, :]
        q_ref[rows, :] = (qk[:, :HEAD].astype(bf16).astype(f32) * HEAD**-0.5).astype(bf16)
        k_ref[rows, :] = qk[:, HEAD:].astype(bf16)
        v_ref[rows, :] = mixed[:, 2 * HEAD : 3 * HEAD].astype(bf16)
        z = dot(h, w_ref[:, f : f + ff])
        z_ref[rows, :] = z
        a_ref[rows, :] = gelu(z).astype(bf16)

    if share > 1:
        o_ref[...] = jnp.zeros_like(o_ref)
        lse_ref[...] = jnp.zeros_like(lse_ref)
    for rows, start, keys in query_tiles(length, share, batch):
        scores = dot_nt(q_ref[rows, :], k_ref[:keys, :])
        seen = visible(start, keys, segc_ref[rows, :], segr_ref[:, :keys])
        scores = jnp.where(seen, scores, low_score)
        peak = jnp.max(scores, axis=1, keepdims=True)
        weights = jnp.exp(scores - peak)
        total = jnp.sum(weights, axis=1, keepdims=True)
        lse_ref[rows, :] = peak + jnp.log(total)
        shares = (weights * (1.0 / total)).astype(bf16)
        o_ref[rows, :] = dot(shares, v_ref[:keys, :]).astype(bf16)

    @pl.loop(0, length // TILE)
    def branch(t):
        rows = pl.ds(t * TILE, TILE)
        out = dot_nt(o_ref[rows, :], w_ref[:, 3 * HEAD : f])
        out = out + dot_nt(a_ref[rows, :], w_ref[:, f + ff : f + 2 * ff])
        part_ref[rows, :] = out.astype(bf16)


def forward(batch, share, ff, h, w, cosine, sine, seg_col, seg_row):
    length, width = h.shape
    column = jax.ShapeDtypeStruct((length, HEAD), bf16)
    return pl.pallas_call(
        functools.partial(forward_kernel, batch, share, ff),
        out_shape=(
            jax.ShapeDtypeStruct((length, width), bf16),
            column,
            column,
            column,
            column,
            jax.ShapeDtypeStruct((length, 1), f32),
            jax.ShapeDtypeStruct((length, ff), bf16),
            jax.ShapeDtypeStruct((length, ff), f32),
        ),
        in_specs=vmem_specs(6),
        out_specs=tuple(vmem_specs(8)),
        compiler_params=pltpu.CompilerParams(vmem_limit_bytes=56 * megabyte),
        name="layer_forward",
    )(h, w, cosine, sine, seg_col, seg_row)


def backward_kernel(batch, share, ff, g_ref, h_ref, w_ref, cos_ref, sin_ref, segc_ref, segr_ref, *refs):
    q_ref, k_ref, v_ref, o_ref, lse_ref, a_ref, z_ref, part_ref, dw_ref = refs[:9]
    dz_ref, do_ref, dq_ref, dk_ref, dv_ref, mix_ref = refs[9:]
    length, width = h_ref.shape
    f = 4 * HEAD

    @pl.loop(0, length // TILE)
    def feed(t):
        rows = pl.ds(t * TILE, TILE)
        g = g_ref[rows, :]
        da = dot(g, w_ref[:, f + ff : f + 2 * ff])
        dz_ref[rows, :] = (da * gelu_slope(z_ref[rows, :])).astype(bf16)
        do_ref[rows, :] = dot(g, w_ref[:, :f])[:, 3 * HEAD :].astype(bf16)

    dk_ref[...] = jnp.zeros_like(dk_ref)
    dv_ref[...] = jnp.zeros_like(dv_ref)
    if share > 1:
        dq_ref[...] = jnp.zeros_like(dq_ref)
    for rows, start, keys in query_tiles(length, share, batch):
        q, head_grad = q_ref[rows, :], do_ref[rows, :]
        scores = dot_nt(q, k_ref[:keys, :])
        seen = visible(start, keys, segc_ref[rows, :], segr_ref[:, :keys])
        shares = jnp.where(seen, jnp.exp(scores - lse_ref[rows, :]), 0.0)
        share_grads = dot_nt(head_grad, v_ref[:keys, :])
        delta = jnp.sum(shares * share_grads, axis=1, keepdims=True)
        score_grads = (shares * (share_grads - delta)).astype(bf16)
        dq_ref[rows, :] = dot(score_grads, k_ref[:keys, :]) * HEAD**-0.5
        dk_ref[:keys, :] += dot_tn(score_grads, q)
        dv_ref[:keys, :] += dot_tn(shares.astype(bf16), head_grad)

    @pl.loop(0, length // TILE)
    def inward(t):
        rows = pl.ds(t * TILE, TILE)
        qk = jnp.concatenate([dq_ref[rows, :], dk_ref[rows, :]], axis=1)
        qk = qk * cos_ref[rows, :] + swap_lanes(qk * sin_ref[rows, :])
        rest = jnp.concatenate([dv_ref[rows, :], jnp.zeros((TILE, HEAD), f32)], axis=1)
        mix = jnp.concatenate([qk, rest], axis=1).astype(bf16)
        mix_ref[rows, :] = mix
        out = dot_nt(mix, w_ref[:, :f]) + dot_nt(dz_ref[rows, :], w_ref[:, f : f + ff])
        part_ref[rows, :] = out.astype(bf16)

    @pl.loop(0, width // TILE)
    def weights(t):
        rows = pl.ds(t * TILE, TILE)
        h, g = h_ref[:, rows], g_ref[:, rows]
        mixed = dot_tn(h, mix_ref[...])
        out = dot_tn(g, o_ref[...])
        dw_ref[rows, :f] = jnp.concatenate([mixed[:, : 3 * HEAD], out], axis=1).astype(bf16)
        dw_ref[rows, f : f + ff] = dot_tn(h, dz_ref[...]).astype(bf16)
        dw_ref[rows, f + ff : f + 2 * ff] = dot_tn(g, a_ref[...]).astype(bf16)


def backward(batch, share, ff, g, h, w, cosine, sine, seg_col, seg_row, kept):
    length, width = h.shape
    return pl.pallas_call(
        functools.partial(backward_kernel, batch, share, ff),
        out_shape=(
            jax.ShapeDtypeStruct((length, width), bf16),
            jax.ShapeDtypeStruct(w.shape, bf16),
        ),
        in_specs=vmem_specs(14),
        out_specs=tuple(vmem_specs(2)),
        scratch_shapes=[
            VM((length, ff), bf16),
            VM((length, HEAD), bf16),
            VM((length, HEAD), f32),
            VM((length, HEAD), f32),
            VM((length, HEAD), f32),
            VM((length, 4 * HEAD), bf16),
        ],
        compiler_params=pltpu.CompilerParams(vmem_limit_bytes=60 * megabyte),
        name="layer_backward",
    )(g, h, w, cosine, sine, seg_col, seg_row, *kept)


def layer_norm(inputs):
    average = jnp.mean(inputs, axis=-1, keepdims=True)
    centred = inputs - average
    spread_here = jnp.mean(centred * centred, axis=-1, keepdims=True)
    inverse = lax.rsqrt(spread_here + norm_eps)
    return (centred * inverse, inverse)


def norm_back(grads, normed_grads, xhat, inverse, gain):
    scaled = normed_grads * gain
    average = jnp.mean(scaled, axis=-1, keepdims=True)
    along = jnp.mean(scaled * xhat, axis=-1, keepdims=True)
    return grads + (scaled - average - xhat * along) * inverse


def rotary_tables(positions):
    column = jnp.arange(HEAD)
    inside = column < ROTARY
    pair_index = column % ROTARY // 2
    frequency = jnp.exp(pair_index.astype(f32) * (-2.0 * math.log(10000.0) / ROTARY))
    angles = positions[:, None] * frequency
    cosine = jnp.where(inside, jnp.cos(angles), 1.0)
    signed = jnp.where(column % 2 == 0, -1.0, 1.0)
    sine = jnp.where(inside, signed * jnp.sin(angles), 0.0)
    return (jnp.tile(cosine, (1, 2)), jnp.tile(sine, (1, 2)))


def pad_lanes(values, width=128):
    return jnp.pad(values, [(0, 0)] * (values.ndim - 1) + [(0, width - values.shape[-1])])


def adam_update(weight, first, second, gradient, factor_clip, rate, decay):
    clipped = gradient * factor_clip
    first_new = beta_one * first + (1.0 - beta_one) * clipped
    second_new = beta_two * second + (1.0 - beta_two) * clipped * clipped
    first_hat = first_new / (1.0 - beta_one**STEP)
    second_hat = second_new / (1.0 - beta_two**STEP)
    weight_new = weight - rate * (first_hat / (jnp.sqrt(second_hat) + adam_eps) + decay * weight)
    return (weight_new, first_new, second_new)


def pack_weights(n, rows, qkv_weight, out_weight, in_weight, down_weight):
    layers, height = qkv_weight.shape[:2]
    members = n // rows
    heads = qkv_weight.shape[3] // HEAD
    share = members // heads
    ff = in_weight.shape[2] // members
    mixed = jnp.concatenate([qkv_weight, out_weight[:, :, None, :]], axis=2).astype(bf16)
    mixed = mixed.reshape(layers, height, 4, heads, HEAD).transpose(0, 3, 1, 2, 4)
    mixed = mixed.reshape(layers, heads, height, 4 * HEAD)
    if share > 1:
        mixed = jnp.repeat(mixed, share, axis=1)
    feeds = [
        weight.astype(bf16).reshape(layers, height, members, ff).transpose(0, 2, 1, 3)
        for weight in (in_weight, down_weight)
    ]
    return jnp.concatenate([mixed] + feeds, axis=3)


def unpack_gradients(grads, heads, ff):
    layers, members, height, unused = grads.shape
    grads = grads.astype(f32)
    share = members // heads
    mixed = grads[..., : 4 * HEAD]
    if share > 1:
        mixed = mixed.reshape(layers, heads, share, height, 4 * HEAD).sum(2)
    mixed = mixed.reshape(layers, heads, height, 4, HEAD).transpose(0, 2, 3, 1, 4)
    mixed = mixed.reshape(layers, height, 4, heads * HEAD)
    feeds = [
        grads[..., 4 * HEAD + k * ff : 4 * HEAD + (k + 1) * ff]
        .transpose(0, 2, 1, 3)
        .reshape(layers, height, members * ff)
        for k in range(2)
    ]
    return (mixed[:, :, :3], mixed[:, :, 3], feeds[0], feeds[1])


def shards_apart(
    n,
    activations,
    cotangent,
    segment_ids,
    position_ids,
    qkv_weight,
    out_weight,
    in_weight,
    down_weight,
    norm_params,
    qkv_first,
    out_first,
    in_first,
    down_first,
    norm_first,
    qkv_second,
    out_second,
    in_second,
    down_second,
    norm_second,
):
    rows, span, width = activations.shape
    members = n // rows
    length = n * span
    half = rows * span // 2
    heads = qkv_weight.shape[3] // HEAD
    share_queries = members // heads
    ff = in_weight.shape[2] // members
    row = lax.axis_index("seq") % rows

    pack = pack_weights(n, rows, qkv_weight, out_weight, in_weight, down_weight)
    norm_low = norm_params.astype(bf16).astype(f32).reshape(LAYERS * 3, -1)
    small = jnp.concatenate(
        [
            pad_lanes(norm_low),
            pad_lanes(position_ids.astype(f32)),
            pad_lanes(segment_ids.astype(f32)),
        ]
    )
    small = jnp.pad(small, ((0, -small.shape[0] % 8), (0, 0)))
    wide = jnp.stack([activations, cotangent], axis=1)
    chunk, table, weights = spread(n, rows, wide, small, pack, 0)
    weights = weights.reshape(LAYERS, width, -1)
    inputs = chunk[:, 0].reshape(rows * span, width)
    out_grads = chunk[:, 1].reshape(rows * span, width)
    own_columns = norm_params.shape[-1]
    norms = table[:, : LAYERS * 3, :own_columns].transpose(1, 0, 2).reshape(LAYERS, 3, width)
    positions = lax.dynamic_index_in_dim(table, LAYERS * 3 + row, 1, False)[:, :span].reshape(length)
    segments = lax.dynamic_index_in_dim(table, LAYERS * 3 + rows + row, 1, False)[:, :span].reshape(length)
    cosine, sine = rotary_tables(positions)
    places = (cosine, sine, segments[:, None], segments[None, :])

    def halves(values):
        return values.astype(bf16).reshape(2, half, width)

    def whole(values):
        return values.reshape(length, width)

    def parts(values):
        return values.reshape(members, 2, half, width)

    xhat_0, inverse_0 = layer_norm(inputs)
    normed = xhat_0 * norms[0, 0] + norms[0, 1]
    got = gather(n, rows, [halves(normed), halves(out_grads)], 1)
    normed_0, grads_1 = whole(got[0]), whole(got[1])
    part, *kept_0 = forward(rows, share_queries, ff, normed_0, weights[0], *places)
    branch = reduce(n, rows, [parts(part)], 2)[0].reshape(inputs.shape)
    middle = inputs + branch + norms[0, 2]
    xhat_1, inverse_1 = layer_norm(middle)
    normed = xhat_1 * norms[1, 0] + norms[1, 1]
    normed_1 = whole(gather(n, rows, [halves(normed)], 3)[0])
    part, *kept_1 = forward(rows, share_queries, ff, normed_1, weights[1], *places)
    back_part, weight_grads_1 = backward(rows, share_queries, ff, grads_1, normed_1, weights[1], *places, kept_1)
    sums = reduce(n, rows, [parts(part), parts(back_part)], 4).reshape((2,) + inputs.shape)
    result = middle + sums[0] + norms[1, 2]
    normed_grads_1 = sums[1]
    grads_mid = norm_back(out_grads, normed_grads_1, xhat_1, inverse_1, norms[1, 0])
    grads_0 = whole(gather(n, rows, [halves(grads_mid)], 5)[0])
    back_part, weight_grads_0 = backward(rows, share_queries, ff, grads_0, normed_0, weights[0], *places, kept_0)
    normed_grads_0 = reduce(n, rows, [parts(back_part)], 6)[0].reshape(inputs.shape)
    input_grad = norm_back(grads_mid, normed_grads_0, xhat_0, inverse_0, norms[0, 0])

    small_grads = jnp.stack(
        [
            jnp.sum(normed_grads_0 * xhat_0, axis=0),
            jnp.sum(normed_grads_0, axis=0),
            jnp.sum(grads_mid, axis=0),
            jnp.sum(normed_grads_1 * xhat_1, axis=0),
            jnp.sum(normed_grads_1, axis=0),
            jnp.sum(out_grads, axis=0),
        ]
    )
    small_grads = pad_lanes(small_grads.reshape(LAYERS * 3, n, own_columns).transpose(1, 0, 2))
    small_grads = jnp.pad(small_grads, ((0, 0), (0, 8 - LAYERS * 3), (0, 0)))
    wide_out = jnp.stack([result.reshape(rows, span, width), input_grad.reshape(rows, span, width)], axis=1)
    height = width // n
    grads, wide_back, table_back = collect(
        n,
        rows,
        weight_grads_0.reshape(n, height, -1),
        weight_grads_1.reshape(n, height, -1),
        wide_out,
        small_grads,
        7,
    )
    norm_grads = jnp.sum(table_back, axis=0)[: LAYERS * 3, :own_columns].reshape(norm_params.shape)
    qkv_grads, out_weight_grads, in_grads, down_grads = unpack_gradients(grads, heads, ff)
    matrix_squares = sum(
        (jnp.sum(block * block) for block in (qkv_grads, out_weight_grads, in_grads, down_grads))
    )
    squares = matrix_squares + jnp.sum(norm_grads * norm_grads) / 2
    everyone = share(n, jnp.full((8, 128), squares, f32), 8)
    grad_norm = jnp.sqrt(jnp.sum(everyone[:, 0, 0]))
    total_parameters = LAYERS * width * (4 * 2 * heads * HEAD + 2 * 2 * members * ff + 3)
    factor_clip = jnp.minimum(1.0, clip_share * math.sqrt(total_parameters) / (grad_norm + 1e-06))
    qkv_new, qkv_first_new, qkv_second_new = adam_update(
        qkv_weight, qkv_first, qkv_second, qkv_grads, factor_clip, rate_matrix, decay_matrix
    )
    out_new, out_first_new, out_second_new = adam_update(
        out_weight, out_first, out_second, out_weight_grads, factor_clip, rate_output, decay_matrix
    )
    in_new, in_first_new, in_second_new = adam_update(
        in_weight, in_first, in_second, in_grads, factor_clip, rate_matrix, decay_matrix
    )
    down_new, down_first_new, down_second_new = adam_update(
        down_weight, down_first, down_second, down_grads, factor_clip, rate_matrix, decay_matrix
    )
    norm_new, norm_first_new, norm_second_new = adam_update(
        norm_params, norm_first, norm_second, norm_grads, factor_clip, rate_vector, 0.0
    )
    bias_clipped = norm_grads[:, 2] * factor_clip
    return (
        wide_back[:, 0],
        wide_back[:, 1],
        grad_norm,
        qkv_new,
        out_new,
        in_new,
        down_new,
        norm_new,
        qkv_first_new,
        out_first_new,
        in_first_new,
        down_first_new,
        norm_first_new,
        qkv_second_new,
        out_second_new,
        in_second_new,
        down_second_new,
        norm_second_new,
        bias_clipped,
    )


def flip(index, bits):
    bit = 1
    while bit <= bits:
        if bits & bit:
            index = index + bit * (1 - 2 * lax.rem(index // bit, 2))
        bit *= 2
    return index


class Net:
    def __init__(self, n, rows, half, pieces, send_sems):
        self.p = Place(n, rows)
        self.half, self.pieces = half, pieces
        self.send_sems, self.used = send_sems, 0
        self.sibling = self.p.sibling()

    def send_sem(self):
        self.used += 1
        return self.send_sems.at[self.used - 1]

    def everybody(self):
        p = self.p
        return [{"seq": lax.rem(p.seq + i, p.n), "tp": p.core} for i in range(1, p.n)]

    def everyone(self):
        p = self.p
        return self.everybody() + [
            {"seq": lax.rem(p.seq + i, p.n), "tp": 1 - p.core} for i in range(p.n)
        ]

    def partner(self):
        return self.p.device(self.p.member, row=1 - self.p.row)

    def a_of(self, k):
        return flip(self.p.a, k)

    def b_of(self, j):
        return flip(self.p.b, j)

    def tokens(self, member, core, piece):
        size = self.half // self.pieces
        start = (member * 2 + core) * self.half + piece * size
        return pl.ds(pl.multiple_of(start, size), size)

    def lines(self, slot, piece):
        size = self.half // self.pieces
        return pl.ds(pl.multiple_of(slot * self.half + piece * size, size), size)

    def own(self):
        start = (self.p.member * 2 + self.p.core) * self.half
        return pl.ds(pl.multiple_of(start, self.half), self.half)

    def tile_rows(self, a):
        size = self.p.nb * 2 * self.half
        return pl.ds(pl.multiple_of(a * size, size), size)

    def width_rows(self, k, width):
        size = width // self.p.na
        return pl.ds(pl.multiple_of(self.a_of(k) * size, size), size)

    def tile(self, k):
        return self.tile_rows(self.a_of(k))

    def far_first(self):
        a, na = self.p.a, self.p.na
        if na != 4:
            return [self.a_of(k) for k in range(na - 1, -1, -1)]
        upper = a // 2
        low = a + upper * (3 - 2 * a)
        order = [3, 2, 1 - low, low]
        return [v + upper * (3 - 2 * v) for v in order]

    def sides(self, distance):
        a, na = self.p.a, self.p.na
        return [
            (a >= distance, a - distance, a < na - 1, a + 1),
            (a + distance < na, a + distance, a > 0, a - 1),
        ]


class Sends:
    def __init__(self, net, lone=0):
        self.sibling = net.sibling
        self.shared = net.send_sem()
        self.lone = [net.send_sem() for _ in range(lone)]
        self.made, self.conditional = 0, []

    def copy(self, src, dst, sem, device, send_sem):
        return pltpu.make_async_remote_copy(
            src_ref=src, dst_ref=dst, send_sem=send_sem, recv_sem=sem, device_id=device, device_id_type=MESH
        )

    def send(self, src, dst, sem, device):
        self.copy(src, dst, sem, device, self.shared).start()
        self.made += 1

    def send_if(self, when, src, dst, sem, device):
        number = len(self.conditional)
        self.conditional.append((when, src, dst, sem, device))
        pl.when(when)(lambda: self.copy(src, dst, sem, device, self.lone[number]).start())

    def finish(self, whole):
        self.copy(whole, whole, self.shared, self.sibling, self.shared).wait_send()
        for number, (when, *copy) in enumerate(self.conditional):
            pl.when(when)(lambda number=number, copy=copy: self.copy(*copy, self.lone[number]).wait_send())
        self.made, self.conditional = 0, []


def wait_for(net, dst, sem):
    pltpu.make_async_remote_copy(
        src_ref=dst,
        dst_ref=dst,
        send_sem=net.send_sems.at[0],
        recv_sem=sem,
        device_id=net.sibling,
        device_id_type=MESH,
    ).wait_recv()


class Gather:
    def __init__(self, net, sems):
        self.net = net
        self.a_sems, self.b_sems, self.core_sems = sems
        self.sends = Sends(net, lone=2 * net.pieces * net.p.na)

    def slot(self, a, b, core, q):
        return self.out.at[self.net.tokens(a * self.net.p.nb + b, core, q), :]

    def to_line(self, a, q, to, when):
        p = self.net.p
        here = self.slot(a, p.b, p.core, q)
        self.sends.send_if(when, here, here, self.a_sems.at[a, q], p.at(to, p.b))

    def to_rest(self, a, q):
        net, p = self.net, self.net.p
        here = self.slot(a, p.b, p.core, q)
        for j in range(1, p.nb):
            self.sends.send(here, here, self.b_sems.at[a * p.nb + p.b, q], p.at(p.a, net.b_of(j)))
        self.sends.send(here, here, self.core_sems.at[a, q], net.sibling)

    def start(self, out):
        p = self.net.p
        self.out = out
        for q in range(self.net.pieces):
            self.to_line(p.a, q, p.a + 1, p.a < p.na - 1)
            self.to_line(p.a, q, p.a - 1, p.a > 0)
            self.to_rest(p.a, q)

    def hop(self, distance):
        net, p = self.net, self.net.p
        for q in range(net.pieces):
            for there, a, more, beyond in net.sides(distance):

                @pl.when(there)
                def _():
                    wait_for(net, self.slot(a, p.b, p.core, q), self.a_sems.at[a, q])

                self.to_line(a, q, beyond, jnp.logical_and(there, more))
                pl.when(there)(lambda: self.to_rest(a, q))

    def side(self, distance):
        net, p = self.net, self.net.p
        for j in range(1, p.nb):
            b = net.b_of(j)
            for q in range(net.pieces):
                for there, a, more, beyond in net.sides(distance)[: 2 if distance else 1]:

                    @pl.when(there)
                    def _():
                        here = self.slot(a, b, p.core, q)
                        wait_for(net, here, self.b_sems.at[a * p.nb + b, q])
                        self.sends.send(here, here, self.core_sems.at[a, q], net.sibling)

    def settle(self, distance):
        net, p = self.net, self.net.p
        size = p.nb * net.half // net.pieces
        for q in range(net.pieces):
            for there, a, more, beyond in net.sides(distance)[: 2 if distance else 1]:

                @pl.when(there)
                def _():
                    wait_for(net, self.out.at[pl.ds(0, size), :], self.core_sems.at[a, q])

    def steps(self):
        na = self.net.p.na
        if na > 1:
            self.hop(1)
        yield None
        self.side(0)
        yield None
        for k in range(na):
            if k + 2 < na:
                self.hop(k + 2)
            if k + 1 < na:
                self.side(k + 1)
            self.settle(k)
            yield k

    def finish(self):
        p = self.net.p
        self.sends.finish(self.out.at[pl.ds(0, (p.na * (p.nb - 1) + p.members) * self.net.half), :])


class Reduce:
    def __init__(self, net, x, total, bufs, sems):
        self.net, self.x, self.total = net, x, total
        self.core_buf, self.b_out, self.b_buf, self.a_out, self.a_buf, self.sum_buf = bufs
        self.core_sems, self.b_sems, self.a_sems = sems
        self.sends = Sends(net, lone=2 * net.pieces * (net.p.na - 1))

    def offer(self, a):
        net, p = self.net, self.net.p
        for j in list(range(1, p.nb)) + [0]:
            m = a * p.nb + net.b_of(j)
            for q in range(net.pieces):
                self.sends.send(
                    self.x.at[net.tokens(m, 1 - p.core, q), :],
                    self.core_buf.at[net.lines(m, q), :],
                    self.core_sems.at[m, q],
                    net.sibling,
                )

    def pair_sum(self, m, q):
        net = self.net
        lines = net.lines(m, q)
        wait_for(net, self.core_buf.at[lines, :], self.core_sems.at[m, q])
        return self.x[net.tokens(m, net.p.core, q), :].astype(f32) + self.core_buf[lines, :].astype(f32)

    def targets(self, distance):
        return self.net.sides(distance)[: 2 if distance else 1]

    def relay(self, distance):
        net, p = self.net, self.net.p
        for there, a, unused_more, unused_beyond in self.targets(distance):
            for j in range(1, p.nb):
                b = net.b_of(j)
                for q in range(net.pieces):

                    @pl.when(there)
                    def _():
                        m, landing = a * p.nb + b, a * p.nb + p.b
                        self.b_out[net.lines(m, q), :] = self.pair_sum(m, q).astype(bf16)
                        self.sends.send(
                            self.b_out.at[net.lines(m, q), :],
                            self.b_buf.at[net.lines(landing, q), :],
                            self.b_sems.at[landing, q],
                            p.at(p.a, b),
                        )

    def row_sum(self, a, q):
        net, p = self.net, self.net.p
        total = self.pair_sum(a * p.nb + p.b, q)
        for j in range(1, p.nb):
            m = a * p.nb + net.b_of(j)
            wait_for(net, self.b_buf.at[net.lines(m, q), :], self.b_sems.at[m, q])
            total = total + self.b_buf[net.lines(m, q), :].astype(f32)
        return total

    def passing(self, up, a, q):
        net, p = self.net, self.net.p
        slot = a if up else p.na + a
        wait_for(net, self.a_buf.at[net.lines(slot, q), :], self.a_sems.at[slot, q])
        return self.a_buf[net.lines(slot, q), :].astype(f32)

    def pass_on(self, distance):
        net, p = self.net, self.net.p
        size = net.half // net.pieces
        for side, (there, a, unused_more, unused_beyond) in enumerate(net.sides(distance)):
            up = side == 1
            behind = p.a > 0 if up else p.a < p.na - 1
            slot = a if up else p.na + a
            for q in range(net.pieces):
                part = slice(q * size, (q + 1) * size)

                @pl.when(there)
                def _():
                    self.sum_buf[part, :] = self.row_sum(a, q)

                @pl.when(jnp.logical_and(there, behind))
                def _():
                    self.sum_buf[part, :] += self.passing(up, a, q)

                @pl.when(there)
                def _():
                    self.a_out[net.lines(slot, q), :] = self.sum_buf[part, :].astype(bf16)

                self.sends.send_if(
                    there,
                    self.a_out.at[net.lines(slot, q), :],
                    self.a_buf.at[net.lines(slot, q), :],
                    self.a_sems.at[slot, q],
                    p.at(p.a + 1 if up else p.a - 1, p.b),
                )

    def arrive(self):
        net, p = self.net, self.net.p
        size = net.half // net.pieces
        for q in range(net.pieces):
            part = slice(q * size, (q + 1) * size)
            self.total[part, :] = self.row_sum(p.a, q)
        for q in range(net.pieces):
            part = slice(q * size, (q + 1) * size)

            @pl.when(p.a > 0)
            def _():
                self.total[part, :] += self.passing(True, p.a, q)

            @pl.when(p.a < p.na - 1)
            def _():
                self.total[part, :] += self.passing(False, p.a, q)

    def steps(self):
        na = self.net.p.na
        for distance in range(na - 1, -1, -1):
            self.relay(distance)
            yield
        for distance in range(na - 1, 0, -1):
            self.pass_on(distance)
            yield
        self.arrive()
        yield

    def finish(self):
        p = self.net.p
        self.sends.finish(self.x.at[pl.ds(0, (p.members + p.na * (p.nb - 1)) * self.net.half), :])


class Spread:
    def __init__(self, net, pack, w, columns, block_sems, cross_sems):
        self.net, self.pack, self.w, self.columns = net, pack, w, columns
        self.block_sems, self.cross_sems = block_sems, cross_sems
        self.height = pack.shape[1]
        self.sends = Sends(net)
        self.sent, self.received = 1, 1

    def here(self, seq):
        return self.w.at[pl.ds(pl.multiple_of(seq * self.height, self.height), self.height), self.columns]

    def start(self):
        net, p = self.net, self.net.p
        block = self.pack.at[p.member, :, self.columns]
        self.sends.send(block, self.here(p.seq), self.cross_sems.at[p.member], net.partner())
        self.here(p.seq)[...] = block[...]

    def send(self, count=None):
        p = self.net.p
        last = p.members if count is None else min(p.members, self.sent + count)
        for k in range(self.sent, last):
            member = flip(p.member, k)
            block = self.pack.at[member, :, self.columns]
            self.sends.send(block, self.here(p.seq), self.block_sems.at[p.member], p.device(member))
        self.sent = last

    def receive(self, count=None):
        net, p = self.net, self.net.p
        last = p.members if count is None else min(p.members, self.received + count)
        for k in range(self.received, last):
            member = flip(p.member, k)
            here = self.here(member * p.rows + p.row)
            wait_for(net, here, self.block_sems.at[member])
            self.sends.send(here, here, self.cross_sems.at[member], net.partner())
        self.received = last

    def settle(self):
        net, p = self.net, self.net.p
        for k in range(p.members):
            member = flip(p.member, k)
            wait_for(net, self.here(member * p.rows + 1 - p.row), self.cross_sems.at[member])

    def finish(self):
        size = (2 * self.net.p.members - 1) * self.height
        self.sends.finish(self.w.at[pl.ds(0, size), self.columns])


class Collect:
    def __init__(self, net, dw, grad, columns, cross_buf, block_out, cross_sems, block_sems):
        self.net, self.dw, self.grad, self.columns = net, dw, grad, columns
        self.cross_buf, self.block_out = cross_buf, block_out
        self.cross_sems, self.block_sems = cross_sems, block_sems
        self.height = grad.shape[1]
        self.sends = Sends(net)
        self.pending = self.order()

    def at(self, seq):
        return self.dw.at[pl.ds(pl.multiple_of(seq * self.height, self.height), self.height), self.columns]

    def order(self):
        return list(range(self.net.p.members - 1, -1, -1))

    def offer(self, k):
        net, p = self.net, self.net.p
        for j in range(p.nb - 1, -1, -1):
            member = net.a_of(k) * p.nb + net.b_of(j)
            self.sends.send(
                self.at(member * p.rows + 1 - p.row),
                self.cross_buf.at[member, :, self.columns],
                self.cross_sems.at[member],
                net.partner(),
            )

    def relay(self, count=None):
        net, p = self.net, self.net.p
        for k in self.pending[:count]:
            member = flip(p.member, k)
            landed = self.cross_buf.at[member, :, self.columns]
            wait_for(net, landed, self.cross_sems.at[member])
            mine = self.at(member * p.rows + p.row)[...]
            total = (mine.astype(f32) + landed[...].astype(f32)).astype(bf16)
            if k:
                block = self.block_out.at[member, :, self.columns]
                block[...] = total
                target = self.grad.at[p.member, :, self.columns]
                self.sends.send(block, target, self.block_sems.at[p.member], p.device(member))
            else:
                self.grad[member, :, self.columns] = total
        self.pending = self.pending[count:] if count is not None else []

    def settle(self):
        squares = jnp.zeros((1, 1), f32)
        for k in [0] + self.order()[:-1]:
            member = flip(self.net.p.member, k)
            if k:
                wait_for(self.net, self.grad.at[member, :, self.columns], self.block_sems.at[member])
            block = self.grad[member, :, self.columns].astype(f32)
            squares = squares + jnp.sum(block * block, axis=(0, 1), keepdims=True)
        return squares

    def finish(self):
        size = (2 * self.net.p.members - 1) * self.height
        self.sends.finish(self.dw.at[pl.ds(0, size), self.columns])


def advance(steps, count=1):
    for _ in range(count):
        next(steps, None)


def drain(steps):
    for _ in steps:
        pass


class Layer:
    def __init__(self, r, layer):
        self.r, self.layer = r, layer
        self.length, self.width = getattr(r, "h%d" % layer).shape
        self.f = 4 * HEAD
        self.ff = (getattr(r, "w%d" % layer).shape[1] - self.f) // 2

    def __getattr__(self, name):
        return getattr(self.r, name + str(self.layer))

    def project(self, rows):
        r, f = self.r, self.f
        h = self.h[rows, :]
        mixed = dot(h, self.w[:, :f])
        qk = mixed[:, : 2 * HEAD]
        qk = qk * r.cos[rows, :] + swap_lanes(qk) * r.sin[rows, :]
        self.q[rows, :] = (qk[:, :HEAD].astype(bf16).astype(f32) * HEAD**-0.5).astype(bf16)
        self.k[rows, :] = qk[:, HEAD:].astype(bf16)
        self.v[rows, :] = mixed[:, 2 * HEAD : 3 * HEAD].astype(bf16)

    def feed(self, rows):
        z = dot(self.h[rows, :], self.w[:, self.f : self.f + self.ff])
        self.z[rows, :] = z
        self.a[rows, :] = gelu(z).astype(bf16)

    def attend(self, i):
        r = self.r
        start, keys = i * TILE, (i + 1) * TILE
        rows = pl.ds(start, TILE)
        scores = dot_nt(self.q[rows, :], self.k[:keys, :])
        seen = visible(start, keys, r.segc[rows, :], r.segr[:, :keys])
        scores = jnp.where(seen, scores, low_score)
        peak = jnp.max(scores, axis=1, keepdims=True)
        weights = jnp.exp(scores - peak)
        total = jnp.sum(weights, axis=1, keepdims=True)
        self.lse[rows, :] = peak + jnp.log(total)
        shares = (weights * (1.0 / total)).astype(bf16)
        self.o[rows, :] = dot(shares, self.v[:keys, :]).astype(bf16)

    def branch(self, rows, part):
        f, ff = self.f, self.ff
        out = dot_nt(self.o[rows, :], self.w[:, 3 * HEAD : f])
        out = out + dot_nt(self.a[rows, :], self.w[:, f + ff : f + 2 * ff])
        part[rows, :] = out.astype(bf16)

    def feed_back(self, rows):
        r, f, ff = self.r, self.f, self.ff
        g = self.g[rows, :]
        da = dot(g, self.w[:, f + ff : f + 2 * ff])
        r.dz[rows, :] = (da * gelu_slope(self.z[rows, :])).astype(bf16)
        r.do[rows, :] = dot(g, self.w[:, :f])[:, 3 * HEAD :].astype(bf16)

    def attend_back(self, i):
        r = self.r
        start, keys = i * TILE, (i + 1) * TILE
        rows = pl.ds(start, TILE)
        q, head_grad = self.q[rows, :], r.do[rows, :]
        scores = dot_nt(q, self.k[:keys, :])
        seen = visible(start, keys, r.segc[rows, :], r.segr[:, :keys])
        shares = jnp.where(seen, jnp.exp(scores - self.lse[rows, :]), 0.0)
        share_grads = dot_nt(head_grad, self.v[:keys, :])
        delta = jnp.sum(shares * share_grads, axis=1, keepdims=True)
        score_grads = (shares * (share_grads - delta)).astype(bf16)
        r.dq[rows, :] = dot(score_grads, self.k[:keys, :]) * HEAD**-0.5
        dk = dot_tn(score_grads, q)
        dv = dot_tn(shares.astype(bf16), head_grad)
        if i + 1 == self.length // TILE:
            r.dk[:keys, :] = dk
            r.dv[:keys, :] = dv
        else:
            r.dk[:keys, :] += dk
            r.dv[:keys, :] += dv

    def inward(self, rows, part):
        r, f, ff = self.r, self.f, self.ff
        qk = jnp.concatenate([r.dq[rows, :], r.dk[rows, :]], axis=1)
        qk = qk * r.cos[rows, :] + swap_lanes(qk * r.sin[rows, :])
        rest = jnp.concatenate([r.dv[rows, :], jnp.zeros((TILE, HEAD), f32)], axis=1)
        mix = jnp.concatenate([qk, rest], axis=1).astype(bf16)
        r.mix[rows, :] = mix
        out = dot_nt(mix, self.w[:, :f]) + dot_nt(r.dz[rows, :], self.w[:, f : f + ff])
        part[rows, :] = out.astype(bf16)

    def head_grads(self, rows):
        r, f = self.r, self.f
        mixed = dot_tn(self.h[:, rows], r.mix[...])
        out = dot_tn(self.g[:, rows], self.o[...])
        self.dw[rows, :f] = jnp.concatenate([mixed[:, : 3 * HEAD], out], axis=1).astype(bf16)

    def feed_grads(self, rows):
        r, f, ff = self.r, self.f, self.ff
        self.dw[rows, f : f + ff] = dot_tn(self.h[:, rows], r.dz[...]).astype(bf16)
        self.dw[rows, f + ff : f + 2 * ff] = dot_tn(self.g[:, rows], self.a[...]).astype(bf16)


def norm_row(r, layer, kind):
    return r.norms[layer * 3 + kind : layer * 3 + kind + 1, :]


def column_sums(values):
    return jnp.sum(values, axis=0, keepdims=True)


def cross_rows(net, r):
    p = net.p
    same = p.core == p.row

    def crossing(i):
        source, landing = ((r.act, r.x0), (r.cot, r.gr1))[i]
        return pltpu.make_async_remote_copy(
            src_ref=source.at[1 - p.row],
            dst_ref=landing,
            send_sem=r.x_sems.at[i],
            recv_sem=r.x_sems.at[2 + i],
            device_id=net.partner(),
            device_id_type=MESH,
        )

    def start(i):
        @pl.when(same)
        def _():
            crossing(i).start()
            if i:
                r.gr1[...] = r.cot[p.row]
            else:
                r.x0[...] = r.act[p.row]

    def arrive(i):
        @pl.when(jnp.logical_not(same))
        def _():
            crossing(i).wait_recv()

    def finish():
        @pl.when(same)
        def _():
            crossing(0).wait_send()
            crossing(1).wait_send()

    return (start, arrive, finish)


def give_back(net, r, i, source, target):
    p = net.p
    same = p.core == p.row

    def copy(j, device, row):
        return pltpu.make_async_remote_copy(
            src_ref=source,
            dst_ref=target.at[row],
            send_sem=r.back_sems.at[i, j],
            recv_sem=r.back_sems.at[i, 2 + row],
            device_id=device,
            device_id_type=MESH,
        )

    def far(j):
        return copy(j, p.device(p.member, row=1 - p.row, core=lax.rem(p.core + j, 2)), p.row)

    @pl.when(same)
    def _():
        copy(0, net.sibling, p.row).start()
        target[p.row] = source[...]

    @pl.when(jnp.logical_not(same))
    def _():
        far(0).start()
        far(1).start()

    def finish():
        @pl.when(same)
        def _():
            copy(0, net.sibling, p.row).wait_send()

        @pl.when(jnp.logical_not(same))
        def _():
            far(0).wait_send()
            far(1).wait_send()
            copy(0, net.sibling, p.row).wait_recv()

        copy(0, net.sibling, 1 - p.row).wait_recv()

    return finish


def share_all(net, sem, out, source):
    p = net.p
    here = p.seq * 2 + p.core
    others = [
        (lax.rem(p.seq + i, p.n), lax.rem(p.core + j, 2)) for i in range(p.n) for j in range(2) if i or j
    ]
    sends = Sends(net)
    for seq, core in others:
        sends.send(source(seq), out.at[here], sem, {"seq": seq, "tp": core})
    whole = out.at[pl.ds(0, len(others))]
    return (lambda: wait_for(net, whole, sem), lambda: sends.finish(whole))


def position_tables(net, r):
    p = net.p
    span = r.act.shape[1]
    lines = []
    for kind in range(2):
        row = LAYERS * 3 + kind * p.rows + p.row
        pieces = [r.table[s, pl.ds(row, 1), :span] for s in range(p.n)]
        lines.append(jnp.concatenate(pieces, axis=1))
    positions, segments = lines
    r.segr[...] = segments
    pair = lax.broadcasted_iota(jnp.int32, (ROTARY, positions.shape[1]), 0) // 2
    angles = jnp.exp(pair.astype(f32) * (-2.0 * math.log(10000.0) / ROTARY)) * positions
    sign = jnp.where(lax.broadcasted_iota(jnp.int32, angles.shape, 0) % 2 == 0, -1.0, 1.0)
    ones = jnp.ones((HEAD - ROTARY, angles.shape[1]), f32)
    cosine, sine = jnp.cos(angles), jnp.sin(angles) * sign
    cosine = jnp.concatenate([cosine, ones, cosine, ones], axis=0)
    sine = jnp.concatenate([sine, ones * 0.0, sine, ones * 0.0], axis=0)
    segments = jnp.broadcast_to(segments, (128, segments.shape[1]))
    for t in range(angles.shape[1] // 128):
        block = slice(t * 128, (t + 1) * 128)
        r.cos[block, :] = cosine[:, block].T
        r.sin[block, :] = sine[:, block].T
        r.segc[block, :] = segments[:, block].T[:, :1]


def pack_layer(r, layer):
    members, ff = r.pack.shape[1], (r.pack.shape[3] - 4 * HEAD) // 2
    f = 4 * HEAD
    for pair in range(members // 2):
        lanes = slice(pair * 2 * HEAD, (pair + 1) * 2 * HEAD)
        kinds = [r.qkv[layer, kind, :, lanes].astype(bf16) for kind in range(3)]
        kinds.append(r.out[layer, :, lanes].astype(bf16))
        for i in range(2):
            own = slice(i * HEAD, (i + 1) * HEAD)
            r.pack[layer, 2 * pair + i, :, :f] = jnp.concatenate([kind[:, own] for kind in kinds], axis=1)
    for member in range(members):
        lanes = slice(member * ff, (member + 1) * ff)
        r.pack[layer, member, :, f : f + ff] = getattr(r, "in")[layer, :, lanes].astype(bf16)
        r.pack[layer, member, :, f + ff :] = r.down[layer, :, lanes].astype(bf16)


def pack_small(r):
    rows, span = r.pos.shape
    r.small[...] = jnp.zeros_like(r.small)
    columns = r.norm.shape[2]
    for layer in range(LAYERS):
        r.small[layer * 3 : layer * 3 + 3, :columns] = r.norm[:, layer, :].astype(bf16).astype(f32)
    r.small[LAYERS * 3 : LAYERS * 3 + rows, :span] = r.pos[...].astype(f32)
    r.small[LAYERS * 3 + rows : LAYERS * 3 + 2 * rows, :span] = r.seg[...].astype(f32)


def whole_part(net, r):
    p = net.p
    n, width = p.n, r.act.shape[2]
    finishes = []

    pack_small(r)
    greet(net.everyone())
    gathers = [Gather(net, r.gather_a), Gather(net, r.gather_b)]
    reduces = [
        Reduce(net, r.part_a, r.total_a, r.bufs_a, r.reduce_a),
        Reduce(net, r.part_b, r.total_b, r.bufs_b, r.reduce_b),
    ]
    table_sends = Sends(net)
    finishes.append(lambda: table_sends.finish(r.table.at[pl.ds(0, n - 1)]))
    for i in range(1, n):
        device = {"seq": lax.rem(p.seq + i, n), "tp": p.core}
        table_sends.send(r.small, r.table.at[p.seq], r.table_sem, device)
    r.table[p.seq] = r.small[...]
    cross_start, cross_arrive, cross_finish = cross_rows(net, r)
    finishes.append(cross_finish)
    cross_start(0)
    f = 4 * HEAD
    ff = (r.w0.shape[1] - f) // 2
    early, late = slice(0, f + ff), slice(f + ff, f + 2 * ff)
    heads, feeds = slice(0, f), slice(f, f + 2 * ff)
    spreads = [
        [
            Spread(net, r.pack.at[k], (r.w0, r.w1)[k], columns, r.block_sems.at[k, i], r.cross_sems.at[k, i])
            for i, columns in enumerate((early, late))
        ]
        for k in range(LAYERS)
    ]
    collects = [
        [
            Collect(
                net,
                (r.dw0, r.dw1)[k],
                r.grads.at[k],
                columns,
                r.cross_buf.at[k],
                r.block_out.at[k],
                r.collect_sems.at[k, i],
                r.block_sems.at[k, i],
            )
            for i, columns in enumerate((feeds, heads))
        ]
        for k in range(LAYERS)
    ]
    finishes.extend(collect.finish for pair in collects for collect in pair)
    pack_layer(r, 0)
    first, second = spreads[0]
    first.start()
    first.send(3)
    wait_for(net, r.table.at[pl.ds(0, n - 1)], r.table_sem)
    own_columns = width // n
    many = 128 // own_columns
    for s in range(0, n, many):
        r.norms[:, s * own_columns : (s + many) * own_columns] = jnp.concatenate(
            [r.table[s + i, 0:8, :own_columns] for i in range(many)], axis=1
        )
    cross_arrive(0)
    xhat, inverse = layer_norm(r.x0[...])
    normed = xhat * norm_row(r, 0, 0) + norm_row(r, 0, 1)
    r.h0[net.own(), :] = normed.astype(bf16)
    gather = gathers[0]
    gather.start(r.h0)
    position_tables(net, r)

    layer = Layer(r, 0)
    tiles = range(layer.length // TILE)
    gather_steps = gather.steps()
    advance(gather_steps)
    first.send()
    first.receive(3)
    advance(gather_steps)
    pack_layer(r, 1)
    advance(gather_steps)
    first.receive(2)
    advance(gather_steps)
    first.receive()
    drain(gather_steps)
    second.start()
    second.send()
    cross_start(1)
    first.settle()
    for k in tiles:
        layer.project(net.tile(k))
        layer.feed(net.tile(k))
    second.receive()
    first, third = spreads[1]
    first.start()
    first.send()
    for i in tiles:
        layer.attend(i)
    second.settle()
    reduce = reduces[0]
    for a in net.far_first():
        layer.branch(net.tile_rows(a), r.part_a)
        reduce.offer(a)
    steps = reduce.steps()
    advance(steps, p.na + 1)
    first.receive(3)
    drain(steps)
    middle = r.x0[...] + (r.total_a[...] + norm_row(r, 0, 2))
    r.x1[...] = middle
    xhat, inverse = layer_norm(middle)
    normed = xhat * norm_row(r, 1, 0) + norm_row(r, 1, 1)
    r.h1[net.own(), :] = normed.astype(bf16)
    gathers[0].finish()
    gather = gathers[1]
    gather.start(r.h1)
    third.start()
    third.send()

    layer = Layer(r, 1)
    gather_steps = gather.steps()
    advance(gather_steps)
    first.receive()
    advance(gather_steps, 2)
    cross_arrive(1)
    r.g1[net.own(), :] = r.gr1[...].astype(bf16)
    advance(gather_steps)
    third.receive()
    grad_gather = gathers[0]
    grad_gather.start(r.g1)
    first.settle()
    for k in tiles:
        layer.project(net.tile(k))
        layer.feed(net.tile(k))
        advance(gather_steps)
    drain(gather_steps)
    grad_steps = grad_gather.steps()
    advance(grad_steps)
    for i in tiles:
        layer.attend(i)
        advance(grad_steps)
    third.settle()
    forward_reduce = reduces[1]
    forward_steps = forward_reduce.steps()
    for a in net.far_first():
        layer.branch(net.tile_rows(a), r.part_b)
        forward_reduce.offer(a)
    drain(grad_steps)
    advance(forward_steps, p.na)

    fed, headed = collects[1]
    for k in tiles:
        layer.feed_back(net.tile(k))
    for i in reversed(tiles):
        layer.attend_back(i)
    reduce = reduces[0]
    reduce.finish()
    for spread in spreads[0] + spreads[1]:
        spread.finish()
    steps = reduce.steps()
    for a in net.far_first():
        layer.inward(net.tile_rows(a), r.part_a)
        reduce.offer(a)
    advance(steps, p.na)
    for k in range(p.na - 1, -1, -1):
        layer.feed_grads(net.width_rows(k, layer.width))
        fed.offer(k)
    advance(forward_steps, p.na - 1)
    for k in range(p.na - 1, -1, -1):
        layer.head_grads(net.width_rows(k, layer.width))
        headed.offer(k)
        if k:
            advance(steps)
    drain(steps)
    xhat, inverse = layer_norm(r.x1[...])
    normed_grads = r.total_a[...]
    below = norm_back(r.gr1[...], normed_grads, xhat, inverse, norm_row(r, 1, 0))
    r.gr0[...] = below
    r.g0[net.own(), :] = below.astype(bf16)
    gather = gathers[1]
    gather.finish()
    gather.start(r.g0)
    r.sums1[...] = jnp.concatenate(
        [
            column_sums(normed_grads * xhat),
            column_sums(normed_grads),
            column_sums(r.gr1[...]),
            jnp.zeros((5, layer.width), f32),
        ]
    )
    drain(forward_steps)
    r.result[...] = r.x1[...] + (r.total_b[...] + norm_row(r, 1, 2))

    layer = Layer(r, 0)
    gather_steps = gather.steps()
    advance(gather_steps, 2)
    for k in tiles:
        advance(gather_steps)
        if k == 1:
            fed.relay()
        layer.feed_back(net.tile(k))
    drain(gather_steps)
    fed.relay()
    finishes.append(give_back(net, r, 0, r.result, r.results))
    fed_0, headed_0 = collects[0]
    for k in range(p.na - 1, -1, -1):
        layer.feed_grads(net.width_rows(k, layer.width))
        fed_0.offer(k)
    headed.relay(4)
    for i in reversed(tiles):
        layer.attend_back(i)
    headed.relay()
    reduce = forward_reduce
    reduce.finish()
    steps = reduce.steps()
    for a in net.far_first():
        layer.inward(net.tile_rows(a), r.part_b)
        reduce.offer(a)
    advance(steps, p.na)
    for k in range(p.na - 1, -1, -1):
        layer.head_grads(net.width_rows(k, layer.width))
        headed_0.offer(k)
        if k:
            advance(steps)
            fed_0.relay(2)
    drain(steps)
    fed_0.relay()
    normed_grads = r.total_b[...]
    xhat, inverse = layer_norm(r.x0[...])
    rows = [
        column_sums(normed_grads * xhat),
        column_sums(normed_grads),
        column_sums(r.gr0[...]),
        r.sums1[0:3, :],
        jnp.zeros((2, width), f32),
    ]
    rows = jnp.concatenate(rows)
    for s in range(n):
        r.small_out[s] = pad_lanes(rows[:, s * own_columns : (s + 1) * own_columns])
    here = p.seq * 2 + p.core
    small_arrive, small_finish = share_all(net, r.small_sem, r.small_in, lambda seq: r.small_out.at[seq])
    finishes.append(small_finish)
    r.small_in[here] = r.small_out[p.seq]
    headed_0.relay()
    r.in_grad[...] = norm_back(r.gr0[...], normed_grads, xhat, inverse, norm_row(r, 0, 0))
    finishes.append(give_back(net, r, 1, r.in_grad, r.in_grads))
    squares = fed.settle() + headed.settle()
    small_arrive()
    norm_grads = jnp.sum(r.small_in[...], axis=0)
    r.norm_grads[...] = norm_grads
    squares = squares + 0.5 * jnp.sum(norm_grads * norm_grads, axis=(0, 1), keepdims=True)
    squares = squares + (fed_0.settle() + headed_0.settle())
    r.squares[here] = jnp.broadcast_to(squares, (8, 128))
    square_arrive, square_finish = share_all(net, r.square_sem, r.squares, lambda seq: r.squares.at[here])
    finishes.append(square_finish)
    square_arrive()
    r.norm_out[...] = jnp.sqrt(jnp.sum(r.squares[...], axis=0))
    for part in gathers + reduces:
        part.finish()
    for finish in finishes:
        finish()


def fused_call(name, part, geometry, ins, outs, scratch, collective_id):
    flat, places = [], []
    for key, spec in scratch.items():
        group = spec if isinstance(spec, tuple) else (spec,)
        places.append((key, len(flat), len(group), isinstance(spec, tuple)))
        flat.extend(group)

    def kernel(*refs):
        r = types.SimpleNamespace(**dict(zip([*ins, *outs], refs)))
        rest = refs[len(ins) + len(outs) :]
        for key, start, count, grouped in places:
            setattr(r, key, rest[start : start + count] if grouped else rest[start])
        part(Net(*geometry, r.send_sems), r)

    results = pl.pallas_call(
        kernel,
        out_shape=tuple(outs.values()),
        in_specs=vmem_specs(len(ins)),
        out_specs=tuple(vmem_specs(len(outs))),
        scratch_shapes=flat,
        compiler_params=remote_params(collective_id),
        name=name,
    )(*ins.values())
    return types.SimpleNamespace(**dict(zip(outs, results)))


def by_kind(array):
    return jnp.swapaxes(array, array.ndim - 3, array.ndim - 2)


def optimizer_kernel(limit, grads_ref, norm_grads_ref, norm_ref, result_ref, in_grad_ref, *refs):
    weights, firsts, seconds = refs[:5], refs[5:10], refs[10:15]
    new_weights, new_firsts, new_seconds = refs[15:20], refs[20:25], refs[25:30]
    bias_ref, total_ref, result_out_ref, in_grad_out_ref = refs[30:]
    result_out_ref[...] = result_ref[...]
    in_grad_out_ref[...] = in_grad_ref[...]
    norm = norm_ref[0:1, 0:1]
    factor = jnp.minimum(1.0, limit / (norm + 1e-06))
    members, ff = grads_ref.shape[1], (grads_ref.shape[3] - 4 * HEAD) // 2
    f = 4 * HEAD

    def update(kind, where, gradient, rate, decay):
        found = adam_update(
            weights[kind][where], firsts[kind][where], seconds[kind][where], gradient, factor, rate, decay
        )
        for ref, value in zip((new_weights[kind], new_firsts[kind], new_seconds[kind]), found):
            ref[where] = value

    blocks = [grads_ref[0, member].astype(f32) for member in range(members)]
    for part in range(4):
        lanes = slice(part * HEAD, (part + 1) * HEAD)
        gradient = jnp.concatenate([block[:, lanes] for block in blocks], axis=1)
        if part < 3:
            update(0, (0, part), gradient, rate_matrix, decay_matrix)
        else:
            update(1, (0,), gradient, rate_output, decay_matrix)
    for member in range(members):
        lanes = slice(member * ff, (member + 1) * ff)
        update(2, (0, slice(None), lanes), blocks[member][:, f : f + ff], rate_matrix, decay_matrix)
        update(3, (0, slice(None), lanes), blocks[member][:, f + ff :], rate_matrix, decay_matrix)

    @pl.when((pl.program_id(0) == 0) & (pl.program_id(1) == 0))
    def _():
        columns = weights[4].shape[2]
        for layer in range(LAYERS):
            gradient = norm_grads_ref[layer * 3 : layer * 3 + 3, :columns]
            update(4, (slice(None), layer), gradient, rate_vector, 0.0)
            bias_ref[layer : layer + 1, :] = gradient[2:3, :] * factor
        total_ref[...] = norm


def optimizer(found, weights, firsts, seconds, parameters):
    layers, height = weights[1].shape[:2]
    rows = height
    grads = found.grads

    def spec(array):
        extent = array.shape
        if extent[0] == 3:
            return pl.BlockSpec(extent, lambda i, j: (0, 0, 0))
        if array.ndim == 4:
            return pl.BlockSpec((1, 3, rows, extent[3]), lambda i, j: (i, 0, j, 0))
        return pl.BlockSpec((1, rows * extent[1] // height, extent[2]), lambda i, j: (i, j, 0))

    def fixed(*extent):
        return pl.BlockSpec(extent, lambda i, j: (0,) * len(extent))

    arrays = [by_kind(array) if i % 5 in (0, 4) else array for i, array in enumerate(weights + firsts + seconds)]
    tokens = [found.results, found.in_grads]
    bias_shape = (layers, weights[4].shape[2])
    made = pl.pallas_call(
        functools.partial(optimizer_kernel, clip_share * math.sqrt(parameters)),
        grid=(layers, height // rows),
        in_specs=[
            pl.BlockSpec((1, grads.shape[1], rows, grads.shape[3]), lambda i, j: (i, 0, j, 0)),
            fixed(8, 128),
            fixed(8, 128),
        ]
        + [spec(array) for array in tokens + arrays],
        out_specs=tuple(
            [spec(array) for array in arrays]
            + [fixed(*bias_shape), fixed(1, 1)]
            + [spec(array) for array in tokens]
        ),
        out_shape=tuple(
            [jax.ShapeDtypeStruct(array.shape, array.dtype) for array in arrays]
            + [jax.ShapeDtypeStruct(bias_shape, f32), jax.ShapeDtypeStruct((1, 1), f32)]
            + [jax.ShapeDtypeStruct(array.shape, array.dtype) for array in tokens]
        ),
        compiler_params=pltpu.CompilerParams(vmem_limit_bytes=56 * megabyte),
        name="optimizer",
    )(grads, found.norm_grads, found.norm_out, *tokens, *arrays)
    count = len(arrays)
    updated = [by_kind(array) if i % 5 in (0, 4) else array for i, array in enumerate(made[:count])]
    bias, norm, result, in_grad = made[count:]
    return (result, in_grad, norm.reshape(()), *updated, bias)


def shards_together(
    n,
    activations,
    cotangent,
    segment_ids,
    position_ids,
    qkv_weight,
    out_weight,
    in_weight,
    down_weight,
    norm_params,
    qkv_first,
    out_first,
    in_first,
    down_first,
    norm_first,
    qkv_second,
    out_second,
    in_second,
    down_second,
    norm_second,
):
    rows, span, width = activations.shape
    members = n // rows
    na, nb = split_sizes(members)
    length = n * span
    half = rows * span // 2
    pieces = 2
    heads = qkv_weight.shape[3] // HEAD
    ff = in_weight.shape[2] // members
    height = width // n
    columns = 4 * HEAD + 2 * ff
    geometry = (n, rows, half, pieces)

    def shape(*extent, kind=f32):
        return jax.ShapeDtypeStruct(extent, kind)

    def scratch_like(shapes, suffix):
        return {key + suffix: VM(value.shape, value.dtype) for key, value in shapes.items()}

    gather_sems = (DMA((na, pieces)), DMA((members, pieces)), DMA((na, pieces)))
    reduce_sems = (DMA((members, pieces)), DMA((members, pieces)), DMA((2 * na, pieces)))
    reduce_bufs = tuple(
        VM((count * half, width), bf16) for count in (members, members, members, 2 * na, 2 * na)
    ) + (VM((half, width), f32),)
    kept = dict(
        q=shape(length, HEAD, kind=bf16),
        k=shape(length, HEAD, kind=bf16),
        v=shape(length, HEAD, kind=bf16),
        o=shape(length, HEAD, kind=bf16),
        lse=shape(length, 1),
        a=shape(length, ff, kind=bf16),
        z=shape(length, ff),
        w=shape(width, columns, kind=bf16),
        dw=shape(width, columns, kind=bf16),
        h=shape(length, width, kind=bf16),
        g=shape(length, width, kind=bf16),
        x=shape(half, width),
        gr=shape(half, width),
    )
    lines = LAYERS * 3 + 2 * rows
    three = fused_call(
        "whole_part",
        whole_part,
        geometry,
        {
            "act": activations,
            "cot": cotangent,
            "seg": segment_ids,
            "pos": position_ids,
            "qkv": by_kind(qkv_weight),
            "out": out_weight,
            "in": in_weight,
            "down": down_weight,
            "norm": by_kind(norm_params),
        },
        dict(
            results=shape(rows, span, width),
            in_grads=shape(rows, span, width),
            grads=shape(LAYERS, members, height, columns, kind=bf16),
            norm_grads=shape(8, 128),
            norm_out=shape(8, 128),
        ),
        dict(
            small=VM((-(-lines // 8) * 8, 128), f32),
            table=VM((n, -(-lines // 8) * 8, 128), f32),
            pack=VM((LAYERS, members, height, columns), bf16),
            norms=VM((8, width), f32),
            cos=VM((length, 128), f32),
            sin=VM((length, 128), f32),
            segc=VM((length, 1), f32),
            segr=VM((1, length), f32),
            **scratch_like(kept, "0"),
            **scratch_like(kept, "1"),
            dz=VM((length, ff), bf16),
            do=VM((length, HEAD), bf16),
            dq=VM((length, HEAD), f32),
            dk=VM((length, HEAD), f32),
            dv=VM((length, HEAD), f32),
            mix=VM((length, 4 * HEAD), bf16),
            part_a=VM((length, width), bf16),
            part_b=VM((length, width), bf16),
            total_a=VM((half, width), f32),
            total_b=VM((half, width), f32),
            bufs_a=reduce_bufs,
            bufs_b=reduce_bufs,
            result=VM((half, width), f32),
            in_grad=VM((half, width), f32),
            sums1=VM((8, width), f32),
            cross_buf=VM((LAYERS, members, height, columns), bf16),
            block_out=VM((LAYERS, members, height, columns), bf16),
            small_out=VM((n, 8, 128), f32),
            small_in=VM((2 * n, 8, 128), f32),
            squares=VM((2 * n, 8, 128), f32),
            reduce_a=reduce_sems,
            reduce_b=reduce_sems,
            gather_a=gather_sems,
            gather_b=gather_sems,
            x_sems=DMA((4,)),
            back_sems=DMA((2, 4)),
            table_sem=DMA,
            small_sem=DMA,
            square_sem=DMA,
            block_sems=DMA((LAYERS, 2, members)),
            cross_sems=DMA((LAYERS, 2, members)),
            collect_sems=DMA((LAYERS, 2, members)),
            send_sems=DMA((2 * (1 + 2 * pieces * na) + 2 * (1 + 2 * pieces * (na - 1)) + 11,)),
        ),
        0,
    )
    return optimizer(
        three,
        (qkv_weight, out_weight, in_weight, down_weight, norm_params),
        (qkv_first, out_first, in_first, down_first, norm_first),
        (qkv_second, out_second, in_second, down_second, norm_second),
        LAYERS * width * (4 * 2 * heads * HEAD + 2 * 2 * members * ff + 3),
    )


def shards(n, activations, *others):
    rows, span, width = activations.shape
    together = 12 * n * span * width * 2 <= 40 * megabyte and rows == 2 and n * span % TILE == 0
    return (shards_together if together else shards_apart)(n, activations, *others)


def solution(mesh):
    tokens = P(None, "seq", None)
    qkv = P(None, "seq", None, "tp")
    matrix = P(None, "seq", "tp")
    norm = P(None, None, "seq")
    kinds = (qkv, matrix, matrix, matrix, norm)
    return jax.shard_map(
        functools.partial(shards, mesh.shape["seq"]),
        mesh=mesh,
        in_specs=(tokens, tokens, P(None, "seq"), P(None, "seq")) + kinds * 3,
        out_specs=(tokens, tokens, P()) + kinds * 3 + (P(None, "seq"),),
        check_vma=False,
    )
```

```python
import functools
import math
import types

import jax
import jax.numpy as jnp
from jax import lax
from jax.experimental import pallas as pl
from jax.experimental.pallas import tpu as pltpu
from jax.sharding import PartitionSpec as P

HEAD = 64
ROTARY = 32
LAYERS = 2
STEP = 10
TILE = 256

norm_eps = 1e-05
beta_one = 0.9
beta_two = 0.999
adam_eps = 1e-08
rate_matrix = 0.05
rate_output = 0.15
rate_vector = 1.0
decay_matrix = 0.1
clip_share = 0.25
low_score = -1e30

MESH = pl.DeviceIdType.MESH
VM = pltpu.VMEM
DMA = pltpu.SemaphoreType.DMA
bf16 = jnp.bfloat16
f32 = jnp.float32
megabyte = 1 << 20


def split_sizes(members):
    nb = 1 << ((members.bit_length() - 1) // 2)
    return (members // nb, nb)


class Place:
    def __init__(self, n, rows):
        self.n, self.rows = n, rows
        self.members = n // rows
        self.na, self.nb = split_sizes(self.members)
        self.seq = lax.axis_index("seq")
        self.core = lax.axis_index("tp")
        self.row = lax.rem(self.seq, rows)
        self.member = self.seq // rows
        self.a = self.member // self.nb
        self.b = lax.rem(self.member, self.nb)

    def am(self, step):
        return lax.rem(self.a + step, self.na)

    def bm(self, step):
        return lax.rem(self.b + step, self.nb)

    def device(self, member, row=None, core=None):
        row = self.row if row is None else row
        return {"seq": member * self.rows + row, "tp": self.core if core is None else core}

    def at(self, a, b):
        return self.device(a * self.nb + b)

    def sibling(self):
        return self.device(self.member, core=1 - self.core)

    def partners(self):
        return [self.device(self.member, row=lax.rem(self.row + i, self.rows)) for i in range(1, self.rows)]

    def axis_peers(self):
        peers = [self.at(self.am(i), self.b) for i in range(1, self.na)]
        peers += [self.at(self.a, self.bm(j)) for j in range(1, self.nb)]
        return peers

    def other_members(self):
        return [self.device(lax.rem(self.member + i, self.members)) for i in range(1, self.members)]


def greet(devices, meanwhile=lambda: None):
    barrier = pltpu.get_barrier_semaphore()
    for device in devices:
        pl.semaphore_signal(barrier, inc=1, device_id=device, device_id_type=MESH)
    meanwhile()
    pl.semaphore_wait(barrier, len(devices))


class Sender:
    def __init__(self, send_sems):
        self.send_sems, self.copies = send_sems, []

    def send(self, src, dst, recv_sem, device):
        copy = pltpu.make_async_remote_copy(
            src_ref=src,
            dst_ref=dst,
            send_sem=self.send_sems.at[len(self.copies)],
            recv_sem=recv_sem,
            device_id=device,
            device_id_type=MESH,
        )
        copy.start()
        self.copies.append(copy)

    def arrived(self, dst, recv_sem, device):
        pltpu.make_async_remote_copy(
            src_ref=dst,
            dst_ref=dst,
            send_sem=self.send_sems.at[0],
            recv_sem=recv_sem,
            device_id=device,
            device_id_type=MESH,
        ).wait_recv()

    def finish(self):
        for copy in self.copies:
            copy.wait_send()


def remote_params(collective_id):
    return pltpu.CompilerParams(
        collective_id=collective_id, has_side_effects=True, vmem_limit_bytes=56 * megabyte
    )


def vmem_specs(count):
    return [pl.BlockSpec(memory_space=VM)] * count


def spread_kernel(n, rows, wide_ref, small_ref, pack_ref, chunk_ref, table_ref, weight_ref, *sems):
    (send_sems, chunk_sems, table_sems, block_sems, cross_sems, local_sems) = sems
    p = Place(n, rows)
    members = p.members
    everybody = [
        {"seq": lax.rem(p.seq + i, n), "tp": p.core} for i in range(1, n)
    ]
    greet(everybody)
    sender = Sender(send_sems)
    partners = [
        (lax.rem(p.row + i, rows), p.device(p.member, row=lax.rem(p.row + i, rows)))
        for i in range(1, rows)
    ]
    for device in everybody:
        sender.send(small_ref, table_ref.at[p.seq], table_sems.at[p.seq], device)
    for row, device in partners:
        sender.send(wide_ref.at[row], chunk_ref.at[p.row], chunk_sems.at[p.row], device)
    for layer in range(LAYERS):
        for i in range(1, members):
            member = lax.rem(p.member + i, members)
            sender.send(
                pack_ref.at[layer, member],
                weight_ref.at[layer, p.seq],
                block_sems.at[layer, p.member],
                p.device(member),
            )
        for row, device in partners:
            sender.send(
                pack_ref.at[layer, p.member],
                weight_ref.at[layer, p.seq],
                cross_sems.at[layer, p.seq],
                device,
            )
    own = [
        pltpu.make_async_copy(small_ref, table_ref.at[p.seq], local_sems.at[0]),
        pltpu.make_async_copy(wide_ref.at[p.row], chunk_ref.at[p.row], local_sems.at[1]),
    ]
    for layer in range(LAYERS):
        own.append(
            pltpu.make_async_copy(
                pack_ref.at[layer, p.member], weight_ref.at[layer, p.seq], local_sems.at[2 + layer]
            )
        )
    for copy in own:
        copy.start()
    for layer in range(LAYERS):
        for i in range(1, members):
            member = lax.rem(p.member + members - i, members)
            block = weight_ref.at[layer, member * rows + p.row]
            sender.arrived(block, block_sems.at[layer, member], p.sibling())
            for row, device in partners:
                sender.send(block, block, cross_sems.at[layer, member * rows + p.row], device)
    for i in range(1, n):
        seq = lax.rem(p.seq + i, n)
        sender.arrived(table_ref.at[seq], table_sems.at[seq], p.sibling())
    for row, device in partners:
        sender.arrived(chunk_ref.at[row], chunk_sems.at[row], p.sibling())
    for layer in range(LAYERS):
        for i in range(members):
            member = lax.rem(p.member + members - i, members)
            for row, device in partners:
                block = weight_ref.at[layer, member * rows + row]
                sender.arrived(block, cross_sems.at[layer, member * rows + row], p.sibling())
    sender.finish()
    for copy in own:
        copy.wait()


def spread(n, rows, wide, small, pack, collective_id):
    layers, members, height, columns = pack.shape
    sends = (n - 1) + (rows - 1) + layers * (members - 1 + members * (rows - 1))
    return pl.pallas_call(
        functools.partial(spread_kernel, n, rows),
        out_shape=(
            jax.ShapeDtypeStruct(wide.shape, wide.dtype),
            jax.ShapeDtypeStruct((n,) + small.shape, small.dtype),
            jax.ShapeDtypeStruct((layers, n, height, columns), pack.dtype),
        ),
        in_specs=vmem_specs(3),
        out_specs=tuple(vmem_specs(3)),
        scratch_shapes=[
            DMA((sends,)),
            DMA((rows,)),
            DMA((n,)),
            DMA((layers, members)),
            DMA((layers, n)),
            DMA((2 + layers,)),
        ],
        compiler_params=remote_params(collective_id),
        name="spread_inputs",
    )(wide, small, pack)


def gather_kernel(n, rows, count, x_ref, out_ref, *sems):
    send_sems, a_sems, b_sems, core_sems, local_sem = sems
    p = Place(n, rows)
    na, nb, core = p.na, p.nb, p.core
    sibling = p.sibling()
    greet(p.axis_peers() + [sibling])
    sender = Sender(send_sems)
    a_steps = [1, na - 1] + list(range(2, na - 1)) if na > 2 else [1]

    def slot(k, a, b):
        return out_ref.at[k, a * nb + b, core]

    for k in range(count):
        mine = x_ref.at[k, core]
        for i in a_steps:
            sender.send(mine, slot(k, p.a, p.b), a_sems.at[k, p.a], p.at(p.am(i), p.b))
        for j in range(1, nb):
            sender.send(mine, slot(k, p.a, p.b), b_sems.at[k, p.member], p.at(p.a, p.bm(j)))
    own = pltpu.make_async_copy(x_ref, out_ref.at[:, p.member], local_sem)
    own.start()
    for k in range(count):
        for i in a_steps:
            a = p.am(i)
            here = slot(k, a, p.b)
            sender.arrived(here, a_sems.at[k, a], sibling)
            for j in range(1, nb):
                sender.send(here, here, b_sems.at[k, a * nb + p.b], p.at(p.a, p.bm(j)))
            sender.send(here, here, core_sems.at[k, a * nb + p.b], sibling)
    for k in range(count):
        for i in [0] + a_steps:
            for j in range(1, nb):
                a, b = p.am(i), p.bm(j)
                here = slot(k, a, b)
                sender.arrived(here, b_sems.at[k, a * nb + b], sibling)
                sender.send(here, here, core_sems.at[k, a * nb + b], sibling)
    for k in range(count):
        for i in range(1, p.members):
            member = lax.rem(p.member + i, p.members)
            sender.arrived(out_ref.at[k, member, 1 - core], core_sems.at[k, member], sibling)
    sender.finish()
    own.wait()


def gather(n, rows, pieces, collective_id):
    stacked = jnp.stack(pieces)
    count, two, height, width = stacked.shape
    members = n // rows
    na, nb = split_sizes(members)
    sends = count * ((na - 1) * (nb + 1) + nb - 1 + na * (nb - 1))
    return pl.pallas_call(
        functools.partial(gather_kernel, n, rows, count),
        out_shape=jax.ShapeDtypeStruct((count, members, two, height, width), stacked.dtype),
        in_specs=vmem_specs(1),
        out_specs=vmem_specs(1)[0],
        scratch_shapes=[
            DMA((sends,)),
            DMA((count, na)),
            DMA((count, members)),
            DMA((count, members)),
            DMA,
        ],
        compiler_params=remote_params(collective_id),
        name="gather_tokens",
    )(stacked)


def reduce_kernel(n, rows, count, *refs):
    x_refs, (out_ref, core_buf, b_buf, a_buf, b_out, a_out) = refs[:count], refs[count : count + 6]
    send_sems, core_sems, b_sems, a_sems, out_sems = refs[count + 6 :]
    p = Place(n, rows)
    na, nb, core = p.na, p.nb, p.core
    sibling = p.sibling()
    greet(p.axis_peers() + [sibling])
    sender = Sender(send_sems)
    a_steps = list(range(2, na - 1)) + [1, na - 1, 0] if na > 2 else [1, 0]
    for k in range(count):
        for i in a_steps:
            for j in list(range(1, nb)) + [0]:
                m = p.am(i) * nb + p.bm(j)
                sender.send(x_refs[k].at[m, 1 - core], core_buf.at[k, m], core_sems.at[k, m], sibling)
    for k in range(count):
        for i in a_steps:
            for j in range(1, nb):
                a, b = p.am(i), p.bm(j)
                m = a * nb + b
                sender.arrived(core_buf.at[k, m], core_sems.at[k, m], sibling)
                b_out[k, m] = (x_refs[k][m, core].astype(f32) + core_buf[k, m].astype(f32)).astype(bf16)
                landing = a * nb + p.b
                sender.send(b_out.at[k, m], b_buf.at[k, landing], b_sems.at[k, landing], p.at(p.a, b))
    for k in range(count):
        for i in a_steps:
            a = p.am(i)
            m = a * nb + p.b
            sender.arrived(core_buf.at[k, m], core_sems.at[k, m], sibling)
            total = x_refs[k][m, core].astype(f32) + core_buf[k, m].astype(f32)
            for j in range(1, nb):
                q = a * nb + p.bm(j)
                sender.arrived(b_buf.at[k, q], b_sems.at[k, q], sibling)
                total = total + b_buf[k, q].astype(f32)
            if i:
                a_out[k, a] = total.astype(bf16)
                sender.send(a_out.at[k, a], a_buf.at[k, p.a], a_sems.at[k, p.a], p.at(a, p.b))
            else:
                out_ref[k, core] = total
    for k in range(count):
        for i in range(1, na):
            a = p.am(i)
            sender.arrived(a_buf.at[k, a], a_sems.at[k, a], sibling)
            out_ref[k, core] += a_buf[k, a].astype(f32)
        sender.send(out_ref.at[k, core], out_ref.at[k, core], out_sems.at[k], sibling)
    for k in range(count):
        sender.arrived(out_ref.at[k, 1 - core], out_sems.at[k], sibling)
    sender.finish()


def reduce(n, rows, pieces, collective_id):
    count = len(pieces)
    members, two, height, width = pieces[0].shape
    na, nb = split_sizes(members)
    sends = count * (members + na * (nb - 1) + na)
    return pl.pallas_call(
        functools.partial(reduce_kernel, n, rows, count),
        out_shape=jax.ShapeDtypeStruct((count, two, height, width), f32),
        in_specs=vmem_specs(count),
        out_specs=vmem_specs(1)[0],
        scratch_shapes=[
            VM((count, members, height, width), bf16),
            VM((count, members, height, width), bf16),
            VM((count, na, height, width), bf16),
            VM((count, members, height, width), bf16),
            VM((count, na, height, width), bf16),
            DMA((sends,)),
            DMA((count, members)),
            DMA((count, members)),
            DMA((count, na)),
            DMA((count,)),
        ],
        compiler_params=remote_params(collective_id),
        name="reduce_tokens",
    )(*pieces)


def collect_kernel(n, rows, *refs):
    (first_ref, second_ref, wide_ref, small_ref, grad_ref, back_ref, table_ref) = refs[:7]
    (cross_buf, block_out, send_sems, cross_sems, block_sems, back_sems, table_sems, local_sems) = refs[7:]
    grads = (first_ref, second_ref)
    p = Place(n, rows)
    members = p.members
    everybody = [{"seq": lax.rem(p.seq + i, n), "tp": p.core} for i in range(1, n)]
    greet(everybody)
    sender = Sender(send_sems)
    partners = [
        (lax.rem(p.row + i, rows), p.device(p.member, row=lax.rem(p.row + i, rows)))
        for i in range(1, rows)
    ]
    order = [lax.rem(p.member + i, members) for i in range(1, members)] + [p.member]
    for i in range(1, n):
        seq = lax.rem(p.seq + i, n)
        sender.send(small_ref.at[seq], table_ref.at[p.seq], table_sems.at[p.seq], {"seq": seq, "tp": p.core})
    for layer in range(LAYERS):
        for member in order:
            for row, device in partners:
                sender.send(
                    grads[layer].at[member * rows + row],
                    cross_buf.at[layer, p.row, member],
                    cross_sems.at[layer, p.row, member],
                    device,
                )
    for row, device in partners:
        sender.send(wide_ref.at[row], back_ref.at[p.row], back_sems.at[p.row], device)
    own = [
        pltpu.make_async_copy(small_ref.at[p.seq], table_ref.at[p.seq], local_sems.at[0]),
        pltpu.make_async_copy(wide_ref.at[p.row], back_ref.at[p.row], local_sems.at[1]),
    ]
    for copy in own:
        copy.start()
    for layer in range(LAYERS):
        for i in list(range(1, members)) + [0]:
            member = lax.rem(p.member + i, members)
            total = grads[layer][member * rows + p.row].astype(f32)
            for row, device in partners:
                buffer = cross_buf.at[layer, row, member]
                sender.arrived(buffer, cross_sems.at[layer, row, member], p.sibling())
                total = total + buffer[...].astype(f32)
            if i:
                block_out[layer, member] = total.astype(bf16)
                sender.send(
                    block_out.at[layer, member],
                    grad_ref.at[layer, p.member],
                    block_sems.at[layer, p.member],
                    p.device(member),
                )
            else:
                grad_ref[layer, member] = total.astype(bf16)
    for i in range(1, n):
        seq = lax.rem(p.seq + i, n)
        sender.arrived(table_ref.at[seq], table_sems.at[seq], p.sibling())
    for row, device in partners:
        sender.arrived(back_ref.at[row], back_sems.at[row], p.sibling())
    for layer in range(LAYERS):
        for i in range(1, members):
            member = lax.rem(p.member + members - i, members)
            sender.arrived(grad_ref.at[layer, member], block_sems.at[layer, member], p.sibling())
    sender.finish()
    for copy in own:
        copy.wait()


def collect(n, rows, first, second, wide, small, collective_id):
    unused, height, columns = first.shape
    members = n // rows
    sends = (n - 1) + (rows - 1) + LAYERS * (members * (rows - 1) + members - 1)
    return pl.pallas_call(
        functools.partial(collect_kernel, n, rows),
        out_shape=(
            jax.ShapeDtypeStruct((LAYERS, members, height, columns), bf16),
            jax.ShapeDtypeStruct(wide.shape, wide.dtype),
            jax.ShapeDtypeStruct(small.shape, small.dtype),
        ),
        in_specs=vmem_specs(4),
        out_specs=tuple(vmem_specs(3)),
        scratch_shapes=[
            VM((LAYERS, rows, members, height, columns), bf16),
            VM((LAYERS, members, height, columns), bf16),
            DMA((sends,)),
            DMA((LAYERS, rows, members)),
            DMA((LAYERS, members)),
            DMA((rows,)),
            DMA((n,)),
            DMA((2,)),
        ],
        compiler_params=remote_params(collective_id),
        name="collect_gradients",
    )(first, second, wide, small)


def share_kernel(n, x_ref, out_ref, send_sems, recv_sems, local_sem):
    seq, core = lax.axis_index("seq"), lax.axis_index("tp")
    others = []
    for i in range(n):
        for j in range(2):
            if i or j:
                others.append((lax.rem(seq + i, n), lax.rem(core + j, 2)))
    greet([{"seq": s, "tp": c} for s, c in others])
    sender = Sender(send_sems)
    here = seq * 2 + core
    for s, c in others:
        sender.send(x_ref, out_ref.at[here], recv_sems.at[here], {"seq": s, "tp": c})
    own = pltpu.make_async_copy(x_ref, out_ref.at[here], local_sem)
    own.start()
    for s, c in others:
        sender.arrived(out_ref.at[s * 2 + c], recv_sems.at[s * 2 + c], {"seq": s, "tp": c})
    sender.finish()
    own.wait()


def share(n, x, collective_id):
    return pl.pallas_call(
        functools.partial(share_kernel, n),
        out_shape=jax.ShapeDtypeStruct((2 * n,) + x.shape, x.dtype),
        in_specs=vmem_specs(1),
        out_specs=vmem_specs(1)[0],
        scratch_shapes=[DMA((2 * n,)), DMA((2 * n,)), DMA],
        compiler_params=remote_params(collective_id),
        name="share_squares",
    )(x)


def dot(left, right):
    return jnp.dot(left, right, preferred_element_type=f32)


def dot_nt(left, right):
    return lax.dot_general(left, right, (((1,), (1,)), ((), ())), preferred_element_type=f32)


def dot_tn(left, right):
    return lax.dot_general(left, right, (((0,), (0,)), ((), ())), preferred_element_type=f32)


def swap_lanes(values):
    width = values.shape[-1]
    lane = lax.broadcasted_iota(jnp.int32, values.shape, 1)
    after = pltpu.roll(values, width - 1, 1)
    before = pltpu.roll(values, 1, 1)
    return jnp.where(lane % 2 == 0, after, before)


gelu_scale = 0.7978845608
gelu_cubic = 0.044715


def gelu(z):
    return 0.5 * z * (1.0 + jnp.tanh(gelu_scale * (z + gelu_cubic * z * z * z)))


def gelu_slope(z):
    inner = jnp.tanh(gelu_scale * (z + gelu_cubic * z * z * z))
    slope = gelu_scale * (1.0 + 3.0 * gelu_cubic * z * z)
    return 0.5 * (1.0 + inner) + 0.5 * z * (1.0 - inner * inner) * slope


def query_tiles(length, share, rows):
    tile = max(64, min(TILE, TILE * 1024 // length))
    first = 0
    if share > 1:
        first = lax.rem(lax.axis_index("seq") // rows, share) * (length // share)
    for i in range(length // share // tile):
        start = pl.multiple_of(first + i * tile, tile) if share > 1 else i * tile
        yield pl.ds(start, tile), start, ((i + 1) * tile if share == 1 else length)


def visible(start, keys, seg_col, seg_row):
    tile = seg_col.shape[0]
    place = start + lax.broadcasted_iota(jnp.int32, (tile, keys), 0)
    other = lax.broadcasted_iota(jnp.int32, (tile, keys), 1)
    return (other <= place) & (seg_col == seg_row)


def forward_kernel(batch, share, ff, h_ref, w_ref, cos_ref, sin_ref, segc_ref, segr_ref, *outs):
    part_ref, q_ref, k_ref, v_ref, o_ref, lse_ref, a_ref, z_ref = outs
    length = h_ref.shape[0]
    f = 4 * HEAD

    @pl.loop(0, length // TILE)
    def project(t):
        rows = pl.ds(t * TILE, TILE)
        h = h_ref[rows, :]
        mixed = dot(h, w_ref[:, :f])
        qk = mixed[:, : 2 * HEAD]
        qk = qk * cos_ref[rows, :] + swap_lanes(qk) * sin_ref[rows, :]
        q_ref[rows, :] = (qk[:, :HEAD].astype(bf16).astype(f32) * HEAD**-0.5).astype(bf16)
        k_ref[rows, :] = qk[:, HEAD:].astype(bf16)
        v_ref[rows, :] = mixed[:, 2 * HEAD : 3 * HEAD].astype(bf16)
        z = dot(h, w_ref[:, f : f + ff])
        z_ref[rows, :] = z
        a_ref[rows, :] = gelu(z).astype(bf16)

    if share > 1:
        o_ref[...] = jnp.zeros_like(o_ref)
        lse_ref[...] = jnp.zeros_like(lse_ref)
    for rows, start, keys in query_tiles(length, share, batch):
        scores = dot_nt(q_ref[rows, :], k_ref[:keys, :])
        seen = visible(start, keys, segc_ref[rows, :], segr_ref[:, :keys])
        scores = jnp.where(seen, scores, low_score)
        peak = jnp.max(scores, axis=1, keepdims=True)
        weights = jnp.exp(scores - peak)
        total = jnp.sum(weights, axis=1, keepdims=True)
        lse_ref[rows, :] = peak + jnp.log(total)
        shares = (weights * (1.0 / total)).astype(bf16)
        o_ref[rows, :] = dot(shares, v_ref[:keys, :]).astype(bf16)

    @pl.loop(0, length // TILE)
    def branch(t):
        rows = pl.ds(t * TILE, TILE)
        out = dot_nt(o_ref[rows, :], w_ref[:, 3 * HEAD : f])
        out = out + dot_nt(a_ref[rows, :], w_ref[:, f + ff : f + 2 * ff])
        part_ref[rows, :] = out.astype(bf16)


def forward(batch, share, ff, h, w, cosine, sine, seg_col, seg_row):
    length, width = h.shape
    column = jax.ShapeDtypeStruct((length, HEAD), bf16)
    return pl.pallas_call(
        functools.partial(forward_kernel, batch, share, ff),
        out_shape=(
            jax.ShapeDtypeStruct((length, width), bf16),
            column,
            column,
            column,
            column,
            jax.ShapeDtypeStruct((length, 1), f32),
            jax.ShapeDtypeStruct((length, ff), bf16),
            jax.ShapeDtypeStruct((length, ff), f32),
        ),
        in_specs=vmem_specs(6),
        out_specs=tuple(vmem_specs(8)),
        compiler_params=pltpu.CompilerParams(vmem_limit_bytes=56 * megabyte),
        name="layer_forward",
    )(h, w, cosine, sine, seg_col, seg_row)


def backward_kernel(batch, share, ff, g_ref, h_ref, w_ref, cos_ref, sin_ref, segc_ref, segr_ref, *refs):
    q_ref, k_ref, v_ref, o_ref, lse_ref, a_ref, z_ref, part_ref, dw_ref = refs[:9]
    dz_ref, do_ref, dq_ref, dk_ref, dv_ref, mix_ref = refs[9:]
    length, width = h_ref.shape
    f = 4 * HEAD

    @pl.loop(0, length // TILE)
    def feed(t):
        rows = pl.ds(t * TILE, TILE)
        g = g_ref[rows, :]
        da = dot(g, w_ref[:, f + ff : f + 2 * ff])
        dz_ref[rows, :] = (da * gelu_slope(z_ref[rows, :])).astype(bf16)
        do_ref[rows, :] = dot(g, w_ref[:, :f])[:, 3 * HEAD :].astype(bf16)

    dk_ref[...] = jnp.zeros_like(dk_ref)
    dv_ref[...] = jnp.zeros_like(dv_ref)
    if share > 1:
        dq_ref[...] = jnp.zeros_like(dq_ref)
    for rows, start, keys in query_tiles(length, share, batch):
        q, head_grad = q_ref[rows, :], do_ref[rows, :]
        scores = dot_nt(q, k_ref[:keys, :])
        seen = visible(start, keys, segc_ref[rows, :], segr_ref[:, :keys])
        shares = jnp.where(seen, jnp.exp(scores - lse_ref[rows, :]), 0.0)
        share_grads = dot_nt(head_grad, v_ref[:keys, :])
        delta = jnp.sum(shares * share_grads, axis=1, keepdims=True)
        score_grads = (shares * (share_grads - delta)).astype(bf16)
        dq_ref[rows, :] = dot(score_grads, k_ref[:keys, :]) * HEAD**-0.5
        dk_ref[:keys, :] += dot_tn(score_grads, q)
        dv_ref[:keys, :] += dot_tn(shares.astype(bf16), head_grad)

    @pl.loop(0, length // TILE)
    def inward(t):
        rows = pl.ds(t * TILE, TILE)
        qk = jnp.concatenate([dq_ref[rows, :], dk_ref[rows, :]], axis=1)
        qk = qk * cos_ref[rows, :] + swap_lanes(qk * sin_ref[rows, :])
        rest = jnp.concatenate([dv_ref[rows, :], jnp.zeros((TILE, HEAD), f32)], axis=1)
        mix = jnp.concatenate([qk, rest], axis=1).astype(bf16)
        mix_ref[rows, :] = mix
        out = dot_nt(mix, w_ref[:, :f]) + dot_nt(dz_ref[rows, :], w_ref[:, f : f + ff])
        part_ref[rows, :] = out.astype(bf16)

    @pl.loop(0, width // TILE)
    def weights(t):
        rows = pl.ds(t * TILE, TILE)
        h, g = h_ref[:, rows], g_ref[:, rows]
        mixed = dot_tn(h, mix_ref[...])
        out = dot_tn(g, o_ref[...])
        dw_ref[rows, :f] = jnp.concatenate([mixed[:, : 3 * HEAD], out], axis=1).astype(bf16)
        dw_ref[rows, f : f + ff] = dot_tn(h, dz_ref[...]).astype(bf16)
        dw_ref[rows, f + ff : f + 2 * ff] = dot_tn(g, a_ref[...]).astype(bf16)


def backward(batch, share, ff, g, h, w, cosine, sine, seg_col, seg_row, kept):
    length, width = h.shape
    return pl.pallas_call(
        functools.partial(backward_kernel, batch, share, ff),
        out_shape=(
            jax.ShapeDtypeStruct((length, width), bf16),
            jax.ShapeDtypeStruct(w.shape, bf16),
        ),
        in_specs=vmem_specs(14),
        out_specs=tuple(vmem_specs(2)),
        scratch_shapes=[
            VM((length, ff), bf16),
            VM((length, HEAD), bf16),
            VM((length, HEAD), f32),
            VM((length, HEAD), f32),
            VM((length, HEAD), f32),
            VM((length, 4 * HEAD), bf16),
        ],
        compiler_params=pltpu.CompilerParams(vmem_limit_bytes=60 * megabyte),
        name="layer_backward",
    )(g, h, w, cosine, sine, seg_col, seg_row, *kept)


def layer_norm(inputs):
    average = jnp.mean(inputs, axis=-1, keepdims=True)
    centred = inputs - average
    spread_here = jnp.mean(centred * centred, axis=-1, keepdims=True)
    inverse = lax.rsqrt(spread_here + norm_eps)
    return (centred * inverse, inverse)


def norm_back(grads, normed_grads, xhat, inverse, gain):
    scaled = normed_grads * gain
    average = jnp.mean(scaled, axis=-1, keepdims=True)
    along = jnp.mean(scaled * xhat, axis=-1, keepdims=True)
    return grads + (scaled - average - xhat * along) * inverse


def rotary_tables(positions):
    column = jnp.arange(HEAD)
    inside = column < ROTARY
    pair_index = column % ROTARY // 2
    frequency = jnp.exp(pair_index.astype(f32) * (-2.0 * math.log(10000.0) / ROTARY))
    angles = positions[:, None] * frequency
    cosine = jnp.where(inside, jnp.cos(angles), 1.0)
    signed = jnp.where(column % 2 == 0, -1.0, 1.0)
    sine = jnp.where(inside, signed * jnp.sin(angles), 0.0)
    return (jnp.tile(cosine, (1, 2)), jnp.tile(sine, (1, 2)))


def pad_lanes(values, width=128):
    return jnp.pad(values, [(0, 0)] * (values.ndim - 1) + [(0, width - values.shape[-1])])


def adam_update(weight, first, second, gradient, factor_clip, rate, decay):
    clipped = gradient * factor_clip
    first_new = beta_one * first + (1.0 - beta_one) * clipped
    second_new = beta_two * second + (1.0 - beta_two) * clipped * clipped
    first_hat = first_new * (1.0 / (1.0 - beta_one**STEP))
    second_hat = second_new * (1.0 / (1.0 - beta_two**STEP))
    weight_new = weight - rate * (first_hat / (jnp.sqrt(second_hat) + adam_eps) + decay * weight)
    return (weight_new, first_new, second_new)


def pack_weights(n, rows, qkv_weight, out_weight, in_weight, down_weight):
    layers, height = qkv_weight.shape[:2]
    members = n // rows
    heads = qkv_weight.shape[3] // HEAD
    share = members // heads
    ff = in_weight.shape[2] // members
    mixed = jnp.concatenate([qkv_weight, out_weight[:, :, None, :]], axis=2).astype(bf16)
    mixed = mixed.reshape(layers, height, 4, heads, HEAD).transpose(0, 3, 1, 2, 4)
    mixed = mixed.reshape(layers, heads, height, 4 * HEAD)
    if share > 1:
        mixed = jnp.repeat(mixed, share, axis=1)
    feeds = [
        weight.astype(bf16).reshape(layers, height, members, ff).transpose(0, 2, 1, 3)
        for weight in (in_weight, down_weight)
    ]
    return jnp.concatenate([mixed] + feeds, axis=3)


def unpack_gradients(grads, heads, ff):
    layers, members, height, unused = grads.shape
    grads = grads.astype(f32)
    share = members // heads
    mixed = grads[..., : 4 * HEAD]
    if share > 1:
        mixed = mixed.reshape(layers, heads, share, height, 4 * HEAD).sum(2)
    mixed = mixed.reshape(layers, heads, height, 4, HEAD).transpose(0, 2, 3, 1, 4)
    mixed = mixed.reshape(layers, height, 4, heads * HEAD)
    feeds = [
        grads[..., 4 * HEAD + k * ff : 4 * HEAD + (k + 1) * ff]
        .transpose(0, 2, 1, 3)
        .reshape(layers, height, members * ff)
        for k in range(2)
    ]
    return (mixed[:, :, :3], mixed[:, :, 3], feeds[0], feeds[1])


def shards_apart(
    n,
    activations,
    cotangent,
    segment_ids,
    position_ids,
    qkv_weight,
    out_weight,
    in_weight,
    down_weight,
    norm_params,
    qkv_first,
    out_first,
    in_first,
    down_first,
    norm_first,
    qkv_second,
    out_second,
    in_second,
    down_second,
    norm_second,
):
    rows, span, width = activations.shape
    members = n // rows
    length = n * span
    half = rows * span // 2
    heads = qkv_weight.shape[3] // HEAD
    share_queries = members // heads
    ff = in_weight.shape[2] // members
    row = lax.axis_index("seq") % rows

    pack = pack_weights(n, rows, qkv_weight, out_weight, in_weight, down_weight)
    norm_low = norm_params.astype(bf16).astype(f32).reshape(LAYERS * 3, -1)
    small = jnp.concatenate(
        [
            pad_lanes(norm_low),
            pad_lanes(position_ids.astype(f32)),
            pad_lanes(segment_ids.astype(f32)),
        ]
    )
    small = jnp.pad(small, ((0, -small.shape[0] % 8), (0, 0)))
    wide = jnp.stack([activations, cotangent], axis=1)
    chunk, table, weights = spread(n, rows, wide, small, pack, 0)
    weights = weights.reshape(LAYERS, width, -1)
    inputs = chunk[:, 0].reshape(rows * span, width)
    out_grads = chunk[:, 1].reshape(rows * span, width)
    own_columns = norm_params.shape[-1]
    norms = table[:, : LAYERS * 3, :own_columns].transpose(1, 0, 2).reshape(LAYERS, 3, width)
    positions = lax.dynamic_index_in_dim(table, LAYERS * 3 + row, 1, False)[:, :span].reshape(length)
    segments = lax.dynamic_index_in_dim(table, LAYERS * 3 + rows + row, 1, False)[:, :span].reshape(length)
    cosine, sine = rotary_tables(positions)
    places = (cosine, sine, segments[:, None], segments[None, :])

    def halves(values):
        return values.astype(bf16).reshape(2, half, width)

    def whole(values):
        return values.reshape(length, width)

    def parts(values):
        return values.reshape(members, 2, half, width)

    xhat_0, inverse_0 = layer_norm(inputs)
    normed = xhat_0 * norms[0, 0] + norms[0, 1]
    got = gather(n, rows, [halves(normed), halves(out_grads)], 1)
    normed_0, grads_1 = whole(got[0]), whole(got[1])
    part, *kept_0 = forward(rows, share_queries, ff, normed_0, weights[0], *places)
    branch = reduce(n, rows, [parts(part)], 2)[0].reshape(inputs.shape)
    middle = inputs + branch + norms[0, 2]
    xhat_1, inverse_1 = layer_norm(middle)
    normed = xhat_1 * norms[1, 0] + norms[1, 1]
    normed_1 = whole(gather(n, rows, [halves(normed)], 3)[0])
    part, *kept_1 = forward(rows, share_queries, ff, normed_1, weights[1], *places)
    back_part, weight_grads_1 = backward(rows, share_queries, ff, grads_1, normed_1, weights[1], *places, kept_1)
    sums = reduce(n, rows, [parts(part), parts(back_part)], 4).reshape((2,) + inputs.shape)
    result = middle + sums[0] + norms[1, 2]
    normed_grads_1 = sums[1]
    grads_mid = norm_back(out_grads, normed_grads_1, xhat_1, inverse_1, norms[1, 0])
    grads_0 = whole(gather(n, rows, [halves(grads_mid)], 5)[0])
    back_part, weight_grads_0 = backward(rows, share_queries, ff, grads_0, normed_0, weights[0], *places, kept_0)
    normed_grads_0 = reduce(n, rows, [parts(back_part)], 6)[0].reshape(inputs.shape)
    input_grad = norm_back(grads_mid, normed_grads_0, xhat_0, inverse_0, norms[0, 0])

    small_grads = jnp.stack(
        [
            jnp.sum(normed_grads_0 * xhat_0, axis=0),
            jnp.sum(normed_grads_0, axis=0),
            jnp.sum(grads_mid, axis=0),
            jnp.sum(normed_grads_1 * xhat_1, axis=0),
            jnp.sum(normed_grads_1, axis=0),
            jnp.sum(out_grads, axis=0),
        ]
    )
    small_grads = pad_lanes(small_grads.reshape(LAYERS * 3, n, own_columns).transpose(1, 0, 2))
    small_grads = jnp.pad(small_grads, ((0, 0), (0, 8 - LAYERS * 3), (0, 0)))
    wide_out = jnp.stack([result.reshape(rows, span, width), input_grad.reshape(rows, span, width)], axis=1)
    height = width // n
    grads, wide_back, table_back = collect(
        n,
        rows,
        weight_grads_0.reshape(n, height, -1),
        weight_grads_1.reshape(n, height, -1),
        wide_out,
        small_grads,
        7,
    )
    norm_grads = jnp.sum(table_back, axis=0)[: LAYERS * 3, :own_columns].reshape(norm_params.shape)
    qkv_grads, out_weight_grads, in_grads, down_grads = unpack_gradients(grads, heads, ff)
    matrix_squares = sum(
        (jnp.sum(block * block) for block in (qkv_grads, out_weight_grads, in_grads, down_grads))
    )
    squares = matrix_squares + jnp.sum(norm_grads * norm_grads) / 2
    everyone = share(n, jnp.full((8, 128), squares, f32), 8)
    grad_norm = jnp.sqrt(jnp.sum(everyone[:, 0, 0]))
    total_parameters = LAYERS * width * (4 * 2 * heads * HEAD + 2 * 2 * members * ff + 3)
    factor_clip = jnp.minimum(1.0, clip_share * math.sqrt(total_parameters) / (grad_norm + 1e-06))
    qkv_new, qkv_first_new, qkv_second_new = adam_update(
        qkv_weight, qkv_first, qkv_second, qkv_grads, factor_clip, rate_matrix, decay_matrix
    )
    out_new, out_first_new, out_second_new = adam_update(
        out_weight, out_first, out_second, out_weight_grads, factor_clip, rate_output, decay_matrix
    )
    in_new, in_first_new, in_second_new = adam_update(
        in_weight, in_first, in_second, in_grads, factor_clip, rate_matrix, decay_matrix
    )
    down_new, down_first_new, down_second_new = adam_update(
        down_weight, down_first, down_second, down_grads, factor_clip, rate_matrix, decay_matrix
    )
    norm_new, norm_first_new, norm_second_new = adam_update(
        norm_params, norm_first, norm_second, norm_grads, factor_clip, rate_vector, 0.0
    )
    bias_clipped = norm_grads[:, 2] * factor_clip
    return (
        wide_back[:, 0],
        wide_back[:, 1],
        grad_norm,
        qkv_new,
        out_new,
        in_new,
        down_new,
        norm_new,
        qkv_first_new,
        out_first_new,
        in_first_new,
        down_first_new,
        norm_first_new,
        qkv_second_new,
        out_second_new,
        in_second_new,
        down_second_new,
        norm_second_new,
        bias_clipped,
    )


def flip(index, bits):
    bit = 1
    while bit <= bits:
        if bits & bit:
            index = index + bit * (1 - 2 * lax.rem(index // bit, 2))
        bit *= 2
    return index


class Net:
    def __init__(self, n, rows, half, pieces, send_sems):
        self.p = Place(n, rows)
        self.half, self.pieces = half, pieces
        self.send_sems, self.used = send_sems, 0
        self.sibling = self.p.sibling()

    def send_sem(self):
        self.used += 1
        return self.send_sems.at[self.used - 1]

    def everybody(self):
        p = self.p
        return [{"seq": lax.rem(p.seq + i, p.n), "tp": p.core} for i in range(1, p.n)]

    def everyone(self):
        p = self.p
        return self.everybody() + [
            {"seq": lax.rem(p.seq + i, p.n), "tp": 1 - p.core} for i in range(p.n)
        ]

    def partner(self):
        return self.p.device(self.p.member, row=1 - self.p.row)

    def a_of(self, k):
        return flip(self.p.a, k)

    def b_of(self, j):
        return flip(self.p.b, j)

    def tokens(self, member, core, piece):
        size = self.half // self.pieces
        start = (member * 2 + core) * self.half + piece * size
        return pl.ds(pl.multiple_of(start, size), size)

    def lines(self, slot, piece):
        size = self.half // self.pieces
        return pl.ds(pl.multiple_of(slot * self.half + piece * size, size), size)

    def own(self):
        start = (self.p.member * 2 + self.p.core) * self.half
        return pl.ds(pl.multiple_of(start, self.half), self.half)

    def tile_rows(self, a):
        size = self.p.nb * 2 * self.half
        return pl.ds(pl.multiple_of(a * size, size), size)

    def width_rows(self, k, width):
        size = width // self.p.na
        return pl.ds(pl.multiple_of(self.a_of(k) * size, size), size)

    def tile(self, k):
        return self.tile_rows(self.a_of(k))

    def far_first(self):
        a, na = self.p.a, self.p.na
        if na != 4:
            return [self.a_of(k) for k in range(na - 1, -1, -1)]
        upper = a // 2
        low = a + upper * (3 - 2 * a)
        order = [3, 2, 1 - low, low]
        return [v + upper * (3 - 2 * v) for v in order]

    def sides(self, distance):
        a, na = self.p.a, self.p.na
        return [
            (a >= distance, a - distance, a < na - 1, a + 1),
            (a + distance < na, a + distance, a > 0, a - 1),
        ]


class Sends:
    def __init__(self, net, lone=0):
        self.sibling = net.sibling
        self.shared = net.send_sem()
        self.lone = [net.send_sem() for _ in range(lone)]
        self.made, self.conditional = 0, []

    def copy(self, src, dst, sem, device, send_sem):
        return pltpu.make_async_remote_copy(
            src_ref=src, dst_ref=dst, send_sem=send_sem, recv_sem=sem, device_id=device, device_id_type=MESH
        )

    def send(self, src, dst, sem, device):
        self.copy(src, dst, sem, device, self.shared).start()
        self.made += 1

    def send_if(self, when, src, dst, sem, device):
        number = len(self.conditional)
        self.conditional.append((when, src, dst, sem, device))
        pl.when(when)(lambda: self.copy(src, dst, sem, device, self.lone[number]).start())

    def finish(self, whole):
        self.copy(whole, whole, self.shared, self.sibling, self.shared).wait_send()
        for number, (when, *copy) in enumerate(self.conditional):
            pl.when(when)(lambda number=number, copy=copy: self.copy(*copy, self.lone[number]).wait_send())
        self.made, self.conditional = 0, []


def wait_for(net, dst, sem):
    pltpu.make_async_remote_copy(
        src_ref=dst,
        dst_ref=dst,
        send_sem=net.send_sems.at[0],
        recv_sem=sem,
        device_id=net.sibling,
        device_id_type=MESH,
    ).wait_recv()


class Gather:
    def __init__(self, net, sems):
        self.net = net
        self.a_sems, self.b_sems, self.core_sems = sems
        self.sends = Sends(net, lone=2 * net.pieces * net.p.na)

    def slot(self, a, b, core, q):
        return self.out.at[self.net.tokens(a * self.net.p.nb + b, core, q), :]

    def to_line(self, a, q, to, when):
        p = self.net.p
        here = self.slot(a, p.b, p.core, q)
        self.sends.send_if(when, here, here, self.a_sems.at[a, q], p.at(to, p.b))

    def to_rest(self, a, q):
        net, p = self.net, self.net.p
        here = self.slot(a, p.b, p.core, q)
        for j in range(1, p.nb):
            self.sends.send(here, here, self.b_sems.at[a * p.nb + p.b, q], p.at(p.a, net.b_of(j)))
        self.sends.send(here, here, self.core_sems.at[a, q], net.sibling)

    def start(self, out):
        p = self.net.p
        self.out = out
        for q in range(self.net.pieces):
            self.to_line(p.a, q, p.a + 1, p.a < p.na - 1)
            self.to_line(p.a, q, p.a - 1, p.a > 0)
            self.to_rest(p.a, q)

    def hop(self, distance):
        net, p = self.net, self.net.p
        for q in range(net.pieces):
            for there, a, more, beyond in net.sides(distance):

                @pl.when(there)
                def _():
                    wait_for(net, self.slot(a, p.b, p.core, q), self.a_sems.at[a, q])

                self.to_line(a, q, beyond, jnp.logical_and(there, more))
                pl.when(there)(lambda: self.to_rest(a, q))

    def side(self, distance):
        net, p = self.net, self.net.p
        for j in range(1, p.nb):
            b = net.b_of(j)
            for q in range(net.pieces):
                for there, a, more, beyond in net.sides(distance)[: 2 if distance else 1]:

                    @pl.when(there)
                    def _():
                        here = self.slot(a, b, p.core, q)
                        wait_for(net, here, self.b_sems.at[a * p.nb + b, q])
                        self.sends.send(here, here, self.core_sems.at[a, q], net.sibling)

    def settle(self, distance):
        net, p = self.net, self.net.p
        size = p.nb * net.half // net.pieces
        for q in range(net.pieces):
            for there, a, more, beyond in net.sides(distance)[: 2 if distance else 1]:

                @pl.when(there)
                def _():
                    wait_for(net, self.out.at[pl.ds(0, size), :], self.core_sems.at[a, q])

    def steps(self):
        na = self.net.p.na
        if na > 1:
            self.hop(1)
        yield None
        self.side(0)
        yield None
        for k in range(na):
            if k + 2 < na:
                self.hop(k + 2)
            if k + 1 < na:
                self.side(k + 1)
            self.settle(k)
            yield k

    def finish(self):
        p = self.net.p
        self.sends.finish(self.out.at[pl.ds(0, (p.na * (p.nb - 1) + p.members) * self.net.half), :])


class Reduce:
    def __init__(self, net, x, total, bufs, sems):
        self.net, self.x, self.total = net, x, total
        self.core_buf, self.b_out, self.b_buf, self.a_out, self.a_buf, self.sum_buf = bufs
        self.core_sems, self.b_sems, self.a_sems = sems
        self.sends = Sends(net, lone=2 * net.pieces * (net.p.na - 1))

    def offer(self, a):
        net, p = self.net, self.net.p
        for j in list(range(1, p.nb)) + [0]:
            m = a * p.nb + net.b_of(j)
            for q in range(net.pieces):
                self.sends.send(
                    self.x.at[net.tokens(m, 1 - p.core, q), :],
                    self.core_buf.at[net.lines(m, q), :],
                    self.core_sems.at[m, q],
                    net.sibling,
                )

    def pair_sum(self, m, q):
        net = self.net
        lines = net.lines(m, q)
        wait_for(net, self.core_buf.at[lines, :], self.core_sems.at[m, q])
        return self.x[net.tokens(m, net.p.core, q), :].astype(f32) + self.core_buf[lines, :].astype(f32)

    def targets(self, distance):
        return self.net.sides(distance)[: 2 if distance else 1]

    def relay(self, distance):
        net, p = self.net, self.net.p
        for there, a, unused_more, unused_beyond in self.targets(distance):
            for j in range(1, p.nb):
                b = net.b_of(j)
                for q in range(net.pieces):

                    @pl.when(there)
                    def _():
                        m, landing = a * p.nb + b, a * p.nb + p.b
                        self.b_out[net.lines(m, q), :] = self.pair_sum(m, q).astype(bf16)
                        self.sends.send(
                            self.b_out.at[net.lines(m, q), :],
                            self.b_buf.at[net.lines(landing, q), :],
                            self.b_sems.at[landing, q],
                            p.at(p.a, b),
                        )

    def row_sum(self, a, q):
        net, p = self.net, self.net.p
        total = self.pair_sum(a * p.nb + p.b, q)
        for j in range(1, p.nb):
            m = a * p.nb + net.b_of(j)
            wait_for(net, self.b_buf.at[net.lines(m, q), :], self.b_sems.at[m, q])
            total = total + self.b_buf[net.lines(m, q), :].astype(f32)
        return total

    def passing(self, up, a, q):
        net, p = self.net, self.net.p
        slot = a if up else p.na + a
        wait_for(net, self.a_buf.at[net.lines(slot, q), :], self.a_sems.at[slot, q])
        return self.a_buf[net.lines(slot, q), :].astype(f32)

    def pass_on(self, distance):
        net, p = self.net, self.net.p
        size = net.half // net.pieces
        for side, (there, a, unused_more, unused_beyond) in enumerate(net.sides(distance)):
            up = side == 1
            behind = p.a > 0 if up else p.a < p.na - 1
            slot = a if up else p.na + a
            for q in range(net.pieces):
                part = slice(q * size, (q + 1) * size)

                @pl.when(there)
                def _():
                    self.sum_buf[part, :] = self.row_sum(a, q)

                @pl.when(jnp.logical_and(there, behind))
                def _():
                    self.sum_buf[part, :] += self.passing(up, a, q)

                @pl.when(there)
                def _():
                    self.a_out[net.lines(slot, q), :] = self.sum_buf[part, :].astype(bf16)

                self.sends.send_if(
                    there,
                    self.a_out.at[net.lines(slot, q), :],
                    self.a_buf.at[net.lines(slot, q), :],
                    self.a_sems.at[slot, q],
                    p.at(p.a + 1 if up else p.a - 1, p.b),
                )

    def arrive(self):
        net, p = self.net, self.net.p
        size = net.half // net.pieces
        for q in range(net.pieces):
            part = slice(q * size, (q + 1) * size)
            self.total[part, :] = self.row_sum(p.a, q)
        for q in range(net.pieces):
            part = slice(q * size, (q + 1) * size)

            @pl.when(p.a > 0)
            def _():
                self.total[part, :] += self.passing(True, p.a, q)

            @pl.when(p.a < p.na - 1)
            def _():
                self.total[part, :] += self.passing(False, p.a, q)

    def steps(self):
        na = self.net.p.na
        for distance in range(na - 1, -1, -1):
            self.relay(distance)
            yield
        for distance in range(na - 1, 0, -1):
            self.pass_on(distance)
            yield
        self.arrive()
        yield

    def finish(self):
        p = self.net.p
        self.sends.finish(self.x.at[pl.ds(0, (p.members + p.na * (p.nb - 1)) * self.net.half), :])


class Spread:
    def __init__(self, net, pack, w, columns, block_sems, cross_sems):
        self.net, self.pack, self.w, self.columns = net, pack, w, columns
        self.block_sems, self.cross_sems = block_sems, cross_sems
        self.height = pack.shape[1]
        self.sends = Sends(net)
        self.sent, self.received = 1, 1

    def here(self, seq):
        return self.w.at[pl.ds(pl.multiple_of(seq * self.height, self.height), self.height), self.columns]

    def start(self):
        net, p = self.net, self.net.p
        block = self.pack.at[p.member, :, self.columns]
        self.sends.send(block, self.here(p.seq), self.cross_sems.at[p.member], net.partner())
        self.here(p.seq)[...] = block[...]

    def send(self, count=None):
        p = self.net.p
        last = p.members if count is None else min(p.members, self.sent + count)
        for k in range(self.sent, last):
            member = flip(p.member, k)
            block = self.pack.at[member, :, self.columns]
            self.sends.send(block, self.here(p.seq), self.block_sems.at[p.member], p.device(member))
        self.sent = last

    def receive(self, count=None):
        net, p = self.net, self.net.p
        last = p.members if count is None else min(p.members, self.received + count)
        for k in range(self.received, last):
            member = flip(p.member, k)
            here = self.here(member * p.rows + p.row)
            wait_for(net, here, self.block_sems.at[member])
            self.sends.send(here, here, self.cross_sems.at[member], net.partner())
        self.received = last

    def settle(self):
        net, p = self.net, self.net.p
        for k in range(p.members):
            member = flip(p.member, k)
            wait_for(net, self.here(member * p.rows + 1 - p.row), self.cross_sems.at[member])

    def finish(self):
        size = (2 * self.net.p.members - 1) * self.height
        self.sends.finish(self.w.at[pl.ds(0, size), self.columns])


class Collect:
    def __init__(self, net, dw, grad, columns, cross_buf, block_out, cross_sems, block_sems):
        self.net, self.dw, self.grad, self.columns = net, dw, grad, columns
        self.cross_buf, self.block_out = cross_buf, block_out
        self.cross_sems, self.block_sems = cross_sems, block_sems
        self.height = grad.shape[1]
        self.sends = Sends(net)
        self.pending = self.order()

    def at(self, seq):
        return self.dw.at[pl.ds(pl.multiple_of(seq * self.height, self.height), self.height), self.columns]

    def order(self):
        return list(range(self.net.p.members - 1, -1, -1))

    def offer(self, k):
        net, p = self.net, self.net.p
        for j in range(p.nb - 1, -1, -1):
            member = net.a_of(k) * p.nb + net.b_of(j)
            self.sends.send(
                self.at(member * p.rows + 1 - p.row),
                self.cross_buf.at[member, :, self.columns],
                self.cross_sems.at[member],
                net.partner(),
            )

    def relay(self, count=None):
        net, p = self.net, self.net.p
        for k in self.pending[:count]:
            member = flip(p.member, k)
            landed = self.cross_buf.at[member, :, self.columns]
            wait_for(net, landed, self.cross_sems.at[member])
            mine = self.at(member * p.rows + p.row)[...]
            total = (mine.astype(f32) + landed[...].astype(f32)).astype(bf16)
            if k:
                block = self.block_out.at[member, :, self.columns]
                block[...] = total
                target = self.grad.at[p.member, :, self.columns]
                self.sends.send(block, target, self.block_sems.at[p.member], p.device(member))
            else:
                self.grad[member, :, self.columns] = total
        self.pending = self.pending[count:] if count is not None else []

    def settle(self):
        squares = jnp.zeros((1, 1), f32)
        for k in [0] + self.order()[:-1]:
            member = flip(self.net.p.member, k)
            if k:
                wait_for(self.net, self.grad.at[member, :, self.columns], self.block_sems.at[member])
            block = self.grad[member, :, self.columns].astype(f32)
            squares = squares + jnp.sum(block * block, axis=(0, 1), keepdims=True)
        return squares

    def finish(self):
        size = (2 * self.net.p.members - 1) * self.height
        self.sends.finish(self.dw.at[pl.ds(0, size), self.columns])


def advance(steps, count=1):
    for _ in range(count):
        next(steps, None)


def drain(steps):
    for _ in steps:
        pass


class Layer:
    def __init__(self, r, layer):
        self.r, self.layer = r, layer
        self.length, self.width = getattr(r, "h%d" % layer).shape
        self.f = 4 * HEAD
        self.ff = (getattr(r, "w%d" % layer).shape[1] - self.f) // 2

    def __getattr__(self, name):
        return getattr(self.r, name + str(self.layer))

    def project(self, rows):
        r, f = self.r, self.f
        h = self.h[rows, :]
        mixed = dot(h, self.w[:, :f])
        qk = mixed[:, : 2 * HEAD]
        qk = qk * r.cos[rows, :] + swap_lanes(qk) * r.sin[rows, :]
        self.q[rows, :] = (qk[:, :HEAD].astype(bf16).astype(f32) * HEAD**-0.5).astype(bf16)
        self.k[rows, :] = qk[:, HEAD:].astype(bf16)
        self.v[rows, :] = mixed[:, 2 * HEAD : 3 * HEAD].astype(bf16)

    def feed(self, rows):
        z = dot(self.h[rows, :], self.w[:, self.f : self.f + self.ff])
        self.z[rows, :] = z
        self.a[rows, :] = gelu(z).astype(bf16)

    def attend(self, i):
        r = self.r
        start, keys = i * TILE, (i + 1) * TILE
        rows = pl.ds(start, TILE)
        scores = dot_nt(self.q[rows, :], self.k[:keys, :])
        seen = visible(start, keys, r.segc[rows, :], r.segr[:, :keys])
        scores = jnp.where(seen, scores, low_score)
        peak = jnp.max(scores, axis=1, keepdims=True)
        weights = jnp.exp(scores - peak)
        total = jnp.sum(weights, axis=1, keepdims=True)
        self.lse[rows, :] = peak + jnp.log(total)
        shares = (weights * (1.0 / total)).astype(bf16)
        self.o[rows, :] = dot(shares, self.v[:keys, :]).astype(bf16)

    def branch(self, rows, part):
        f, ff = self.f, self.ff
        out = dot_nt(self.o[rows, :], self.w[:, 3 * HEAD : f])
        out = out + dot_nt(self.a[rows, :], self.w[:, f + ff : f + 2 * ff])
        part[rows, :] = out.astype(bf16)

    def feed_back(self, rows):
        r, f, ff = self.r, self.f, self.ff
        g = self.g[rows, :]
        da = dot(g, self.w[:, f + ff : f + 2 * ff])
        r.dz[rows, :] = (da * gelu_slope(self.z[rows, :])).astype(bf16)
        r.do[rows, :] = dot(g, self.w[:, :f])[:, 3 * HEAD :].astype(bf16)

    def attend_back(self, i):
        r = self.r
        start, keys = i * TILE, (i + 1) * TILE
        rows = pl.ds(start, TILE)
        q, head_grad = self.q[rows, :], r.do[rows, :]
        scores = dot_nt(q, self.k[:keys, :])
        seen = visible(start, keys, r.segc[rows, :], r.segr[:, :keys])
        shares = jnp.where(seen, jnp.exp(scores - self.lse[rows, :]), 0.0)
        share_grads = dot_nt(head_grad, self.v[:keys, :])
        delta = jnp.sum(shares * share_grads, axis=1, keepdims=True)
        score_grads = (shares * (share_grads - delta)).astype(bf16)
        r.dq[rows, :] = dot(score_grads, self.k[:keys, :]) * HEAD**-0.5
        dk = dot_tn(score_grads, q)
        dv = dot_tn(shares.astype(bf16), head_grad)
        if i + 1 == self.length // TILE:
            r.dk[:keys, :] = dk
            r.dv[:keys, :] = dv
        else:
            r.dk[:keys, :] += dk
            r.dv[:keys, :] += dv

    def inward(self, rows, part):
        r, f, ff = self.r, self.f, self.ff
        qk = jnp.concatenate([r.dq[rows, :], r.dk[rows, :]], axis=1)
        qk = qk * r.cos[rows, :] + swap_lanes(qk * r.sin[rows, :])
        rest = jnp.concatenate([r.dv[rows, :], jnp.zeros((TILE, HEAD), f32)], axis=1)
        mix = jnp.concatenate([qk, rest], axis=1).astype(bf16)
        r.mix[rows, :] = mix
        out = dot_nt(mix, self.w[:, :f]) + dot_nt(r.dz[rows, :], self.w[:, f : f + ff])
        part[rows, :] = out.astype(bf16)

    def head_grads(self, rows):
        r, f = self.r, self.f
        mixed = dot_tn(self.h[:, rows], r.mix[...])
        out = dot_tn(self.g[:, rows], self.o[...])
        self.dw[rows, :f] = jnp.concatenate([mixed[:, : 3 * HEAD], out], axis=1).astype(bf16)

    def feed_grads(self, rows):
        r, f, ff = self.r, self.f, self.ff
        self.dw[rows, f : f + ff] = dot_tn(self.h[:, rows], r.dz[...]).astype(bf16)
        self.dw[rows, f + ff : f + 2 * ff] = dot_tn(self.g[:, rows], self.a[...]).astype(bf16)


def norm_row(r, layer, kind):
    return r.norms[layer * 3 + kind : layer * 3 + kind + 1, :]


def column_sums(values):
    return jnp.sum(values, axis=0, keepdims=True)


def cross_rows(net, r):
    p = net.p
    same = p.core == p.row

    def crossing(i):
        source, landing = ((r.act, r.x0), (r.cot, r.gr1))[i]
        return pltpu.make_async_remote_copy(
            src_ref=source.at[1 - p.row],
            dst_ref=landing,
            send_sem=r.x_sems.at[i],
            recv_sem=r.x_sems.at[2 + i],
            device_id=net.partner(),
            device_id_type=MESH,
        )

    def start(i):
        @pl.when(same)
        def _():
            crossing(i).start()
            if i:
                r.gr1[...] = r.cot[p.row]
            else:
                r.x0[...] = r.act[p.row]

    def arrive(i):
        @pl.when(jnp.logical_not(same))
        def _():
            crossing(i).wait_recv()

    def finish():
        @pl.when(same)
        def _():
            crossing(0).wait_send()
            crossing(1).wait_send()

    return (start, arrive, finish)


def give_back(net, r, i, source, target):
    p = net.p
    same = p.core == p.row

    def copy(j, device, row):
        return pltpu.make_async_remote_copy(
            src_ref=source,
            dst_ref=target.at[row],
            send_sem=r.back_sems.at[i, j],
            recv_sem=r.back_sems.at[i, 2 + row],
            device_id=device,
            device_id_type=MESH,
        )

    def far(j):
        return copy(j, p.device(p.member, row=1 - p.row, core=lax.rem(p.core + j, 2)), p.row)

    @pl.when(same)
    def _():
        copy(0, net.sibling, p.row).start()
        target[p.row] = source[...]

    @pl.when(jnp.logical_not(same))
    def _():
        far(0).start()
        far(1).start()

    def finish():
        @pl.when(same)
        def _():
            copy(0, net.sibling, p.row).wait_send()

        @pl.when(jnp.logical_not(same))
        def _():
            far(0).wait_send()
            far(1).wait_send()
            copy(0, net.sibling, p.row).wait_recv()

        copy(0, net.sibling, 1 - p.row).wait_recv()

    return finish


def share_all(net, sem, out, source):
    p = net.p
    here = p.seq * 2 + p.core
    others = [
        (lax.rem(p.seq + i, p.n), lax.rem(p.core + j, 2)) for i in range(p.n) for j in range(2) if i or j
    ]
    sends = Sends(net)
    for seq, core in others:
        sends.send(source(seq), out.at[here], sem, {"seq": seq, "tp": core})
    whole = out.at[pl.ds(0, len(others))]
    return (lambda: wait_for(net, whole, sem), lambda: sends.finish(whole))


def position_tables(net, r):
    p = net.p
    span = r.act.shape[1]
    lines = []
    for kind in range(2):
        row = LAYERS * 3 + kind * p.rows + p.row
        pieces = [r.table[s, pl.ds(row, 1), :span] for s in range(p.n)]
        lines.append(jnp.concatenate(pieces, axis=1))
    positions, segments = lines
    r.segr[...] = segments
    pair = lax.broadcasted_iota(jnp.int32, (ROTARY, positions.shape[1]), 0) // 2
    angles = jnp.exp(pair.astype(f32) * (-2.0 * math.log(10000.0) / ROTARY)) * positions
    sign = jnp.where(lax.broadcasted_iota(jnp.int32, angles.shape, 0) % 2 == 0, -1.0, 1.0)
    ones = jnp.ones((HEAD - ROTARY, angles.shape[1]), f32)
    cosine, sine = jnp.cos(angles), jnp.sin(angles) * sign
    cosine = jnp.concatenate([cosine, ones, cosine, ones], axis=0)
    sine = jnp.concatenate([sine, ones * 0.0, sine, ones * 0.0], axis=0)
    segments = jnp.broadcast_to(segments, (128, segments.shape[1]))
    for t in range(angles.shape[1] // 128):
        block = slice(t * 128, (t + 1) * 128)
        r.cos[block, :] = cosine[:, block].T
        r.sin[block, :] = sine[:, block].T
        r.segc[block, :] = segments[:, block].T[:, :1]


def pack_layer(r, layer):
    members, ff = r.pack.shape[1], (r.pack.shape[3] - 4 * HEAD) // 2
    f = 4 * HEAD
    for pair in range(members // 2):
        lanes = slice(pair * 2 * HEAD, (pair + 1) * 2 * HEAD)
        kinds = [r.qkv[layer, kind, :, lanes].astype(bf16) for kind in range(3)]
        kinds.append(r.out[layer, :, lanes].astype(bf16))
        for i in range(2):
            own = slice(i * HEAD, (i + 1) * HEAD)
            r.pack[layer, 2 * pair + i, :, :f] = jnp.concatenate([kind[:, own] for kind in kinds], axis=1)
    for member in range(members):
        lanes = slice(member * ff, (member + 1) * ff)
        r.pack[layer, member, :, f : f + ff] = getattr(r, "in")[layer, :, lanes].astype(bf16)
        r.pack[layer, member, :, f + ff :] = r.down[layer, :, lanes].astype(bf16)


def pack_small(r):
    rows, span = r.pos.shape
    r.small[...] = jnp.zeros_like(r.small)
    columns = r.norm.shape[2]
    for layer in range(LAYERS):
        r.small[layer * 3 : layer * 3 + 3, :columns] = r.norm[:, layer, :].astype(bf16).astype(f32)
    r.small[LAYERS * 3 : LAYERS * 3 + rows, :span] = r.pos[...].astype(f32)
    r.small[LAYERS * 3 + rows : LAYERS * 3 + 2 * rows, :span] = r.seg[...].astype(f32)


def whole_part(net, r):
    p = net.p
    n, width = p.n, r.act.shape[2]
    finishes = []

    def pack_first():
        pack_small(r)
        pack_layer(r, 0)

    greet(net.everyone(), pack_first)
    gathers = [Gather(net, r.gather_a), Gather(net, r.gather_b)]
    reduces = [
        Reduce(net, r.part_a, r.total_a, r.bufs_a, r.reduce_a),
        Reduce(net, r.part_b, r.total_b, r.bufs_b, r.reduce_b),
    ]
    table_sends = Sends(net)
    finishes.append(lambda: table_sends.finish(r.table.at[pl.ds(0, n - 1)]))
    for i in range(1, n):
        device = {"seq": lax.rem(p.seq + i, n), "tp": p.core}
        table_sends.send(r.small, r.table.at[p.seq], r.table_sem, device)
    r.table[p.seq] = r.small[...]
    cross_start, cross_arrive, cross_finish = cross_rows(net, r)
    finishes.append(cross_finish)
    cross_start(0)
    f = 4 * HEAD
    ff = (r.w0.shape[1] - f) // 2
    early, late = slice(0, f + ff), slice(f + ff, f + 2 * ff)
    heads, feeds = slice(0, f), slice(f, f + 2 * ff)
    spreads = [
        [
            Spread(net, r.pack.at[k], (r.w0, r.w1)[k], columns, r.block_sems.at[k, i], r.cross_sems.at[k, i])
            for i, columns in enumerate((early, late))
        ]
        for k in range(LAYERS)
    ]
    collects = [
        [
            Collect(
                net,
                (r.dw0, r.dw1)[k],
                r.grads.at[k],
                columns,
                r.cross_buf.at[k],
                r.block_out.at[k],
                r.collect_sems.at[k, i],
                r.block_sems.at[k, i],
            )
            for i, columns in enumerate((feeds, heads))
        ]
        for k in range(LAYERS)
    ]
    finishes.extend(collect.finish for pair in collects for collect in pair)
    first, second = spreads[0]
    first.start()
    first.send(3)
    wait_for(net, r.table.at[pl.ds(0, n - 1)], r.table_sem)
    own_columns = width // n
    many = 128 // own_columns
    for s in range(0, n, many):
        r.norms[:, s * own_columns : (s + many) * own_columns] = jnp.concatenate(
            [r.table[s + i, 0:8, :own_columns] for i in range(many)], axis=1
        )
    cross_arrive(0)
    xhat, inverse = layer_norm(r.x0[...])
    normed = xhat * norm_row(r, 0, 0) + norm_row(r, 0, 1)
    r.h0[net.own(), :] = normed.astype(bf16)
    gather = gathers[0]
    gather.start(r.h0)
    position_tables(net, r)

    layer = Layer(r, 0)
    tiles = range(layer.length // TILE)
    gather_steps = gather.steps()
    advance(gather_steps)
    first.send()
    first.receive(3)
    advance(gather_steps)
    pack_layer(r, 1)
    advance(gather_steps)
    first.receive(2)
    advance(gather_steps)
    first.receive()
    drain(gather_steps)
    second.start()
    second.send()
    cross_start(1)
    first.settle()
    for k in tiles:
        layer.project(net.tile(k))
        layer.feed(net.tile(k))
    second.receive()
    first, third = spreads[1]
    first.start()
    first.send()
    for i in tiles:
        layer.attend(i)
    second.settle()
    reduce = reduces[0]
    for a in net.far_first():
        layer.branch(net.tile_rows(a), r.part_a)
        reduce.offer(a)
    steps = reduce.steps()
    advance(steps, p.na + 1)
    first.receive(3)
    drain(steps)
    middle = r.x0[...] + (r.total_a[...] + norm_row(r, 0, 2))
    r.x1[...] = middle
    xhat, inverse = layer_norm(middle)
    normed = xhat * norm_row(r, 1, 0) + norm_row(r, 1, 1)
    r.h1[net.own(), :] = normed.astype(bf16)
    gathers[0].finish()
    gather = gathers[1]
    gather.start(r.h1)
    third.start()
    third.send()

    layer = Layer(r, 1)
    gather_steps = gather.steps()
    advance(gather_steps)
    first.receive()
    advance(gather_steps, 2)
    cross_arrive(1)
    r.g1[net.own(), :] = r.gr1[...].astype(bf16)
    advance(gather_steps)
    grad_gather = gathers[0]
    grad_gather.start(r.g1)
    first.settle()
    for k in tiles:
        layer.project(net.tile(k))
        layer.feed(net.tile(k))
        advance(gather_steps)
    drain(gather_steps)
    third.receive()
    grad_steps = grad_gather.steps()
    advance(grad_steps)
    for i in tiles:
        layer.attend(i)
        advance(grad_steps)
    third.settle()
    forward_reduce = reduces[1]
    forward_steps = forward_reduce.steps()
    for a in net.far_first():
        layer.branch(net.tile_rows(a), r.part_b)
        forward_reduce.offer(a)
    drain(grad_steps)
    advance(forward_steps, p.na)

    fed, headed = collects[1]
    for k in tiles:
        layer.feed_back(net.tile(k))
    for i in reversed(tiles):
        layer.attend_back(i)
    reduce = reduces[0]
    reduce.finish()
    for spread in spreads[0] + spreads[1]:
        spread.finish()
    steps = reduce.steps()
    for a in net.far_first():
        layer.inward(net.tile_rows(a), r.part_a)
        reduce.offer(a)
    advance(steps, p.na)
    for k in range(p.na - 1, -1, -1):
        layer.feed_grads(net.width_rows(k, layer.width))
        fed.offer(k)
    advance(forward_steps, p.na - 1)
    for k in range(p.na - 1, -1, -1):
        layer.head_grads(net.width_rows(k, layer.width))
        headed.offer(k)
        if k:
            advance(steps)
    drain(steps)
    xhat, inverse = layer_norm(r.x1[...])
    normed_grads = r.total_a[...]
    below = norm_back(r.gr1[...], normed_grads, xhat, inverse, norm_row(r, 1, 0))
    r.gr0[...] = below
    r.g0[net.own(), :] = below.astype(bf16)
    gather = gathers[1]
    gather.finish()
    gather.start(r.g0)
    r.sums1[...] = jnp.concatenate(
        [
            column_sums(normed_grads * xhat),
            column_sums(normed_grads),
            column_sums(r.gr1[...]),
            jnp.zeros((5, layer.width), f32),
        ]
    )
    drain(forward_steps)
    r.result[...] = r.x1[...] + (r.total_b[...] + norm_row(r, 1, 2))

    layer = Layer(r, 0)
    gather_steps = gather.steps()
    advance(gather_steps, 2)
    for k in tiles:
        advance(gather_steps)
        if k == 1:
            fed.relay()
        layer.feed_back(net.tile(k))
    drain(gather_steps)
    fed.relay()
    finishes.append(give_back(net, r, 0, r.result, r.results))
    fed_0, headed_0 = collects[0]
    for k in range(p.na - 1, -1, -1):
        layer.feed_grads(net.width_rows(k, layer.width))
        fed_0.offer(k)
    headed.relay(4)
    for i in reversed(tiles):
        layer.attend_back(i)
    headed.relay()
    reduce = forward_reduce
    reduce.finish()
    steps = reduce.steps()
    for a in net.far_first():
        layer.inward(net.tile_rows(a), r.part_b)
        reduce.offer(a)
    advance(steps, p.na)
    for k in range(p.na - 1, -1, -1):
        layer.head_grads(net.width_rows(k, layer.width))
        headed_0.offer(k)
        if k:
            advance(steps)
            fed_0.relay(2)
    drain(steps)
    fed_0.relay()
    normed_grads = r.total_b[...]
    xhat, inverse = layer_norm(r.x0[...])
    rows = [
        column_sums(normed_grads * xhat),
        column_sums(normed_grads),
        column_sums(r.gr0[...]),
        r.sums1[0:3, :],
        jnp.zeros((2, width), f32),
    ]
    rows = jnp.concatenate(rows)
    for s in range(n):
        r.small_out[s] = pad_lanes(rows[:, s * own_columns : (s + 1) * own_columns])
    here = p.seq * 2 + p.core
    small_arrive, small_finish = share_all(net, r.small_sem, r.small_in, lambda seq: r.small_out.at[seq])
    finishes.append(small_finish)
    r.small_in[here] = r.small_out[p.seq]
    headed_0.relay()
    r.in_grad[...] = norm_back(r.gr0[...], normed_grads, xhat, inverse, norm_row(r, 0, 0))
    finishes.append(give_back(net, r, 1, r.in_grad, r.in_grads))
    squares = fed.settle() + headed.settle()
    small_arrive()
    norm_grads = jnp.sum(r.small_in[...], axis=0)
    r.norm_grads[...] = norm_grads
    squares = squares + 0.5 * jnp.sum(norm_grads * norm_grads, axis=(0, 1), keepdims=True)
    squares = squares + (fed_0.settle() + headed_0.settle())
    r.squares[here] = jnp.broadcast_to(squares, (8, 128))
    square_arrive, square_finish = share_all(net, r.square_sem, r.squares, lambda seq: r.squares.at[here])
    finishes.append(square_finish)
    square_arrive()
    r.norm_out[...] = jnp.sqrt(jnp.sum(r.squares[...], axis=0))
    for part in gathers + reduces:
        part.finish()
    for finish in finishes:
        finish()


def fused_call(name, part, geometry, ins, outs, scratch, collective_id):
    flat, places = [], []
    for key, spec in scratch.items():
        group = spec if isinstance(spec, tuple) else (spec,)
        places.append((key, len(flat), len(group), isinstance(spec, tuple)))
        flat.extend(group)

    def kernel(*refs):
        r = types.SimpleNamespace(**dict(zip([*ins, *outs], refs)))
        rest = refs[len(ins) + len(outs) :]
        for key, start, count, grouped in places:
            setattr(r, key, rest[start : start + count] if grouped else rest[start])
        part(Net(*geometry, r.send_sems), r)

    results = pl.pallas_call(
        kernel,
        out_shape=tuple(outs.values()),
        in_specs=vmem_specs(len(ins)),
        out_specs=tuple(vmem_specs(len(outs))),
        scratch_shapes=flat,
        compiler_params=remote_params(collective_id),
        name=name,
    )(*ins.values())
    return types.SimpleNamespace(**dict(zip(outs, results)))


def by_kind(array):
    return jnp.swapaxes(array, array.ndim - 3, array.ndim - 2)


def optimizer_kernel(limit, grads_ref, norm_grads_ref, norm_ref, result_ref, in_grad_ref, *refs):
    weights, firsts, seconds = refs[:5], refs[5:10], refs[10:15]
    new_weights, new_firsts, new_seconds = refs[15:20], refs[20:25], refs[25:30]
    bias_ref, total_ref, result_out_ref, in_grad_out_ref = refs[30:]
    result_out_ref[...] = result_ref[...]
    in_grad_out_ref[...] = in_grad_ref[...]
    norm = norm_ref[0:1, 0:1]
    factor = jnp.minimum(1.0, limit / (norm + 1e-06))
    members, ff = grads_ref.shape[1], (grads_ref.shape[3] - 4 * HEAD) // 2
    f = 4 * HEAD

    def update(kind, where, gradient, rate, decay):
        found = adam_update(
            weights[kind][where], firsts[kind][where], seconds[kind][where], gradient, factor, rate, decay
        )
        for ref, value in zip((new_weights[kind], new_firsts[kind], new_seconds[kind]), found):
            ref[where] = value

    blocks = [grads_ref[0, member].astype(f32) for member in range(members)]
    for part in range(4):
        lanes = slice(part * HEAD, (part + 1) * HEAD)
        gradient = jnp.concatenate([block[:, lanes] for block in blocks], axis=1)
        if part < 3:
            update(0, (0, part), gradient, rate_matrix, decay_matrix)
        else:
            update(1, (0,), gradient, rate_output, decay_matrix)
    for member in range(members):
        lanes = slice(member * ff, (member + 1) * ff)
        update(2, (0, slice(None), lanes), blocks[member][:, f : f + ff], rate_matrix, decay_matrix)
        update(3, (0, slice(None), lanes), blocks[member][:, f + ff :], rate_matrix, decay_matrix)

    @pl.when((pl.program_id(0) == 0) & (pl.program_id(1) == 0))
    def _():
        columns = weights[4].shape[2]
        for layer in range(LAYERS):
            gradient = norm_grads_ref[layer * 3 : layer * 3 + 3, :columns]
            update(4, (slice(None), layer), gradient, rate_vector, 0.0)
            bias_ref[layer : layer + 1, :] = gradient[2:3, :] * factor
        total_ref[...] = norm


def optimizer(found, weights, firsts, seconds, parameters):
    layers, height = weights[1].shape[:2]
    rows = height
    grads = found.grads

    def spec(array):
        extent = array.shape
        if extent[0] == 3:
            return pl.BlockSpec(extent, lambda i, j: (0, 0, 0))
        if array.ndim == 4:
            return pl.BlockSpec((1, 3, rows, extent[3]), lambda i, j: (i, 0, j, 0))
        return pl.BlockSpec((1, rows * extent[1] // height, extent[2]), lambda i, j: (i, j, 0))

    def fixed(*extent):
        return pl.BlockSpec(extent, lambda i, j: (0,) * len(extent))

    arrays = [by_kind(array) if i % 5 in (0, 4) else array for i, array in enumerate(weights + firsts + seconds)]
    tokens = [found.results, found.in_grads]
    bias_shape = (layers, weights[4].shape[2])
    made = pl.pallas_call(
        functools.partial(optimizer_kernel, clip_share * math.sqrt(parameters)),
        grid=(layers, height // rows),
        in_specs=[
            pl.BlockSpec((1, grads.shape[1], rows, grads.shape[3]), lambda i, j: (i, 0, j, 0)),
            fixed(8, 128),
            fixed(8, 128),
        ]
        + [spec(array) for array in tokens + arrays],
        out_specs=tuple(
            [spec(array) for array in arrays]
            + [fixed(*bias_shape), fixed(1, 1)]
            + [spec(array) for array in tokens]
        ),
        out_shape=tuple(
            [jax.ShapeDtypeStruct(array.shape, array.dtype) for array in arrays]
            + [jax.ShapeDtypeStruct(bias_shape, f32), jax.ShapeDtypeStruct((1, 1), f32)]
            + [jax.ShapeDtypeStruct(array.shape, array.dtype) for array in tokens]
        ),
        compiler_params=pltpu.CompilerParams(vmem_limit_bytes=56 * megabyte),
        name="optimizer",
    )(grads, found.norm_grads, found.norm_out, *tokens, *arrays)
    count = len(arrays)
    updated = [by_kind(array) if i % 5 in (0, 4) else array for i, array in enumerate(made[:count])]
    bias, norm, result, in_grad = made[count:]
    return (result, in_grad, norm.reshape(()), *updated, bias)


def shards_together(
    n,
    activations,
    cotangent,
    segment_ids,
    position_ids,
    qkv_weight,
    out_weight,
    in_weight,
    down_weight,
    norm_params,
    qkv_first,
    out_first,
    in_first,
    down_first,
    norm_first,
    qkv_second,
    out_second,
    in_second,
    down_second,
    norm_second,
):
    rows, span, width = activations.shape
    members = n // rows
    na, nb = split_sizes(members)
    length = n * span
    half = rows * span // 2
    pieces = 2
    heads = qkv_weight.shape[3] // HEAD
    ff = in_weight.shape[2] // members
    height = width // n
    columns = 4 * HEAD + 2 * ff
    geometry = (n, rows, half, pieces)

    def shape(*extent, kind=f32):
        return jax.ShapeDtypeStruct(extent, kind)

    def scratch_like(shapes, suffix):
        return {key + suffix: VM(value.shape, value.dtype) for key, value in shapes.items()}

    gather_sems = (DMA((na, pieces)), DMA((members, pieces)), DMA((na, pieces)))
    reduce_sems = (DMA((members, pieces)), DMA((members, pieces)), DMA((2 * na, pieces)))
    reduce_bufs = tuple(
        VM((count * half, width), bf16) for count in (members, members, members, 2 * na, 2 * na)
    ) + (VM((half, width), f32),)
    kept = dict(
        q=shape(length, HEAD, kind=bf16),
        k=shape(length, HEAD, kind=bf16),
        v=shape(length, HEAD, kind=bf16),
        o=shape(length, HEAD, kind=bf16),
        lse=shape(length, 1),
        a=shape(length, ff, kind=bf16),
        z=shape(length, ff),
        w=shape(width, columns, kind=bf16),
        dw=shape(width, columns, kind=bf16),
        h=shape(length, width, kind=bf16),
        g=shape(length, width, kind=bf16),
        x=shape(half, width),
        gr=shape(half, width),
    )
    lines = LAYERS * 3 + 2 * rows
    three = fused_call(
        "whole_part",
        whole_part,
        geometry,
        {
            "act": activations,
            "cot": cotangent,
            "seg": segment_ids,
            "pos": position_ids,
            "qkv": by_kind(qkv_weight),
            "out": out_weight,
            "in": in_weight,
            "down": down_weight,
            "norm": by_kind(norm_params),
        },
        dict(
            results=shape(rows, span, width),
            in_grads=shape(rows, span, width),
            grads=shape(LAYERS, members, height, columns, kind=bf16),
            norm_grads=shape(8, 128),
            norm_out=shape(8, 128),
        ),
        dict(
            small=VM((-(-lines // 8) * 8, 128), f32),
            table=VM((n, -(-lines // 8) * 8, 128), f32),
            pack=VM((LAYERS, members, height, columns), bf16),
            norms=VM((8, width), f32),
            cos=VM((length, 128), f32),
            sin=VM((length, 128), f32),
            segc=VM((length, 1), f32),
            segr=VM((1, length), f32),
            **scratch_like(kept, "0"),
            **scratch_like(kept, "1"),
            dz=VM((length, ff), bf16),
            do=VM((length, HEAD), bf16),
            dq=VM((length, HEAD), f32),
            dk=VM((length, HEAD), f32),
            dv=VM((length, HEAD), f32),
            mix=VM((length, 4 * HEAD), bf16),
            part_a=VM((length, width), bf16),
            part_b=VM((length, width), bf16),
            total_a=VM((half, width), f32),
            total_b=VM((half, width), f32),
            bufs_a=reduce_bufs,
            bufs_b=reduce_bufs,
            result=VM((half, width), f32),
            in_grad=VM((half, width), f32),
            sums1=VM((8, width), f32),
            cross_buf=VM((LAYERS, members, height, columns), bf16),
            block_out=VM((LAYERS, members, height, columns), bf16),
            small_out=VM((n, 8, 128), f32),
            small_in=VM((2 * n, 8, 128), f32),
            squares=VM((2 * n, 8, 128), f32),
            reduce_a=reduce_sems,
            reduce_b=reduce_sems,
            gather_a=gather_sems,
            gather_b=gather_sems,
            x_sems=DMA((4,)),
            back_sems=DMA((2, 4)),
            table_sem=DMA,
            small_sem=DMA,
            square_sem=DMA,
            block_sems=DMA((LAYERS, 2, members)),
            cross_sems=DMA((LAYERS, 2, members)),
            collect_sems=DMA((LAYERS, 2, members)),
            send_sems=DMA((2 * (1 + 2 * pieces * na) + 2 * (1 + 2 * pieces * (na - 1)) + 11,)),
        ),
        0,
    )
    return optimizer(
        three,
        (qkv_weight, out_weight, in_weight, down_weight, norm_params),
        (qkv_first, out_first, in_first, down_first, norm_first),
        (qkv_second, out_second, in_second, down_second, norm_second),
        LAYERS * width * (4 * 2 * heads * HEAD + 2 * 2 * members * ff + 3),
    )


def shards(n, activations, *others):
    rows, span, width = activations.shape
    together = 12 * n * span * width * 2 <= 40 * megabyte and rows == 2 and n * span % TILE == 0
    return (shards_together if together else shards_apart)(n, activations, *others)


def solution(mesh):
    tokens = P(None, "seq", None)
    qkv = P(None, "seq", None, "tp")
    matrix = P(None, "seq", "tp")
    norm = P(None, None, "seq")
    kinds = (qkv, matrix, matrix, matrix, norm)
    return jax.shard_map(
        functools.partial(shards, mesh.shape["seq"]),
        mesh=mesh,
        in_specs=(tokens, tokens, P(None, "seq"), P(None, "seq")) + kinds * 3,
        out_specs=(tokens, tokens, P()) + kinds * 3 + (P(None, "seq"),),
        check_vma=False,
    )
```
